32 devices in a mesh: rows: 16 (over z, y, x), cols: 2 (over core).
Axes of the slice: x: 2, y: 2, z: 4, core: 2. Of those that a mesh axis runs over, the one named last changes fastest.
Arguments:
- sketch: bfloat16 [131072, 256], P(('rows', 'cols')), may hold values from -6 to 6
- blocks: bfloat16 [256, 256, 256], P(('rows', 'cols')), may hold values from -0.375 to 0.375
- block_rows: int32 [256], P(('rows', 'cols')), may hold values from 0 to 3, as said below
- block_cols: int32 [256], P(('rows', 'cols')), may hold values from 0 to 255
- counts: int32 [32], P(('rows', 'cols')), may hold values from 1 to 8, as said below
Outputs:
- basis: float32 [16384, 256], P(('rows', 'cols'))
- factor: float32 [256, 256], replicated
The draws below stay inside these ranges and needn't reach their ends.
Inputs may be any that keep to these rules, and one draw needn't show every extreme that they name: Within one device's 8 slots the pairs (block_rows, block_cols) are distinct. `counts`: some device has exactly 8 live slots.
All inputs are finite; a program needn't handle non-finite values.
Results may differ from the reference program's by a relative error of at most 0.0003.
Values may be sent and summed in bfloat16 or wider, within the bound.
No kernel may reach another device: no remote copies, remote signals or barrier semaphores. Data moves between devices by JAX's collectives and lax.ppermute only.
A program may use at most 64 MiB of HBM per device.

```python
import jax
import jax.numpy as jnp
from jax import lax

V = 131072
BS = 256
K = 256
RB = 4
BLK = 8
M = 16384
PB = 256
N_ROWS = 16
N_COLS = 2


def positions(key):
    devices = N_ROWS * N_COLS
    keys = jax.random.split(jax.random.fold_in(key, 11), devices)
    picked = jax.vmap(lambda single: jax.random.permutation(single, RB * PB)[:BLK])(keys)
    return picked.reshape(devices * BLK).astype(jnp.int32)


def draw_block_rows(key, part):
    return (positions(key) // PB).astype(jnp.int32)


def draw_block_cols(key, part):
    return (positions(key) % PB).astype(jnp.int32)


def draw_counts(key, part):
    devices = N_ROWS * N_COLS
    first = jax.random.randint(jax.random.fold_in(key, 21), (devices,), 0, BLK)
    second = jax.random.randint(jax.random.fold_in(key, 22), (devices,), 0, BLK)
    busiest = jax.random.randint(jax.random.fold_in(key, 23), (), 0, devices)
    loads = 1 + jnp.minimum(first, second)
    return jnp.where(jnp.arange(devices, dtype=jnp.int32) == busiest, BLK, loads).astype(jnp.int32)


def levels(rng, shape, cuts, smallest, largest):
    factor_of, own = 1.0, jax.random.fold_in(rng, 6)
    for dim, shards_of in cuts:
        draws = jnp.exp(jax.random.uniform(jax.random.fold_in(own, dim), (shards_of,), jnp.float32, smallest / len(cuts), largest / len(cuts)))
        factor_of = factor_of * jnp.repeat(draws, shape[dim] // shards_of).reshape([-1 if axis == dim else 1 for axis in range(len(shape))])
    return factor_of


def bell_draw(stream_key, dims, deviation, reach, cuts=(), kind=jnp.bfloat16):
    drawn = deviation * jax.random.normal(stream_key, dims, jnp.float32)
    if cuts:
        drawn = drawn * levels(stream_key, dims, cuts, -0.22, 0.18)
    return jnp.clip(drawn, -reach, reach).astype(kind)


def setup_inputs(seed: int = 0) -> dict:
    seeds = jax.random.split(jax.random.key(seed), 6)
    return {
        "sketch": bell_draw(seeds[0], (V, K), 1.0, 6.0, ((0, 32),)),
        "blocks": bell_draw(seeds[1], (N_ROWS * N_COLS * BLK, BS, BS), BS ** -0.5, 0.375, ((0, 32),)),
        "block_rows": draw_block_rows(jax.random.fold_in(seeds[5], 71), 0),
        "block_cols": draw_block_cols(jax.random.fold_in(seeds[5], 71), 0),
        "counts": draw_counts(jax.random.fold_in(seeds[5], 71), 0),
    }


def reference(sketch, blocks, block_rows, block_cols, counts):
    group_rows = V // (N_ROWS * N_COLS)
    highest = lax.Precision.HIGHEST

    def slab_rows(row_index):

        def add_panel(column, total):
            device = row_index * N_COLS + column
            tiles = lax.dynamic_slice_in_dim(blocks, device * BLK, BLK, 0).astype(jnp.float32)
            row_ids = lax.dynamic_slice_in_dim(block_rows, device * BLK, BLK, 0)
            col_ids = lax.dynamic_slice_in_dim(block_cols, device * BLK, BLK, 0)
            live_count = lax.dynamic_index_in_dim(counts, device, 0, keepdims=False)
            offsets = (col_ids * BS // group_rows * N_COLS + column) * group_rows + col_ids * BS % group_rows
            chosen = jax.vmap(lambda offset: lax.dynamic_slice_in_dim(sketch, offset.astype(jnp.int32), BS, 0))(offsets)
            products = jnp.einsum('bij,bjk->bik', tiles, chosen.astype(jnp.float32), precision=highest)
            selector = ((row_ids[:, None] == jnp.arange(RB, dtype=jnp.int32)[None, :]) & (jnp.arange(BLK, dtype=jnp.int32) < live_count)[:, None]).astype(jnp.float32)
            return total + jnp.einsum('br,bik->rik', selector, products, precision=highest)
        return lax.fori_loop(0, N_COLS, add_panel, jnp.zeros((RB, BS, K), jnp.float32))
    sketched = lax.map(slab_rows, jnp.arange(N_ROWS, dtype=jnp.int32)).reshape(M, K)
    gram_matrix = jnp.dot(sketched.T, sketched, precision=highest)
    lower_factor = jnp.linalg.cholesky(gram_matrix)
    root_rows = jnp.sqrt(jnp.float32(M))
    solved = lax.linalg.triangular_solve(lower_factor, sketched, left_side=False, lower=True, transpose_a=True)
    return (solved * root_rows, lower_factor.T / root_rows)
```

```python
import functools

import jax
import jax.numpy as jnp
from jax import lax
from jax.experimental import pallas as pl
from jax.experimental.pallas import tpu as pltpu
from jax.sharding import PartitionSpec as P

RB = 4
HIGHEST = lax.Precision.HIGHEST
VMEM = pl.BlockSpec(memory_space=pltpu.VMEM)
SMEM = pl.BlockSpec(memory_space=pltpu.SMEM)
MIB = 1024 * 1024


def pick_kernel(index_ref, stripes_ref, out_ref):
    def body(i, carry):
        out_ref[i] = stripes_ref[index_ref[i]]
        return carry

    lax.fori_loop(0, out_ref.shape[0], body, 0, unroll=8)


def pick(indices, stripes):
    count = indices.shape[0]
    _, height, columns = stripes.shape
    return pl.pallas_call(
        pick_kernel,
        out_shape=jax.ShapeDtypeStruct((count, height, columns), stripes.dtype),
        in_specs=[SMEM, VMEM],
        out_specs=VMEM,
        compiler_params=pltpu.CompilerParams(vmem_limit_bytes=24 * MIB),
        name="pick_stripes",
    )(indices, stripes)


def product_kernel(rows_ref, counts_ref, blocks_ref, chosen_ref, out_ref):
    slots, width, _ = blocks_ref.shape
    columns = out_ref.shape[1]
    out_ref[...] = jnp.zeros_like(out_ref)
    for s in range(slots):

        @pl.when(s < counts_ref[0])
        def _():
            piece = chosen_ref[:, s].reshape(width, columns)
            product = jnp.dot(blocks_ref[s], piece, preferred_element_type=jnp.float32)
            at = pl.ds(pl.multiple_of(rows_ref[s] * width, width), width)
            out_ref[at, :] += product


def block_products(block_rows, counts, blocks, chosen):
    _, width, _ = blocks.shape
    columns = chosen.shape[-1]
    return pl.pallas_call(
        product_kernel,
        out_shape=jax.ShapeDtypeStruct((RB * width, columns), jnp.float32),
        in_specs=[SMEM, SMEM, VMEM, VMEM],
        out_specs=VMEM,
        compiler_params=pltpu.CompilerParams(vmem_limit_bytes=24 * MIB),
        name="block_products",
    )(block_rows, counts, blocks, chosen)


def gram_kernel(kept_ref, other_ref, total_ref, gram_ref):
    total = kept_ref[...] + other_ref[...]
    total_ref[...] = total
    gram_ref[...] = lax.dot_general(
        total, total, (((0,), (0,)), ((), ())), precision=HIGHEST, preferred_element_type=jnp.float32
    )


def sum_and_gram(kept, other):
    rows, columns = kept.shape
    return pl.pallas_call(
        gram_kernel,
        out_shape=(
            jax.ShapeDtypeStruct((rows, columns), jnp.float32),
            jax.ShapeDtypeStruct((columns, columns), jnp.float32),
        ),
        in_specs=[VMEM, VMEM],
        out_specs=(VMEM, VMEM),
        compiler_params=pltpu.CompilerParams(vmem_limit_bytes=24 * MIB),
        name="sum_and_gram",
    )(kept, other)


def matmul(a, b, precision):
    return jnp.dot(a, b, precision=precision, preferred_element_type=jnp.float32)


def matmul_nt(a, b, precision):
    return lax.dot_general(
        a, b, (((1,), (1,)), ((), ())), precision=precision, preferred_element_type=jnp.float32
    )


def factor_kernel(total_rows, gram_ref, own_ref, basis_ref, factor_ref, scaled, inverse):
    n = gram_ref.shape[0]
    row_ids = lax.broadcasted_iota(jnp.int32, (n, n), 0)
    col_ids = lax.broadcasted_iota(jnp.int32, (n, n), 1)
    diagonal = row_ids == col_ids
    identity = diagonal.astype(jnp.float32)
    half = jnp.where(row_ids > col_ids, 1.0, jnp.where(diagonal, 0.5, 0.0))
    gram = gram_ref[...]
    on_diagonal = jnp.where(diagonal, gram, 0.0)
    down = jnp.sqrt(jnp.sum(on_diagonal, axis=1, keepdims=True))
    across = jnp.sqrt(jnp.sum(on_diagonal, axis=0, keepdims=True))
    up_down = 1.0 / down
    up_across = 1.0 / across
    scaled[...] = gram * up_down * up_across

    def refine(precision):
        w = inverse[...]
        residual = matmul_nt(matmul(w, scaled[...], precision), w, precision) - identity
        inverse[...] = w - matmul(residual * half, w, precision)
        return jnp.sum(residual * residual)

    inverse[...] = identity - (scaled[...] - identity) * half
    refine(lax.Precision.DEFAULT)

    def going(state):
        step, size = state
        return (step < 8) & (size > 1e-6)

    def advance(state):
        return state[0] + 1, refine(HIGHEST)

    _, size = lax.while_loop(going, advance, (jnp.int32(0), jnp.float32(1.0)))

    @pl.when(jnp.logical_not(size <= 1e-6))
    def _():
        inverse[...] = identity
        ids = lax.broadcasted_iota(jnp.int32, (n, 1), 0)

        def eliminate(j, carry):
            pivot_row = scaled[pl.ds(j, 1), :]
            inverse_row = inverse[pl.ds(j, 1), :]
            column = jnp.sum(jnp.where(col_ids == j, scaled[...], 0.0), axis=1, keepdims=True)
            pivot = jnp.sum(jnp.where(ids == j, column, 0.0), axis=0, keepdims=True)
            root = 1.0 / jnp.sqrt(pivot)
            ratio = jnp.where(ids > j, column / pivot, jnp.where(ids == j, 1.0 - root, 0.0))
            scaled[...] = scaled[...] - ratio * pivot_row
            inverse[...] = inverse[...] - ratio * inverse_row
            return carry

        lax.fori_loop(0, n, eliminate, 0)
        scaled[...] = gram_ref[...] * up_down * up_across

    w = inverse[...]
    root_rows = jnp.sqrt(jnp.float32(total_rows))
    upper = matmul(w, scaled[...], HIGHEST) * across / root_rows
    factor_ref[...] = jnp.where(row_ids <= col_ids, upper, 0.0)
    basis_ref[...] = matmul_nt(own_ref[...] * up_across, w, HIGHEST) * root_rows


def factor_and_basis(total_rows, gram, own):
    columns = gram.shape[0]
    return pl.pallas_call(
        functools.partial(factor_kernel, total_rows),
        out_shape=(
            jax.ShapeDtypeStruct(own.shape, jnp.float32),
            jax.ShapeDtypeStruct((columns, columns), jnp.float32),
        ),
        in_specs=[VMEM, VMEM],
        out_specs=(VMEM, VMEM),
        scratch_shapes=[pltpu.VMEM((columns, columns), jnp.float32)] * 2,
        compiler_params=pltpu.CompilerParams(vmem_limit_bytes=24 * MIB),
        name="factor_and_basis",
    )(gram, own)


def sum_everywhere(gram, axes, devices):
    columns = gram.shape[0]
    if columns % devices:
        return lax.psum(gram, axes)
    pieces = gram.reshape(devices, columns // devices, columns)
    pieces = lax.all_to_all(pieces, axes, split_axis=0, concat_axis=0, tiled=True)
    return lax.all_gather(jnp.sum(pieces, axis=0), axes, axis=0, tiled=True)


def local(sketch, blocks, block_rows, block_cols, counts):
    slots, width, _ = blocks.shape
    columns = sketch.shape[1]
    rows = lax.axis_size("rows")
    cols = lax.axis_size("cols")
    height = width // rows
    stripes = sketch.reshape(-1, rows, height, columns).swapaxes(0, 1)
    stripes = lax.all_to_all(stripes, "rows", split_axis=0, concat_axis=0, tiled=True)
    stripes = stripes.reshape(-1, height, columns)
    wanted = lax.all_gather(block_cols, "rows", axis=0, tiled=True)
    sent = pick(wanted, stripes).reshape(rows, slots, height, columns)
    chosen = lax.all_to_all(sent, "rows", split_axis=0, concat_axis=0, tiled=True)
    if height % 16:
        chosen = chosen.swapaxes(0, 1).reshape(1, slots, width, columns)
    partial_rows = block_products(block_rows, counts, blocks, chosen)
    share = RB * width // cols
    me = lax.axis_index("cols")
    if cols == 2:
        kept = lax.dynamic_slice_in_dim(partial_rows, me * share, share, 0)
        given = lax.dynamic_slice_in_dim(partial_rows, (1 - me) * share, share, 0)
        other = lax.ppermute(given, "cols", [(0, 1), (1, 0)])
    else:
        kept = lax.psum_scatter(partial_rows, "cols", scatter_dimension=0, tiled=True)
        other = jnp.zeros_like(kept)
    own, gram = sum_and_gram(kept, other)
    gram = sum_everywhere(gram, ("rows", "cols"), rows * cols)
    return factor_and_basis(RB * width * rows, gram, own)


def solution(mesh):
    in_specs = (
        P(("rows", "cols"), None),
        P(("rows", "cols"), None, None),
        P(("rows", "cols")),
        P(("rows", "cols")),
        P(("rows", "cols")),
    )
    out_specs = (P(("rows", "cols"), None), P())
    return jax.shard_map(local, mesh=mesh, in_specs=in_specs, out_specs=out_specs, check_vma=False)
```

```python
import functools

import jax
import jax.numpy as jnp
from jax import lax
from jax.experimental import pallas as pl
from jax.experimental.pallas import tpu as pltpu
from jax.sharding import PartitionSpec as P

RB = 4
HIGHEST = lax.Precision.HIGHEST
VMEM = pl.BlockSpec(memory_space=pltpu.VMEM)
SMEM = pl.BlockSpec(memory_space=pltpu.SMEM)
MIB = 1024 * 1024


KEPT = 8


def plan_kernel(per, table_ref, places_ref, kept_ref, most_ref):
    devices = table_ref.shape[0]
    slots = places_ref.shape[1]
    panel = per * lax.axis_size("rows")
    cols = lax.axis_size("cols")
    table = table_ref[...]
    block = lax.broadcasted_iota(jnp.int32, (devices, panel), 1)
    device = lax.broadcasted_iota(jnp.int32, (devices, panel), 0)
    asked = [(table[:, s : s + 1] == block) & (s < table[:, slots : slots + 1]) for s in range(slots)]
    some = functools.reduce(jnp.logical_or, asked)
    first = lax.broadcasted_iota(jnp.int32, (panel, panel), 0)
    second = lax.broadcasted_iota(jnp.int32, (panel, panel), 1)
    before = (first // per == second // per) & (first < second)
    before = jnp.where(before, 1.0, 0.0).astype(jnp.bfloat16)
    touched = [
        jnp.max(jnp.where(some & (device % cols == c), 1.0, 0.0), axis=0, keepdims=True) for c in range(cols)
    ]
    line = lax.broadcasted_iota(jnp.int32, (8, panel), 0)
    touched = sum(jnp.where(line == c, touched[c], 0.0) for c in range(cols))
    rank = jnp.dot(touched.astype(jnp.bfloat16), before, preferred_element_type=jnp.float32)
    most = jnp.max(rank + touched, axis=(0, 1), keepdims=True)
    most_ref[...] = jnp.broadcast_to(most, most_ref.shape).astype(jnp.int32)
    here = line == lax.axis_index("cols")
    touched = jnp.max(jnp.where(here, touched, 0.0), axis=0, keepdims=True)
    rank = jnp.max(jnp.where(here, rank, 0.0), axis=0, keepdims=True)
    ids = lax.broadcasted_iota(jnp.int32, (1, panel), 1)
    place = (ids // per * KEPT).astype(jnp.float32) + rank
    slot = lax.broadcasted_iota(jnp.int32, places_ref.shape, 1)
    places = jnp.zeros(places_ref.shape, jnp.float32)
    for s in range(slots):
        found = jnp.sum(jnp.where(asked[s], place, 0.0), axis=1, keepdims=True)
        places = jnp.where(slot == s, found, places)
    places_ref[...] = jnp.minimum(places.astype(jnp.int32), panel // per * KEPT - 1)
    mine = (touched > 0.5) & (ids // per == lax.axis_index("rows"))
    wanted_rank = lax.broadcasted_iota(jnp.int32, (KEPT, panel), 0).astype(jnp.float32)
    chosen = jnp.where(mine & (rank == wanted_rank), (ids % per).astype(jnp.float32), 0.0)
    chosen = jnp.sum(chosen, axis=1, keepdims=True).astype(jnp.int32)
    kept_ref[...] = jnp.broadcast_to(chosen, kept_ref.shape)


def plan(table, slots, per):
    devices = table.shape[0]
    return pl.pallas_call(
        functools.partial(plan_kernel, per),
        out_shape=(
            jax.ShapeDtypeStruct((devices, slots), jnp.int32),
            jax.ShapeDtypeStruct((KEPT, 128), jnp.int32),
            jax.ShapeDtypeStruct((8, 128), jnp.int32),
        ),
        in_specs=[VMEM],
        out_specs=(VMEM, VMEM, VMEM),
        name="plan",
    )(table)


def keep_kernel(kept_ref, sketch_ref, out_ref):
    for k in range(out_ref.shape[1]):
        out_ref[:, k] = sketch_ref[kept_ref[k]]


def keep(kept, sketch):
    _, rows, height, columns = sketch.shape
    return pl.pallas_call(
        keep_kernel,
        out_shape=jax.ShapeDtypeStruct((rows, KEPT, height, columns), sketch.dtype),
        in_specs=[SMEM, VMEM],
        out_specs=VMEM,
        compiler_params=pltpu.CompilerParams(vmem_limit_bytes=24 * MIB),
        name="keep_blocks",
    )(kept, sketch)


def pick_kernel(places_ref, stripes_ref, out_ref):
    slots = out_ref.shape[1]

    def body(r, carry):
        for s in range(slots):
            out_ref[r, s] = stripes_ref[places_ref[r, s]]
        return carry

    lax.fori_loop(0, out_ref.shape[0], body, 0)


def pick(places, stripes):
    _, height, columns = stripes.shape
    return pl.pallas_call(
        pick_kernel,
        out_shape=jax.ShapeDtypeStruct((*places.shape, height, columns), stripes.dtype),
        in_specs=[SMEM, VMEM],
        out_specs=VMEM,
        compiler_params=pltpu.CompilerParams(vmem_limit_bytes=24 * MIB),
        name="pick_stripes",
    )(places, stripes)


def product_kernel(rows_ref, counts_ref, blocks_ref, chosen_ref, out_ref):
    slots, width, _ = blocks_ref.shape
    columns = out_ref.shape[1]
    out_ref[...] = jnp.zeros_like(out_ref)
    for s in range(slots):

        @pl.when(s < counts_ref[0])
        def _():
            piece = chosen_ref[:, s].reshape(width, columns)
            product = jnp.dot(blocks_ref[s], piece, preferred_element_type=jnp.float32)
            at = pl.ds(pl.multiple_of(rows_ref[s] * width, width), width)
            out_ref[at, :] += product


def block_products(block_rows, counts, blocks, chosen):
    _, width, _ = blocks.shape
    columns = chosen.shape[-1]
    return pl.pallas_call(
        product_kernel,
        out_shape=jax.ShapeDtypeStruct((RB * width, columns), jnp.float32),
        in_specs=[SMEM, SMEM, VMEM, VMEM],
        out_specs=VMEM,
        compiler_params=pltpu.CompilerParams(vmem_limit_bytes=24 * MIB),
        name="block_products",
    )(block_rows, counts, blocks, chosen)


def gram_kernel(kept_ref, other_ref, total_ref, gram_ref):
    total = kept_ref[...] + other_ref[...]
    total_ref[...] = total
    gram_ref[...] = lax.dot_general(
        total, total, (((0,), (0,)), ((), ())), precision=HIGHEST, preferred_element_type=jnp.float32
    )


def sum_and_gram(kept, other):
    rows, columns = kept.shape
    return pl.pallas_call(
        gram_kernel,
        out_shape=(
            jax.ShapeDtypeStruct((rows, columns), jnp.float32),
            jax.ShapeDtypeStruct((columns, columns), jnp.float32),
        ),
        in_specs=[VMEM, VMEM],
        out_specs=(VMEM, VMEM),
        compiler_params=pltpu.CompilerParams(vmem_limit_bytes=24 * MIB),
        name="sum_and_gram",
    )(kept, other)


def matmul(a, b, precision):
    return jnp.dot(a, b, precision=precision, preferred_element_type=jnp.float32)


def matmul_nt(a, b, precision):
    return lax.dot_general(
        a, b, (((1,), (1,)), ((), ())), precision=precision, preferred_element_type=jnp.float32
    )


def factor_kernel(total_rows, gram_ref, own_ref, basis_ref, factor_ref, scaled, inverse):
    n = gram_ref.shape[0]
    row_ids = lax.broadcasted_iota(jnp.int32, (n, n), 0)
    col_ids = lax.broadcasted_iota(jnp.int32, (n, n), 1)
    diagonal = row_ids == col_ids
    identity = diagonal.astype(jnp.float32)
    half = jnp.where(row_ids > col_ids, 1.0, jnp.where(diagonal, 0.5, 0.0))
    gram = gram_ref[...]
    on_diagonal = jnp.where(diagonal, gram, 0.0)
    down = jnp.sqrt(jnp.sum(on_diagonal, axis=1, keepdims=True))
    across = jnp.sqrt(jnp.sum(on_diagonal, axis=0, keepdims=True))
    up_down = 1.0 / down
    up_across = 1.0 / across
    scaled[...] = gram * up_down * up_across

    def refine(precision):
        w = inverse[...]
        residual = matmul_nt(matmul(w, scaled[...], precision), w, precision) - identity
        inverse[...] = w - matmul(residual * half, w, precision)
        return jnp.sum(residual * residual)

    inverse[...] = identity - (scaled[...] - identity) * half
    refine(lax.Precision.DEFAULT)

    def going(state):
        step, size = state
        return (step < 8) & (size > 1e-6)

    def advance(state):
        return state[0] + 1, refine(HIGHEST)

    _, size = lax.while_loop(going, advance, (jnp.int32(0), jnp.float32(1.0)))

    @pl.when(jnp.logical_not(size <= 1e-6))
    def _():
        inverse[...] = identity
        ids = lax.broadcasted_iota(jnp.int32, (n, 1), 0)

        def eliminate(j, carry):
            pivot_row = scaled[pl.ds(j, 1), :]
            inverse_row = inverse[pl.ds(j, 1), :]
            column = jnp.sum(jnp.where(col_ids == j, scaled[...], 0.0), axis=1, keepdims=True)
            pivot = jnp.sum(jnp.where(ids == j, column, 0.0), axis=0, keepdims=True)
            root = 1.0 / jnp.sqrt(pivot)
            ratio = jnp.where(ids > j, column / pivot, jnp.where(ids == j, 1.0 - root, 0.0))
            scaled[...] = scaled[...] - ratio * pivot_row
            inverse[...] = inverse[...] - ratio * inverse_row
            return carry

        lax.fori_loop(0, n, eliminate, 0)
        scaled[...] = gram_ref[...] * up_down * up_across

    w = inverse[...]
    root_rows = jnp.sqrt(jnp.float32(total_rows))
    upper = matmul(w, scaled[...], HIGHEST) * across / root_rows
    factor_ref[...] = jnp.where(row_ids <= col_ids, upper, 0.0)
    basis_ref[...] = matmul_nt(own_ref[...] * up_across, w, HIGHEST) * root_rows


def factor_and_basis(total_rows, gram, own):
    columns = gram.shape[0]
    return pl.pallas_call(
        functools.partial(factor_kernel, total_rows),
        out_shape=(
            jax.ShapeDtypeStruct(own.shape, jnp.float32),
            jax.ShapeDtypeStruct((columns, columns), jnp.float32),
        ),
        in_specs=[VMEM, VMEM],
        out_specs=(VMEM, VMEM),
        scratch_shapes=[pltpu.VMEM((columns, columns), jnp.float32)] * 2,
        compiler_params=pltpu.CompilerParams(vmem_limit_bytes=24 * MIB),
        name="factor_and_basis",
    )(gram, own)


def sum_everywhere(gram, axes, devices):
    columns = gram.shape[0]
    if columns % devices:
        return lax.psum(gram, axes)
    pieces = gram.reshape(devices, columns // devices, columns)
    pieces = lax.all_to_all(pieces, axes, split_axis=0, concat_axis=0, tiled=True)
    return spread(jnp.sum(pieces, axis=0), axes, devices).reshape(columns, columns)


def spread(piece, axes, devices):
    copies = jnp.broadcast_to(piece[None], (devices, *piece.shape))
    return lax.all_to_all(copies, axes, split_axis=0, concat_axis=0, tiled=True)


def turn(stripes):
    stripes = lax.all_to_all(stripes, "rows", split_axis=0, concat_axis=0, tiled=True)
    return stripes.reshape(-1, *stripes.shape[2:])


def stripes_for_panel(sketch, block_cols, counts, slots, rows, cols):
    per = sketch.shape[0]
    if per <= KEPT:
        wanted = lax.all_gather(block_cols, "rows", axis=0, tiled=False)
        return pick(wanted, turn(sketch.swapaxes(0, 1)))
    devices = rows * cols
    line = jnp.concatenate([block_cols, counts, jnp.zeros((7,), jnp.int32)])
    table = spread(line, ("rows", "cols"), devices)
    places, kept, most = plan(table, slots, per)

    def mine(values):
        values = values.reshape(rows, cols, -1)
        return lax.dynamic_index_in_dim(values, lax.axis_index("cols"), 1, keepdims=False)

    def some():
        return pick(mine(places), turn(keep(kept[:, 0], sketch)))

    def every():
        return pick(mine(table)[:, :slots], turn(sketch.swapaxes(0, 1)))

    return lax.cond(most[0, 0] <= KEPT, some, every)


def local(sketch, blocks, block_rows, block_cols, counts):
    slots, width, _ = blocks.shape
    columns = sketch.shape[1]
    rows = lax.axis_size("rows")
    cols = lax.axis_size("cols")
    height = width // rows
    sketch = sketch.reshape(-1, rows, height, columns)
    sent = stripes_for_panel(sketch, block_cols, counts, slots, rows, cols)
    chosen = lax.all_to_all(sent, "rows", split_axis=0, concat_axis=0, tiled=True)
    if height % 16:
        chosen = chosen.swapaxes(0, 1).reshape(1, slots, width, columns)
    partial_rows = block_products(block_rows, counts, blocks, chosen)
    share = RB * width // cols
    me = lax.axis_index("cols")
    if cols == 2:
        kept = lax.dynamic_slice_in_dim(partial_rows, me * share, share, 0)
        given = lax.dynamic_slice_in_dim(partial_rows, (1 - me) * share, share, 0)
        other = lax.ppermute(given, "cols", [(0, 1), (1, 0)])
    else:
        kept = lax.psum_scatter(partial_rows, "cols", scatter_dimension=0, tiled=True)
        other = jnp.zeros_like(kept)
    own, gram = sum_and_gram(kept, other)
    gram = sum_everywhere(gram, ("rows", "cols"), rows * cols)
    return factor_and_basis(RB * width * rows, gram, own)


def solution(mesh):
    in_specs = (
        P(("rows", "cols"), None),
        P(("rows", "cols"), None, None),
        P(("rows", "cols")),
        P(("rows", "cols")),
        P(("rows", "cols")),
    )
    out_specs = (P(("rows", "cols"), None), P())
    return jax.shard_map(local, mesh=mesh, in_specs=in_specs, out_specs=out_specs, check_vma=False)
```

```python
import functools

import jax
import jax.numpy as jnp
from jax import lax
from jax.experimental import pallas as pl
from jax.experimental.pallas import tpu as pltpu
from jax.sharding import PartitionSpec as P

RB = 4
HIGHEST = lax.Precision.HIGHEST
VMEM = pl.BlockSpec(memory_space=pltpu.VMEM)
SMEM = pl.BlockSpec(memory_space=pltpu.SMEM)
MIB = 1024 * 1024


LEVELS = (16, 24)


def cut_kernel(sketch_ref, out_ref, sems):
    copies = [
        pltpu.make_async_copy(sketch_ref.at[:, j], out_ref.at[j], sems.at[j]) for j in range(out_ref.shape[0])
    ]
    for copy in copies:
        copy.start()
    for copy in copies:
        copy.wait()


def cut(sketch):
    blocks, pieces, height, columns = sketch.shape
    return pl.pallas_call(
        cut_kernel,
        out_shape=jax.ShapeDtypeStruct((pieces, blocks, height, columns), sketch.dtype),
        in_specs=[pl.BlockSpec(memory_space=pl.ANY)],
        out_specs=pl.BlockSpec(memory_space=pl.ANY),
        scratch_shapes=[pltpu.SemaphoreType.DMA((pieces,))],
        name="cut_stripes",
    )(sketch)


def plan_kernel(per, table_ref, places_ref, list_ref, most_ref):
    devices = table_ref.shape[0]
    slots = places_ref.shape[1]
    rows, cols = lax.axis_size("rows"), lax.axis_size("cols")
    panel = per * rows
    part = panel // 2
    table = table_ref[...]
    block = lax.broadcasted_iota(jnp.int32, (devices, panel), 1)
    device = lax.broadcasted_iota(jnp.int32, (devices, panel), 0)
    asked = [(table[:, s : s + 1] == block) & (s < table[:, slots : slots + 1]) for s in range(slots)]
    some = functools.reduce(jnp.logical_or, asked) & (device // (devices // 2) != block // part)
    lines = -(-2 * cols // 8) * 8
    line = lax.broadcasted_iota(jnp.int32, (lines, panel), 0)
    touched = jnp.zeros((lines, panel), jnp.float32)
    for h in range(2):
        for c in range(cols):
            group = some & (device // (devices // 2) == h) & (device % cols == c)
            found = jnp.max(jnp.where(group, 1.0, 0.0), axis=0, keepdims=True)
            touched = jnp.where(line == h * cols + c, found, touched)
    most = jnp.max(jnp.sum(touched, axis=1, keepdims=True), axis=0, keepdims=True)
    most_ref[...] = jnp.broadcast_to(most, most_ref.shape).astype(jnp.int32)
    touched = touched.astype(jnp.bfloat16)
    first = lax.broadcasted_iota(jnp.int32, (panel, panel), 0)
    second = lax.broadcasted_iota(jnp.int32, (panel, panel), 1)
    after = jnp.where(first > second, 1.0, 0.0).astype(jnp.bfloat16)
    same = jnp.where(first == second, 1.0, 0.0).astype(jnp.bfloat16)
    nt = (((1,), (1,)), ((), ()))
    half = lax.axis_index("rows") // (rows // 2)
    c = lax.axis_index("cols")
    rank = lax.dot_general(touched, after, nt, preferred_element_type=jnp.float32)
    rank = jnp.sum(jnp.where(line == half * cols + c, rank, 0.0), axis=0, keepdims=True)
    ids = lax.broadcasted_iota(jnp.int32, (1, panel), 1)
    place = jnp.where(ids // part == half, ids - half * part, part + rank.astype(jnp.int32))
    slot = lax.broadcasted_iota(jnp.int32, places_ref.shape, 1)
    places = jnp.zeros(places_ref.shape, jnp.int32)
    for s in range(slots):
        found = jnp.sum(jnp.where(asked[s], place, 0), axis=1, keepdims=True)
        places = jnp.where(slot == s, found, places)
    places_ref[...] = places
    line = lax.broadcasted_iota(jnp.int32, (panel, lines), 1)
    mine = line == (1 - half) * cols + c
    there = lax.dot_general(same, touched, nt, preferred_element_type=jnp.float32)
    there = jnp.sum(jnp.where(mine, there, 0.0), axis=1, keepdims=True)
    rank = lax.dot_general(after, touched, nt, preferred_element_type=jnp.float32)
    rank = jnp.sum(jnp.where(mine, rank, 0.0), axis=1, keepdims=True).astype(jnp.int32)
    ids = lax.broadcasted_iota(jnp.int32, (panel, list_ref.shape[1]), 0)
    number = lax.broadcasted_iota(jnp.int32, (panel, list_ref.shape[1]), 1)
    listed = jnp.where((there > 0.5) & (rank == number), ids - half * part, 0)
    list_ref[...] = jnp.broadcast_to(jnp.sum(listed, axis=0, keepdims=True), list_ref.shape)


def plan(table, slots, per):
    devices = table.shape[0]
    return pl.pallas_call(
        functools.partial(plan_kernel, per),
        out_shape=(
            jax.ShapeDtypeStruct((devices, slots), jnp.int32),
            jax.ShapeDtypeStruct((8, 128), jnp.int32),
            jax.ShapeDtypeStruct((8, 128), jnp.int32),
        ),
        in_specs=[VMEM],
        out_specs=(VMEM, VMEM, VMEM),
        name="plan",
    )(table)


def list_kernel(list_ref, stripes_ref, out_ref):
    for k in range(out_ref.shape[0]):
        out_ref[k] = stripes_ref[list_ref[0, k]]


def listed(numbers, stripes, count):
    return pl.pallas_call(
        list_kernel,
        out_shape=jax.ShapeDtypeStruct((count, *stripes.shape[1:]), stripes.dtype),
        in_specs=[SMEM, VMEM],
        out_specs=VMEM,
        compiler_params=pltpu.CompilerParams(vmem_limit_bytes=24 * MIB),
        name="listed_stripes",
    )(numbers, stripes)


def pick_kernel(places_ref, own_ref, other_ref, out_ref):
    members, slots = out_ref.shape[:2]
    rows, cols = lax.axis_size("rows"), lax.axis_size("cols")
    here = own_ref.shape[0]
    half = lax.axis_index("rows") // (rows // 2)
    c = lax.axis_index("cols")

    def body(m, carry):
        device = (half * members + m) * cols + c
        for s in range(slots):
            place = places_ref[device, s]

            @pl.when(place < here)
            def _():
                out_ref[m, s] = own_ref[jnp.minimum(place, here - 1)]

            @pl.when(place >= here)
            def _():
                out_ref[m, s] = other_ref[jnp.clip(place - here, 0, other_ref.shape[0] - 1)]

        return carry

    lax.fori_loop(0, members, body, 0)


def pick(places, own, other, members):
    return pl.pallas_call(
        pick_kernel,
        out_shape=jax.ShapeDtypeStruct((members, places.shape[1], *own.shape[1:]), own.dtype),
        in_specs=[SMEM, VMEM, VMEM],
        out_specs=VMEM,
        compiler_params=pltpu.CompilerParams(vmem_limit_bytes=24 * MIB),
        name="pick_stripes",
    )(places, own, other)


def product_kernel(rows_ref, counts_ref, blocks_ref, chosen_ref, out_ref):
    slots, width, _ = blocks_ref.shape
    columns = out_ref.shape[1]
    out_ref[...] = jnp.zeros_like(out_ref)
    for s in range(slots):

        @pl.when(s < counts_ref[0])
        def _():
            piece = chosen_ref[:, s].reshape(width, columns)
            product = jnp.dot(blocks_ref[s], piece, preferred_element_type=jnp.float32)
            at = pl.ds(pl.multiple_of(rows_ref[s] * width, width), width)
            out_ref[at, :] += product


def block_products(block_rows, counts, blocks, chosen):
    _, width, _ = blocks.shape
    columns = chosen.shape[-1]
    return pl.pallas_call(
        product_kernel,
        out_shape=jax.ShapeDtypeStruct((RB * width, columns), jnp.float32),
        in_specs=[SMEM, SMEM, VMEM, VMEM],
        out_specs=VMEM,
        compiler_params=pltpu.CompilerParams(vmem_limit_bytes=24 * MIB),
        name="block_products",
    )(block_rows, counts, blocks, chosen)


def gram_kernel(mine_ref, other_ref, own_ref, gram_ref, slab):
    c = lax.axis_index("cols")
    share, width = own_ref.shape[0], gram_ref.shape[1]
    slab[...] = mine_ref[...] + other_ref[...]
    own_ref[...] = slab[pl.ds(pl.multiple_of(c * share, share), share), :]
    right = slab[:, pl.ds(pl.multiple_of(c * width, width), width)]
    gram_ref[...] = lax.dot_general(
        slab[...], right, (((0,), (0,)), ((), ())), precision=HIGHEST, preferred_element_type=jnp.float32
    )


def sum_and_gram(mine, other):
    rows, columns = mine.shape
    return pl.pallas_call(
        gram_kernel,
        out_shape=(
            jax.ShapeDtypeStruct((rows // 2, columns), jnp.float32),
            jax.ShapeDtypeStruct((columns, columns // 2), jnp.float32),
        ),
        in_specs=[VMEM, VMEM],
        out_specs=(VMEM, VMEM),
        scratch_shapes=[pltpu.VMEM((rows, columns), jnp.float32)],
        compiler_params=pltpu.CompilerParams(vmem_limit_bytes=24 * MIB),
        name="sum_and_gram",
    )(mine, other)


def matmul(a, b, precision):
    return jnp.dot(a, b, precision=precision, preferred_element_type=jnp.float32)


def matmul_nt(a, b, precision):
    return lax.dot_general(
        a, b, (((1,), (1,)), ((), ())), precision=precision, preferred_element_type=jnp.float32
    )


def factor_kernel(total_rows, gram_ref, own_ref, basis_ref, factor_ref, whole, scaled, inverse):
    n = factor_ref.shape[0]
    width = gram_ref.shape[-1]
    for c in range(n // width):
        whole[:, c * width : (c + 1) * width] = gram_ref[:, c].reshape(n, width)
    row_ids = lax.broadcasted_iota(jnp.int32, (n, n), 0)
    col_ids = lax.broadcasted_iota(jnp.int32, (n, n), 1)
    diagonal = row_ids == col_ids
    identity = diagonal.astype(jnp.float32)
    half = jnp.where(row_ids > col_ids, 1.0, jnp.where(diagonal, 0.5, 0.0))
    gram = whole[...]
    on_diagonal = jnp.where(diagonal, gram, 0.0)
    down = jnp.sqrt(jnp.sum(on_diagonal, axis=1, keepdims=True))
    across = jnp.sqrt(jnp.sum(on_diagonal, axis=0, keepdims=True))
    up_down = 1.0 / down
    up_across = 1.0 / across
    scaled[...] = gram * up_down * up_across

    def refine(precision):
        w = inverse[...]
        residual = matmul_nt(matmul(w, scaled[...], precision), w, precision) - identity
        inverse[...] = w - matmul(residual * half, w, precision)
        return jnp.sum(residual * residual)

    inverse[...] = identity - (scaled[...] - identity) * half
    refine(lax.Precision.DEFAULT)

    def going(state):
        step, size = state
        return (step < 8) & (size > 1e-6)

    def advance(state):
        return state[0] + 1, refine(HIGHEST)

    _, size = lax.while_loop(going, advance, (jnp.int32(0), jnp.float32(1.0)))

    @pl.when(jnp.logical_not(size <= 1e-6))
    def _():
        inverse[...] = identity
        ids = lax.broadcasted_iota(jnp.int32, (n, 1), 0)

        def eliminate(j, carry):
            pivot_row = scaled[pl.ds(j, 1), :]
            inverse_row = inverse[pl.ds(j, 1), :]
            column = jnp.sum(jnp.where(col_ids == j, scaled[...], 0.0), axis=1, keepdims=True)
            pivot = jnp.sum(jnp.where(ids == j, column, 0.0), axis=0, keepdims=True)
            root = 1.0 / jnp.sqrt(pivot)
            ratio = jnp.where(ids > j, column / pivot, jnp.where(ids == j, 1.0 - root, 0.0))
            scaled[...] = scaled[...] - ratio * pivot_row
            inverse[...] = inverse[...] - ratio * inverse_row
            return carry

        lax.fori_loop(0, n, eliminate, 0)
        scaled[...] = whole[...] * up_down * up_across

    w = inverse[...]
    root_rows = jnp.sqrt(jnp.float32(total_rows))
    upper = matmul(w, scaled[...], HIGHEST) * across / root_rows
    factor_ref[...] = jnp.where(row_ids <= col_ids, upper, 0.0)
    basis_ref[...] = matmul_nt(own_ref[...] * up_across, w, HIGHEST) * root_rows


def factor_and_basis(total_rows, gram, own):
    columns = own.shape[1]
    return pl.pallas_call(
        functools.partial(factor_kernel, total_rows),
        out_shape=(
            jax.ShapeDtypeStruct(own.shape, jnp.float32),
            jax.ShapeDtypeStruct((columns, columns), jnp.float32),
        ),
        in_specs=[VMEM, VMEM],
        out_specs=(VMEM, VMEM),
        scratch_shapes=[pltpu.VMEM((columns, columns), jnp.float32)] * 3,
        compiler_params=pltpu.CompilerParams(vmem_limit_bytes=24 * MIB),
        name="factor_and_basis",
    )(gram, own)


def spread(piece, axes, devices):
    copies = jnp.broadcast_to(piece[None], (devices, *piece.shape))
    return lax.all_to_all(copies, axes, split_axis=0, concat_axis=0, tiled=True)


def exchange(pieces, rows):
    groups = [list(range(rows // 2)), list(range(rows // 2, rows))]
    return lax.all_to_all(pieces, "rows", split_axis=0, concat_axis=0, axis_index_groups=groups, tiled=True)


def fetch(sketch, block_cols, counts, slots, width):
    rows, cols = lax.axis_size("rows"), lax.axis_size("cols")
    members = rows // 2
    height = width // members
    columns = sketch.shape[1]
    sketch = sketch.reshape(-1, members, height, columns)
    per = sketch.shape[0]
    stripes = exchange(cut(sketch), rows).reshape(-1, height, columns)
    devices = rows * cols
    line = jnp.concatenate([block_cols, counts, jnp.zeros((7,), jnp.int32)])
    table = spread(line, ("rows", "cols"), devices)
    places, numbers, most = plan(table, slots, per)
    swap = [(r, (r + members) % rows) for r in range(rows)]
    largest = min(per * members, slots * members, 128)

    def with_other(count):
        def run():
            other = lax.ppermute(listed(numbers, stripes, count), "rows", swap)
            return pick(places, stripes, other, members)

        return run

    levels = [level for level in LEVELS if level < largest]
    level = sum((most[0, 0] > level).astype(jnp.int32) for level in levels)
    picked = lax.switch(level, [with_other(count) for count in (*levels, largest)])
    return exchange(picked, rows)


def local(sketch, blocks, block_rows, block_cols, counts):
    slots, width, _ = blocks.shape
    columns = sketch.shape[1]
    rows, cols = lax.axis_size("rows"), lax.axis_size("cols")
    chosen = fetch(sketch, block_cols, counts, slots, width)
    if chosen.shape[2] % 16:
        chosen = chosen.swapaxes(0, 1).reshape(1, slots, width, columns)
    partial_rows = block_products(block_rows, counts, blocks, chosen)
    if cols == 2:
        other = lax.ppermute(partial_rows, "cols", [(0, 1), (1, 0)])
        own, gram = sum_and_gram(partial_rows, other)
        pieces = gram.reshape(rows, -1, columns // 2)
        pieces = lax.all_to_all(pieces, "rows", split_axis=0, concat_axis=0, tiled=True)
        gram = spread(jnp.sum(pieces, axis=0), ("rows", "cols"), rows * cols)
        gram = gram.reshape(rows, cols, -1, columns // 2)
    else:
        own = lax.psum_scatter(partial_rows, "cols", scatter_dimension=0, tiled=True)
        gram = lax.psum(matmul(own.T, own, HIGHEST), ("rows", "cols"))
        gram = gram.reshape(1, 1, columns, columns)
    return factor_and_basis(RB * width * rows, gram, own)


def solution(mesh):
    in_specs = (
        P(("rows", "cols"), None),
        P(("rows", "cols"), None, None),
        P(("rows", "cols")),
        P(("rows", "cols")),
        P(("rows", "cols")),
    )
    out_specs = (P(("rows", "cols"), None), P())
    return jax.shard_map(local, mesh=mesh, in_specs=in_specs, out_specs=out_specs, check_vma=False)
```

```python
import functools

import jax
import jax.numpy as jnp
from jax import lax
from jax.experimental import pallas as pl
from jax.experimental.pallas import tpu as pltpu
from jax.sharding import PartitionSpec as P

RB = 4
HIGHEST = lax.Precision.HIGHEST
VMEM = pl.BlockSpec(memory_space=pltpu.VMEM)
SMEM = pl.BlockSpec(memory_space=pltpu.SMEM)
MIB = 1024 * 1024


LEVELS = (12, 14, 16, 18, 20, 22, 24)


def cut_kernel(cols_ref, counts_ref, sketch_ref, table_ref, *out_refs):
    members = len(out_refs)
    me = lax.axis_index("rows") % members
    for d in range(members):
        out_refs[d][...] = sketch_ref[:, me ^ d]
    lane = lax.broadcasted_iota(jnp.int32, table_ref.shape, 2)
    table = jnp.where(lane == cols_ref.shape[0], counts_ref[0], 0)
    for s in range(cols_ref.shape[0]):
        table = jnp.where(lane == s, cols_ref[s], table)
    table_ref[...] = table


def cut(block_cols, counts, sketch, devices):
    blocks, members, height, columns = sketch.shape
    return pl.pallas_call(
        cut_kernel,
        out_shape=(
            jax.ShapeDtypeStruct((devices, 1, 128), jnp.int32),
            *[jax.ShapeDtypeStruct((blocks, height, columns), sketch.dtype)] * members,
        ),
        in_specs=[SMEM, SMEM, VMEM],
        out_specs=(VMEM,) * (members + 1),
        compiler_params=pltpu.CompilerParams(vmem_limit_bytes=24 * MIB),
        name="cut_stripes",
    )(block_cols, counts, sketch)


def plan_kernel(per, levels, table_ref, places_ref, list_ref, level_ref):
    devices = table_ref.shape[0]
    slots = places_ref.shape[1]
    rows, cols = lax.axis_size("rows"), lax.axis_size("cols")
    panel = per * rows
    part = panel // 2
    table = table_ref[:, 0, :]
    block = lax.broadcasted_iota(jnp.int32, (devices, panel), 1)
    device = lax.broadcasted_iota(jnp.int32, (devices, panel), 0)
    asked = [(table[:, s : s + 1] == block) & (s < table[:, slots : slots + 1]) for s in range(slots)]
    some = functools.reduce(jnp.logical_or, asked) & (device // (devices // 2) != block // part)
    lines = -(-2 * cols // 8) * 8
    line = lax.broadcasted_iota(jnp.int32, (lines, panel), 0)
    touched = jnp.zeros((lines, panel), jnp.float32)
    for h in range(2):
        for c in range(cols):
            group = some & (device // (devices // 2) == h) & (device % cols == c)
            found = jnp.max(jnp.where(group, 1.0, 0.0), axis=0, keepdims=True)
            touched = jnp.where(line == h * cols + c, found, touched)
    most = jnp.max(jnp.sum(touched, axis=1, keepdims=True)).astype(jnp.int32)
    level_ref[0] = sum((most > level).astype(jnp.int32) for level in levels)
    touched = touched.astype(jnp.bfloat16)
    first = lax.broadcasted_iota(jnp.int32, (panel, panel), 0)
    second = lax.broadcasted_iota(jnp.int32, (panel, panel), 1)
    after = jnp.where(first > second, 1.0, 0.0).astype(jnp.bfloat16)
    same = jnp.where(first == second, 1.0, 0.0).astype(jnp.bfloat16)
    nt = (((1,), (1,)), ((), ()))
    half = lax.axis_index("rows") // (rows // 2)
    c = lax.axis_index("cols")
    rank = lax.dot_general(touched, after, nt, preferred_element_type=jnp.float32)
    rank = jnp.sum(jnp.where(line == half * cols + c, rank, 0.0), axis=0, keepdims=True)
    ids = lax.broadcasted_iota(jnp.int32, (1, panel), 1)
    place = jnp.where(ids // part == half, ids - half * part, part + rank.astype(jnp.int32))
    slot = lax.broadcasted_iota(jnp.int32, places_ref.shape, 1)
    places = jnp.zeros(places_ref.shape, jnp.int32)
    for s in range(slots):
        found = jnp.sum(jnp.where(asked[s], place, 0), axis=1, keepdims=True)
        places = jnp.where(slot == s, found, places)
    places_ref[...] = places
    line = lax.broadcasted_iota(jnp.int32, (panel, lines), 1)
    mine = line == (1 - half) * cols + c
    there = lax.dot_general(same, touched, nt, preferred_element_type=jnp.float32)
    there = jnp.sum(jnp.where(mine, there, 0.0), axis=1, keepdims=True)
    rank = lax.dot_general(after, touched, nt, preferred_element_type=jnp.float32)
    rank = jnp.sum(jnp.where(mine, rank, 0.0), axis=1, keepdims=True).astype(jnp.int32)
    ids = lax.broadcasted_iota(jnp.int32, (panel, list_ref.shape[1]), 0)
    number = lax.broadcasted_iota(jnp.int32, (panel, list_ref.shape[1]), 1)
    listed = jnp.where((there > 0.5) & (rank == number), ids - half * part, 0)
    list_ref[...] = jnp.broadcast_to(jnp.sum(listed, axis=0, keepdims=True), list_ref.shape)


def plan(table, slots, per, levels):
    devices = table.shape[0]
    return pl.pallas_call(
        functools.partial(plan_kernel, per, levels),
        out_shape=(
            jax.ShapeDtypeStruct((devices, slots), jnp.int32),
            jax.ShapeDtypeStruct((8, 128), jnp.int32),
            jax.ShapeDtypeStruct((1,), jnp.int32),
        ),
        in_specs=[VMEM],
        out_specs=(VMEM, VMEM, SMEM),
        compiler_params=pltpu.CompilerParams(vmem_limit_bytes=48 * MIB),
        name="plan",
    )(table)


def list_kernel(list_ref, *refs):
    *stripe_refs, out_ref, all_ref = refs
    members = len(stripe_refs)
    me = lax.axis_index("rows") % members
    per = stripe_refs[0].shape[0]
    for d in range(members):
        all_ref[pl.ds((me ^ d) * per, per)] = stripe_refs[d][...]
    for k in range(out_ref.shape[0]):
        out_ref[k] = all_ref[list_ref[0, k]]


def listed(numbers, stripes, count):
    per, height, columns = stripes[0].shape
    return pl.pallas_call(
        list_kernel,
        out_shape=(
            jax.ShapeDtypeStruct((count, height, columns), stripes[0].dtype),
            jax.ShapeDtypeStruct((len(stripes) * per, height, columns), stripes[0].dtype),
        ),
        in_specs=[SMEM] + [VMEM] * len(stripes),
        out_specs=(VMEM, VMEM),
        compiler_params=pltpu.CompilerParams(vmem_limit_bytes=24 * MIB),
        name="listed_stripes",
    )(numbers, *stripes)


def pick_kernel(places_ref, own_ref, other_ref, *out_refs):
    members = len(out_refs)
    rows, cols = lax.axis_size("rows"), lax.axis_size("cols")
    here = own_ref.shape[0]
    me = lax.axis_index("rows")
    c = lax.axis_index("cols")
    for d in range(members):
        out_ref = out_refs[d]
        device = (me ^ d) * cols + c

        def body(s, carry):
            place = places_ref[device, s]

            @pl.when(place < here)
            def _():
                out_ref[s] = own_ref[jnp.minimum(place, here - 1)]

            @pl.when(place >= here)
            def _():
                out_ref[s] = other_ref[jnp.clip(place - here, 0, other_ref.shape[0] - 1)]

            return carry

        lax.fori_loop(0, out_ref.shape[0], body, 0)


def pick(places, own, other, members):
    return pl.pallas_call(
        pick_kernel,
        out_shape=(jax.ShapeDtypeStruct((places.shape[1], *own.shape[1:]), own.dtype),) * members,
        in_specs=[SMEM, VMEM, VMEM],
        out_specs=(VMEM,) * members,
        compiler_params=pltpu.CompilerParams(vmem_limit_bytes=24 * MIB),
        name="pick_stripes",
    )(places, own, other)


def product_kernel(rows_ref, counts_ref, blocks_ref, *refs):
    *chosen_refs, out_ref, whole = refs
    slots, width, _ = blocks_ref.shape
    columns = out_ref.shape[1]
    members = len(chosen_refs)
    me = lax.axis_index("rows") % members
    for d in range(members):
        whole[me ^ d] = chosen_refs[d][...]
    out_ref[...] = jnp.zeros_like(out_ref)
    for s in range(slots):

        @pl.when(s < counts_ref[0])
        def _():
            piece = whole[:, s].reshape(width, columns)
            product = jnp.dot(blocks_ref[s], piece, preferred_element_type=jnp.float32)
            at = pl.ds(pl.multiple_of(rows_ref[s] * width, width), width)
            out_ref[at, :] += product


def block_products(block_rows, counts, blocks, chosen):
    _, width, _ = blocks.shape
    columns = chosen[0].shape[-1]
    return pl.pallas_call(
        product_kernel,
        out_shape=jax.ShapeDtypeStruct((RB * width, columns), jnp.float32),
        in_specs=[SMEM, SMEM, VMEM] + [VMEM] * len(chosen),
        out_specs=VMEM,
        scratch_shapes=[pltpu.VMEM((len(chosen), *chosen[0].shape), chosen[0].dtype)],
        compiler_params=pltpu.CompilerParams(vmem_limit_bytes=24 * MIB),
        name="block_products",
    )(block_rows, counts, blocks, *chosen)


def gram_kernel(mine_ref, other_ref, own_ref, gram_ref, slab):
    c = lax.axis_index("cols")
    share, width = own_ref.shape[0], gram_ref.shape[1]
    slab[...] = mine_ref[...] + other_ref[...]
    own_ref[...] = slab[pl.ds(pl.multiple_of(c * share, share), share), :]
    right = slab[:, pl.ds(pl.multiple_of(c * width, width), width)]
    gram_ref[...] = lax.dot_general(
        slab[...], right, (((0,), (0,)), ((), ())), precision=HIGHEST, preferred_element_type=jnp.float32
    )


def sum_and_gram(mine, other):
    rows, columns = mine.shape
    return pl.pallas_call(
        gram_kernel,
        out_shape=(
            jax.ShapeDtypeStruct((rows // 2, columns), jnp.float32),
            jax.ShapeDtypeStruct((columns, columns // 2), jnp.float32),
        ),
        in_specs=[VMEM, VMEM],
        out_specs=(VMEM, VMEM),
        scratch_shapes=[pltpu.VMEM((rows, columns), jnp.float32)],
        compiler_params=pltpu.CompilerParams(vmem_limit_bytes=24 * MIB),
        name="sum_and_gram",
    )(mine, other)


def matmul(a, b, precision):
    return jnp.dot(a, b, precision=precision, preferred_element_type=jnp.float32)


def matmul_nt(a, b, precision):
    return lax.dot_general(
        a, b, (((1,), (1,)), ((), ())), precision=precision, preferred_element_type=jnp.float32
    )


def factor_kernel(total_rows, gram_ref, own_ref, basis_ref, factor_ref, whole, scaled, inverse):
    n = factor_ref.shape[0]
    width = gram_ref.shape[-1]
    for c in range(n // width):
        whole[:, c * width : (c + 1) * width] = gram_ref[:, c].reshape(n, width)
    row_ids = lax.broadcasted_iota(jnp.int32, (n, n), 0)
    col_ids = lax.broadcasted_iota(jnp.int32, (n, n), 1)
    diagonal = row_ids == col_ids
    identity = diagonal.astype(jnp.float32)
    half = jnp.where(row_ids > col_ids, 1.0, jnp.where(diagonal, 0.5, 0.0))
    gram = whole[...]
    on_diagonal = jnp.where(diagonal, gram, 0.0)
    down = jnp.sqrt(jnp.sum(on_diagonal, axis=1, keepdims=True))
    across = jnp.sqrt(jnp.sum(on_diagonal, axis=0, keepdims=True))
    up_down = 1.0 / down
    up_across = 1.0 / across
    scaled[...] = gram * up_down * up_across

    def refine(precision):
        w = inverse[...]
        residual = matmul_nt(matmul(w, scaled[...], precision), w, precision) - identity
        inverse[...] = w - matmul(residual * half, w, precision)
        return jnp.sum(residual * residual)

    inverse[...] = identity - (scaled[...] - identity) * half
    refine(lax.Precision.DEFAULT)

    def going(state):
        step, size = state
        return (step < 8) & (size > 1e-6)

    def advance(state):
        return state[0] + 1, refine(HIGHEST)

    _, size = lax.while_loop(going, advance, (jnp.int32(0), jnp.float32(1.0)))

    @pl.when(jnp.logical_not(size <= 1e-6))
    def _():
        inverse[...] = identity
        ids = lax.broadcasted_iota(jnp.int32, (n, 1), 0)

        def eliminate(j, carry):
            pivot_row = scaled[pl.ds(j, 1), :]
            inverse_row = inverse[pl.ds(j, 1), :]
            column = jnp.sum(jnp.where(col_ids == j, scaled[...], 0.0), axis=1, keepdims=True)
            pivot = jnp.sum(jnp.where(ids == j, column, 0.0), axis=0, keepdims=True)
            root = 1.0 / jnp.sqrt(pivot)
            ratio = jnp.where(ids > j, column / pivot, jnp.where(ids == j, 1.0 - root, 0.0))
            scaled[...] = scaled[...] - ratio * pivot_row
            inverse[...] = inverse[...] - ratio * inverse_row
            return carry

        lax.fori_loop(0, n, eliminate, 0)
        scaled[...] = whole[...] * up_down * up_across

    w = inverse[...]
    root_rows = jnp.sqrt(jnp.float32(total_rows))
    upper = matmul(w, scaled[...], HIGHEST) * across / root_rows
    factor_ref[...] = jnp.where(row_ids <= col_ids, upper, 0.0)
    basis_ref[...] = matmul_nt(own_ref[...] * up_across, w, HIGHEST) * root_rows


def factor_and_basis(total_rows, gram, own):
    columns = own.shape[1]
    return pl.pallas_call(
        functools.partial(factor_kernel, total_rows),
        out_shape=(
            jax.ShapeDtypeStruct(own.shape, jnp.float32),
            jax.ShapeDtypeStruct((columns, columns), jnp.float32),
        ),
        in_specs=[VMEM, VMEM],
        out_specs=(VMEM, VMEM),
        scratch_shapes=[pltpu.VMEM((columns, columns), jnp.float32)] * 3,
        compiler_params=pltpu.CompilerParams(vmem_limit_bytes=24 * MIB),
        name="factor_and_basis",
    )(gram, own)


def spread(piece, axes, devices):
    copies = jnp.broadcast_to(piece[None], (devices, *piece.shape))
    return lax.all_to_all(copies, axes, split_axis=0, concat_axis=0, tiled=True)


def exchange(pieces, rows):
    return [pieces[0]] + [
        lax.ppermute(piece, "rows", [(r, r ^ d) for r in range(rows)]) for d, piece in enumerate(pieces) if d
    ]


def fetch(sketch, block_cols, counts, slots, width):
    rows, cols = lax.axis_size("rows"), lax.axis_size("cols")
    members = rows // 2
    height = width // members
    columns = sketch.shape[1]
    sketch = sketch.reshape(-1, members, height, columns)
    per = sketch.shape[0]
    devices = rows * cols
    table, *stripes = cut(block_cols, counts, sketch, devices)
    stripes = exchange(stripes, rows)
    table = lax.all_to_all(table, ("rows", "cols"), split_axis=0, concat_axis=0, tiled=True)
    swap = [(r, (r + members) % rows) for r in range(rows)]
    largest = min(per * members, slots * members, 128)
    levels = tuple(level for level in LEVELS if level < largest)
    places, numbers, level = plan(table, slots, per, levels)

    def with_other(count):
        def run():
            sent, own = listed(numbers, stripes, count)
            return pick(places, own, lax.ppermute(sent, "rows", swap), members)

        return run

    picked = lax.switch(level[0], [with_other(count) for count in (*levels, largest)])
    return exchange(picked, rows)


def local(sketch, blocks, block_rows, block_cols, counts):
    slots, width, _ = blocks.shape
    columns = sketch.shape[1]
    rows, cols = lax.axis_size("rows"), lax.axis_size("cols")
    chosen = fetch(sketch, block_cols, counts, slots, width)
    if chosen[0].shape[1] % 16:
        order = lax.axis_index("rows") % len(chosen) ^ jnp.arange(len(chosen))
        chosen = [jnp.stack(chosen)[order].swapaxes(0, 1).reshape(1, slots, width, columns)[0]]
    partial_rows = block_products(block_rows, counts, blocks, chosen)
    if cols == 2:
        other = lax.ppermute(partial_rows, "cols", [(0, 1), (1, 0)])
        own, gram = sum_and_gram(partial_rows, other)
        pieces = gram.reshape(rows, -1, columns // 2)
        pieces = lax.all_to_all(pieces, "rows", split_axis=0, concat_axis=0, tiled=True)
        gram = spread(jnp.sum(pieces, axis=0), ("rows", "cols"), rows * cols)
        gram = gram.reshape(rows, cols, -1, columns // 2)
    else:
        own = lax.psum_scatter(partial_rows, "cols", scatter_dimension=0, tiled=True)
        gram = lax.psum(matmul(own.T, own, HIGHEST), ("rows", "cols"))
        gram = gram.reshape(1, 1, columns, columns)
    return factor_and_basis(RB * width * rows, gram, own)


def solution(mesh):
    in_specs = (
        P(("rows", "cols"), None),
        P(("rows", "cols"), None, None),
        P(("rows", "cols")),
        P(("rows", "cols")),
        P(("rows", "cols")),
    )
    out_specs = (P(("rows", "cols"), None), P())
    return jax.shard_map(local, mesh=mesh, in_specs=in_specs, out_specs=out_specs, check_vma=False)
```

```python
import functools

import jax
import jax.numpy as jnp
from jax import lax
from jax.experimental import pallas as pl
from jax.experimental.pallas import tpu as pltpu
from jax.sharding import PartitionSpec as P

RB = 4
HIGHEST = lax.Precision.HIGHEST
VMEM = pl.BlockSpec(memory_space=pltpu.VMEM)
SMEM = pl.BlockSpec(memory_space=pltpu.SMEM)
MIB = 1024 * 1024


LEVELS = (12, 14, 16, 18, 20, 24)
TABLE_ROWS = 16


def row_kernel(cols_ref, counts_ref, out_ref):
    slots = cols_ref.shape[0]
    rows, cols = lax.axis_size("rows"), lax.axis_size("cols")
    mine = lax.axis_index("rows") // (rows // 2) * cols + lax.axis_index("cols")
    row = lax.broadcasted_iota(jnp.int32, out_ref.shape, 0)
    lane = lax.broadcasted_iota(jnp.int32, out_ref.shape, 1)
    table = jnp.where(lane == slots, counts_ref[0], 0)
    for s in range(slots):
        table = jnp.where(lane == s, cols_ref[s], table)
    out_ref[...] = jnp.where(row == mine, table, 0).astype(jnp.float32).astype(out_ref.dtype)


def table_row(block_cols, counts, columns, dtype):
    return pl.pallas_call(
        row_kernel,
        out_shape=jax.ShapeDtypeStruct((TABLE_ROWS, columns), dtype),
        in_specs=[SMEM, SMEM],
        out_specs=VMEM,
        name="table_row",
    )(block_cols, counts)


def cut_kernel(sketch_ref, here_ref, across_ref, *out_refs):
    members = len(out_refs)
    me = lax.axis_index("rows") % members
    blocks, _, height, columns = sketch_ref.shape
    unit = out_refs[0].shape[1]
    pieces = blocks * height // unit
    table = (here_ref[...].astype(jnp.float32) + across_ref[...].astype(jnp.float32)).astype(here_ref.dtype)
    for d in range(members):
        out_refs[d][:pieces] = sketch_ref[:, me ^ d].reshape(pieces, unit, columns)
        out_refs[d][pieces:] = table.reshape(-1, unit, columns)


def cut(sketch, here, across):
    blocks, members, height, columns = sketch.shape
    unit = min(height, TABLE_ROWS)
    pieces = (blocks * height + TABLE_ROWS) // unit
    return pl.pallas_call(
        cut_kernel,
        out_shape=(jax.ShapeDtypeStruct((pieces, unit, columns), sketch.dtype),) * members,
        in_specs=[VMEM] * 3,
        out_specs=(VMEM,) * members,
        compiler_params=pltpu.CompilerParams(vmem_limit_bytes=24 * MIB),
        name="cut_stripes",
    )(sketch, here, across)


def plan_kernel(levels, *refs):
    *stripe_refs, all_ref, places_ref, list_ref, level_ref = refs
    rows, cols = lax.axis_size("rows"), lax.axis_size("cols")
    members = len(stripe_refs)
    me = lax.axis_index("rows") % members
    half = lax.axis_index("rows") // members
    c = lax.axis_index("cols")
    part, height, columns = all_ref.shape
    per = part // members
    panel = part * 2
    slots = places_ref.shape[1]
    unit = stripe_refs[0].shape[1]
    pieces = per * height // unit
    lines = places_ref.shape[0] // members
    tables = []
    for d in range(members):
        all_ref[pl.ds((me ^ d) * per, per)] = stripe_refs[d][:pieces].reshape(per, height, columns)
        tables.append(stripe_refs[d][pieces:].reshape(TABLE_ROWS, columns).astype(jnp.float32)[:lines])
    table = jnp.concatenate(tables, axis=0).astype(jnp.int32)
    block = lax.broadcasted_iota(jnp.int32, (members * lines, panel), 1)
    line = lax.broadcasted_iota(jnp.int32, (members * lines, panel), 0) % lines
    asked = [(table[:, s : s + 1] == block) & (s < table[:, slots : slots + 1]) for s in range(slots)]
    some = functools.reduce(jnp.logical_or, asked) & (line // cols != block // part)
    some = jnp.where(some, 1.0, 0.0)
    touched = functools.reduce(jnp.maximum, [some[d * lines : (d + 1) * lines] for d in range(members)])
    most = jnp.max(jnp.sum(touched, axis=1, keepdims=True)).astype(jnp.int32)
    level_ref[0] = sum((most > level).astype(jnp.int32) for level in levels)
    touched = touched.astype(jnp.bfloat16)
    first = lax.broadcasted_iota(jnp.int32, (panel, panel), 0)
    second = lax.broadcasted_iota(jnp.int32, (panel, panel), 1)
    after = jnp.where(first > second, 1.0, 0.0).astype(jnp.bfloat16)
    same = jnp.where(first == second, 1.0, 0.0).astype(jnp.bfloat16)
    nt = (((1,), (1,)), ((), ()))
    rank = lax.dot_general(touched, after, nt, preferred_element_type=jnp.float32)
    line = lax.broadcasted_iota(jnp.int32, (lines, panel), 0)
    rank = jnp.sum(jnp.where(line == half * cols + c, rank, 0.0), axis=0, keepdims=True)
    ids = lax.broadcasted_iota(jnp.int32, (1, panel), 1)
    place = jnp.where(ids // part == half, ids - half * part, part + rank.astype(jnp.int32))
    slot = lax.broadcasted_iota(jnp.int32, places_ref.shape, 1)
    places = jnp.zeros(places_ref.shape, jnp.int32)
    for s in range(slots):
        found = jnp.sum(jnp.where(asked[s], place, 0), axis=1, keepdims=True)
        places = jnp.where(slot == s, found, places)
    places_ref[...] = places
    line = lax.broadcasted_iota(jnp.int32, (panel, lines), 1)
    mine = line == (1 - half) * cols + c
    there = lax.dot_general(same, touched, nt, preferred_element_type=jnp.float32)
    there = jnp.sum(jnp.where(mine, there, 0.0), axis=1, keepdims=True)
    rank = lax.dot_general(after, touched, nt, preferred_element_type=jnp.float32)
    rank = jnp.sum(jnp.where(mine, rank, 0.0), axis=1, keepdims=True).astype(jnp.int32)
    ids = lax.broadcasted_iota(jnp.int32, (panel, list_ref.shape[1]), 0)
    number = lax.broadcasted_iota(jnp.int32, (panel, list_ref.shape[1]), 1)
    listed = jnp.where((there > 0.5) & (rank == number), ids - half * part, 0)
    list_ref[...] = jnp.broadcast_to(jnp.sum(listed, axis=0, keepdims=True), list_ref.shape)


def plan(stripes, slots, per, height, levels):
    members = len(stripes)
    columns = stripes[0].shape[-1]
    lines = max(8, 2 * lax.axis_size("cols"))
    return pl.pallas_call(
        functools.partial(plan_kernel, levels),
        out_shape=(
            jax.ShapeDtypeStruct((members * per, height, columns), stripes[0].dtype),
            jax.ShapeDtypeStruct((members * lines, slots), jnp.int32),
            jax.ShapeDtypeStruct((8, 128), jnp.int32),
            jax.ShapeDtypeStruct((1,), jnp.int32),
        ),
        in_specs=[VMEM] * members,
        out_specs=(VMEM, VMEM, VMEM, SMEM),
        compiler_params=pltpu.CompilerParams(vmem_limit_bytes=48 * MIB),
        name="plan",
    )(*stripes)


def list_kernel(list_ref, all_ref, out_ref):
    for k in range(out_ref.shape[0]):
        out_ref[k] = all_ref[list_ref[0, k]]


def listed(numbers, stripes, count):
    return pl.pallas_call(
        list_kernel,
        out_shape=jax.ShapeDtypeStruct((count, *stripes.shape[1:]), stripes.dtype),
        in_specs=[SMEM, VMEM],
        out_specs=VMEM,
        compiler_params=pltpu.CompilerParams(vmem_limit_bytes=24 * MIB),
        name="listed_stripes",
    )(numbers, stripes)


def pick_kernel(places_ref, own_ref, other_ref, *out_refs):
    members = len(out_refs)
    rows, cols = lax.axis_size("rows"), lax.axis_size("cols")
    here, there = own_ref.shape[0], other_ref.shape[0]
    lines = places_ref.shape[0] // members
    line = lax.axis_index("rows") // members * cols + lax.axis_index("cols")
    for d in range(members):
        out_ref = out_refs[d]

        def body(s, carry):
            place = places_ref[d * lines + line, s]
            own = own_ref[jnp.minimum(place, here - 1)]
            other = other_ref[jnp.clip(place - here, 0, there - 1)]
            out_ref[s] = lax.select(place < here, own, other)
            return carry

        lax.fori_loop(0, out_ref.shape[0], body, 0, unroll=True)


def pick(places, own, other, members):
    return pl.pallas_call(
        pick_kernel,
        out_shape=(jax.ShapeDtypeStruct((places.shape[1], *own.shape[1:]), own.dtype),) * members,
        in_specs=[SMEM, VMEM, VMEM],
        out_specs=(VMEM,) * members,
        compiler_params=pltpu.CompilerParams(vmem_limit_bytes=24 * MIB),
        name="pick_stripes",
    )(places, own, other)


def product_kernel(rows_ref, counts_ref, blocks_ref, *refs):
    *chosen_refs, out_ref, whole = refs
    slots, width, _ = blocks_ref.shape
    columns = out_ref.shape[1]
    members = len(chosen_refs)
    me = lax.axis_index("rows") % members
    for d in range(members):
        whole[me ^ d] = chosen_refs[d][...]
    out_ref[...] = jnp.zeros_like(out_ref)
    for s in range(slots):

        @pl.when(s < counts_ref[0])
        def _():
            piece = whole[:, s].reshape(width, columns)
            product = jnp.dot(blocks_ref[s], piece, preferred_element_type=jnp.float32)
            at = pl.ds(pl.multiple_of(rows_ref[s] * width, width), width)
            out_ref[at, :] += product


def block_products(block_rows, counts, blocks, chosen):
    _, width, _ = blocks.shape
    columns = chosen[0].shape[-1]
    return pl.pallas_call(
        product_kernel,
        out_shape=jax.ShapeDtypeStruct((RB * width, columns), jnp.float32),
        in_specs=[SMEM, SMEM, VMEM] + [VMEM] * len(chosen),
        out_specs=VMEM,
        scratch_shapes=[pltpu.VMEM((len(chosen), *chosen[0].shape), chosen[0].dtype)],
        compiler_params=pltpu.CompilerParams(vmem_limit_bytes=24 * MIB),
        name="block_products",
    )(block_rows, counts, blocks, *chosen)


def gram_kernel(mine_ref, other_ref, own_ref, gram_ref, slab):
    c = lax.axis_index("cols")
    share, width = own_ref.shape[0], gram_ref.shape[1]
    slab[...] = mine_ref[...] + other_ref[...]
    own_ref[...] = slab[pl.ds(pl.multiple_of(c * share, share), share), :]
    right = slab[:, pl.ds(pl.multiple_of(c * width, width), width)]
    gram_ref[...] = lax.dot_general(
        slab[...], right, (((0,), (0,)), ((), ())), precision=HIGHEST, preferred_element_type=jnp.float32
    )


def sum_and_gram(mine, other):
    rows, columns = mine.shape
    return pl.pallas_call(
        gram_kernel,
        out_shape=(
            jax.ShapeDtypeStruct((rows // 2, columns), jnp.float32),
            jax.ShapeDtypeStruct((columns, columns // 2), jnp.float32),
        ),
        in_specs=[VMEM, VMEM],
        out_specs=(VMEM, VMEM),
        scratch_shapes=[pltpu.VMEM((rows, columns), jnp.float32)],
        compiler_params=pltpu.CompilerParams(vmem_limit_bytes=24 * MIB),
        name="sum_and_gram",
    )(mine, other)


def matmul(a, b, precision):
    return jnp.dot(a, b, precision=precision, preferred_element_type=jnp.float32)


def matmul_nt(a, b, precision):
    return lax.dot_general(
        a, b, (((1,), (1,)), ((), ())), precision=precision, preferred_element_type=jnp.float32
    )


def factor_kernel(total_rows, gram_ref, own_ref, basis_ref, factor_ref, whole, scaled, inverse):
    n = factor_ref.shape[0]
    width = gram_ref.shape[-1]
    for c in range(n // width):
        whole[:, c * width : (c + 1) * width] = gram_ref[:, c].reshape(n, width)
    row_ids = lax.broadcasted_iota(jnp.int32, (n, n), 0)
    col_ids = lax.broadcasted_iota(jnp.int32, (n, n), 1)
    diagonal = row_ids == col_ids
    identity = diagonal.astype(jnp.float32)
    half = jnp.where(row_ids > col_ids, 1.0, jnp.where(diagonal, 0.5, 0.0))
    gram = whole[...]
    on_diagonal = jnp.where(diagonal, gram, 0.0)
    down = jnp.sqrt(jnp.sum(on_diagonal, axis=1, keepdims=True))
    across = jnp.sqrt(jnp.sum(on_diagonal, axis=0, keepdims=True))
    up_down = 1.0 / down
    up_across = 1.0 / across
    scaled[...] = gram * up_down * up_across

    def refine(precision):
        w = inverse[...]
        residual = matmul_nt(matmul(w, scaled[...], precision), w, precision) - identity
        inverse[...] = w - matmul(residual * half, w, lax.Precision.DEFAULT)
        return jnp.sum(residual * residual)

    inverse[...] = identity - (scaled[...] - identity) * half
    refine(lax.Precision.DEFAULT)

    def going(state):
        step, size = state
        return (step < 8) & (size > 1e-6)

    def advance(state):
        return state[0] + 1, refine(HIGHEST)

    _, size = lax.while_loop(going, advance, (jnp.int32(0), jnp.float32(1.0)))

    @pl.when(jnp.logical_not(size <= 1e-6))
    def _():
        inverse[...] = identity
        ids = lax.broadcasted_iota(jnp.int32, (n, 1), 0)

        def eliminate(j, carry):
            pivot_row = scaled[pl.ds(j, 1), :]
            inverse_row = inverse[pl.ds(j, 1), :]
            column = jnp.sum(jnp.where(col_ids == j, scaled[...], 0.0), axis=1, keepdims=True)
            pivot = jnp.sum(jnp.where(ids == j, column, 0.0), axis=0, keepdims=True)
            root = 1.0 / jnp.sqrt(pivot)
            ratio = jnp.where(ids > j, column / pivot, jnp.where(ids == j, 1.0 - root, 0.0))
            scaled[...] = scaled[...] - ratio * pivot_row
            inverse[...] = inverse[...] - ratio * inverse_row
            return carry

        lax.fori_loop(0, n, eliminate, 0)
        scaled[...] = whole[...] * up_down * up_across

    w = inverse[...]
    root_rows = jnp.sqrt(jnp.float32(total_rows))
    upper = matmul(w, scaled[...], HIGHEST) * across / root_rows
    factor_ref[...] = jnp.where(row_ids <= col_ids, upper, 0.0)
    basis_ref[...] = matmul_nt(own_ref[...] * up_across, w, HIGHEST) * root_rows


def factor_and_basis(total_rows, gram, own):
    columns = own.shape[1]
    return pl.pallas_call(
        functools.partial(factor_kernel, total_rows),
        out_shape=(
            jax.ShapeDtypeStruct(own.shape, jnp.float32),
            jax.ShapeDtypeStruct((columns, columns), jnp.float32),
        ),
        in_specs=[VMEM, VMEM],
        out_specs=(VMEM, VMEM),
        scratch_shapes=[pltpu.VMEM((columns, columns), jnp.float32)] * 3,
        compiler_params=pltpu.CompilerParams(vmem_limit_bytes=24 * MIB),
        name="factor_and_basis",
    )(gram, own)


def spread(piece, axes, devices):
    copies = jnp.broadcast_to(piece[None], (devices, *piece.shape))
    return lax.all_to_all(copies, axes, split_axis=0, concat_axis=0, tiled=True)


def exchange(pieces, rows):
    far = sorted(range(2, len(pieces)), key=lambda d: (-d.bit_count(), -d))
    arrived = [pieces[0]] + [None] * (len(pieces) - 1)
    for d in [1, *far]:
        arrived[d] = lax.ppermute(pieces[d], "rows", [(r, r ^ d) for r in range(rows)])
    return arrived


def fetch(sketch, block_cols, counts, slots, width):
    rows, cols = lax.axis_size("rows"), lax.axis_size("cols")
    members = rows // 2
    height = width // members
    columns = sketch.shape[1]
    sketch = sketch.reshape(-1, members, height, columns)
    per = sketch.shape[0]
    swap = [(r, (r + members) % rows) for r in range(rows)]
    row = table_row(block_cols, counts, columns, sketch.dtype)
    if cols == 2:
        here = row + lax.ppermute(row, "cols", [(0, 1), (1, 0)])
    else:
        here = lax.psum(row, "cols")
    across = lax.ppermute(here, "rows", swap)
    stripes = exchange(cut(sketch, here, across), rows)
    largest = min(per * members, slots * members, 128)
    levels = tuple(level for level in LEVELS if level < largest)
    own, places, numbers, level = plan(stripes, slots, per, height, levels)

    def with_other(count):
        def run():
            other = lax.ppermute(listed(numbers, own, count), "rows", swap)
            return pick(places, own, other, members)

        return run

    picked = lax.switch(level[0], [with_other(count) for count in (*levels, largest)])
    return exchange(picked, rows)


def local(sketch, blocks, block_rows, block_cols, counts):
    slots, width, _ = blocks.shape
    columns = sketch.shape[1]
    rows, cols = lax.axis_size("rows"), lax.axis_size("cols")
    chosen = fetch(sketch, block_cols, counts, slots, width)
    if chosen[0].shape[1] % 16:
        order = lax.axis_index("rows") % len(chosen) ^ jnp.arange(len(chosen))
        chosen = [jnp.stack(chosen)[order].swapaxes(0, 1).reshape(1, slots, width, columns)[0]]
    partial_rows = block_products(block_rows, counts, blocks, chosen)
    if cols == 2:
        other = lax.ppermute(partial_rows, "cols", [(0, 1), (1, 0)])
        own, gram = sum_and_gram(partial_rows, other)
        pieces = gram.reshape(rows, -1, columns // 2)
        pieces = lax.all_to_all(pieces, "rows", split_axis=0, concat_axis=0, tiled=True)
        gram = spread(jnp.sum(pieces, axis=0), ("rows", "cols"), rows * cols)
        gram = gram.reshape(rows, cols, -1, columns // 2)
    else:
        own = lax.psum_scatter(partial_rows, "cols", scatter_dimension=0, tiled=True)
        gram = lax.psum(matmul(own.T, own, HIGHEST), ("rows", "cols"))
        gram = gram.reshape(1, 1, columns, columns)
    return factor_and_basis(RB * width * rows, gram, own)


def solution(mesh):
    in_specs = (
        P(("rows", "cols"), None),
        P(("rows", "cols"), None, None),
        P(("rows", "cols")),
        P(("rows", "cols")),
        P(("rows", "cols")),
    )
    out_specs = (P(("rows", "cols"), None), P())
    return jax.shard_map(local, mesh=mesh, in_specs=in_specs, out_specs=out_specs, check_vma=False)
```

```python
import functools

import jax
import jax.numpy as jnp
from jax import lax
from jax.experimental import pallas as pl
from jax.experimental.pallas import tpu as pltpu
from jax.sharding import PartitionSpec as P

RB = 4
HIGHEST = lax.Precision.HIGHEST
VMEM = pl.BlockSpec(memory_space=pltpu.VMEM)
SMEM = pl.BlockSpec(memory_space=pltpu.SMEM)
MIB = 1024 * 1024


LEVELS = (12, 14, 16, 18, 20, 24)
TABLE_ROWS = 16


def distances(members):
    return [0, 1, 2, *range(members - 1, 2, -1)]


def cut_kernel(sketch_ref, *out_refs):
    members = len(out_refs)
    me = lax.axis_index("rows") % members
    for ref, d in zip(out_refs, distances(members)):
        ref[...] = sketch_ref[:, me ^ d].reshape(ref.shape)


def cut(sketch):
    blocks, members, height, columns = sketch.shape
    unit = min(height, TABLE_ROWS)
    size = sketch.size * sketch.dtype.itemsize
    return pl.pallas_call(
        cut_kernel,
        out_shape=(jax.ShapeDtypeStruct((blocks * height // unit, unit, columns), sketch.dtype),) * members,
        in_specs=[VMEM],
        out_specs=(VMEM,) * members,
        compiler_params=pltpu.CompilerParams(vmem_limit_bytes=24 * MIB),
        cost_estimate=pl.CostEstimate(flops=0, bytes_accessed=2 * size, transcendentals=0),
        name="cut_stripes",
    )(sketch)


def stamp_kernel(*refs):
    members = (len(refs) - 4) // 2
    line_refs, stripe_refs, out_refs = refs[:4], refs[4 : 4 + members], refs[4 + members :]
    cols = lax.axis_size("cols")
    half, c = lax.axis_index("rows") // members, lax.axis_index("cols")
    pieces = stripe_refs[0].shape[0]
    row = lax.broadcasted_iota(jnp.int32, (TABLE_ROWS, 128), 0)
    table = jnp.zeros((TABLE_ROWS, 128), jnp.int32)
    if cols == 2:
        places = [half * 2 + c, half * 2 + 1 - c, (1 - half) * 2 + c, (1 - half) * 2 + 1 - c]
        for place, line_ref in zip(places, line_refs):
            table = jnp.where(row == place, line_ref[...], table)
    else:
        for k in range(cols):
            table = jnp.where(row == half * cols + k, line_refs[0][k : k + 1], table)
            table = jnp.where(row == (1 - half) * cols + k, line_refs[1][k : k + 1], table)
    table = table.astype(jnp.float32).astype(out_refs[0].dtype)
    for stripe_ref, out_ref in zip(stripe_refs, out_refs):
        out_ref[:pieces] = stripe_ref[...]
        out_ref[pieces:, :, :128] = table.reshape(-1, out_ref.shape[1], 128)


def stamp(lines, stripes):
    pieces, unit, columns = stripes[0].shape
    pieces += TABLE_ROWS // unit
    members = len(stripes)
    return pl.pallas_call(
        stamp_kernel,
        out_shape=(jax.ShapeDtypeStruct((pieces, unit, columns), stripes[0].dtype),) * members,
        in_specs=[VMEM] * (4 + members),
        out_specs=(VMEM,) * members,
        compiler_params=pltpu.CompilerParams(vmem_limit_bytes=24 * MIB),
        name="stamp_stripes",
    )(*lines, *stripes)


def plan_kernel(levels, *refs):
    *stripe_refs, all_ref, places_ref, list_ref, level_ref = refs
    rows, cols = lax.axis_size("rows"), lax.axis_size("cols")
    members = len(stripe_refs)
    me = lax.axis_index("rows") % members
    half = lax.axis_index("rows") // members
    c = lax.axis_index("cols")
    part, height, columns = all_ref.shape
    per = part // members
    panel = part * 2
    slots = places_ref.shape[1]
    unit = stripe_refs[0].shape[1]
    pieces = per * height // unit
    lines = places_ref.shape[0] // members
    tables = []
    for ref, d in zip(stripe_refs, distances(members)):
        all_ref[pl.ds((me ^ d) * per, per)] = ref[:pieces].reshape(per, height, columns)
        tables.append(ref[pieces:, :, :128].reshape(TABLE_ROWS, 128).astype(jnp.float32)[:lines])
    table = jnp.concatenate(tables, axis=0).astype(jnp.int32)
    block = lax.broadcasted_iota(jnp.int32, (members * lines, panel), 1)
    line = lax.broadcasted_iota(jnp.int32, (members * lines, panel), 0) % lines
    asked = [(table[:, s : s + 1] == block) & (s < table[:, slots : slots + 1]) for s in range(slots)]
    some = functools.reduce(jnp.logical_or, asked) & (line // cols != block // part)
    some = jnp.where(some, 1.0, 0.0)
    touched = functools.reduce(jnp.maximum, [some[d * lines : (d + 1) * lines] for d in range(members)])
    most = jnp.max(jnp.sum(touched, axis=1, keepdims=True)).astype(jnp.int32)
    level_ref[0] = sum((most > level).astype(jnp.int32) for level in levels)
    touched = touched.astype(jnp.bfloat16)
    first = lax.broadcasted_iota(jnp.int32, (panel, panel), 0)
    second = lax.broadcasted_iota(jnp.int32, (panel, panel), 1)
    after = jnp.where(first > second, 1.0, 0.0).astype(jnp.bfloat16)
    same = jnp.where(first == second, 1.0, 0.0).astype(jnp.bfloat16)
    nt = (((1,), (1,)), ((), ()))
    rank = lax.dot_general(touched, after, nt, preferred_element_type=jnp.float32)
    line = lax.broadcasted_iota(jnp.int32, (lines, panel), 0)
    rank = jnp.sum(jnp.where(line == half * cols + c, rank, 0.0), axis=0, keepdims=True)
    ids = lax.broadcasted_iota(jnp.int32, (1, panel), 1)
    place = jnp.where(ids // part == half, ids - half * part, part + rank.astype(jnp.int32))
    slot = lax.broadcasted_iota(jnp.int32, places_ref.shape, 1)
    places = jnp.zeros(places_ref.shape, jnp.int32)
    for s in range(slots):
        found = jnp.sum(jnp.where(asked[s], place, 0), axis=1, keepdims=True)
        places = jnp.where(slot == s, found, places)
    places_ref[...] = places
    line = lax.broadcasted_iota(jnp.int32, (panel, lines), 1)
    mine = line == (1 - half) * cols + c
    there = lax.dot_general(same, touched, nt, preferred_element_type=jnp.float32)
    there = jnp.sum(jnp.where(mine, there, 0.0), axis=1, keepdims=True)
    rank = lax.dot_general(after, touched, nt, preferred_element_type=jnp.float32)
    rank = jnp.sum(jnp.where(mine, rank, 0.0), axis=1, keepdims=True).astype(jnp.int32)
    ids = lax.broadcasted_iota(jnp.int32, (panel, list_ref.shape[1]), 0)
    number = lax.broadcasted_iota(jnp.int32, (panel, list_ref.shape[1]), 1)
    listed = jnp.where((there > 0.5) & (rank == number), ids - half * part, 0)
    list_ref[...] = jnp.broadcast_to(jnp.sum(listed, axis=0, keepdims=True), list_ref.shape)


def plan(stripes, slots, per, height, levels):
    members = len(stripes)
    columns = stripes[0].shape[-1]
    lines = max(8, 2 * lax.axis_size("cols"))
    return pl.pallas_call(
        functools.partial(plan_kernel, levels),
        out_shape=(
            jax.ShapeDtypeStruct((members * per, height, columns), stripes[0].dtype),
            jax.ShapeDtypeStruct((members * lines, slots), jnp.int32),
            jax.ShapeDtypeStruct((8, 128), jnp.int32),
            jax.ShapeDtypeStruct((1,), jnp.int32),
        ),
        in_specs=[VMEM] * members,
        out_specs=(VMEM, VMEM, VMEM, SMEM),
        compiler_params=pltpu.CompilerParams(vmem_limit_bytes=48 * MIB),
        name="plan",
    )(*stripes)


def list_kernel(list_ref, all_ref, out_ref):
    for k in range(out_ref.shape[0]):
        out_ref[k] = all_ref[list_ref[0, k]]


def listed(numbers, stripes, count):
    return pl.pallas_call(
        list_kernel,
        out_shape=jax.ShapeDtypeStruct((count, *stripes.shape[1:]), stripes.dtype),
        in_specs=[SMEM, VMEM],
        out_specs=VMEM,
        compiler_params=pltpu.CompilerParams(vmem_limit_bytes=24 * MIB),
        name="listed_stripes",
    )(numbers, stripes)


def pick_kernel(places_ref, own_ref, other_ref, *out_refs):
    members = len(out_refs)
    rows, cols = lax.axis_size("rows"), lax.axis_size("cols")
    here, there = own_ref.shape[0], other_ref.shape[0]
    lines = places_ref.shape[0] // members
    line = lax.axis_index("rows") // members * cols + lax.axis_index("cols")
    for d in range(members):
        out_ref = out_refs[d]

        def body(s, carry):
            place = places_ref[d * lines + line, s]
            own = own_ref[jnp.minimum(place, here - 1)]
            other = other_ref[jnp.clip(place - here, 0, there - 1)]
            out_ref[s] = lax.select(place < here, own, other)
            return carry

        lax.fori_loop(0, out_ref.shape[0], body, 0, unroll=True)


def pick(places, own, other, members):
    return pl.pallas_call(
        pick_kernel,
        out_shape=(jax.ShapeDtypeStruct((places.shape[1], *own.shape[1:]), own.dtype),) * members,
        in_specs=[SMEM, VMEM, VMEM],
        out_specs=(VMEM,) * members,
        compiler_params=pltpu.CompilerParams(vmem_limit_bytes=24 * MIB),
        name="pick_stripes",
    )(places, own, other)


def product_kernel(rows_ref, counts_ref, blocks_ref, *refs):
    *chosen_refs, out_ref, whole = refs
    slots, width, _ = blocks_ref.shape
    columns = out_ref.shape[1]
    members = len(chosen_refs)
    me = lax.axis_index("rows") % members
    for ref, d in zip(chosen_refs, distances(members) if members > 1 else [0]):
        whole[me ^ d] = ref[...]
    out_ref[...] = jnp.zeros_like(out_ref)
    for s in range(slots):

        @pl.when(s < counts_ref[0])
        def _():
            piece = whole[:, s].reshape(width, columns)
            product = jnp.dot(blocks_ref[s], piece, preferred_element_type=jnp.float32)
            at = pl.ds(pl.multiple_of(rows_ref[s] * width, width), width)
            out_ref[at, :] += product


def block_products(block_rows, counts, blocks, chosen):
    _, width, _ = blocks.shape
    columns = chosen[0].shape[-1]
    return pl.pallas_call(
        product_kernel,
        out_shape=jax.ShapeDtypeStruct((RB * width, columns), jnp.float32),
        in_specs=[SMEM, SMEM, VMEM] + [VMEM] * len(chosen),
        out_specs=VMEM,
        scratch_shapes=[pltpu.VMEM((len(chosen), *chosen[0].shape), chosen[0].dtype)],
        compiler_params=pltpu.CompilerParams(vmem_limit_bytes=24 * MIB),
        name="block_products",
    )(block_rows, counts, blocks, *chosen)


def gram_kernel(mine_ref, other_ref, own_ref, *refs):
    *gram_refs, slab = refs
    c = lax.axis_index("cols")
    me = lax.axis_index("rows") % len(gram_refs)
    share, (height, width) = own_ref.shape[0], gram_refs[0].shape
    slab[...] = mine_ref[...] + other_ref[...]
    own_ref[...] = slab[pl.ds(pl.multiple_of(c * share, share), share), :]
    right = slab[:, pl.ds(pl.multiple_of(c * width, width), width)]
    gram = lax.dot_general(
        slab[...], right, (((0,), (0,)), ((), ())), precision=HIGHEST, preferred_element_type=jnp.float32
    )
    for q in range(len(gram_refs)):
        for d in range(len(gram_refs)):

            @pl.when(me ^ d == q)
            def _():
                gram_refs[d][...] = gram[q * height : (q + 1) * height]


def sum_and_gram(mine, other):
    rows, columns = mine.shape
    return pl.pallas_call(
        gram_kernel,
        out_shape=(
            jax.ShapeDtypeStruct((rows // 2, columns), jnp.float32),
            *[jax.ShapeDtypeStruct((columns // 4, columns // 2), jnp.float32)] * 4,
        ),
        in_specs=[VMEM, VMEM],
        out_specs=(VMEM,) * 5,
        scratch_shapes=[pltpu.VMEM((rows, columns), jnp.float32)],
        compiler_params=pltpu.CompilerParams(vmem_limit_bytes=24 * MIB),
        name="sum_and_gram",
    )(mine, other)


def stack_kernel(*refs):
    *quarter_refs, out_ref = refs
    me = lax.axis_index("rows") % len(quarter_refs)
    height = quarter_refs[0].shape[0]
    for d, ref in enumerate(quarter_refs):
        out_ref[pl.ds(pl.multiple_of((me ^ d) * height, height), height), :] = ref[...]


def stack(quarters):
    height, width = quarters[0].shape
    return pl.pallas_call(
        stack_kernel,
        out_shape=jax.ShapeDtypeStruct((len(quarters) * height, width), jnp.float32),
        in_specs=[VMEM] * len(quarters),
        out_specs=VMEM,
        name="stack_quarters",
    )(*quarters)


def matmul(a, b, precision):
    return jnp.dot(a, b, precision=precision, preferred_element_type=jnp.float32)


def matmul_nt(a, b, precision):
    return lax.dot_general(
        a, b, (((1,), (1,)), ((), ())), precision=precision, preferred_element_type=jnp.float32
    )


def factor_kernel(total_rows, *refs):
    *gram_refs, own_ref, basis_ref, factor_ref, whole, scaled, inverse = refs
    n = factor_ref.shape[0]
    if len(gram_refs) == 1:
        whole[...] = gram_refs[0][...]
    else:
        c = lax.axis_index("cols")
        width = n // 2
        whole[:, pl.ds(pl.multiple_of(c * width, width), width)] = gram_refs[0][...]
        whole[:, pl.ds(pl.multiple_of((1 - c) * width, width), width)] = gram_refs[1][...]
    row_ids = lax.broadcasted_iota(jnp.int32, (n, n), 0)
    col_ids = lax.broadcasted_iota(jnp.int32, (n, n), 1)
    diagonal = row_ids == col_ids
    identity = diagonal.astype(jnp.float32)
    half = jnp.where(row_ids > col_ids, 1.0, jnp.where(diagonal, 0.5, 0.0))
    gram = whole[...]
    on_diagonal = jnp.where(diagonal, gram, 0.0)
    down = jnp.sqrt(jnp.sum(on_diagonal, axis=1, keepdims=True))
    across = jnp.sqrt(jnp.sum(on_diagonal, axis=0, keepdims=True))
    up_down = 1.0 / down
    up_across = 1.0 / across
    scaled[...] = gram * up_down * up_across

    def refine(precision):
        w = inverse[...]
        residual = matmul_nt(matmul(w, scaled[...], precision), w, precision) - identity
        inverse[...] = w - matmul(residual * half, w, lax.Precision.DEFAULT)
        return jnp.sum(residual * residual)

    inverse[...] = identity - (scaled[...] - identity) * half
    refine(lax.Precision.DEFAULT)

    def going(state):
        step, size = state
        return (step < 8) & (size > 1e-6)

    def advance(state):
        return state[0] + 1, refine(HIGHEST)

    _, size = lax.while_loop(going, advance, (jnp.int32(0), jnp.float32(1.0)))

    @pl.when(jnp.logical_not(size <= 1e-6))
    def _():
        inverse[...] = identity
        ids = lax.broadcasted_iota(jnp.int32, (n, 1), 0)

        def eliminate(j, carry):
            pivot_row = scaled[pl.ds(j, 1), :]
            inverse_row = inverse[pl.ds(j, 1), :]
            column = jnp.sum(jnp.where(col_ids == j, scaled[...], 0.0), axis=1, keepdims=True)
            pivot = jnp.sum(jnp.where(ids == j, column, 0.0), axis=0, keepdims=True)
            root = 1.0 / jnp.sqrt(pivot)
            ratio = jnp.where(ids > j, column / pivot, jnp.where(ids == j, 1.0 - root, 0.0))
            scaled[...] = scaled[...] - ratio * pivot_row
            inverse[...] = inverse[...] - ratio * inverse_row
            return carry

        lax.fori_loop(0, n, eliminate, 0)
        scaled[...] = whole[...] * up_down * up_across

    w = inverse[...]
    root_rows = jnp.sqrt(jnp.float32(total_rows))
    upper = matmul(w, scaled[...], HIGHEST) * across / root_rows
    factor_ref[...] = jnp.where(row_ids <= col_ids, upper, 0.0)
    basis_ref[...] = matmul_nt(own_ref[...] * up_across, w, HIGHEST) * root_rows


def factor_and_basis(total_rows, grams, own):
    columns = own.shape[1]
    return pl.pallas_call(
        functools.partial(factor_kernel, total_rows),
        out_shape=(
            jax.ShapeDtypeStruct(own.shape, jnp.float32),
            jax.ShapeDtypeStruct((columns, columns), jnp.float32),
        ),
        in_specs=[VMEM] * (len(grams) + 1),
        out_specs=(VMEM, VMEM),
        scratch_shapes=[pltpu.VMEM((columns, columns), jnp.float32)] * 3,
        compiler_params=pltpu.CompilerParams(vmem_limit_bytes=24 * MIB),
        name="factor_and_basis",
    )(*grams, own)


def moved(piece, rows, d):
    return lax.ppermute(piece, "rows", [(r, r ^ d) for r in range(rows)])


def exchange(pieces, rows):
    order = distances(len(pieces))
    return [moved(piece, rows, d) if d else piece for piece, d in zip(pieces, order)]


def table_lines(block_cols, counts):
    rows, cols = lax.axis_size("rows"), lax.axis_size("cols")
    line = jnp.concatenate([block_cols, counts, jnp.zeros((128 - block_cols.shape[0] - 1,), jnp.int32)])[None]
    swap = [(r, (r + rows // 2) % rows) for r in range(rows)]
    if cols != 2:
        lines = lax.all_gather(line, "cols", axis=0, tiled=True)
        lines = [lines, lax.ppermute(lines, "rows", swap)]
        return [*lines, *lines]
    across = [(r * 2 + c, to * 2 + 1 - c) for r, to in swap for c in range(2)]
    return [
        line,
        lax.ppermute(line, "cols", [(0, 1), (1, 0)]),
        lax.ppermute(line, "rows", swap),
        lax.ppermute(line, ("rows", "cols"), across),
    ]


def fetch(sketch, block_cols, counts, slots, width):
    rows = lax.axis_size("rows")
    members = rows // 2
    height = width // members
    columns = sketch.shape[1]
    sketch = sketch.reshape(-1, members, height, columns)
    per = sketch.shape[0]
    stripes = exchange(stamp(table_lines(block_cols, counts), cut(sketch)), rows)
    largest = min(per * members, slots * members, 128)
    levels = tuple(level for level in LEVELS if level < largest)
    own, places, numbers, level = plan(stripes, slots, per, height, levels)

    def with_other(count):
        def run():
            swap = [(r, (r + members) % rows) for r in range(rows)]
            other = lax.ppermute(listed(numbers, own, count), "rows", swap)
            return pick(places, own, other, members)

        return run

    picked = lax.switch(level[0], [with_other(count) for count in (*levels, largest)])
    return exchange(picked, rows)


def gram_halves(quarters, rows):
    first, *rest = quarters
    for d, quarter in enumerate(rest):
        first = first + moved(quarter, rows, d + 1)
    total = (first + moved(first, rows, 4)) + (moved(first, rows, 8) + moved(first, rows, 12))
    half = stack([total] + [moved(total, rows, d) for d in range(1, 4)])
    return half, lax.ppermute(half, "cols", [(0, 1), (1, 0)])


def local(sketch, blocks, block_rows, block_cols, counts):
    slots, width, _ = blocks.shape
    columns = sketch.shape[1]
    rows, cols = lax.axis_size("rows"), lax.axis_size("cols")
    chosen = fetch(sketch, block_cols, counts, slots, width)
    if chosen[0].shape[1] % 16:
        order = jnp.argsort(lax.axis_index("rows") % len(chosen) ^ jnp.array(distances(len(chosen))))
        chosen = [jnp.stack(chosen)[order].swapaxes(0, 1).reshape(1, slots, width, columns)[0]]
    partial_rows = block_products(block_rows, counts, blocks, chosen)
    if (rows, cols) == (16, 2):
        other = lax.ppermute(partial_rows, "cols", [(0, 1), (1, 0)])
        own, *quarters = sum_and_gram(partial_rows, other)
        grams = gram_halves(quarters, rows)
    else:
        own = lax.psum_scatter(partial_rows, "cols", scatter_dimension=0, tiled=True)
        grams = [lax.psum(matmul(own.T, own, HIGHEST), ("rows", "cols"))]
    return factor_and_basis(RB * width * rows, grams, own)


def solution(mesh):
    in_specs = (
        P(("rows", "cols"), None),
        P(("rows", "cols"), None, None),
        P(("rows", "cols")),
        P(("rows", "cols")),
        P(("rows", "cols")),
    )
    out_specs = (P(("rows", "cols"), None), P())
    return jax.shard_map(local, mesh=mesh, in_specs=in_specs, out_specs=out_specs, check_vma=False)
```

```python
import functools

import jax
import jax.numpy as jnp
from jax import lax
from jax.experimental import pallas as pl
from jax.experimental.pallas import tpu as pltpu
from jax.sharding import PartitionSpec as P

RB = 4
HIGHEST = lax.Precision.HIGHEST
VMEM = pl.BlockSpec(memory_space=pltpu.VMEM)
SMEM = pl.BlockSpec(memory_space=pltpu.SMEM)
MIB = 1024 * 1024


ACROSS = (12, 14, 16, 18, 20, 24)
WITHIN = (6, 7, 8)


def table_kernel(cols_ref, counts_ref, out_ref):
    slots = cols_ref.shape[0]
    lane = lax.broadcasted_iota(jnp.int32, out_ref.shape, 2)
    table = jnp.where(lane == slots, counts_ref[0], 0)
    for s in range(slots):
        table = jnp.where(lane == s, cols_ref[s], table)
    out_ref[...] = table


def table_copies(block_cols, counts, devices):
    return pl.pallas_call(
        table_kernel,
        out_shape=jax.ShapeDtypeStruct((devices, 1, 128), jnp.int32),
        in_specs=[SMEM, SMEM],
        out_specs=VMEM,
        name="table_copies",
    )(block_cols, counts)


def plan_kernel(per, within, across, table_ref, places_ref, lists_ref, *level_refs):
    devices = table_ref.shape[0]
    slots = places_ref.shape[1]
    rows, cols = lax.axis_size("rows"), lax.axis_size("cols")
    panel = per * rows
    part = panel // 2
    table = table_ref[:, 0, :]
    block = lax.broadcasted_iota(jnp.int32, (devices, panel), 1)
    device = lax.broadcasted_iota(jnp.int32, (devices, panel), 0)
    side, core = device // (devices // 2), device % cols
    asked = [(table[:, s : s + 1] == block) & (s < table[:, slots : slots + 1]) for s in range(slots)]
    some = functools.reduce(jnp.logical_or, asked)
    lines = -(-cols // 8) * 8
    line = lax.broadcasted_iota(jnp.int32, (3 * lines, panel), 0)
    asks = jnp.zeros((3 * lines, panel), jnp.float32)
    for c in range(cols):
        for h in range(2):
            found = jnp.max(jnp.where(some & (core == c) & (side == h), 1.0, 0.0), axis=0, keepdims=True)
            asks = jnp.where(line == c, jnp.maximum(asks, found), asks)
            asks = jnp.where((line == lines * (1 + h) + c) & (block[:1] // part != h), found, asks)
    first = lax.broadcasted_iota(jnp.int32, (panel, panel), 0)
    second = lax.broadcasted_iota(jnp.int32, (panel, panel), 1)
    after = first > second
    near = jnp.where(after & (first // per == second // per), 1.0, 0.0).astype(jnp.bfloat16)
    after = jnp.where(after, 1.0, 0.0).astype(jnp.bfloat16)
    same = jnp.where(first == second, 1.0, 0.0).astype(jnp.bfloat16)
    nt = (((1,), (1,)), ((), ()))

    def ranks(a, b):
        return lax.dot_general(a, b, nt, preferred_element_type=jnp.float32)

    short = asks.astype(jnp.bfloat16)
    near_rank = ranks(short, near)
    far_rank = ranks(short, after)
    longest = jnp.max(jnp.where(line < lines, near_rank + asks, 0.0)).astype(jnp.int32)
    level_refs[0][0] = sum((longest > level).astype(jnp.int32) for level in within)
    longest = jnp.max(jnp.where(line < lines, 0.0, far_rank + asks)).astype(jnp.int32)
    level_refs[1][0] = sum((longest > level).astype(jnp.int32) for level in across)
    me = lax.axis_index("rows")
    half, c = me // (rows // 2), lax.axis_index("cols")

    def row(values, number):
        return jnp.sum(jnp.where(line == number, values, 0.0), axis=0, keepdims=True)

    ids = lax.broadcasted_iota(jnp.int32, (1, panel), 1)
    here = ids // per * per - half * part + row(near_rank, c).astype(jnp.int32)
    there = part + row(far_rank, lines * (1 + half) + c).astype(jnp.int32)
    place = jnp.where(ids // part == half, here, there)
    slot = lax.broadcasted_iota(jnp.int32, places_ref.shape, 1)
    places = jnp.zeros(places_ref.shape, jnp.int32)
    for s in range(slots):
        found = jnp.sum(jnp.where(asked[s], place, 0), axis=1, keepdims=True)
        places = jnp.where(slot == s, found, places)
    places_ref[...] = places
    line = lax.broadcasted_iota(jnp.int32, (panel, 3 * lines), 1)

    def column(values, number):
        return jnp.sum(jnp.where(line == number, values, 0.0), axis=1, keepdims=True)

    turned, near_rank, far_rank = ranks(same, short), ranks(near, short), ranks(after, short)
    ids = lax.broadcasted_iota(jnp.int32, (panel, 1), 0)
    number = lax.broadcasted_iota(jnp.int32, (panel, lists_ref.shape[1]), 1)
    near_rank = column(near_rank, c).astype(jnp.int32)
    here = ids // per * per - half * part + near_rank
    other = lines * (2 - half) + c
    sent = (column(turned, other) > 0.5) & (column(far_rank, other).astype(jnp.int32) == number)
    sent = jnp.sum(jnp.where(sent, here, 0), axis=0, keepdims=True)
    kept = (column(turned, c) > 0.5) & (ids // per == me) & (near_rank == number)
    kept = jnp.sum(jnp.where(kept, ids % per, 0), axis=0, keepdims=True)
    lists_ref[...] = jnp.where(lax.broadcasted_iota(jnp.int32, lists_ref.shape, 0) == 0, sent, kept)


def plan(table, slots, per, within, across):
    devices = table.shape[0]
    return pl.pallas_call(
        functools.partial(plan_kernel, per, within, across),
        out_shape=(
            jax.ShapeDtypeStruct((devices, slots), jnp.int32),
            jax.ShapeDtypeStruct((8, 128), jnp.int32),
            jax.ShapeDtypeStruct((1,), jnp.int32),
            jax.ShapeDtypeStruct((1,), jnp.int32),
        ),
        in_specs=[VMEM],
        out_specs=(VMEM, VMEM, SMEM, SMEM),
        compiler_params=pltpu.CompilerParams(vmem_limit_bytes=48 * MIB),
        name="plan",
    )(table)


def cut_kernel(lists_ref, sketch_ref, *out_refs):
    members = len(out_refs)
    me = lax.axis_index("rows") % members
    for k in range(out_refs[0].shape[0]):
        for d, out_ref in enumerate(out_refs):
            out_ref[k] = sketch_ref[lists_ref[1, k], me ^ d]


def cut(lists, sketch, count):
    _, members, height, columns = sketch.shape
    return pl.pallas_call(
        cut_kernel,
        out_shape=(jax.ShapeDtypeStruct((count, height, columns), sketch.dtype),) * members,
        in_specs=[SMEM, VMEM],
        out_specs=(VMEM,) * members,
        compiler_params=pltpu.CompilerParams(vmem_limit_bytes=24 * MIB),
        name="cut_stripes",
    )(lists, sketch)


def order_kernel(*refs):
    *stripe_refs, all_ref = refs
    members = len(stripe_refs)
    me = lax.axis_index("rows") % members
    per = all_ref.shape[0] // members
    for d, ref in enumerate(stripe_refs):
        all_ref[pl.ds((me ^ d) * per, ref.shape[0])] = ref[...]


def order(stripes, per):
    _, height, columns = stripes[0].shape
    return pl.pallas_call(
        order_kernel,
        out_shape=jax.ShapeDtypeStruct((len(stripes) * per, height, columns), stripes[0].dtype),
        in_specs=[VMEM] * len(stripes),
        out_specs=VMEM,
        compiler_params=pltpu.CompilerParams(vmem_limit_bytes=24 * MIB),
        name="order_stripes",
    )(*stripes)


def list_kernel(list_ref, all_ref, out_ref):
    for k in range(out_ref.shape[0]):
        out_ref[k] = all_ref[list_ref[0, k]]


def listed(numbers, stripes, count):
    return pl.pallas_call(
        list_kernel,
        out_shape=jax.ShapeDtypeStruct((count, *stripes.shape[1:]), stripes.dtype),
        in_specs=[SMEM, VMEM],
        out_specs=VMEM,
        compiler_params=pltpu.CompilerParams(vmem_limit_bytes=24 * MIB),
        name="listed_stripes",
    )(numbers, stripes)


def pick_kernel(places_ref, own_ref, other_ref, *out_refs):
    members = len(out_refs)
    cols = lax.axis_size("cols")
    here, there = own_ref.shape[0], other_ref.shape[0]
    me = lax.axis_index("rows")
    c = lax.axis_index("cols")
    for d in range(members):
        out_ref = out_refs[d]

        def body(s, carry):
            place = places_ref[(me ^ d) * cols + c, s]
            own = own_ref[jnp.minimum(place, here - 1)]
            other = other_ref[jnp.clip(place - here, 0, there - 1)]
            out_ref[s] = lax.select(place < here, own, other)
            return carry

        lax.fori_loop(0, out_ref.shape[0], body, 0, unroll=True)


def pick(places, own, other, members):
    return pl.pallas_call(
        pick_kernel,
        out_shape=(jax.ShapeDtypeStruct((places.shape[1], *own.shape[1:]), own.dtype),) * members,
        in_specs=[SMEM, VMEM, VMEM],
        out_specs=(VMEM,) * members,
        compiler_params=pltpu.CompilerParams(vmem_limit_bytes=24 * MIB),
        name="pick_stripes",
    )(places, own, other)


def product_kernel(rows_ref, counts_ref, blocks_ref, *refs):
    *chosen_refs, out_ref, whole = refs
    slots, width, _ = blocks_ref.shape
    columns = out_ref.shape[1]
    members = len(chosen_refs)
    me = lax.axis_index("rows") % members
    for d in range(members):
        whole[me ^ d] = chosen_refs[d][...]
    out_ref[...] = jnp.zeros_like(out_ref)
    for s in range(slots):

        @pl.when(s < counts_ref[0])
        def _():
            piece = whole[:, s].reshape(width, columns)
            product = jnp.dot(blocks_ref[s], piece, preferred_element_type=jnp.float32)
            at = pl.ds(pl.multiple_of(rows_ref[s] * width, width), width)
            out_ref[at, :] += product


def block_products(block_rows, counts, blocks, chosen):
    _, width, _ = blocks.shape
    columns = chosen[0].shape[-1]
    return pl.pallas_call(
        product_kernel,
        out_shape=jax.ShapeDtypeStruct((RB * width, columns), jnp.float32),
        in_specs=[SMEM, SMEM, VMEM] + [VMEM] * len(chosen),
        out_specs=VMEM,
        scratch_shapes=[pltpu.VMEM((len(chosen), *chosen[0].shape), chosen[0].dtype)],
        compiler_params=pltpu.CompilerParams(vmem_limit_bytes=24 * MIB),
        name="block_products",
    )(block_rows, counts, blocks, *chosen)


def gram_kernel(mine_ref, other_ref, own_ref, gram_ref, slab):
    c = lax.axis_index("cols")
    share, width = own_ref.shape[0], gram_ref.shape[1]
    slab[...] = mine_ref[...] + other_ref[...]
    own_ref[...] = slab[pl.ds(pl.multiple_of(c * share, share), share), :]
    right = slab[:, pl.ds(pl.multiple_of(c * width, width), width)]
    gram_ref[...] = lax.dot_general(
        slab[...], right, (((0,), (0,)), ((), ())), precision=HIGHEST, preferred_element_type=jnp.float32
    )


def sum_and_gram(mine, other):
    rows, columns = mine.shape
    return pl.pallas_call(
        gram_kernel,
        out_shape=(
            jax.ShapeDtypeStruct((rows // 2, columns), jnp.float32),
            jax.ShapeDtypeStruct((columns, columns // 2), jnp.float32),
        ),
        in_specs=[VMEM, VMEM],
        out_specs=(VMEM, VMEM),
        scratch_shapes=[pltpu.VMEM((rows, columns), jnp.float32)],
        compiler_params=pltpu.CompilerParams(vmem_limit_bytes=24 * MIB),
        name="sum_and_gram",
    )(mine, other)


def matmul(a, b, precision):
    return jnp.dot(a, b, precision=precision, preferred_element_type=jnp.float32)


def matmul_nt(a, b, precision):
    return lax.dot_general(
        a, b, (((1,), (1,)), ((), ())), precision=precision, preferred_element_type=jnp.float32
    )


def factor_kernel(total_rows, gram_ref, own_ref, basis_ref, factor_ref, whole, scaled, inverse):
    n = factor_ref.shape[0]
    width = gram_ref.shape[-1]
    for c in range(n // width):
        whole[:, c * width : (c + 1) * width] = gram_ref[:, c].reshape(n, width)
    row_ids = lax.broadcasted_iota(jnp.int32, (n, n), 0)
    col_ids = lax.broadcasted_iota(jnp.int32, (n, n), 1)
    diagonal = row_ids == col_ids
    identity = diagonal.astype(jnp.float32)
    half = jnp.where(row_ids > col_ids, 1.0, jnp.where(diagonal, 0.5, 0.0))
    gram = whole[...]
    on_diagonal = jnp.where(diagonal, gram, 0.0)
    down = jnp.sqrt(jnp.sum(on_diagonal, axis=1, keepdims=True))
    across = jnp.sqrt(jnp.sum(on_diagonal, axis=0, keepdims=True))
    up_down = 1.0 / down
    up_across = 1.0 / across
    scaled[...] = gram * up_down * up_across

    def refine(precision):
        w = inverse[...]
        residual = matmul_nt(matmul(w, scaled[...], precision), w, precision) - identity
        inverse[...] = w - matmul(residual * half, w, lax.Precision.DEFAULT)
        return jnp.sum(residual * residual)

    inverse[...] = identity - (scaled[...] - identity) * half
    refine(lax.Precision.DEFAULT)

    def going(state):
        step, size = state
        return (step < 8) & (size > 1e-6)

    def advance(state):
        return state[0] + 1, refine(HIGHEST)

    _, size = lax.while_loop(going, advance, (jnp.int32(0), jnp.float32(1.0)))

    @pl.when(jnp.logical_not(size <= 1e-6))
    def _():
        inverse[...] = identity
        ids = lax.broadcasted_iota(jnp.int32, (n, 1), 0)

        def eliminate(j, carry):
            pivot_row = scaled[pl.ds(j, 1), :]
            inverse_row = inverse[pl.ds(j, 1), :]
            column = jnp.sum(jnp.where(col_ids == j, scaled[...], 0.0), axis=1, keepdims=True)
            pivot = jnp.sum(jnp.where(ids == j, column, 0.0), axis=0, keepdims=True)
            root = 1.0 / jnp.sqrt(pivot)
            ratio = jnp.where(ids > j, column / pivot, jnp.where(ids == j, 1.0 - root, 0.0))
            scaled[...] = scaled[...] - ratio * pivot_row
            inverse[...] = inverse[...] - ratio * inverse_row
            return carry

        lax.fori_loop(0, n, eliminate, 0)
        scaled[...] = whole[...] * up_down * up_across

    w = inverse[...]
    root_rows = jnp.sqrt(jnp.float32(total_rows))
    upper = matmul(w, scaled[...], HIGHEST) * across / root_rows
    factor_ref[...] = jnp.where(row_ids <= col_ids, upper, 0.0)
    basis_ref[...] = matmul_nt(own_ref[...] * up_across, w, HIGHEST) * root_rows


def factor_and_basis(total_rows, gram, own):
    columns = own.shape[1]
    return pl.pallas_call(
        functools.partial(factor_kernel, total_rows),
        out_shape=(
            jax.ShapeDtypeStruct(own.shape, jnp.float32),
            jax.ShapeDtypeStruct((columns, columns), jnp.float32),
        ),
        in_specs=[VMEM, VMEM],
        out_specs=(VMEM, VMEM),
        scratch_shapes=[pltpu.VMEM((columns, columns), jnp.float32)] * 3,
        compiler_params=pltpu.CompilerParams(vmem_limit_bytes=24 * MIB),
        name="factor_and_basis",
    )(gram, own)


def spread(piece, axes, devices):
    copies = jnp.broadcast_to(piece[None], (devices, *piece.shape))
    return lax.all_to_all(copies, axes, split_axis=0, concat_axis=0, tiled=True)


def exchange(pieces, rows):
    far = sorted(range(2, len(pieces)), key=lambda d: (-d.bit_count(), -d))
    arrived = [pieces[0]] + [None] * (len(pieces) - 1)
    for d in [1, *far]:
        arrived[d] = lax.ppermute(pieces[d], "rows", [(r, r ^ d) for r in range(rows)])
    return arrived


def fetch(sketch, block_cols, counts, slots, width):
    rows, cols = lax.axis_size("rows"), lax.axis_size("cols")
    members = rows // 2
    height = width // members
    columns = sketch.shape[1]
    sketch = sketch.reshape(-1, members, height, columns)
    per = sketch.shape[0]
    largest = min(per * members, slots * members, 128)
    within = tuple(level for level in WITHIN if level < per)
    across = tuple(level for level in ACROSS if level < largest)
    table = table_copies(block_cols, counts, rows * cols)
    table = lax.all_to_all(table, ("rows", "cols"), split_axis=0, concat_axis=0, tiled=True)
    places, lists, near, far = plan(table, slots, per, within, across)

    def within_half(count):
        def run():
            return order(exchange(cut(lists, sketch, count), rows), per)

        return run

    own = lax.switch(near[0], [within_half(count) for count in (*within, per)])

    def across_halves(count):
        def run():
            swap = [(r, (r + members) % rows) for r in range(rows)]
            other = lax.ppermute(listed(lists, own, count), "rows", swap)
            return pick(places, own, other, members)

        return run

    picked = lax.switch(far[0], [across_halves(count) for count in (*across, largest)])
    return exchange(picked, rows)


def local(sketch, blocks, block_rows, block_cols, counts):
    slots, width, _ = blocks.shape
    columns = sketch.shape[1]
    rows, cols = lax.axis_size("rows"), lax.axis_size("cols")
    chosen = fetch(sketch, block_cols, counts, slots, width)
    if chosen[0].shape[1] % 16:
        order = lax.axis_index("rows") % len(chosen) ^ jnp.arange(len(chosen))
        chosen = [jnp.stack(chosen)[order].swapaxes(0, 1).reshape(1, slots, width, columns)[0]]
    partial_rows = block_products(block_rows, counts, blocks, chosen)
    if cols == 2:
        other = lax.ppermute(partial_rows, "cols", [(0, 1), (1, 0)])
        own, gram = sum_and_gram(partial_rows, other)
        pieces = gram.reshape(rows, -1, columns // 2)
        pieces = lax.all_to_all(pieces, "rows", split_axis=0, concat_axis=0, tiled=True)
        gram = spread(jnp.sum(pieces, axis=0), ("rows", "cols"), rows * cols)
        gram = gram.reshape(rows, cols, -1, columns // 2)
    else:
        own = lax.psum_scatter(partial_rows, "cols", scatter_dimension=0, tiled=True)
        gram = lax.psum(matmul(own.T, own, HIGHEST), ("rows", "cols"))
        gram = gram.reshape(1, 1, columns, columns)
    return factor_and_basis(RB * width * rows, gram, own)


def solution(mesh):
    in_specs = (
        P(("rows", "cols"), None),
        P(("rows", "cols"), None, None),
        P(("rows", "cols")),
        P(("rows", "cols")),
        P(("rows", "cols")),
    )
    out_specs = (P(("rows", "cols"), None), P())
    return jax.shard_map(local, mesh=mesh, in_specs=in_specs, out_specs=out_specs, check_vma=False)
```

```python
import functools

import jax
import jax.numpy as jnp
from jax import lax
from jax.experimental import pallas as pl
from jax.experimental.pallas import tpu as pltpu
from jax.sharding import PartitionSpec as P

RB = 4
HIGHEST = lax.Precision.HIGHEST
VMEM = pl.BlockSpec(memory_space=pltpu.VMEM)
SMEM = pl.BlockSpec(memory_space=pltpu.SMEM)
MIB = 1024 * 1024


ACROSS = (12, 14, 16, 18, 20, 24)
WITHIN = (6, 7, 8)


def table_kernel(cols_ref, counts_ref, out_ref):
    slots = cols_ref.shape[0]
    lane = lax.broadcasted_iota(jnp.int32, out_ref.shape, 2)
    table = jnp.where(lane == slots, counts_ref[0], 0)
    for s in range(slots):
        table = jnp.where(lane == s, cols_ref[s], table)
    out_ref[...] = table


def table_copies(block_cols, counts, devices):
    return pl.pallas_call(
        table_kernel,
        out_shape=jax.ShapeDtypeStruct((devices, 1, 128), jnp.int32),
        in_specs=[SMEM, SMEM],
        out_specs=VMEM,
        name="table_copies",
    )(block_cols, counts)


def plan_kernel(per, within, across, table_ref, places_ref, lists_ref, *level_refs):
    devices = table_ref.shape[0]
    slots = places_ref.shape[1]
    rows, cols = lax.axis_size("rows"), lax.axis_size("cols")
    panel = per * rows
    part = panel // 2
    table = table_ref[:, 0, :]
    block = lax.broadcasted_iota(jnp.int32, (devices, panel), 1)
    device = lax.broadcasted_iota(jnp.int32, (devices, panel), 0)
    side, core = device // (devices // 2), device % cols
    asked = [(table[:, s : s + 1] == block) & (s < table[:, slots : slots + 1]) for s in range(slots)]
    some = functools.reduce(jnp.logical_or, asked)
    lines = -(-cols // 8) * 8
    line = lax.broadcasted_iota(jnp.int32, (3 * lines, panel), 0)
    asks = jnp.zeros((3 * lines, panel), jnp.float32)
    for c in range(cols):
        for h in range(2):
            found = jnp.max(jnp.where(some & (core == c) & (side == h), 1.0, 0.0), axis=0, keepdims=True)
            asks = jnp.where(line == c, jnp.maximum(asks, found), asks)
            asks = jnp.where((line == lines * (1 + h) + c) & (block[:1] // part != h), found, asks)
    first = lax.broadcasted_iota(jnp.int32, (panel, panel), 0)
    second = lax.broadcasted_iota(jnp.int32, (panel, panel), 1)
    after = first > second
    near = jnp.where(after & (first // per == second // per), 1.0, 0.0).astype(jnp.bfloat16)
    after = jnp.where(after, 1.0, 0.0).astype(jnp.bfloat16)
    same = jnp.where(first == second, 1.0, 0.0).astype(jnp.bfloat16)
    nt = (((1,), (1,)), ((), ()))

    def ranks(a, b):
        return lax.dot_general(a, b, nt, preferred_element_type=jnp.float32)

    short = asks.astype(jnp.bfloat16)
    near_rank = ranks(short, near)
    far_rank = ranks(short, after)
    longest = jnp.max(jnp.where(line < lines, near_rank + asks, 0.0)).astype(jnp.int32)
    level_refs[0][0] = sum((longest > level).astype(jnp.int32) for level in within)
    longest = jnp.max(jnp.where(line < lines, 0.0, far_rank + asks)).astype(jnp.int32)
    level_refs[1][0] = sum((longest > level).astype(jnp.int32) for level in across)
    me = lax.axis_index("rows")
    half, c = me // (rows // 2), lax.axis_index("cols")

    def row(values, number):
        return jnp.sum(jnp.where(line == number, values, 0.0), axis=0, keepdims=True)

    ids = lax.broadcasted_iota(jnp.int32, (1, panel), 1)
    here = ids // per * per - half * part + row(near_rank, c).astype(jnp.int32)
    there = part + row(far_rank, lines * (1 + half) + c).astype(jnp.int32)
    place = jnp.where(ids // part == half, here, there)
    slot = lax.broadcasted_iota(jnp.int32, places_ref.shape, 1)
    places = jnp.zeros(places_ref.shape, jnp.int32)
    for s in range(slots):
        found = jnp.sum(jnp.where(asked[s], place, 0), axis=1, keepdims=True)
        places = jnp.where(slot == s, found, places)
    places_ref[...] = places
    line = lax.broadcasted_iota(jnp.int32, (panel, 3 * lines), 1)

    def column(values, number):
        return jnp.sum(jnp.where(line == number, values, 0.0), axis=1, keepdims=True)

    turned, near_rank, far_rank = ranks(same, short), ranks(near, short), ranks(after, short)
    ids = lax.broadcasted_iota(jnp.int32, (panel, 1), 0)
    number = lax.broadcasted_iota(jnp.int32, (panel, lists_ref.shape[1]), 1)
    near_rank = column(near_rank, c).astype(jnp.int32)
    here = ids // per * per - half * part + near_rank
    other = lines * (2 - half) + c
    sent = (column(turned, other) > 0.5) & (column(far_rank, other).astype(jnp.int32) == number)
    sent = jnp.sum(jnp.where(sent, here, 0), axis=0, keepdims=True)
    kept = (column(turned, c) > 0.5) & (ids // per == me) & (near_rank == number)
    kept = jnp.sum(jnp.where(kept, ids % per, 0), axis=0, keepdims=True)
    lists_ref[...] = jnp.where(lax.broadcasted_iota(jnp.int32, lists_ref.shape, 0) == 0, sent, kept)


def plan(table, slots, per, within, across):
    devices = table.shape[0]
    return pl.pallas_call(
        functools.partial(plan_kernel, per, within, across),
        out_shape=(
            jax.ShapeDtypeStruct((devices, slots), jnp.int32),
            jax.ShapeDtypeStruct((8, 128), jnp.int32),
            jax.ShapeDtypeStruct((1,), jnp.int32),
            jax.ShapeDtypeStruct((1,), jnp.int32),
        ),
        in_specs=[VMEM],
        out_specs=(VMEM, VMEM, SMEM, SMEM),
        compiler_params=pltpu.CompilerParams(vmem_limit_bytes=48 * MIB),
        name="plan",
    )(table)


def distances(members):
    return [0, *sorted(range(1, members), key=lambda d: (-d.bit_count(), -d))]


def turn_kernel(sketch_ref, out_ref):
    members = out_ref.shape[0]
    me = lax.axis_index("rows") % members
    for i, d in enumerate(distances(members)):
        out_ref[i] = sketch_ref[:, me ^ d]


def turn(sketch):
    blocks, members, height, columns = sketch.shape
    return pl.pallas_call(
        turn_kernel,
        out_shape=jax.ShapeDtypeStruct((members, blocks, height, columns), sketch.dtype),
        in_specs=[VMEM],
        out_specs=VMEM,
        compiler_params=pltpu.CompilerParams(vmem_limit_bytes=24 * MIB),
        cost_estimate=pl.CostEstimate(flops=0, bytes_accessed=4 * sketch.size, transcendentals=0),
        name="turn_stripes",
    )(sketch)


def cut_kernel(lists_ref, stripes_ref, *out_refs):
    for k in range(out_refs[0].shape[0]):
        for i, out_ref in enumerate(out_refs):
            out_ref[k] = stripes_ref[i, lists_ref[1, k]]


def cut(lists, stripes, count):
    members, _, height, columns = stripes.shape
    return pl.pallas_call(
        cut_kernel,
        out_shape=(jax.ShapeDtypeStruct((count, height, columns), stripes.dtype),) * members,
        in_specs=[SMEM, VMEM],
        out_specs=(VMEM,) * members,
        compiler_params=pltpu.CompilerParams(vmem_limit_bytes=24 * MIB),
        name="cut_stripes",
    )(lists, stripes)


def order_kernel(*refs):
    *stripe_refs, all_ref = refs
    members = len(stripe_refs)
    me = lax.axis_index("rows") % members
    per = all_ref.shape[0] // members
    for ref, d in zip(stripe_refs, distances(members)):
        all_ref[pl.ds((me ^ d) * per, ref.shape[0])] = ref[...]


def order(stripes, per):
    _, height, columns = stripes[0].shape
    return pl.pallas_call(
        order_kernel,
        out_shape=jax.ShapeDtypeStruct((len(stripes) * per, height, columns), stripes[0].dtype),
        in_specs=[VMEM] * len(stripes),
        out_specs=VMEM,
        compiler_params=pltpu.CompilerParams(vmem_limit_bytes=24 * MIB),
        name="order_stripes",
    )(*stripes)


def list_kernel(list_ref, all_ref, out_ref):
    for k in range(out_ref.shape[0]):
        out_ref[k] = all_ref[list_ref[0, k]]


def listed(numbers, stripes, count):
    return pl.pallas_call(
        list_kernel,
        out_shape=jax.ShapeDtypeStruct((count, *stripes.shape[1:]), stripes.dtype),
        in_specs=[SMEM, VMEM],
        out_specs=VMEM,
        compiler_params=pltpu.CompilerParams(vmem_limit_bytes=24 * MIB),
        name="listed_stripes",
    )(numbers, stripes)


def pick_kernel(places_ref, own_ref, other_ref, *out_refs):
    members = len(out_refs)
    cols = lax.axis_size("cols")
    here, there = own_ref.shape[0], other_ref.shape[0]
    me = lax.axis_index("rows")
    c = lax.axis_index("cols")
    for d, out_ref in zip(distances(members), out_refs):

        def body(s, carry):
            place = places_ref[(me ^ d) * cols + c, s]
            own = own_ref[jnp.minimum(place, here - 1)]
            other = other_ref[jnp.clip(place - here, 0, there - 1)]
            out_ref[s] = lax.select(place < here, own, other)
            return carry

        lax.fori_loop(0, out_ref.shape[0], body, 0, unroll=True)


def pick(places, own, other, members):
    return pl.pallas_call(
        pick_kernel,
        out_shape=(jax.ShapeDtypeStruct((places.shape[1], *own.shape[1:]), own.dtype),) * members,
        in_specs=[SMEM, VMEM, VMEM],
        out_specs=(VMEM,) * members,
        compiler_params=pltpu.CompilerParams(vmem_limit_bytes=24 * MIB),
        name="pick_stripes",
    )(places, own, other)


def product_kernel(rows_ref, counts_ref, blocks_ref, *refs):
    *chosen_refs, out_ref, whole = refs
    slots, width, _ = blocks_ref.shape
    columns = out_ref.shape[1]
    members = len(chosen_refs)
    me = lax.axis_index("rows") % members
    for ref, d in zip(chosen_refs, distances(members) if members > 1 else [0]):
        whole[me ^ d] = ref[...]
    out_ref[...] = jnp.zeros_like(out_ref)
    for s in range(slots):

        @pl.when(s < counts_ref[0])
        def _():
            piece = whole[:, s].reshape(width, columns)
            product = jnp.dot(blocks_ref[s], piece, preferred_element_type=jnp.float32)
            at = pl.ds(pl.multiple_of(rows_ref[s] * width, width), width)
            out_ref[at, :] += product


def block_products(block_rows, counts, blocks, chosen):
    _, width, _ = blocks.shape
    columns = chosen[0].shape[-1]
    return pl.pallas_call(
        product_kernel,
        out_shape=jax.ShapeDtypeStruct((RB * width, columns), jnp.float32),
        in_specs=[SMEM, SMEM, VMEM] + [VMEM] * len(chosen),
        out_specs=VMEM,
        scratch_shapes=[pltpu.VMEM((len(chosen), *chosen[0].shape), chosen[0].dtype)],
        compiler_params=pltpu.CompilerParams(vmem_limit_bytes=24 * MIB),
        name="block_products",
    )(block_rows, counts, blocks, *chosen)


def gram_kernel(mine_ref, other_ref, own_ref, gram_ref, slab):
    c = lax.axis_index("cols")
    share, width = own_ref.shape[0], gram_ref.shape[1]
    slab[...] = mine_ref[...] + other_ref[...]
    own_ref[...] = slab[pl.ds(pl.multiple_of(c * share, share), share), :]
    right = slab[:, pl.ds(pl.multiple_of(c * width, width), width)]
    gram_ref[...] = lax.dot_general(
        slab[...], right, (((0,), (0,)), ((), ())), precision=HIGHEST, preferred_element_type=jnp.float32
    )


def sum_and_gram(mine, other):
    rows, columns = mine.shape
    return pl.pallas_call(
        gram_kernel,
        out_shape=(
            jax.ShapeDtypeStruct((rows // 2, columns), jnp.float32),
            jax.ShapeDtypeStruct((columns, columns // 2), jnp.float32),
        ),
        in_specs=[VMEM, VMEM],
        out_specs=(VMEM, VMEM),
        scratch_shapes=[pltpu.VMEM((rows, columns), jnp.float32)],
        compiler_params=pltpu.CompilerParams(vmem_limit_bytes=24 * MIB),
        name="sum_and_gram",
    )(mine, other)


def matmul(a, b, precision):
    return jnp.dot(a, b, precision=precision, preferred_element_type=jnp.float32)


def matmul_nt(a, b, precision):
    return lax.dot_general(
        a, b, (((1,), (1,)), ((), ())), precision=precision, preferred_element_type=jnp.float32
    )


def factor_kernel(total_rows, gram_ref, own_ref, basis_ref, factor_ref, whole, scaled, inverse):
    n = factor_ref.shape[0]
    width = gram_ref.shape[-1]
    for c in range(n // width):
        whole[:, c * width : (c + 1) * width] = gram_ref[:, c].reshape(n, width)
    row_ids = lax.broadcasted_iota(jnp.int32, (n, n), 0)
    col_ids = lax.broadcasted_iota(jnp.int32, (n, n), 1)
    diagonal = row_ids == col_ids
    identity = diagonal.astype(jnp.float32)
    half = jnp.where(row_ids > col_ids, 1.0, jnp.where(diagonal, 0.5, 0.0))
    gram = whole[...]
    on_diagonal = jnp.where(diagonal, gram, 0.0)
    down = jnp.sqrt(jnp.sum(on_diagonal, axis=1, keepdims=True))
    across = jnp.sqrt(jnp.sum(on_diagonal, axis=0, keepdims=True))
    up_down = 1.0 / down
    up_across = 1.0 / across
    scaled[...] = gram * up_down * up_across

    def refine(precision):
        w = inverse[...]
        residual = matmul_nt(matmul(w, scaled[...], precision), w, precision) - identity
        inverse[...] = w - matmul(residual * half, w, lax.Precision.DEFAULT)
        return jnp.sum(residual * residual)

    inverse[...] = identity - (scaled[...] - identity) * half
    refine(lax.Precision.DEFAULT)

    def going(state):
        step, size = state
        return (step < 8) & (size > 1e-6)

    def advance(state):
        return state[0] + 1, refine(HIGHEST)

    _, size = lax.while_loop(going, advance, (jnp.int32(0), jnp.float32(1.0)))

    @pl.when(jnp.logical_not(size <= 1e-6))
    def _():
        inverse[...] = identity
        ids = lax.broadcasted_iota(jnp.int32, (n, 1), 0)

        def eliminate(j, carry):
            pivot_row = scaled[pl.ds(j, 1), :]
            inverse_row = inverse[pl.ds(j, 1), :]
            column = jnp.sum(jnp.where(col_ids == j, scaled[...], 0.0), axis=1, keepdims=True)
            pivot = jnp.sum(jnp.where(ids == j, column, 0.0), axis=0, keepdims=True)
            root = 1.0 / jnp.sqrt(pivot)
            ratio = jnp.where(ids > j, column / pivot, jnp.where(ids == j, 1.0 - root, 0.0))
            scaled[...] = scaled[...] - ratio * pivot_row
            inverse[...] = inverse[...] - ratio * inverse_row
            return carry

        lax.fori_loop(0, n, eliminate, 0)
        scaled[...] = whole[...] * up_down * up_across

    w = inverse[...]
    root_rows = jnp.sqrt(jnp.float32(total_rows))
    upper = matmul(w, scaled[...], HIGHEST) * across / root_rows
    factor_ref[...] = jnp.where(row_ids <= col_ids, upper, 0.0)
    basis_ref[...] = matmul_nt(own_ref[...] * up_across, w, HIGHEST) * root_rows


def factor_and_basis(total_rows, gram, own):
    columns = own.shape[1]
    return pl.pallas_call(
        functools.partial(factor_kernel, total_rows),
        out_shape=(
            jax.ShapeDtypeStruct(own.shape, jnp.float32),
            jax.ShapeDtypeStruct((columns, columns), jnp.float32),
        ),
        in_specs=[VMEM, VMEM],
        out_specs=(VMEM, VMEM),
        scratch_shapes=[pltpu.VMEM((columns, columns), jnp.float32)] * 3,
        compiler_params=pltpu.CompilerParams(vmem_limit_bytes=24 * MIB),
        name="factor_and_basis",
    )(gram, own)


def spread(piece, axes, devices):
    copies = jnp.broadcast_to(piece[None], (devices, *piece.shape))
    return lax.all_to_all(copies, axes, split_axis=0, concat_axis=0, tiled=True)


def exchange(pieces, rows):
    order = distances(len(pieces))
    return [
        lax.ppermute(piece, "rows", [(r, r ^ d) for r in range(rows)]) if d else piece
        for piece, d in zip(pieces, order)
    ]


def fetch(sketch, block_cols, counts, slots, width):
    rows, cols = lax.axis_size("rows"), lax.axis_size("cols")
    members = rows // 2
    height = width // members
    columns = sketch.shape[1]
    sketch = sketch.reshape(-1, members, height, columns)
    per = sketch.shape[0]
    largest = min(per * members, slots * members, 128)
    within = tuple(level for level in WITHIN if level < per)
    across = tuple(level for level in ACROSS if level < largest)
    stripes = turn(sketch)
    table = table_copies(block_cols, counts, rows * cols)
    table = lax.all_to_all(table, ("rows", "cols"), split_axis=0, concat_axis=0, tiled=True)
    places, lists, near, far = plan(table, slots, per, within, across)

    def within_half(count):
        def run():
            return order(exchange(cut(lists, stripes, count), rows), per)

        return run

    own = lax.switch(near[0], [within_half(count) for count in (*within, per)])

    def across_halves(count):
        def run():
            swap = [(r, (r + members) % rows) for r in range(rows)]
            other = lax.ppermute(listed(lists, own, count), "rows", swap)
            return pick(places, own, other, members)

        return run

    picked = lax.switch(far[0], [across_halves(count) for count in (*across, largest)])
    return exchange(picked, rows)


def local(sketch, blocks, block_rows, block_cols, counts):
    slots, width, _ = blocks.shape
    columns = sketch.shape[1]
    rows, cols = lax.axis_size("rows"), lax.axis_size("cols")
    chosen = fetch(sketch, block_cols, counts, slots, width)
    if chosen[0].shape[1] % 16:
        order = jnp.argsort(lax.axis_index("rows") % len(chosen) ^ jnp.array(distances(len(chosen))))
        chosen = [jnp.stack(chosen)[order].swapaxes(0, 1).reshape(1, slots, width, columns)[0]]
    partial_rows = block_products(block_rows, counts, blocks, chosen)
    if cols == 2:
        other = lax.ppermute(partial_rows, "cols", [(0, 1), (1, 0)])
        own, gram = sum_and_gram(partial_rows, other)
        pieces = gram.reshape(rows, -1, columns // 2)
        pieces = lax.all_to_all(pieces, "rows", split_axis=0, concat_axis=0, tiled=True)
        gram = spread(jnp.sum(pieces, axis=0), ("rows", "cols"), rows * cols)
        gram = gram.reshape(rows, cols, -1, columns // 2)
    else:
        own = lax.psum_scatter(partial_rows, "cols", scatter_dimension=0, tiled=True)
        gram = lax.psum(matmul(own.T, own, HIGHEST), ("rows", "cols"))
        gram = gram.reshape(1, 1, columns, columns)
    return factor_and_basis(RB * width * rows, gram, own)


def solution(mesh):
    in_specs = (
        P(("rows", "cols"), None),
        P(("rows", "cols"), None, None),
        P(("rows", "cols")),
        P(("rows", "cols")),
        P(("rows", "cols")),
    )
    out_specs = (P(("rows", "cols"), None), P())
    return jax.shard_map(local, mesh=mesh, in_specs=in_specs, out_specs=out_specs, check_vma=False)
```

```python
import functools

import jax
import jax.numpy as jnp
from jax import lax
from jax.experimental import pallas as pl
from jax.experimental.pallas import tpu as pltpu
from jax.sharding import PartitionSpec as P

RB = 4
HIGHEST = lax.Precision.HIGHEST
VMEM = pl.BlockSpec(memory_space=pltpu.VMEM)
SMEM = pl.BlockSpec(memory_space=pltpu.SMEM)
MIB = 1024 * 1024


ACROSS = ((14, 5), (16, 5), (20, 5), (20, 6), (24, 6), (24, 8))
WITHIN = (6, 7, 8)


def table_kernel(cols_ref, counts_ref, out_ref):
    slots = cols_ref.shape[0]
    lane = lax.broadcasted_iota(jnp.int32, out_ref.shape, 2)
    table = jnp.where(lane == slots, counts_ref[0], 0)
    for s in range(slots):
        table = jnp.where(lane == s, cols_ref[s], table)
    out_ref[...] = table


def table_copies(block_cols, counts, devices):
    return pl.pallas_call(
        table_kernel,
        out_shape=jax.ShapeDtypeStruct((devices, 1, 128), jnp.int32),
        in_specs=[SMEM, SMEM],
        out_specs=VMEM,
        name="table_copies",
    )(block_cols, counts)


def plan_kernel(per, within, across, table_ref, near_ref, far_ref, spots_ref, lists_ref, *level_refs):
    devices = table_ref.shape[0]
    slots = spots_ref.shape[1]
    rows, cols = lax.axis_size("rows"), lax.axis_size("cols")
    panel = per * rows
    part = panel // 2
    groups = [range(at, min(at + 64, devices)) for at in range(0, devices, 64)]

    def read(group):
        table = table_ref[group.start : group.stop, 0, :]
        shape = (len(group), panel)
        block = lax.broadcasted_iota(jnp.int32, shape, 1)
        device = lax.broadcasted_iota(jnp.int32, shape, 0) + group.start
        asked = [(table[:, s : s + 1] == block) & (s < table[:, slots : slots + 1]) for s in range(slots)]
        return table, asked, device // (devices // 2), device % cols

    lines = -(-cols // 8) * 8
    line = lax.broadcasted_iota(jnp.int32, (3 * lines, panel), 0)
    ids = lax.broadcasted_iota(jnp.int32, (1, panel), 1)
    asks = jnp.zeros((3 * lines, panel), jnp.float32)
    for group in groups:
        _, asked, side, core = read(group)
        some = functools.reduce(jnp.logical_or, asked)
        for c in range(cols):
            for h in range(2):
                found = jnp.max(jnp.where(some & (core == c) & (side == h), 1.0, 0.0), axis=0, keepdims=True)
                reached = (line == c) | ((line == lines * (1 + h) + c) & (ids // part != h))
                asks = jnp.where(reached, jnp.maximum(asks, found), asks)
    first = lax.broadcasted_iota(jnp.int32, (panel, panel), 0)
    second = lax.broadcasted_iota(jnp.int32, (panel, panel), 1)
    after = first > second
    near = jnp.where(after & (first // per == second // per), 1.0, 0.0).astype(jnp.bfloat16)
    after = jnp.where(after, 1.0, 0.0).astype(jnp.bfloat16)
    same = jnp.where(first == second, 1.0, 0.0).astype(jnp.bfloat16)
    nt = (((1,), (1,)), ((), ()))

    def ranks(a, b):
        return lax.dot_general(a, b, nt, preferred_element_type=jnp.float32)

    short = asks.astype(jnp.bfloat16)
    near_rank = ranks(short, near)
    far_rank = ranks(short, after)
    longest = jnp.max(jnp.where(line < lines, near_rank + asks, 0.0)).astype(jnp.int32)
    level_refs[0][0] = sum((longest > level).astype(jnp.int32) for level in within)
    longest = jnp.max(jnp.where(line < lines, 0.0, far_rank + asks)).astype(jnp.int32)
    me = lax.axis_index("rows")
    half, c = me // (rows // 2), lax.axis_index("cols")

    def row(values, number):
        return jnp.sum(jnp.where(line == number, values, 0.0), axis=0, keepdims=True)

    here = ids // per * per - half * part + row(near_rank, c).astype(jnp.int32)
    there = row(far_rank, lines * (1 + half) + c).astype(jnp.int32)
    place = jnp.where(ids // part == half, here, there)
    most = jnp.zeros((1, 1), jnp.float32)
    for group in groups:
        table, asked, side, _ = read(group)
        size = len(group)
        slot = lax.broadcasted_iota(jnp.int32, (size, slots), 1)
        nears = fars = spots = jnp.zeros((size, slots), jnp.int32)
        n_near = n_far = jnp.zeros((size, 1), jnp.int32)
        for s in range(slots):
            found = jnp.sum(jnp.where(asked[s], place, 0), axis=1, keepdims=True)
            live = s < table[:, slots : slots + 1]
            is_near = table[:, s : s + 1] // part == side[:, :1]
            nears = jnp.where((slot == n_near) & live & is_near, found, nears)
            fars = jnp.where((slot == n_far) & live & jnp.logical_not(is_near), found, fars)
            spots = jnp.where(slot == s, jnp.where(is_near, n_near, slots + n_far), spots)
            n_near = n_near + jnp.where(live & is_near, 1, 0)
            n_far = n_far + jnp.where(live & jnp.logical_not(is_near), 1, 0)
        at = slice(group.start, group.stop)
        near_ref[at], far_ref[at], spots_ref[at] = nears, fars, spots
        counts = jnp.maximum(n_near, n_far).astype(jnp.float32)
        most = jnp.maximum(most, jnp.max(counts, axis=0, keepdims=True))
    most = jnp.max(most).astype(jnp.int32)
    level_refs[1][0] = sum(((longest > count) | (most > some)).astype(jnp.int32) for count, some in across)
    line = lax.broadcasted_iota(jnp.int32, (panel, 3 * lines), 1)

    def column(values, number):
        return jnp.sum(jnp.where(line == number, values, 0.0), axis=1, keepdims=True)

    turned, near_rank, far_rank = ranks(same, short), ranks(near, short), ranks(after, short)
    ids = lax.broadcasted_iota(jnp.int32, (panel, 1), 0)
    number = lax.broadcasted_iota(jnp.int32, (panel, lists_ref.shape[1]), 1)
    near_rank = column(near_rank, c).astype(jnp.int32)
    here = ids // per * per - half * part + near_rank
    other = lines * (2 - half) + c
    sent = (column(turned, other) > 0.5) & (column(far_rank, other).astype(jnp.int32) == number)
    sent = jnp.sum(jnp.where(sent, here, 0), axis=0, keepdims=True)
    kept = (column(turned, c) > 0.5) & (ids // per == me) & (near_rank == number)
    kept = jnp.sum(jnp.where(kept, ids % per, 0), axis=0, keepdims=True)
    lists_ref[...] = jnp.where(lax.broadcasted_iota(jnp.int32, lists_ref.shape, 0) == 0, sent, kept)


def plan(table, slots, per, within, across):
    devices = table.shape[0]
    return pl.pallas_call(
        functools.partial(plan_kernel, per, within, across),
        out_shape=(
            *[jax.ShapeDtypeStruct((devices, slots), jnp.int32)] * 3,
            jax.ShapeDtypeStruct((8, 128), jnp.int32),
            jax.ShapeDtypeStruct((1,), jnp.int32),
            jax.ShapeDtypeStruct((1,), jnp.int32),
        ),
        in_specs=[VMEM],
        out_specs=(VMEM, VMEM, VMEM, VMEM, SMEM, SMEM),
        compiler_params=pltpu.CompilerParams(vmem_limit_bytes=48 * MIB),
        name="plan",
    )(table)


def distances(members):
    return [0, *sorted(range(1, members), key=lambda d: (-d.bit_count(), -d))]


def turn_kernel(sketch_ref, out_ref):
    members = out_ref.shape[0]
    me = lax.axis_index("rows") % members
    for i, d in enumerate(distances(members)):
        out_ref[i] = sketch_ref[:, me ^ d]


def turn(sketch):
    blocks, members, height, columns = sketch.shape
    return pl.pallas_call(
        turn_kernel,
        out_shape=jax.ShapeDtypeStruct((members, blocks, height, columns), sketch.dtype),
        in_specs=[VMEM],
        out_specs=VMEM,
        compiler_params=pltpu.CompilerParams(vmem_limit_bytes=24 * MIB),
        cost_estimate=pl.CostEstimate(flops=0, bytes_accessed=4 * sketch.size, transcendentals=0),
        name="turn_stripes",
    )(sketch)


def cut_kernel(lists_ref, stripes_ref, *out_refs):
    for k in range(out_refs[0].shape[0]):
        for i, out_ref in enumerate(out_refs):
            out_ref[k] = stripes_ref[i, lists_ref[1, k]]


def cut(lists, stripes, count):
    members, _, height, columns = stripes.shape
    return pl.pallas_call(
        cut_kernel,
        out_shape=(jax.ShapeDtypeStruct((count, height, columns), stripes.dtype),) * members,
        in_specs=[SMEM, VMEM],
        out_specs=(VMEM,) * members,
        compiler_params=pltpu.CompilerParams(vmem_limit_bytes=24 * MIB),
        name="cut_stripes",
    )(lists, stripes)


def order_kernel(*refs):
    *stripe_refs, all_ref = refs
    members = len(stripe_refs)
    me = lax.axis_index("rows") % members
    per = all_ref.shape[0] // members
    for ref, d in zip(stripe_refs, distances(members)):
        all_ref[pl.ds((me ^ d) * per, ref.shape[0])] = ref[...]


def order(stripes, per):
    _, height, columns = stripes[0].shape
    return pl.pallas_call(
        order_kernel,
        out_shape=jax.ShapeDtypeStruct((len(stripes) * per, height, columns), stripes[0].dtype),
        in_specs=[VMEM] * len(stripes),
        out_specs=VMEM,
        compiler_params=pltpu.CompilerParams(vmem_limit_bytes=24 * MIB),
        name="order_stripes",
    )(*stripes)


def list_kernel(list_ref, all_ref, out_ref):
    for k in range(out_ref.shape[0]):
        out_ref[k] = all_ref[list_ref[0, k]]


def listed(numbers, stripes, count):
    return pl.pallas_call(
        list_kernel,
        out_shape=jax.ShapeDtypeStruct((count, *stripes.shape[1:]), stripes.dtype),
        in_specs=[SMEM, VMEM],
        out_specs=VMEM,
        compiler_params=pltpu.CompilerParams(vmem_limit_bytes=24 * MIB),
        name="listed_stripes",
    )(numbers, stripes)


def pick_kernel(places_ref, stripes_ref, *out_refs):
    me = lax.axis_index("rows")
    c = lax.axis_index("cols")
    last = stripes_ref.shape[0] - 1
    for d, out_ref in zip(distances(len(out_refs)), out_refs):
        for s in range(out_ref.shape[0]):
            place = places_ref[(me ^ d) * lax.axis_size("cols") + c, s]
            out_ref[s] = stripes_ref[jnp.minimum(place, last)]


def pick(places, stripes, count, members):
    return pl.pallas_call(
        pick_kernel,
        out_shape=(jax.ShapeDtypeStruct((count, *stripes.shape[1:]), stripes.dtype),) * members,
        in_specs=[SMEM, VMEM],
        out_specs=(VMEM,) * members,
        compiler_params=pltpu.CompilerParams(vmem_limit_bytes=24 * MIB),
        name="pick_stripes",
    )(places, stripes)


def product_kernel(rows_ref, counts_ref, spots_ref, blocks_ref, *refs):
    *chosen_refs, out_ref, whole = refs
    slots, width, _ = blocks_ref.shape
    members, spots, _, columns = whole.shape
    me = lax.axis_index("rows")
    device = me * lax.axis_size("cols") + lax.axis_index("cols")
    for i, d in enumerate(distances(members)):
        near_ref, far_ref = chosen_refs[i], chosen_refs[members + i]
        whole[me % members ^ d, : near_ref.shape[0]] = near_ref[...]
        whole[me % members ^ d, slots : slots + far_ref.shape[0]] = far_ref[...]
    out_ref[...] = jnp.zeros_like(out_ref)
    for s in range(slots):

        @pl.when(s < counts_ref[0])
        def _():
            piece = whole[:, jnp.minimum(spots_ref[device, s], spots - 1)].reshape(width, columns)
            product = jnp.dot(blocks_ref[s], piece, preferred_element_type=jnp.float32)
            at = pl.ds(pl.multiple_of(rows_ref[s] * width, width), width)
            out_ref[at, :] += product


def block_products(block_rows, counts, spots, blocks, near, far):
    slots, width, _ = blocks.shape
    _, height, columns = near[0].shape
    members = len(near)
    return pl.pallas_call(
        product_kernel,
        out_shape=jax.ShapeDtypeStruct((RB * width, columns), jnp.float32),
        in_specs=[SMEM, SMEM, SMEM, VMEM] + [VMEM] * (2 * members),
        out_specs=VMEM,
        scratch_shapes=[pltpu.VMEM((members, 2 * slots, height, columns), near[0].dtype)],
        compiler_params=pltpu.CompilerParams(vmem_limit_bytes=32 * MIB),
        name="block_products",
    )(block_rows, counts, spots, blocks, *near, *far)


def gram_kernel(mine_ref, other_ref, own_ref, gram_ref, slab):
    c = lax.axis_index("cols")
    share, width = own_ref.shape[0], gram_ref.shape[1]
    slab[...] = mine_ref[...] + other_ref[...]
    own_ref[...] = slab[pl.ds(pl.multiple_of(c * share, share), share), :]
    right = slab[:, pl.ds(pl.multiple_of(c * width, width), width)]
    gram_ref[...] = lax.dot_general(
        slab[...], right, (((0,), (0,)), ((), ())), precision=HIGHEST, preferred_element_type=jnp.float32
    )


def sum_and_gram(mine, other):
    rows, columns = mine.shape
    return pl.pallas_call(
        gram_kernel,
        out_shape=(
            jax.ShapeDtypeStruct((rows // 2, columns), jnp.float32),
            jax.ShapeDtypeStruct((columns, columns // 2), jnp.float32),
        ),
        in_specs=[VMEM, VMEM],
        out_specs=(VMEM, VMEM),
        scratch_shapes=[pltpu.VMEM((rows, columns), jnp.float32)],
        compiler_params=pltpu.CompilerParams(vmem_limit_bytes=24 * MIB),
        name="sum_and_gram",
    )(mine, other)


def matmul(a, b, precision):
    return jnp.dot(a, b, precision=precision, preferred_element_type=jnp.float32)


def matmul_nt(a, b, precision):
    return lax.dot_general(
        a, b, (((1,), (1,)), ((), ())), precision=precision, preferred_element_type=jnp.float32
    )


def split_matmul(times, passes, a, b):
    a_high, b_high = a.astype(jnp.bfloat16), b.astype(jnp.bfloat16)
    result = times(a_high, b_high, None)
    if passes == 3:
        a_low = (a - a_high.astype(jnp.float32)).astype(jnp.bfloat16)
        b_low = (b - b_high.astype(jnp.float32)).astype(jnp.bfloat16)
        result += times(a_high, b_low, None) + times(a_low, b_high, None)
    return result


def factor_kernel(total_rows, gram_ref, own_ref, basis_ref, factor_ref, whole, scaled, inverse, product):
    n = factor_ref.shape[0]
    width = gram_ref.shape[-1]
    for c in range(n // width):
        whole[:, c * width : (c + 1) * width] = gram_ref[:, c].reshape(n, width)
    row_ids = lax.broadcasted_iota(jnp.int32, (n, n), 0)
    col_ids = lax.broadcasted_iota(jnp.int32, (n, n), 1)
    diagonal = row_ids == col_ids
    identity = diagonal.astype(jnp.float32)
    half = jnp.where(row_ids > col_ids, 1.0, jnp.where(diagonal, 0.5, 0.0))
    gram = whole[...]
    on_diagonal = jnp.where(diagonal, gram, 0.0)
    down = jnp.sqrt(jnp.sum(on_diagonal, axis=1, keepdims=True))
    across = jnp.sqrt(jnp.sum(on_diagonal, axis=0, keepdims=True))
    up_down = 1.0 / down
    up_across = 1.0 / across
    scaled[...] = gram * up_down * up_across

    def refine(times, times_nt):
        w = inverse[...]
        upper = times(w, scaled[...])
        residual = times_nt(upper, w) - identity
        step = residual * half
        inverse[...] = w - matmul(step, w, lax.Precision.DEFAULT)
        product[...] = upper - matmul(step, upper, lax.Precision.DEFAULT)
        return jnp.sum(residual * residual)

    def exactly(times):
        return functools.partial(times, precision=HIGHEST)

    inverse[...] = identity - (scaled[...] - identity) * half
    for passes in (1, 3):
        refine(functools.partial(split_matmul, matmul, passes), functools.partial(split_matmul, matmul_nt, passes))

    def going(state):
        step, size = state
        return (step < 8) & (size > 1e-6)

    def advance(state):
        return state[0] + 1, refine(exactly(matmul), exactly(matmul_nt))

    _, size = lax.while_loop(going, advance, (jnp.int32(0), jnp.float32(1.0)))

    @pl.when(jnp.logical_not(size <= 1e-6))
    def _():
        inverse[...] = identity
        ids = lax.broadcasted_iota(jnp.int32, (n, 1), 0)

        def eliminate(j, carry):
            pivot_row = scaled[pl.ds(j, 1), :]
            inverse_row = inverse[pl.ds(j, 1), :]
            column = jnp.sum(jnp.where(col_ids == j, scaled[...], 0.0), axis=1, keepdims=True)
            pivot = jnp.sum(jnp.where(ids == j, column, 0.0), axis=0, keepdims=True)
            root = 1.0 / jnp.sqrt(pivot)
            ratio = jnp.where(ids > j, column / pivot, jnp.where(ids == j, 1.0 - root, 0.0))
            scaled[...] = scaled[...] - ratio * pivot_row
            inverse[...] = inverse[...] - ratio * inverse_row
            return carry

        lax.fori_loop(0, n, eliminate, 0)
        product[...] = matmul(inverse[...], whole[...] * up_down * up_across, HIGHEST)

    w = inverse[...]
    root_rows = jnp.sqrt(jnp.float32(total_rows))
    upper = product[...] * across / root_rows
    factor_ref[...] = jnp.where(row_ids <= col_ids, upper, 0.0)
    basis_ref[...] = matmul_nt(own_ref[...] * up_across, w, HIGHEST) * root_rows


def factor_and_basis(total_rows, gram, own):
    columns = own.shape[1]
    return pl.pallas_call(
        functools.partial(factor_kernel, total_rows),
        out_shape=(
            jax.ShapeDtypeStruct(own.shape, jnp.float32),
            jax.ShapeDtypeStruct((columns, columns), jnp.float32),
        ),
        in_specs=[VMEM, VMEM],
        out_specs=(VMEM, VMEM),
        scratch_shapes=[pltpu.VMEM((columns, columns), jnp.float32)] * 4,
        compiler_params=pltpu.CompilerParams(vmem_limit_bytes=24 * MIB),
        name="factor_and_basis",
    )(gram, own)


def spread(piece, axes, devices):
    copies = jnp.broadcast_to(piece[None], (devices, *piece.shape))
    return lax.all_to_all(copies, axes, split_axis=0, concat_axis=0, tiled=True)


def exchange(pieces, rows):
    order = distances(len(pieces))
    return [
        lax.ppermute(piece, "rows", [(r, r ^ d) for r in range(rows)]) if d else piece
        for piece, d in zip(pieces, order)
    ]


def fetch_and_multiply(sketch, blocks, block_rows, block_cols, counts):
    slots, width, _ = blocks.shape
    rows, cols = lax.axis_size("rows"), lax.axis_size("cols")
    members = rows // 2
    height = width // members
    columns = sketch.shape[1]
    sketch = sketch.reshape(-1, members, height, columns)
    per = sketch.shape[0]
    largest = min(per * members, slots * members, 128)
    within = tuple(level for level in WITHIN if level < per)
    across = tuple(level for level in ACROSS if level[0] < largest and members <= 8 and slots >= 8)
    stripes = turn(sketch)
    table = table_copies(block_cols, counts, rows * cols)
    table = lax.all_to_all(table, ("rows", "cols"), split_axis=0, concat_axis=0, tiled=True)
    near, far, spots, lists, level_within, level_across = plan(table, slots, per, within, across)

    def within_half(count):
        def run():
            return order(exchange(cut(lists, stripes, count), rows), per)

        return run

    own = lax.switch(level_within[0], [within_half(count) for count in (*within, per)])

    def across_halves(count, some):
        def run():
            swap = [(r, (r + members) % rows) for r in range(rows)]
            other = lax.ppermute(listed(lists, own, count), "rows", swap)
            nears = exchange(pick(near, own, some, members), rows)
            fars = exchange(pick(far, other, some, members), rows)
            return block_products(block_rows, counts, spots, blocks, nears, fars)

        return run

    return lax.switch(level_across[0], [across_halves(*level) for level in (*across, (largest, slots))])


def local(sketch, blocks, block_rows, block_cols, counts):
    _, width, _ = blocks.shape
    columns = sketch.shape[1]
    rows, cols = lax.axis_size("rows"), lax.axis_size("cols")
    partial_rows = fetch_and_multiply(sketch, blocks, block_rows, block_cols, counts)
    if cols == 2:
        other = lax.ppermute(partial_rows, "cols", [(0, 1), (1, 0)])
        own, gram = sum_and_gram(partial_rows, other)
        pieces = gram.reshape(rows, -1, columns // 2)
        pieces = lax.all_to_all(pieces, "rows", split_axis=0, concat_axis=0, tiled=True)
        gram = spread(jnp.sum(pieces, axis=0), ("rows", "cols"), rows * cols)
        gram = gram.reshape(rows, cols, -1, columns // 2)
    else:
        own = lax.psum_scatter(partial_rows, "cols", scatter_dimension=0, tiled=True)
        gram = lax.psum(matmul(own.T, own, HIGHEST), ("rows", "cols"))
        gram = gram.reshape(1, 1, columns, columns)
    return factor_and_basis(RB * width * rows, gram, own)


def solution(mesh):
    in_specs = (
        P(("rows", "cols"), None),
        P(("rows", "cols"), None, None),
        P(("rows", "cols")),
        P(("rows", "cols")),
        P(("rows", "cols")),
    )
    out_specs = (P(("rows", "cols"), None), P())
    return jax.shard_map(local, mesh=mesh, in_specs=in_specs, out_specs=out_specs, check_vma=False)
```

```python
import functools

import jax
import jax.numpy as jnp
from jax import lax
from jax.experimental import pallas as pl
from jax.experimental.pallas import tpu as pltpu
from jax.sharding import PartitionSpec as P

RB = 4
HIGHEST = lax.Precision.HIGHEST
VMEM = pl.BlockSpec(memory_space=pltpu.VMEM)
SMEM = pl.BlockSpec(memory_space=pltpu.SMEM)
MIB = 1024 * 1024


ACROSS = ((14, 5), (16, 5), (20, 5), (20, 6), (24, 6), (24, 8))
WITHIN = (6, 7, 8)


def table_kernel(cols_ref, counts_ref, out_ref):
    slots = cols_ref.shape[0]
    lane = lax.broadcasted_iota(jnp.int32, out_ref.shape, 2)
    table = jnp.where(lane == slots, counts_ref[0], 0)
    for s in range(slots):
        table = jnp.where(lane == s, cols_ref[s], table)
    out_ref[...] = table


def table_copies(block_cols, counts, devices):
    return pl.pallas_call(
        table_kernel,
        out_shape=jax.ShapeDtypeStruct((devices, 1, 128), jnp.int32),
        in_specs=[SMEM, SMEM],
        out_specs=VMEM,
        name="table_copies",
    )(block_cols, counts)


def over(values, size):
    return values >> (size.bit_length() - 1)


def plan_kernel(per, within, across, table_ref, near_ref, far_ref, spots_ref, lists_ref, *level_refs):
    devices = table_ref.shape[0]
    slots = spots_ref.shape[1]
    rows, cols = lax.axis_size("rows"), lax.axis_size("cols")
    panel = per * rows
    part = panel // 2
    groups = [range(at, min(at + 64, devices)) for at in range(0, devices, 64)]

    def read(group):
        table = table_ref[group.start : group.stop, 0, :]
        shape = (len(group), panel)
        block = lax.broadcasted_iota(jnp.int32, shape, 1)
        device = lax.broadcasted_iota(jnp.int32, shape, 0) + group.start
        asked = [(table[:, s : s + 1] == block) & (s < table[:, slots : slots + 1]) for s in range(slots)]
        return table, asked, over(device, devices // 2), device & (cols - 1)

    lines = -(-cols // 8) * 8
    line = lax.broadcasted_iota(jnp.int32, (3 * lines, panel), 0)
    ids = lax.broadcasted_iota(jnp.int32, (1, panel), 1)
    asks = jnp.zeros((3 * lines, panel), jnp.float32)
    for group in groups:
        _, asked, side, core = read(group)
        some = functools.reduce(jnp.logical_or, asked)
        for c in range(cols):
            for h in range(2):
                found = jnp.max(jnp.where(some & (core == c) & (side == h), 1.0, 0.0), axis=0, keepdims=True)
                reached = (line == c) | ((line == lines * (1 + h) + c) & (over(ids, part) != h))
                asks = jnp.where(reached, jnp.maximum(asks, found), asks)
    first = lax.broadcasted_iota(jnp.int32, (panel, panel), 0)
    second = lax.broadcasted_iota(jnp.int32, (panel, panel), 1)
    after = first > second
    near = jnp.where(after & ((first ^ second) < per), 1.0, 0.0).astype(jnp.bfloat16)
    after = jnp.where(after, 1.0, 0.0).astype(jnp.bfloat16)
    same = jnp.where(first == second, 1.0, 0.0).astype(jnp.bfloat16)
    nt = (((1,), (1,)), ((), ()))

    def ranks(a, b):
        return lax.dot_general(a, b, nt, preferred_element_type=jnp.float32)

    short = asks.astype(jnp.bfloat16)
    near_rank = ranks(short, near)
    far_rank = ranks(short, after)
    longest = jnp.max(jnp.where(line < lines, near_rank + asks, 0.0)).astype(jnp.int32)
    level_refs[0][0] = sum((longest > level).astype(jnp.int32) for level in within)
    longest = jnp.max(jnp.where(line < lines, 0.0, far_rank + asks)).astype(jnp.int32)
    me = lax.axis_index("rows")
    half, c = over(me, rows // 2), lax.axis_index("cols")

    def row(values, number):
        return jnp.sum(jnp.where(line == number, values, 0.0), axis=0, keepdims=True)

    here = (ids & -per) - half * part + row(near_rank, c).astype(jnp.int32)
    there = row(far_rank, lines * (1 + half) + c).astype(jnp.int32)
    place = jnp.where(over(ids, part) == half, here, there)
    most = jnp.zeros((1, 1), jnp.float32)
    for group in groups:
        table, asked, side, _ = read(group)
        size = len(group)
        slot = lax.broadcasted_iota(jnp.int32, (size, slots), 1)
        nears = fars = spots = jnp.zeros((size, slots), jnp.int32)
        n_near = n_far = jnp.zeros((size, 1), jnp.int32)
        for s in range(slots):
            found = jnp.sum(jnp.where(asked[s], place, 0), axis=1, keepdims=True)
            live = s < table[:, slots : slots + 1]
            is_near = over(table[:, s : s + 1], part) == side[:, :1]
            nears = jnp.where((slot == n_near) & live & is_near, found, nears)
            fars = jnp.where((slot == n_far) & live & jnp.logical_not(is_near), found, fars)
            spots = jnp.where(slot == s, jnp.where(is_near, n_near, slots + n_far), spots)
            n_near = n_near + jnp.where(live & is_near, 1, 0)
            n_far = n_far + jnp.where(live & jnp.logical_not(is_near), 1, 0)
        at = slice(group.start, group.stop)
        near_ref[at], far_ref[at], spots_ref[at] = nears, fars, spots
        counts = jnp.maximum(n_near, n_far).astype(jnp.float32)
        most = jnp.maximum(most, jnp.max(counts, axis=0, keepdims=True))
    most = jnp.max(most).astype(jnp.int32)
    level_refs[1][0] = sum(((longest > count) | (most > some)).astype(jnp.int32) for count, some in across)
    line = lax.broadcasted_iota(jnp.int32, (panel, 3 * lines), 1)

    def column(values, number):
        return jnp.sum(jnp.where(line == number, values, 0.0), axis=1, keepdims=True)

    turned, near_rank, far_rank = ranks(same, short), ranks(near, short), ranks(after, short)
    ids = lax.broadcasted_iota(jnp.int32, (panel, 1), 0)
    number = lax.broadcasted_iota(jnp.int32, (panel, lists_ref.shape[1]), 1)
    near_rank = column(near_rank, c).astype(jnp.int32)
    here = (ids & -per) - half * part + near_rank
    other = lines * (2 - half) + c
    sent = (column(turned, other) > 0.5) & (column(far_rank, other).astype(jnp.int32) == number)
    sent = jnp.sum(jnp.where(sent, here, 0), axis=0, keepdims=True)
    kept = (column(turned, c) > 0.5) & (over(ids, per) == me) & (near_rank == number)
    kept = jnp.sum(jnp.where(kept, ids & (per - 1), 0), axis=0, keepdims=True)
    lists_ref[...] = jnp.where(lax.broadcasted_iota(jnp.int32, lists_ref.shape, 0) == 0, sent, kept)


def plan(table, slots, per, within, across):
    devices = table.shape[0]
    return pl.pallas_call(
        functools.partial(plan_kernel, per, within, across),
        out_shape=(
            *[jax.ShapeDtypeStruct((devices, slots), jnp.int32)] * 3,
            jax.ShapeDtypeStruct((8, 128), jnp.int32),
            jax.ShapeDtypeStruct((1,), jnp.int32),
            jax.ShapeDtypeStruct((1,), jnp.int32),
        ),
        in_specs=[VMEM],
        out_specs=(VMEM, VMEM, VMEM, VMEM, SMEM, SMEM),
        compiler_params=pltpu.CompilerParams(vmem_limit_bytes=48 * MIB),
        name="plan",
    )(table)


def distances(members):
    return [0, *sorted(range(1, members), key=lambda d: (-d.bit_count(), -d))]


def turn_kernel(sketch_ref, out_ref):
    members = out_ref.shape[0]
    me = lax.axis_index("rows") % members
    for i, d in enumerate(distances(members)):
        out_ref[i] = sketch_ref[:, me ^ d]


def turn(sketch):
    blocks, members, height, columns = sketch.shape
    return pl.pallas_call(
        turn_kernel,
        out_shape=jax.ShapeDtypeStruct((members, blocks, height, columns), sketch.dtype),
        in_specs=[VMEM],
        out_specs=VMEM,
        compiler_params=pltpu.CompilerParams(vmem_limit_bytes=24 * MIB),
        cost_estimate=pl.CostEstimate(flops=0, bytes_accessed=4 * sketch.size, transcendentals=0),
        name="turn_stripes",
    )(sketch)


def cut_kernel(lists_ref, stripes_ref, *out_refs):
    for k in range(out_refs[0].shape[0]):
        for i, out_ref in enumerate(out_refs):
            out_ref[k] = stripes_ref[i, lists_ref[1, k]]


def cut(lists, stripes, count):
    members, _, height, columns = stripes.shape
    return pl.pallas_call(
        cut_kernel,
        out_shape=(jax.ShapeDtypeStruct((count, height, columns), stripes.dtype),) * members,
        in_specs=[SMEM, VMEM],
        out_specs=(VMEM,) * members,
        compiler_params=pltpu.CompilerParams(vmem_limit_bytes=24 * MIB),
        name="cut_stripes",
    )(lists, stripes)


def order_kernel(*refs):
    *stripe_refs, all_ref = refs
    members = len(stripe_refs)
    me = lax.axis_index("rows") % members
    per = all_ref.shape[0] // members
    for ref, d in zip(stripe_refs, distances(members)):
        all_ref[pl.ds((me ^ d) * per, ref.shape[0])] = ref[...]


def order(stripes, per):
    _, height, columns = stripes[0].shape
    return pl.pallas_call(
        order_kernel,
        out_shape=jax.ShapeDtypeStruct((len(stripes) * per, height, columns), stripes[0].dtype),
        in_specs=[VMEM] * len(stripes),
        out_specs=VMEM,
        compiler_params=pltpu.CompilerParams(vmem_limit_bytes=24 * MIB),
        name="order_stripes",
    )(*stripes)


def list_kernel(list_ref, all_ref, out_ref):
    for k in range(out_ref.shape[0]):
        out_ref[k] = all_ref[list_ref[0, k]]


def listed(numbers, stripes, count):
    return pl.pallas_call(
        list_kernel,
        out_shape=jax.ShapeDtypeStruct((count, *stripes.shape[1:]), stripes.dtype),
        in_specs=[SMEM, VMEM],
        out_specs=VMEM,
        compiler_params=pltpu.CompilerParams(vmem_limit_bytes=24 * MIB),
        name="listed_stripes",
    )(numbers, stripes)


def pick_kernel(places_ref, stripes_ref, *out_refs):
    me = lax.axis_index("rows")
    c = lax.axis_index("cols")
    last = stripes_ref.shape[0] - 1
    for d, out_ref in zip(distances(len(out_refs)), out_refs):
        for s in range(out_ref.shape[0]):
            place = places_ref[(me ^ d) * lax.axis_size("cols") + c, s]
            out_ref[s] = stripes_ref[jnp.minimum(place, last)]


def pick(places, stripes, count, members):
    return pl.pallas_call(
        pick_kernel,
        out_shape=(jax.ShapeDtypeStruct((count, *stripes.shape[1:]), stripes.dtype),) * members,
        in_specs=[SMEM, VMEM],
        out_specs=(VMEM,) * members,
        compiler_params=pltpu.CompilerParams(vmem_limit_bytes=24 * MIB),
        name="pick_stripes",
    )(places, stripes)


def gather_kernel(spots_ref, *refs):
    *chosen_refs, out_ref = refs
    members, slots = out_ref.shape[:2]
    me = lax.axis_index("rows")
    device = me * lax.axis_size("cols") + lax.axis_index("cols")
    for s in range(slots):
        spot = spots_ref[device, s]

        def put(chosen_refs, at):
            for ref, d in zip(chosen_refs, distances(members)):
                out_ref[me % members ^ d, s] = ref[jnp.minimum(at, ref.shape[0] - 1)]

        pl.when(spot < slots)(functools.partial(put, chosen_refs[:members], spot))
        pl.when(spot >= slots)(functools.partial(put, chosen_refs[members:], spot - slots))


def gather(spots, near, far):
    _, height, columns = near[0].shape
    members, slots = len(near), spots.shape[1]
    return pl.pallas_call(
        gather_kernel,
        out_shape=jax.ShapeDtypeStruct((members, slots, height, columns), near[0].dtype),
        in_specs=[SMEM] + [VMEM] * (2 * members),
        out_specs=VMEM,
        compiler_params=pltpu.CompilerParams(vmem_limit_bytes=24 * MIB),
        name="gather_stripes",
    )(spots, *near, *far)


def product_kernel(rows_ref, counts_ref, blocks_ref, chosen_ref, out_ref):
    slots, width, _ = blocks_ref.shape
    columns = out_ref.shape[1]
    out_ref[...] = jnp.zeros_like(out_ref)
    for s in range(slots):

        @pl.when(s < counts_ref[0])
        def _():
            piece = chosen_ref[:, s].reshape(width, columns)
            product = jnp.dot(blocks_ref[s], piece, preferred_element_type=jnp.float32)
            at = pl.ds(pl.multiple_of(rows_ref[s] * width, width), width)
            out_ref[at, :] += product


def block_products(block_rows, counts, blocks, chosen):
    _, width, _ = blocks.shape
    columns = chosen.shape[-1]
    return pl.pallas_call(
        product_kernel,
        out_shape=jax.ShapeDtypeStruct((RB * width, columns), jnp.float32),
        in_specs=[SMEM, SMEM, VMEM, VMEM],
        out_specs=VMEM,
        compiler_params=pltpu.CompilerParams(vmem_limit_bytes=24 * MIB),
        name="block_products",
    )(block_rows, counts, blocks, chosen)


def gram_kernel(mine_ref, other_ref, own_ref, gram_ref, slab):
    c = lax.axis_index("cols")
    share, width = own_ref.shape[0], gram_ref.shape[1]
    slab[...] = mine_ref[...] + other_ref[...]
    own_ref[...] = slab[pl.ds(pl.multiple_of(c * share, share), share), :]
    right = slab[:, pl.ds(pl.multiple_of(c * width, width), width)]
    gram_ref[...] = lax.dot_general(
        slab[...], right, (((0,), (0,)), ((), ())), precision=HIGHEST, preferred_element_type=jnp.float32
    )


def sum_and_gram(mine, other):
    rows, columns = mine.shape
    return pl.pallas_call(
        gram_kernel,
        out_shape=(
            jax.ShapeDtypeStruct((rows // 2, columns), jnp.float32),
            jax.ShapeDtypeStruct((columns, columns // 2), jnp.float32),
        ),
        in_specs=[VMEM, VMEM],
        out_specs=(VMEM, VMEM),
        scratch_shapes=[pltpu.VMEM((rows, columns), jnp.float32)],
        compiler_params=pltpu.CompilerParams(vmem_limit_bytes=24 * MIB),
        name="sum_and_gram",
    )(mine, other)


def matmul(a, b, precision):
    return jnp.dot(a, b, precision=precision, preferred_element_type=jnp.float32)


def matmul_nt(a, b, precision):
    return lax.dot_general(
        a, b, (((1,), (1,)), ((), ())), precision=precision, preferred_element_type=jnp.float32
    )


def split_matmul(times, passes, a, b):
    a_high, b_high = a.astype(jnp.bfloat16), b.astype(jnp.bfloat16)
    result = times(a_high, b_high, None)
    if passes == 3:
        a_low = (a - a_high.astype(jnp.float32)).astype(jnp.bfloat16)
        b_low = (b - b_high.astype(jnp.float32)).astype(jnp.bfloat16)
        result += times(a_high, b_low, None) + times(a_low, b_high, None)
    return result


def factor_kernel(total_rows, gram_ref, own_ref, basis_ref, factor_ref, whole, scaled, inverse, product):
    n = factor_ref.shape[0]
    width = gram_ref.shape[-1]
    for c in range(n // width):
        whole[:, c * width : (c + 1) * width] = gram_ref[:, c].reshape(n, width)
    row_ids = lax.broadcasted_iota(jnp.int32, (n, n), 0)
    col_ids = lax.broadcasted_iota(jnp.int32, (n, n), 1)
    diagonal = row_ids == col_ids
    identity = diagonal.astype(jnp.float32)
    half = jnp.where(row_ids > col_ids, 1.0, jnp.where(diagonal, 0.5, 0.0))
    gram = whole[...]
    on_diagonal = jnp.where(diagonal, gram, 0.0)
    down = jnp.sqrt(jnp.sum(on_diagonal, axis=1, keepdims=True))
    across = jnp.sqrt(jnp.sum(on_diagonal, axis=0, keepdims=True))
    up_down = 1.0 / down
    up_across = 1.0 / across
    scaled[...] = gram * up_down * up_across

    def refine(times, times_nt):
        w = inverse[...]
        upper = times(w, scaled[...])
        residual = times_nt(upper, w) - identity
        step = residual * half
        inverse[...] = w - matmul(step, w, lax.Precision.DEFAULT)
        product[...] = upper - matmul(step, upper, lax.Precision.DEFAULT)
        return jnp.sum(residual * residual)

    def exactly(times):
        return functools.partial(times, precision=HIGHEST)

    inverse[...] = identity - (scaled[...] - identity) * half
    for passes in (1, 3):
        refine(functools.partial(split_matmul, matmul, passes), functools.partial(split_matmul, matmul_nt, passes))

    def going(state):
        step, size = state
        return (step < 8) & (size > 1e-6)

    def advance(state):
        return state[0] + 1, refine(exactly(matmul), exactly(matmul_nt))

    _, size = lax.while_loop(going, advance, (jnp.int32(0), jnp.float32(1.0)))

    @pl.when(jnp.logical_not(size <= 1e-6))
    def _():
        inverse[...] = identity
        ids = lax.broadcasted_iota(jnp.int32, (n, 1), 0)

        def eliminate(j, carry):
            pivot_row = scaled[pl.ds(j, 1), :]
            inverse_row = inverse[pl.ds(j, 1), :]
            column = jnp.sum(jnp.where(col_ids == j, scaled[...], 0.0), axis=1, keepdims=True)
            pivot = jnp.sum(jnp.where(ids == j, column, 0.0), axis=0, keepdims=True)
            root = 1.0 / jnp.sqrt(pivot)
            ratio = jnp.where(ids > j, column / pivot, jnp.where(ids == j, 1.0 - root, 0.0))
            scaled[...] = scaled[...] - ratio * pivot_row
            inverse[...] = inverse[...] - ratio * inverse_row
            return carry

        lax.fori_loop(0, n, eliminate, 0)
        product[...] = matmul(inverse[...], whole[...] * up_down * up_across, HIGHEST)

    w = inverse[...]
    root_rows = jnp.sqrt(jnp.float32(total_rows))
    upper = product[...] * across / root_rows
    factor_ref[...] = jnp.where(row_ids <= col_ids, upper, 0.0)
    basis_ref[...] = matmul_nt(own_ref[...] * up_across, w, HIGHEST) * root_rows


def factor_and_basis(total_rows, gram, own):
    columns = own.shape[1]
    return pl.pallas_call(
        functools.partial(factor_kernel, total_rows),
        out_shape=(
            jax.ShapeDtypeStruct(own.shape, jnp.float32),
            jax.ShapeDtypeStruct((columns, columns), jnp.float32),
        ),
        in_specs=[VMEM, VMEM],
        out_specs=(VMEM, VMEM),
        scratch_shapes=[pltpu.VMEM((columns, columns), jnp.float32)] * 4,
        compiler_params=pltpu.CompilerParams(vmem_limit_bytes=24 * MIB),
        name="factor_and_basis",
    )(gram, own)


def spread(piece, axes, devices):
    copies = jnp.broadcast_to(piece[None], (devices, *piece.shape))
    return lax.all_to_all(copies, axes, split_axis=0, concat_axis=0, tiled=True)


def exchange(pieces, rows):
    order = distances(len(pieces))
    return [
        lax.ppermute(piece, "rows", [(r, r ^ d) for r in range(rows)]) if d else piece
        for piece, d in zip(pieces, order)
    ]


def fetch_and_multiply(sketch, blocks, block_rows, block_cols, counts):
    slots, width, _ = blocks.shape
    rows, cols = lax.axis_size("rows"), lax.axis_size("cols")
    members = rows // 2
    height = width // members
    columns = sketch.shape[1]
    sketch = sketch.reshape(-1, members, height, columns)
    per = sketch.shape[0]
    largest = min(per * members, slots * members, 128)
    within = tuple(level for level in WITHIN if level < per)
    across = tuple(level for level in ACROSS if level[0] < largest and members <= 8 and slots >= 8)
    stripes = turn(sketch)
    table = table_copies(block_cols, counts, rows * cols)
    table = lax.all_to_all(table, ("rows", "cols"), split_axis=0, concat_axis=0, tiled=True)
    near, far, spots, lists, level_within, level_across = plan(table, slots, per, within, across)

    def within_half(count):
        def run():
            return order(exchange(cut(lists, stripes, count), rows), per)

        return run

    own = lax.switch(level_within[0], [within_half(count) for count in (*within, per)])

    def across_halves(count, some):
        def run():
            swap = [(r, (r + members) % rows) for r in range(rows)]
            other = lax.ppermute(listed(lists, own, count), "rows", swap)
            nears = exchange(pick(near, own, some, members), rows)
            fars = exchange(pick(far, other, some, members), rows)
            return gather(spots, nears, fars)

        return run

    chosen = lax.switch(level_across[0], [across_halves(*level) for level in (*across, (largest, slots))])
    return block_products(block_rows, counts, blocks, chosen)


def local(sketch, blocks, block_rows, block_cols, counts):
    _, width, _ = blocks.shape
    columns = sketch.shape[1]
    rows, cols = lax.axis_size("rows"), lax.axis_size("cols")
    partial_rows = fetch_and_multiply(sketch, blocks, block_rows, block_cols, counts)
    if cols == 2:
        other = lax.ppermute(partial_rows, "cols", [(0, 1), (1, 0)])
        own, gram = sum_and_gram(partial_rows, other)
        pieces = gram.reshape(rows, -1, columns // 2)
        pieces = lax.all_to_all(pieces, "rows", split_axis=0, concat_axis=0, tiled=True)
        gram = spread(jnp.sum(pieces, axis=0), ("rows", "cols"), rows * cols)
        gram = gram.reshape(rows, cols, -1, columns // 2)
    else:
        own = lax.psum_scatter(partial_rows, "cols", scatter_dimension=0, tiled=True)
        gram = lax.psum(matmul(own.T, own, HIGHEST), ("rows", "cols"))
        gram = gram.reshape(1, 1, columns, columns)
    return factor_and_basis(RB * width * rows, gram, own)


def solution(mesh):
    in_specs = (
        P(("rows", "cols"), None),
        P(("rows", "cols"), None, None),
        P(("rows", "cols")),
        P(("rows", "cols")),
        P(("rows", "cols")),
    )
    out_specs = (P(("rows", "cols"), None), P())
    return jax.shard_map(local, mesh=mesh, in_specs=in_specs, out_specs=out_specs, check_vma=False)
```

```python
import functools

import jax
import jax.numpy as jnp
from jax import lax
from jax.experimental import pallas as pl
from jax.experimental.pallas import tpu as pltpu
from jax.sharding import PartitionSpec as P

RB = 4
HIGHEST = lax.Precision.HIGHEST
VMEM = pl.BlockSpec(memory_space=pltpu.VMEM)
SMEM = pl.BlockSpec(memory_space=pltpu.SMEM)
MIB = 1024 * 1024


ACROSS = ((14, 5), (16, 5), (20, 5), (20, 6), (24, 6), (24, 8))
WITHIN = (6, 7, 8)


def table_kernel(cols_ref, counts_ref, out_ref):
    slots = cols_ref.shape[0]
    lane = lax.broadcasted_iota(jnp.int32, out_ref.shape, 2)
    table = jnp.where(lane == slots, counts_ref[0], 0)
    for s in range(slots):
        table = jnp.where(lane == s, cols_ref[s], table)
    out_ref[...] = table


def table_copies(block_cols, counts, devices):
    return pl.pallas_call(
        table_kernel,
        out_shape=jax.ShapeDtypeStruct((devices, 1, 128), jnp.int32),
        in_specs=[SMEM, SMEM],
        out_specs=VMEM,
        name="table_copies",
    )(block_cols, counts)


def over(values, size):
    return values >> (size.bit_length() - 1)


def plan_kernel(slots, per, within, across, table_ref, near_ref, far_ref, spots_ref, lists_ref, *level_refs):
    devices = table_ref.shape[0]
    rows, cols = lax.axis_size("rows"), lax.axis_size("cols")
    panel = per * rows
    part = panel // 2
    groups = [range(at, min(at + 64, devices)) for at in range(0, devices, 64)]

    def read(group):
        table = table_ref[group.start : group.stop, 0, :]
        lane = lax.broadcasted_iota(jnp.int32, table.shape, 1)
        counts = table[:, slots : slots + 1]
        table = jnp.where(lane < counts, table, -1)
        block = lax.broadcasted_iota(jnp.int32, (len(group), panel), 1)
        return table, counts, [table[:, s : s + 1] == block for s in range(slots)]

    lines = -(-cols // 8) * 8
    line = lax.broadcasted_iota(jnp.int32, (3 * lines, panel), 0)
    ids = lax.broadcasted_iota(jnp.int32, (1, panel), 1)
    asks = jnp.zeros((3 * lines, panel), jnp.float32)
    for group in groups:
        _, _, asked = read(group)
        some = jnp.where(functools.reduce(jnp.logical_or, asked), 1.0, 0.0).astype(jnp.bfloat16)
        shape = (3 * lines, len(group))
        number = lax.broadcasted_iota(jnp.int32, shape, 0)
        device = lax.broadcasted_iota(jnp.int32, shape, 1) + group.start
        core, side = device & (cols - 1), over(device, devices // 2)
        reads = (number == core) | (number == lines * (1 + side) + core)
        asks += jnp.dot(jnp.where(reads, 1.0, 0.0).astype(jnp.bfloat16), some, preferred_element_type=jnp.float32)
    own_half = (line >= lines) & (over(line - lines, lines) == over(lax.broadcasted_iota(jnp.int32, line.shape, 1), part))
    asks = jnp.where((asks > 0.5) & jnp.logical_not(own_half), 1.0, 0.0)
    first = lax.broadcasted_iota(jnp.int32, (panel, panel), 0)
    second = lax.broadcasted_iota(jnp.int32, (panel, panel), 1)
    after = first > second
    near = jnp.where(after & ((first ^ second) < per), 1.0, 0.0).astype(jnp.bfloat16)
    after = jnp.where(after, 1.0, 0.0).astype(jnp.bfloat16)
    same = jnp.where(first == second, 1.0, 0.0).astype(jnp.bfloat16)
    nt = (((1,), (1,)), ((), ()))

    def ranks(a, b):
        return lax.dot_general(a, b, nt, preferred_element_type=jnp.float32)

    short = asks.astype(jnp.bfloat16)
    near_rank = ranks(short, near)
    far_rank = ranks(short, after)
    longest = jnp.max(jnp.where(line < lines, near_rank + asks, 0.0)).astype(jnp.int32)
    level_refs[0][0] = sum((longest > level).astype(jnp.int32) for level in within)
    longest = jnp.max(jnp.where(line < lines, 0.0, far_rank + asks)).astype(jnp.int32)
    me = lax.axis_index("rows")
    half, c = over(me, rows // 2), lax.axis_index("cols")

    def row(values, number):
        return jnp.sum(jnp.where(line == number, values, 0.0), axis=0, keepdims=True)

    here = (ids & -per) - half * part + row(near_rank, c).astype(jnp.int32)
    there = row(far_rank, lines * (1 + half) + c).astype(jnp.int32)
    place = jnp.where(over(ids, part) == half, here, there)
    most = jnp.zeros((1, 1), jnp.float32)
    lane = lax.broadcasted_iota(jnp.int32, (table_ref.shape[2],) * 2, 1)
    before = lax.broadcasted_iota(jnp.int32, lane.shape, 0) < lane
    before = jnp.where(before, 1.0, 0.0).astype(jnp.bfloat16)
    for group in groups:
        table, counts, asked = read(group)
        lane = lax.broadcasted_iota(jnp.int32, table.shape, 1)
        side = over(lax.broadcasted_iota(jnp.int32, table.shape, 0) + group.start, devices // 2)
        is_near = (table >= 0) & (over(table, part) == side)
        n_near = jnp.dot(
            jnp.where(is_near, 1.0, 0.0).astype(jnp.bfloat16), before, preferred_element_type=jnp.float32
        ).astype(jnp.int32)
        n_far = lane - n_near
        near_key = jnp.where(is_near, n_near, -1)
        far_key = jnp.where((table >= 0) & jnp.logical_not(is_near), n_far, -1)
        nears = fars = jnp.zeros(table.shape, jnp.int32)
        for s in range(slots):
            found = jnp.sum(jnp.where(asked[s], place, 0), axis=1, keepdims=True)
            nears = jnp.where(near_key[:, s : s + 1] == lane, found, nears)
            fars = jnp.where(far_key[:, s : s + 1] == lane, found, fars)
        at = slice(group.start, group.stop)
        near_ref[at], far_ref[at] = nears, fars
        spots_ref[at] = jnp.where(lane < slots, jnp.where(is_near, n_near, slots + n_far), 0)
        longest_part = jnp.maximum(near_key, far_key).astype(jnp.float32) + 1.0
        most = jnp.maximum(most, jnp.max(jnp.max(longest_part, axis=1, keepdims=True), axis=0, keepdims=True))
    most = jnp.max(most).astype(jnp.int32)
    level_refs[1][0] = sum(((longest > count) | (most > some)).astype(jnp.int32) for count, some in across)
    line = lax.broadcasted_iota(jnp.int32, (panel, 3 * lines), 1)

    def column(values, number):
        return jnp.sum(jnp.where(line == number, values, 0.0), axis=1, keepdims=True)

    turned, near_rank, far_rank = ranks(same, short), ranks(near, short), ranks(after, short)
    ids = lax.broadcasted_iota(jnp.int32, (panel, 1), 0)
    number = lax.broadcasted_iota(jnp.int32, (panel, lists_ref.shape[1]), 1)
    near_rank = column(near_rank, c).astype(jnp.int32)
    here = (ids & -per) - half * part + near_rank
    other = lines * (2 - half) + c
    sent = (column(turned, other) > 0.5) & (column(far_rank, other).astype(jnp.int32) == number)
    sent = jnp.sum(jnp.where(sent, here, 0), axis=0, keepdims=True)
    kept = (column(turned, c) > 0.5) & (over(ids, per) == me) & (near_rank == number)
    kept = jnp.sum(jnp.where(kept, ids & (per - 1), 0), axis=0, keepdims=True)
    lists_ref[...] = jnp.where(lax.broadcasted_iota(jnp.int32, lists_ref.shape, 0) == 0, sent, kept)


def plan(table, slots, per, within, across):
    devices = table.shape[0]
    return pl.pallas_call(
        functools.partial(plan_kernel, slots, per, within, across),
        out_shape=(
            *[jax.ShapeDtypeStruct((devices, 128), jnp.int32)] * 3,
            jax.ShapeDtypeStruct((8, 128), jnp.int32),
            jax.ShapeDtypeStruct((1,), jnp.int32),
            jax.ShapeDtypeStruct((1,), jnp.int32),
        ),
        in_specs=[VMEM],
        out_specs=(VMEM, VMEM, VMEM, VMEM, SMEM, SMEM),
        compiler_params=pltpu.CompilerParams(vmem_limit_bytes=48 * MIB),
        name="plan",
    )(table)


def distances(members):
    return [0, *sorted(range(1, members), key=lambda d: (-d.bit_count(), -d))]


def turn_kernel(sketch_ref, out_ref):
    members = out_ref.shape[0]
    me = lax.axis_index("rows") % members
    for i, d in enumerate(distances(members)):
        out_ref[i] = sketch_ref[:, me ^ d]


def turn(sketch):
    blocks, members, height, columns = sketch.shape
    return pl.pallas_call(
        turn_kernel,
        out_shape=jax.ShapeDtypeStruct((members, blocks, height, columns), sketch.dtype),
        in_specs=[VMEM],
        out_specs=VMEM,
        compiler_params=pltpu.CompilerParams(vmem_limit_bytes=24 * MIB),
        cost_estimate=pl.CostEstimate(flops=0, bytes_accessed=4 * sketch.size, transcendentals=0),
        name="turn_stripes",
    )(sketch)


def cut_kernel(lists_ref, stripes_ref, *out_refs):
    for k in range(out_refs[0].shape[0]):
        for i, out_ref in enumerate(out_refs):
            out_ref[k] = stripes_ref[i, lists_ref[1, k]]


def cut(lists, stripes, count):
    members, _, height, columns = stripes.shape
    return pl.pallas_call(
        cut_kernel,
        out_shape=(jax.ShapeDtypeStruct((count, height, columns), stripes.dtype),) * members,
        in_specs=[SMEM, VMEM],
        out_specs=(VMEM,) * members,
        compiler_params=pltpu.CompilerParams(vmem_limit_bytes=24 * MIB),
        name="cut_stripes",
    )(lists, stripes)


def order_kernel(*refs):
    *stripe_refs, all_ref = refs
    members = len(stripe_refs)
    me = lax.axis_index("rows") % members
    per = all_ref.shape[0] // members
    for ref, d in zip(stripe_refs, distances(members)):
        all_ref[pl.ds((me ^ d) * per, ref.shape[0])] = ref[...]


def order(stripes, per):
    _, height, columns = stripes[0].shape
    return pl.pallas_call(
        order_kernel,
        out_shape=jax.ShapeDtypeStruct((len(stripes) * per, height, columns), stripes[0].dtype),
        in_specs=[VMEM] * len(stripes),
        out_specs=VMEM,
        compiler_params=pltpu.CompilerParams(vmem_limit_bytes=24 * MIB),
        name="order_stripes",
    )(*stripes)


def list_kernel(list_ref, all_ref, out_ref):
    for k in range(out_ref.shape[0]):
        out_ref[k] = all_ref[list_ref[0, k]]


def listed(numbers, stripes, count):
    return pl.pallas_call(
        list_kernel,
        out_shape=jax.ShapeDtypeStruct((count, *stripes.shape[1:]), stripes.dtype),
        in_specs=[SMEM, VMEM],
        out_specs=VMEM,
        compiler_params=pltpu.CompilerParams(vmem_limit_bytes=24 * MIB),
        name="listed_stripes",
    )(numbers, stripes)


def split(members):
    far = [d for d in distances(members) if d.bit_count() > 1]
    return far, [0] + [1 << bit for bit in reversed(range(members.bit_length() - 1))]


def device_at(d):
    return (lax.axis_index("rows") ^ d) * lax.axis_size("cols") + lax.axis_index("cols")


def early_kernel(members, near_ref, own_ref, *out_refs):
    last = own_ref.shape[0] - 1
    for d, out_ref in zip(split(members)[0], out_refs):
        for s in range(out_ref.shape[0]):
            out_ref[s] = own_ref[jnp.minimum(near_ref[device_at(d), s], last)]


def pick_early(near, own, count, members):
    far = split(members)[0]
    return pl.pallas_call(
        functools.partial(early_kernel, members),
        out_shape=(jax.ShapeDtypeStruct((count, *own.shape[1:]), own.dtype),) * len(far),
        in_specs=[SMEM, VMEM],
        out_specs=(VMEM,) * len(far),
        compiler_params=pltpu.CompilerParams(vmem_limit_bytes=24 * MIB),
        name="pick_early",
    )(near, own)


def late_kernel(members, near_ref, far_ref, spots_ref, own_ref, other_ref, *out_refs):
    far, full = split(members)
    slots = out_refs[-1].shape[0]
    here, there = own_ref.shape[0] - 1, other_ref.shape[0] - 1
    for d, out_ref in zip(far, out_refs):
        for s in range(out_ref.shape[0]):
            out_ref[s] = other_ref[jnp.minimum(far_ref[device_at(d), s], there)]
    for d, out_ref in zip(full, out_refs[len(far) :]):
        device = device_at(d)
        for s in range(slots):
            spot = spots_ref[device, s]
            own = own_ref[jnp.minimum(near_ref[device, jnp.minimum(spot, slots - 1)], here)]
            other = other_ref[jnp.minimum(far_ref[device, jnp.maximum(spot - slots, 0)], there)]
            out_ref[s] = lax.select(spot < slots, own, other)


def pick_late(near, far, spots, own, other, count, slots, members):
    in_two, in_one = split(members)
    shape = own.shape[1:]
    picked = pl.pallas_call(
        functools.partial(late_kernel, members),
        out_shape=(
            *[jax.ShapeDtypeStruct((count, *shape), own.dtype)] * len(in_two),
            *[jax.ShapeDtypeStruct((slots, *shape), own.dtype)] * len(in_one),
        ),
        in_specs=[SMEM] * 3 + [VMEM] * 2,
        out_specs=(VMEM,) * members,
        compiler_params=pltpu.CompilerParams(vmem_limit_bytes=24 * MIB),
        name="pick_late",
    )(near, far, spots, own, other)
    return picked[: len(in_two)], picked[len(in_two) :]


def gather_kernel(spots_ref, *refs):
    *chosen_refs, out_ref = refs
    members, slots = out_ref.shape[:2]
    far, full = split(members)
    late_refs, full_refs = chosen_refs[: len(far)], chosen_refs[len(far) : members]
    early_refs = chosen_refs[members:]
    me = lax.axis_index("rows") % members
    for ref, d in zip(full_refs, full):
        out_ref[me ^ d] = ref[...]
    for s in range(slots):
        spot = spots_ref[device_at(0), s]

        def put(refs, at):
            for ref, d in zip(refs, far):
                out_ref[me ^ d, s] = ref[jnp.minimum(at, ref.shape[0] - 1)]

        pl.when(spot < slots)(functools.partial(put, early_refs, spot))
        pl.when(spot >= slots)(functools.partial(put, late_refs, spot - slots))


def gather(spots, late, full, early):
    members = len(late) + len(full)
    return pl.pallas_call(
        gather_kernel,
        out_shape=jax.ShapeDtypeStruct((members, *full[0].shape), full[0].dtype),
        in_specs=[SMEM] + [VMEM] * (members + len(early)),
        out_specs=VMEM,
        compiler_params=pltpu.CompilerParams(vmem_limit_bytes=24 * MIB),
        name="gather_stripes",
    )(spots, *late, *full, *early)


def product_kernel(rows_ref, counts_ref, blocks_ref, chosen_ref, out_ref):
    slots, width, _ = blocks_ref.shape
    columns = out_ref.shape[1]
    out_ref[...] = jnp.zeros_like(out_ref)
    for s in range(slots):

        @pl.when(s < counts_ref[0])
        def _():
            piece = chosen_ref[:, s].reshape(width, columns)
            product = jnp.dot(blocks_ref[s], piece, preferred_element_type=jnp.float32)
            at = pl.ds(pl.multiple_of(rows_ref[s] * width, width), width)
            out_ref[at, :] += product


def block_products(block_rows, counts, blocks, chosen):
    _, width, _ = blocks.shape
    columns = chosen.shape[-1]
    return pl.pallas_call(
        product_kernel,
        out_shape=jax.ShapeDtypeStruct((RB * width, columns), jnp.float32),
        in_specs=[SMEM, SMEM, VMEM, VMEM],
        out_specs=VMEM,
        compiler_params=pltpu.CompilerParams(vmem_limit_bytes=24 * MIB),
        name="block_products",
    )(block_rows, counts, blocks, chosen)


def gram_kernel(mine_ref, other_ref, own_ref, gram_ref, slab):
    c = lax.axis_index("cols")
    share, width = own_ref.shape[0], gram_ref.shape[1]
    slab[...] = mine_ref[...] + other_ref[...]
    own_ref[...] = slab[pl.ds(pl.multiple_of(c * share, share), share), :]
    right = slab[:, pl.ds(pl.multiple_of(c * width, width), width)]
    gram_ref[...] = lax.dot_general(
        slab[...], right, (((0,), (0,)), ((), ())), precision=HIGHEST, preferred_element_type=jnp.float32
    )


def sum_and_gram(mine, other):
    rows, columns = mine.shape
    return pl.pallas_call(
        gram_kernel,
        out_shape=(
            jax.ShapeDtypeStruct((rows // 2, columns), jnp.float32),
            jax.ShapeDtypeStruct((columns, columns // 2), jnp.float32),
        ),
        in_specs=[VMEM, VMEM],
        out_specs=(VMEM, VMEM),
        scratch_shapes=[pltpu.VMEM((rows, columns), jnp.float32)],
        compiler_params=pltpu.CompilerParams(vmem_limit_bytes=24 * MIB),
        name="sum_and_gram",
    )(mine, other)


def matmul(a, b, precision):
    return jnp.dot(a, b, precision=precision, preferred_element_type=jnp.float32)


def matmul_nt(a, b, precision):
    return lax.dot_general(
        a, b, (((1,), (1,)), ((), ())), precision=precision, preferred_element_type=jnp.float32
    )


def split_matmul(times, passes, a, b):
    a_high, b_high = a.astype(jnp.bfloat16), b.astype(jnp.bfloat16)
    result = times(a_high, b_high, None)
    if passes == 3:
        a_low = (a - a_high.astype(jnp.float32)).astype(jnp.bfloat16)
        b_low = (b - b_high.astype(jnp.float32)).astype(jnp.bfloat16)
        result += times(a_high, b_low, None) + times(a_low, b_high, None)
    return result


def factor_kernel(total_rows, gram_ref, own_ref, basis_ref, factor_ref, whole, scaled, inverse, product):
    n = factor_ref.shape[0]
    width = gram_ref.shape[-1]
    for c in range(n // width):
        whole[:, c * width : (c + 1) * width] = gram_ref[:, c].reshape(n, width)
    row_ids = lax.broadcasted_iota(jnp.int32, (n, n), 0)
    col_ids = lax.broadcasted_iota(jnp.int32, (n, n), 1)
    diagonal = row_ids == col_ids
    identity = diagonal.astype(jnp.float32)
    half = jnp.where(row_ids > col_ids, 1.0, jnp.where(diagonal, 0.5, 0.0))
    gram = whole[...]
    on_diagonal = jnp.where(diagonal, gram, 0.0)
    down = jnp.sqrt(jnp.sum(on_diagonal, axis=1, keepdims=True))
    across = jnp.sqrt(jnp.sum(on_diagonal, axis=0, keepdims=True))
    up_down = 1.0 / down
    up_across = 1.0 / across
    scaled[...] = gram * up_down * up_across

    def refine(times, times_nt):
        w = inverse[...]
        upper = times(w, scaled[...])
        residual = times_nt(upper, w) - identity
        step = residual * half
        inverse[...] = w - matmul(step, w, lax.Precision.DEFAULT)
        product[...] = upper - matmul(step, upper, lax.Precision.DEFAULT)
        return jnp.sum(residual * residual)

    def exactly(times):
        return functools.partial(times, precision=HIGHEST)

    inverse[...] = identity - (scaled[...] - identity) * half
    for passes in (1, 3):
        refine(functools.partial(split_matmul, matmul, passes), functools.partial(split_matmul, matmul_nt, passes))

    def going(state):
        step, size = state
        return (step < 8) & (size > 1e-6)

    def advance(state):
        return state[0] + 1, refine(exactly(matmul), exactly(matmul_nt))

    _, size = lax.while_loop(going, advance, (jnp.int32(0), jnp.float32(1.0)))

    @pl.when(jnp.logical_not(size <= 1e-6))
    def _():
        inverse[...] = identity
        ids = lax.broadcasted_iota(jnp.int32, (n, 1), 0)

        def eliminate(j, carry):
            pivot_row = scaled[pl.ds(j, 1), :]
            inverse_row = inverse[pl.ds(j, 1), :]
            column = jnp.sum(jnp.where(col_ids == j, scaled[...], 0.0), axis=1, keepdims=True)
            pivot = jnp.sum(jnp.where(ids == j, column, 0.0), axis=0, keepdims=True)
            root = 1.0 / jnp.sqrt(pivot)
            ratio = jnp.where(ids > j, column / pivot, jnp.where(ids == j, 1.0 - root, 0.0))
            scaled[...] = scaled[...] - ratio * pivot_row
            inverse[...] = inverse[...] - ratio * inverse_row
            return carry

        lax.fori_loop(0, n, eliminate, 0)
        product[...] = matmul(inverse[...], whole[...] * up_down * up_across, HIGHEST)

    w = inverse[...]
    root_rows = jnp.sqrt(jnp.float32(total_rows))
    upper = product[...] * across / root_rows
    factor_ref[...] = jnp.where(row_ids <= col_ids, upper, 0.0)
    basis_ref[...] = matmul_nt(own_ref[...] * up_across, w, HIGHEST) * root_rows


def factor_and_basis(total_rows, gram, own):
    columns = own.shape[1]
    return pl.pallas_call(
        functools.partial(factor_kernel, total_rows),
        out_shape=(
            jax.ShapeDtypeStruct(own.shape, jnp.float32),
            jax.ShapeDtypeStruct((columns, columns), jnp.float32),
        ),
        in_specs=[VMEM, VMEM],
        out_specs=(VMEM, VMEM),
        scratch_shapes=[pltpu.VMEM((columns, columns), jnp.float32)] * 4,
        compiler_params=pltpu.CompilerParams(vmem_limit_bytes=24 * MIB),
        name="factor_and_basis",
    )(gram, own)


def spread(piece, axes, devices):
    copies = jnp.broadcast_to(piece[None], (devices, *piece.shape))
    return lax.all_to_all(copies, axes, split_axis=0, concat_axis=0, tiled=True)


def exchange(pieces, order, rows):
    return [
        lax.ppermute(piece, "rows", [(r, r ^ d) for r in range(rows)]) if d else piece
        for piece, d in zip(pieces, order)
    ]


def fetch_and_multiply(sketch, blocks, block_rows, block_cols, counts):
    slots, width, _ = blocks.shape
    rows, cols = lax.axis_size("rows"), lax.axis_size("cols")
    members = rows // 2
    height = width // members
    columns = sketch.shape[1]
    sketch = sketch.reshape(-1, members, height, columns)
    per = sketch.shape[0]
    largest = min(per * members, slots * members, 128)
    within = tuple(level for level in WITHIN if level < per)
    across = tuple(level for level in ACROSS if level[0] < largest and members <= 8 and slots >= 8)
    stripes = turn(sketch)
    table = table_copies(block_cols, counts, rows * cols)
    table = lax.all_to_all(table, ("rows", "cols"), split_axis=0, concat_axis=0, tiled=True)
    near, far, spots, lists, level_within, level_across = plan(table, slots, per, within, across)

    def within_half(count):
        def run():
            return order(exchange(cut(lists, stripes, count), distances(members), rows), per)

        return run

    own = lax.switch(level_within[0], [within_half(count) for count in (*within, per)])

    in_two, in_one = split(members)

    def across_halves(count, some):
        def run():
            swap = [(r, (r + members) % rows) for r in range(rows)]
            other = lax.ppermute(listed(lists, own, count), "rows", swap)
            early = exchange(pick_early(near, own, some, members), in_two, rows)
            late, full = pick_late(near, far, spots, own, other, some, slots, members)
            return gather(spots, exchange(late, in_two, rows), exchange(full, in_one, rows), early)

        return run

    chosen = lax.switch(level_across[0], [across_halves(*level) for level in (*across, (largest, slots))])
    return block_products(block_rows, counts, blocks, chosen)


def local(sketch, blocks, block_rows, block_cols, counts):
    _, width, _ = blocks.shape
    columns = sketch.shape[1]
    rows, cols = lax.axis_size("rows"), lax.axis_size("cols")
    partial_rows = fetch_and_multiply(sketch, blocks, block_rows, block_cols, counts)
    if cols == 2:
        other = lax.ppermute(partial_rows, "cols", [(0, 1), (1, 0)])
        own, gram = sum_and_gram(partial_rows, other)
        pieces = gram.reshape(rows, -1, columns // 2)
        pieces = lax.all_to_all(pieces, "rows", split_axis=0, concat_axis=0, tiled=True)
        gram = spread(jnp.sum(pieces, axis=0), ("rows", "cols"), rows * cols)
        gram = gram.reshape(rows, cols, -1, columns // 2)
    else:
        own = lax.psum_scatter(partial_rows, "cols", scatter_dimension=0, tiled=True)
        gram = lax.psum(matmul(own.T, own, HIGHEST), ("rows", "cols"))
        gram = gram.reshape(1, 1, columns, columns)
    return factor_and_basis(RB * width * rows, gram, own)


def solution(mesh):
    in_specs = (
        P(("rows", "cols"), None),
        P(("rows", "cols"), None, None),
        P(("rows", "cols")),
        P(("rows", "cols")),
        P(("rows", "cols")),
    )
    out_specs = (P(("rows", "cols"), None), P())
    return jax.shard_map(local, mesh=mesh, in_specs=in_specs, out_specs=out_specs, check_vma=False)
```

```python
import functools

import jax
import jax.numpy as jnp
from jax import lax
from jax.experimental import pallas as pl
from jax.experimental.pallas import tpu as pltpu
from jax.sharding import PartitionSpec as P

RB = 4
HIGHEST = lax.Precision.HIGHEST
VMEM = pl.BlockSpec(memory_space=pltpu.VMEM)
SMEM = pl.BlockSpec(memory_space=pltpu.SMEM)
MIB = 1024 * 1024


ACROSS = (12, 14, 16, 18, 20, 24)
WITHIN = 8


def table_kernel(cols_ref, counts_ref, out_ref):
    slots = cols_ref.shape[0]
    lane = lax.broadcasted_iota(jnp.int32, out_ref.shape, 2)
    table = jnp.where(lane == slots, counts_ref[0], 0)
    for s in range(slots):
        table = jnp.where(lane == s, cols_ref[s], table)
    out_ref[...] = table


def table_copies(block_cols, counts, devices):
    return pl.pallas_call(
        table_kernel,
        out_shape=jax.ShapeDtypeStruct((devices, 1, 128), jnp.int32),
        in_specs=[SMEM, SMEM],
        out_specs=VMEM,
        name="table_copies",
    )(block_cols, counts)


def over(values, size):
    return values >> (size.bit_length() - 1)


def plan_kernel(slots, per, within, across, table_ref, places_ref, lists_ref, *level_refs):
    devices = table_ref.shape[0]
    rows, cols = lax.axis_size("rows"), lax.axis_size("cols")
    panel = per * rows
    part = panel // 2
    groups = [range(at, min(at + 64, devices)) for at in range(0, devices, 64)]

    def read(group):
        table = table_ref[group.start : group.stop, 0, :]
        lane = lax.broadcasted_iota(jnp.int32, table.shape, 1)
        counts = table[:, slots : slots + 1]
        table = jnp.where(lane < counts, table, -1)
        block = lax.broadcasted_iota(jnp.int32, (len(group), panel), 1)
        return table, counts, [table[:, s : s + 1] == block for s in range(slots)]

    lines = -(-cols // 8) * 8
    line = lax.broadcasted_iota(jnp.int32, (3 * lines, panel), 0)
    ids = lax.broadcasted_iota(jnp.int32, (1, panel), 1)
    asks = jnp.zeros((3 * lines, panel), jnp.float32)
    for group in groups:
        _, _, asked = read(group)
        some = jnp.where(functools.reduce(jnp.logical_or, asked), 1.0, 0.0).astype(jnp.bfloat16)
        shape = (3 * lines, len(group))
        number = lax.broadcasted_iota(jnp.int32, shape, 0)
        device = lax.broadcasted_iota(jnp.int32, shape, 1) + group.start
        core, side = device & (cols - 1), over(device, devices // 2)
        reads = (number == core) | (number == lines * (1 + side) + core)
        asks += jnp.dot(jnp.where(reads, 1.0, 0.0).astype(jnp.bfloat16), some, preferred_element_type=jnp.float32)
    own_half = (line >= lines) & (over(line - lines, lines) == over(lax.broadcasted_iota(jnp.int32, line.shape, 1), part))
    asks = jnp.where((asks > 0.5) & jnp.logical_not(own_half), 1.0, 0.0)
    first = lax.broadcasted_iota(jnp.int32, (panel, panel), 0)
    second = lax.broadcasted_iota(jnp.int32, (panel, panel), 1)
    after = first > second
    near = jnp.where(after & ((first ^ second) < per), 1.0, 0.0).astype(jnp.bfloat16)
    after = jnp.where(after, 1.0, 0.0).astype(jnp.bfloat16)
    same = jnp.where(first == second, 1.0, 0.0).astype(jnp.bfloat16)
    nt = (((1,), (1,)), ((), ()))

    def ranks(a, b):
        return lax.dot_general(a, b, nt, preferred_element_type=jnp.float32)

    short = asks.astype(jnp.bfloat16)
    near_rank = ranks(short, near)
    far_rank = ranks(short, after)
    longest = jnp.max(jnp.where(line < lines, near_rank + asks, 0.0)).astype(jnp.int32)
    level_refs[0][0] = (longest > within).astype(jnp.int32)
    longest = jnp.max(jnp.where(line < lines, 0.0, far_rank + asks)).astype(jnp.int32)
    level_refs[1][0] = sum((longest > level).astype(jnp.int32) for level in across)
    me = lax.axis_index("rows")
    half, c = over(me, rows // 2), lax.axis_index("cols")

    def row(values, number):
        return jnp.sum(jnp.where(line == number, values, 0.0), axis=0, keepdims=True)

    here = (ids & -per) - half * part + row(near_rank, c).astype(jnp.int32)
    there = part + row(far_rank, lines * (1 + half) + c).astype(jnp.int32)
    place = jnp.where(over(ids, part) == half, here, there)
    for group in groups:
        table, _, asked = read(group)
        lane = lax.broadcasted_iota(jnp.int32, table.shape, 1)
        places = jnp.zeros(table.shape, jnp.int32)
        for s in range(slots):
            found = jnp.sum(jnp.where(asked[s], place, 0), axis=1, keepdims=True)
            places = jnp.where(lane == s, found, places)
        places_ref[group.start : group.stop] = places
    line = lax.broadcasted_iota(jnp.int32, (panel, 3 * lines), 1)

    def column(values, number):
        return jnp.sum(jnp.where(line == number, values, 0.0), axis=1, keepdims=True)

    turned, near_rank, far_rank = ranks(same, short), ranks(near, short), ranks(after, short)
    ids = lax.broadcasted_iota(jnp.int32, (panel, 1), 0)
    number = lax.broadcasted_iota(jnp.int32, (panel, lists_ref.shape[1]), 1)
    near_rank = column(near_rank, c).astype(jnp.int32)
    here = (ids & -per) - half * part + near_rank
    other = lines * (2 - half) + c
    sent = (column(turned, other) > 0.5) & (column(far_rank, other).astype(jnp.int32) == number)
    sent = jnp.sum(jnp.where(sent, here, 0), axis=0, keepdims=True)
    kept = (column(turned, c) > 0.5) & (over(ids, per) == me) & (near_rank == number)
    kept = jnp.sum(jnp.where(kept, ids & (per - 1), 0), axis=0, keepdims=True)
    lists_ref[...] = jnp.where(lax.broadcasted_iota(jnp.int32, lists_ref.shape, 0) == 0, sent, kept)


def plan(table, slots, per, within, across):
    devices = table.shape[0]
    return pl.pallas_call(
        functools.partial(plan_kernel, slots, per, within, across),
        out_shape=(
            jax.ShapeDtypeStruct((devices, 128), jnp.int32),
            jax.ShapeDtypeStruct((8, 128), jnp.int32),
            jax.ShapeDtypeStruct((1,), jnp.int32),
            jax.ShapeDtypeStruct((1,), jnp.int32),
        ),
        in_specs=[VMEM],
        out_specs=(VMEM, VMEM, SMEM, SMEM),
        compiler_params=pltpu.CompilerParams(vmem_limit_bytes=48 * MIB),
        name="plan",
    )(table)


def distances(members):
    return [0, *sorted(range(1, members), key=lambda d: (-d.bit_count(), -d))]


def turn_kernel(sketch_ref, out_ref):
    members = out_ref.shape[0]
    me = lax.axis_index("rows") % members
    for i, d in enumerate(distances(members)):
        out_ref[i] = sketch_ref[:, me ^ d]


def turn(sketch):
    blocks, members, height, columns = sketch.shape
    return pl.pallas_call(
        turn_kernel,
        out_shape=jax.ShapeDtypeStruct((members, blocks, height, columns), sketch.dtype),
        in_specs=[VMEM],
        out_specs=VMEM,
        compiler_params=pltpu.CompilerParams(vmem_limit_bytes=24 * MIB),
        cost_estimate=pl.CostEstimate(flops=0, bytes_accessed=4 * sketch.size, transcendentals=0),
        name="turn_stripes",
    )(sketch)


def cut_kernel(start, lists_ref, stripes_ref, *out_refs):
    for k in range(out_refs[0].shape[0]):
        for i, out_ref in enumerate(out_refs):
            out_ref[k] = stripes_ref[i, lists_ref[1, start + k]]


def cut(lists, stripes, start, stop):
    members, _, height, columns = stripes.shape
    return pl.pallas_call(
        functools.partial(cut_kernel, start),
        out_shape=(jax.ShapeDtypeStruct((stop - start, height, columns), stripes.dtype),) * members,
        in_specs=[SMEM, VMEM],
        out_specs=(VMEM,) * members,
        compiler_params=pltpu.CompilerParams(vmem_limit_bytes=24 * MIB),
        name="cut_stripes",
    )(lists, stripes)


def order_kernel(members, *refs):
    *stripe_refs, all_ref = refs
    me = lax.axis_index("rows") % members
    per = all_ref.shape[0] // members
    for i, d in enumerate(distances(members)):
        at = (me ^ d) * per
        for ref in stripe_refs[i::members]:
            all_ref[pl.ds(at, ref.shape[0])] = ref[...]
            at = at + ref.shape[0]


def order(stripes, members, per):
    _, height, columns = stripes[0].shape
    return pl.pallas_call(
        functools.partial(order_kernel, members),
        out_shape=jax.ShapeDtypeStruct((members * per, height, columns), stripes[0].dtype),
        in_specs=[VMEM] * len(stripes),
        out_specs=VMEM,
        compiler_params=pltpu.CompilerParams(vmem_limit_bytes=24 * MIB),
        name="order_stripes",
    )(*stripes)


def list_kernel(list_ref, all_ref, out_ref):
    for k in range(out_ref.shape[0]):
        out_ref[k] = all_ref[list_ref[0, k]]


def listed(numbers, stripes, count):
    return pl.pallas_call(
        list_kernel,
        out_shape=jax.ShapeDtypeStruct((count, *stripes.shape[1:]), stripes.dtype),
        in_specs=[SMEM, VMEM],
        out_specs=VMEM,
        compiler_params=pltpu.CompilerParams(vmem_limit_bytes=24 * MIB),
        name="listed_stripes",
    )(numbers, stripes)


def pick_kernel(places_ref, own_ref, other_ref, *refs):
    *out_refs, whole = refs
    here = own_ref.shape[0]
    whole[:here] = own_ref[...]
    whole[here:] = other_ref[...]
    for d, out_ref in zip(distances(len(out_refs)), out_refs):
        device = (lax.axis_index("rows") ^ d) * lax.axis_size("cols") + lax.axis_index("cols")
        for s in range(out_ref.shape[0]):
            out_ref[s] = whole[jnp.minimum(places_ref[device, s], whole.shape[0] - 1)]


def pick(places, own, other, slots, members):
    shape = own.shape[1:]
    return pl.pallas_call(
        pick_kernel,
        out_shape=(jax.ShapeDtypeStruct((slots, *shape), own.dtype),) * members,
        in_specs=[SMEM, VMEM, VMEM],
        out_specs=(VMEM,) * members,
        scratch_shapes=[pltpu.VMEM((own.shape[0] + other.shape[0], *shape), own.dtype)],
        compiler_params=pltpu.CompilerParams(vmem_limit_bytes=24 * MIB),
        name="pick_stripes",
    )(places, own, other)


def product_kernel(rows_ref, counts_ref, blocks_ref, *refs):
    *chosen_refs, out_ref, whole = refs
    slots, width, _ = blocks_ref.shape
    columns = out_ref.shape[1]
    members = len(chosen_refs)
    me = lax.axis_index("rows") % members
    for ref, d in zip(chosen_refs, distances(members) if members > 1 else [0]):
        whole[me ^ d] = ref[...]
    out_ref[...] = jnp.zeros_like(out_ref)
    for s in range(slots):

        @pl.when(s < counts_ref[0])
        def _():
            piece = whole[:, s].reshape(width, columns)
            product = jnp.dot(blocks_ref[s], piece, preferred_element_type=jnp.float32)
            at = pl.ds(pl.multiple_of(rows_ref[s] * width, width), width)
            out_ref[at, :] += product


def block_products(block_rows, counts, blocks, chosen):
    _, width, _ = blocks.shape
    columns = chosen[0].shape[-1]
    return pl.pallas_call(
        product_kernel,
        out_shape=jax.ShapeDtypeStruct((RB * width, columns), jnp.float32),
        in_specs=[SMEM, SMEM, VMEM] + [VMEM] * len(chosen),
        out_specs=VMEM,
        scratch_shapes=[pltpu.VMEM((len(chosen), *chosen[0].shape), chosen[0].dtype)],
        compiler_params=pltpu.CompilerParams(vmem_limit_bytes=24 * MIB),
        name="block_products",
    )(block_rows, counts, blocks, *chosen)


def gram_kernel(mine_ref, other_ref, own_ref, gram_ref, slab):
    c = lax.axis_index("cols")
    share, width = own_ref.shape[0], gram_ref.shape[1]
    slab[...] = mine_ref[...] + other_ref[...]
    own_ref[...] = slab[pl.ds(pl.multiple_of(c * share, share), share), :]
    right = slab[:, pl.ds(pl.multiple_of(c * width, width), width)]
    gram_ref[...] = lax.dot_general(
        slab[...], right, (((0,), (0,)), ((), ())), precision=HIGHEST, preferred_element_type=jnp.float32
    )


def sum_and_gram(mine, other):
    rows, columns = mine.shape
    return pl.pallas_call(
        gram_kernel,
        out_shape=(
            jax.ShapeDtypeStruct((rows // 2, columns), jnp.float32),
            jax.ShapeDtypeStruct((columns, columns // 2), jnp.float32),
        ),
        in_specs=[VMEM, VMEM],
        out_specs=(VMEM, VMEM),
        scratch_shapes=[pltpu.VMEM((rows, columns), jnp.float32)],
        compiler_params=pltpu.CompilerParams(vmem_limit_bytes=24 * MIB),
        name="sum_and_gram",
    )(mine, other)


def matmul(a, b, precision):
    return jnp.dot(a, b, precision=precision, preferred_element_type=jnp.float32)


def matmul_nt(a, b, precision):
    return lax.dot_general(
        a, b, (((1,), (1,)), ((), ())), precision=precision, preferred_element_type=jnp.float32
    )


def split_matmul(times, passes, a, b):
    a_high, b_high = a.astype(jnp.bfloat16), b.astype(jnp.bfloat16)
    result = times(a_high, b_high, None)
    if passes == 3:
        a_low = (a - a_high.astype(jnp.float32)).astype(jnp.bfloat16)
        b_low = (b - b_high.astype(jnp.float32)).astype(jnp.bfloat16)
        result += times(a_high, b_low, None) + times(a_low, b_high, None)
    return result


def factor_kernel(total_rows, gram_ref, own_ref, basis_ref, factor_ref, whole, scaled, inverse, product):
    n = factor_ref.shape[0]
    width = gram_ref.shape[-1]
    for c in range(n // width):
        whole[:, c * width : (c + 1) * width] = gram_ref[:, c].reshape(n, width)
    row_ids = lax.broadcasted_iota(jnp.int32, (n, n), 0)
    col_ids = lax.broadcasted_iota(jnp.int32, (n, n), 1)
    diagonal = row_ids == col_ids
    identity = diagonal.astype(jnp.float32)
    half = jnp.where(row_ids > col_ids, 1.0, jnp.where(diagonal, 0.5, 0.0))
    gram = whole[...]
    on_diagonal = jnp.where(diagonal, gram, 0.0)
    down = jnp.sqrt(jnp.sum(on_diagonal, axis=1, keepdims=True))
    across = jnp.sqrt(jnp.sum(on_diagonal, axis=0, keepdims=True))
    up_down = 1.0 / down
    up_across = 1.0 / across
    scaled[...] = gram * up_down * up_across

    def refine(times, times_nt):
        w = inverse[...]
        upper = times(w, scaled[...])
        residual = times_nt(upper, w) - identity
        step = residual * half
        inverse[...] = w - matmul(step, w, lax.Precision.DEFAULT)
        product[...] = upper - matmul(step, upper, lax.Precision.DEFAULT)
        return jnp.sum(residual * residual)

    def exactly(times):
        return functools.partial(times, precision=HIGHEST)

    inverse[...] = identity - (scaled[...] - identity) * half
    for passes in (1, 3):
        refine(functools.partial(split_matmul, matmul, passes), functools.partial(split_matmul, matmul_nt, passes))

    def going(state):
        step, size = state
        return (step < 8) & (size > 1e-6)

    def advance(state):
        return state[0] + 1, refine(exactly(matmul), exactly(matmul_nt))

    _, size = lax.while_loop(going, advance, (jnp.int32(0), jnp.float32(1.0)))

    @pl.when(jnp.logical_not(size <= 1e-6))
    def _():
        inverse[...] = identity
        ids = lax.broadcasted_iota(jnp.int32, (n, 1), 0)

        def eliminate(j, carry):
            pivot_row = scaled[pl.ds(j, 1), :]
            inverse_row = inverse[pl.ds(j, 1), :]
            column = jnp.sum(jnp.where(col_ids == j, scaled[...], 0.0), axis=1, keepdims=True)
            pivot = jnp.sum(jnp.where(ids == j, column, 0.0), axis=0, keepdims=True)
            root = 1.0 / jnp.sqrt(pivot)
            ratio = jnp.where(ids > j, column / pivot, jnp.where(ids == j, 1.0 - root, 0.0))
            scaled[...] = scaled[...] - ratio * pivot_row
            inverse[...] = inverse[...] - ratio * inverse_row
            return carry

        lax.fori_loop(0, n, eliminate, 0)
        product[...] = matmul(inverse[...], whole[...] * up_down * up_across, HIGHEST)

    w = inverse[...]
    root_rows = jnp.sqrt(jnp.float32(total_rows))
    upper = product[...] * across / root_rows
    factor_ref[...] = jnp.where(row_ids <= col_ids, upper, 0.0)
    basis_ref[...] = matmul_nt(own_ref[...] * up_across, w, HIGHEST) * root_rows


def factor_and_basis(total_rows, gram, own):
    columns = own.shape[1]
    return pl.pallas_call(
        functools.partial(factor_kernel, total_rows),
        out_shape=(
            jax.ShapeDtypeStruct(own.shape, jnp.float32),
            jax.ShapeDtypeStruct((columns, columns), jnp.float32),
        ),
        in_specs=[VMEM, VMEM],
        out_specs=(VMEM, VMEM),
        scratch_shapes=[pltpu.VMEM((columns, columns), jnp.float32)] * 4,
        compiler_params=pltpu.CompilerParams(vmem_limit_bytes=24 * MIB),
        name="factor_and_basis",
    )(gram, own)


def spread(piece, axes, devices):
    copies = jnp.broadcast_to(piece[None], (devices, *piece.shape))
    return lax.all_to_all(copies, axes, split_axis=0, concat_axis=0, tiled=True)


def exchange(pieces, rows):
    order = distances(len(pieces))
    return [
        lax.ppermute(piece, "rows", [(r, r ^ d) for r in range(rows)]) if d else piece
        for piece, d in zip(pieces, order)
    ]


def fetch(sketch, block_cols, counts, slots, width):
    rows, cols = lax.axis_size("rows"), lax.axis_size("cols")
    members = rows // 2
    height = width // members
    columns = sketch.shape[1]
    sketch = sketch.reshape(-1, members, height, columns)
    per = sketch.shape[0]
    largest = min(per * members, slots * members, 128)
    within = min(per, WITHIN)
    across = tuple(level for level in ACROSS if level < largest)
    stripes = turn(sketch)
    table = table_copies(block_cols, counts, rows * cols)
    table = lax.all_to_all(table, ("rows", "cols"), split_axis=0, concat_axis=0, tiled=True)
    places, lists, more, far = plan(table, slots, per, within, across)
    first = exchange(cut(lists, stripes, 0, within), rows)

    def as_sent():
        return order(first, members, per)

    def with_rest():
        return order(first + exchange(cut(lists, stripes, within, per), rows), members, per)

    own = lax.cond(more[0] > 0, with_rest, as_sent) if within < per else as_sent()

    def across_halves(count):
        def run():
            swap = [(r, (r + members) % rows) for r in range(rows)]
            other = lax.ppermute(listed(lists, own, count), "rows", swap)
            return pick(places, own, other, slots, members)

        return run

    picked = lax.switch(far[0], [across_halves(count) for count in (*across, largest)])
    return exchange(picked, rows)


def local(sketch, blocks, block_rows, block_cols, counts):
    slots, width, _ = blocks.shape
    columns = sketch.shape[1]
    rows, cols = lax.axis_size("rows"), lax.axis_size("cols")
    chosen = fetch(sketch, block_cols, counts, slots, width)
    if chosen[0].shape[1] % 16:
        order = jnp.argsort(lax.axis_index("rows") % len(chosen) ^ jnp.array(distances(len(chosen))))
        chosen = [jnp.stack(chosen)[order].swapaxes(0, 1).reshape(1, slots, width, columns)[0]]
    partial_rows = block_products(block_rows, counts, blocks, chosen)
    if cols == 2:
        other = lax.ppermute(partial_rows, "cols", [(0, 1), (1, 0)])
        own, gram = sum_and_gram(partial_rows, other)
        pieces = gram.reshape(rows, -1, columns // 2)
        pieces = lax.all_to_all(pieces, "rows", split_axis=0, concat_axis=0, tiled=True)
        gram = spread(jnp.sum(pieces, axis=0), ("rows", "cols"), rows * cols)
        gram = gram.reshape(rows, cols, -1, columns // 2)
    else:
        own = lax.psum_scatter(partial_rows, "cols", scatter_dimension=0, tiled=True)
        gram = lax.psum(matmul(own.T, own, HIGHEST), ("rows", "cols"))
        gram = gram.reshape(1, 1, columns, columns)
    return factor_and_basis(RB * width * rows, gram, own)


def solution(mesh):
    in_specs = (
        P(("rows", "cols"), None),
        P(("rows", "cols"), None, None),
        P(("rows", "cols")),
        P(("rows", "cols")),
        P(("rows", "cols")),
    )
    out_specs = (P(("rows", "cols"), None), P())
    return jax.shard_map(local, mesh=mesh, in_specs=in_specs, out_specs=out_specs, check_vma=False)
```

```python
import functools

import jax
import jax.numpy as jnp
from jax import lax
from jax.experimental import pallas as pl
from jax.experimental.pallas import tpu as pltpu
from jax.sharding import PartitionSpec as P

RB = 4
HIGHEST = lax.Precision.HIGHEST
VMEM = pl.BlockSpec(memory_space=pltpu.VMEM)
SMEM = pl.BlockSpec(memory_space=pltpu.SMEM)
MIB = 1024 * 1024


ACROSS = (12, 14, 16, 18, 20, 24)
WITHIN = 8


def table_kernel(cols_ref, counts_ref, out_ref):
    slots = cols_ref.shape[0]
    lane = lax.broadcasted_iota(jnp.int32, out_ref.shape, 2)
    table = jnp.where(lane == slots, counts_ref[0], 0)
    for s in range(slots):
        table = jnp.where(lane == s, cols_ref[s], table)
    out_ref[...] = table


def table_copies(block_cols, counts, devices):
    return pl.pallas_call(
        table_kernel,
        out_shape=jax.ShapeDtypeStruct((devices, 1, 128), jnp.int32),
        in_specs=[SMEM, SMEM],
        out_specs=VMEM,
        name="table_copies",
    )(block_cols, counts)


def over(values, size):
    return values >> (size.bit_length() - 1)


def plan_kernel(slots, per, within, across, table_ref, places_ref, lists_ref, *level_refs):
    devices = table_ref.shape[0]
    rows, cols = lax.axis_size("rows"), lax.axis_size("cols")
    panel = per * rows
    part = panel // 2
    groups = [range(at, min(at + 64, devices)) for at in range(0, devices, 64)]

    def read(group):
        table = table_ref[group.start : group.stop, 0, :]
        lane = lax.broadcasted_iota(jnp.int32, table.shape, 1)
        counts = table[:, slots : slots + 1]
        table = jnp.where(lane < counts, table, -1)
        block = lax.broadcasted_iota(jnp.int32, (len(group), panel), 1)
        return table, counts, [table[:, s : s + 1] == block for s in range(slots)]

    lines = -(-cols // 8) * 8
    line = lax.broadcasted_iota(jnp.int32, (3 * lines, panel), 0)
    ids = lax.broadcasted_iota(jnp.int32, (1, panel), 1)
    asks = jnp.zeros((3 * lines, panel), jnp.float32)
    for group in groups:
        _, _, asked = read(group)
        some = jnp.where(functools.reduce(jnp.logical_or, asked), 1.0, 0.0).astype(jnp.bfloat16)
        shape = (3 * lines, len(group))
        number = lax.broadcasted_iota(jnp.int32, shape, 0)
        device = lax.broadcasted_iota(jnp.int32, shape, 1) + group.start
        core, side = device & (cols - 1), over(device, devices // 2)
        reads = (number == core) | (number == lines * (1 + side) + core)
        asks += jnp.dot(jnp.where(reads, 1.0, 0.0).astype(jnp.bfloat16), some, preferred_element_type=jnp.float32)
    own_half = (line >= lines) & (over(line - lines, lines) == over(lax.broadcasted_iota(jnp.int32, line.shape, 1), part))
    asks = jnp.where((asks > 0.5) & jnp.logical_not(own_half), 1.0, 0.0)
    first = lax.broadcasted_iota(jnp.int32, (panel, panel), 0)
    second = lax.broadcasted_iota(jnp.int32, (panel, panel), 1)
    after = first > second
    near = jnp.where(after & ((first ^ second) < per), 1.0, 0.0).astype(jnp.bfloat16)
    after = jnp.where(after, 1.0, 0.0).astype(jnp.bfloat16)
    same = jnp.where(first == second, 1.0, 0.0).astype(jnp.bfloat16)
    nt = (((1,), (1,)), ((), ()))

    def ranks(a, b):
        return lax.dot_general(a, b, nt, preferred_element_type=jnp.float32)

    short = asks.astype(jnp.bfloat16)
    near_rank = ranks(short, near)
    far_rank = ranks(short, after)
    longest = jnp.max(jnp.where(line < lines, near_rank + asks, 0.0)).astype(jnp.int32)
    level_refs[0][0] = (longest > within).astype(jnp.int32)
    longest = jnp.max(jnp.where(line < lines, 0.0, far_rank + asks)).astype(jnp.int32)
    level_refs[1][0] = sum((longest > level).astype(jnp.int32) for level in across)
    me = lax.axis_index("rows")
    half, c = over(me, rows // 2), lax.axis_index("cols")

    def row(values, number):
        return jnp.sum(jnp.where(line == number, values, 0.0), axis=0, keepdims=True)

    here = (ids & -per) - half * part + row(near_rank, c).astype(jnp.int32)
    there = part + row(far_rank, lines * (1 + half) + c).astype(jnp.int32)
    place = jnp.where(over(ids, part) == half, here, there)
    for group in groups:
        table, _, asked = read(group)
        lane = lax.broadcasted_iota(jnp.int32, table.shape, 1)
        places = jnp.zeros(table.shape, jnp.int32)
        for s in range(slots):
            found = jnp.sum(jnp.where(asked[s], place, 0), axis=1, keepdims=True)
            places = jnp.where(lane == s, found, places)
        places_ref[group.start : group.stop] = places
    line = lax.broadcasted_iota(jnp.int32, (panel, 3 * lines), 1)

    def column(values, number):
        return jnp.sum(jnp.where(line == number, values, 0.0), axis=1, keepdims=True)

    turned, near_rank, far_rank = ranks(same, short), ranks(near, short), ranks(after, short)
    ids = lax.broadcasted_iota(jnp.int32, (panel, 1), 0)
    number = lax.broadcasted_iota(jnp.int32, (panel, lists_ref.shape[1]), 1)
    near_rank = column(near_rank, c).astype(jnp.int32)
    here = (ids & -per) - half * part + near_rank
    other = lines * (2 - half) + c
    sent = (column(turned, other) > 0.5) & (column(far_rank, other).astype(jnp.int32) == number)
    sent = jnp.sum(jnp.where(sent, here, 0), axis=0, keepdims=True)
    kept = (column(turned, c) > 0.5) & (over(ids, per) == me) & (near_rank == number)
    kept = jnp.sum(jnp.where(kept, ids & (per - 1), 0), axis=0, keepdims=True)
    lists_ref[...] = jnp.where(lax.broadcasted_iota(jnp.int32, lists_ref.shape, 0) == 0, sent, kept)


def plan(table, slots, per, within, across):
    devices = table.shape[0]
    return pl.pallas_call(
        functools.partial(plan_kernel, slots, per, within, across),
        out_shape=(
            jax.ShapeDtypeStruct((devices, 128), jnp.int32),
            jax.ShapeDtypeStruct((8, 128), jnp.int32),
            jax.ShapeDtypeStruct((1,), jnp.int32),
            jax.ShapeDtypeStruct((1,), jnp.int32),
        ),
        in_specs=[VMEM],
        out_specs=(VMEM, VMEM, SMEM, SMEM),
        compiler_params=pltpu.CompilerParams(vmem_limit_bytes=48 * MIB),
        name="plan",
    )(table)


def distances(members):
    return [0, *sorted(range(1, members), key=lambda d: (-d.bit_count(), -d))]


def turn_kernel(sketch_ref, out_ref):
    members = out_ref.shape[0]
    me = lax.axis_index("rows") % members
    for i, d in enumerate(distances(members)):
        out_ref[i] = sketch_ref[:, me ^ d]


def turn(sketch):
    blocks, members, height, columns = sketch.shape
    return pl.pallas_call(
        turn_kernel,
        out_shape=jax.ShapeDtypeStruct((members, blocks, height, columns), sketch.dtype),
        in_specs=[VMEM],
        out_specs=VMEM,
        compiler_params=pltpu.CompilerParams(vmem_limit_bytes=24 * MIB),
        cost_estimate=pl.CostEstimate(flops=0, bytes_accessed=4 * sketch.size, transcendentals=0),
        name="turn_stripes",
    )(sketch)


def copy_group(out_ref, refs):
    for at in range(0, len(refs), 8):
        values = [ref[...] for ref in refs[at : at + 8]]
        for k, value in enumerate(values):
            out_ref[at + k] = value


def cut_kernel(start, lists_ref, stripes_ref, *out_refs):
    numbers = [lists_ref[1, start + k] for k in range(out_refs[0].shape[0])]
    for i, out_ref in enumerate(out_refs):
        copy_group(out_ref, [stripes_ref.at[i, number] for number in numbers])


def cut(lists, stripes, start, stop):
    members, _, height, columns = stripes.shape
    return pl.pallas_call(
        functools.partial(cut_kernel, start),
        out_shape=(jax.ShapeDtypeStruct((stop - start, height, columns), stripes.dtype),) * members,
        in_specs=[SMEM, VMEM],
        out_specs=(VMEM,) * members,
        compiler_params=pltpu.CompilerParams(vmem_limit_bytes=24 * MIB),
        name="cut_stripes",
    )(lists, stripes)


def order_kernel(members, *refs):
    *stripe_refs, all_ref = refs
    me = lax.axis_index("rows") % members
    per = all_ref.shape[0] // members
    for i, d in enumerate(distances(members)):
        at = (me ^ d) * per
        for ref in stripe_refs[i::members]:
            all_ref[pl.ds(at, ref.shape[0])] = ref[...]
            at = at + ref.shape[0]


def order(stripes, members, per):
    _, height, columns = stripes[0].shape
    return pl.pallas_call(
        functools.partial(order_kernel, members),
        out_shape=jax.ShapeDtypeStruct((members * per, height, columns), stripes[0].dtype),
        in_specs=[VMEM] * len(stripes),
        out_specs=VMEM,
        compiler_params=pltpu.CompilerParams(vmem_limit_bytes=24 * MIB),
        name="order_stripes",
    )(*stripes)


def list_kernel(list_ref, all_ref, out_ref):
    copy_group(out_ref, [all_ref.at[list_ref[0, k]] for k in range(out_ref.shape[0])])


def listed(numbers, stripes, count):
    return pl.pallas_call(
        list_kernel,
        out_shape=jax.ShapeDtypeStruct((count, *stripes.shape[1:]), stripes.dtype),
        in_specs=[SMEM, VMEM],
        out_specs=VMEM,
        compiler_params=pltpu.CompilerParams(vmem_limit_bytes=24 * MIB),
        name="listed_stripes",
    )(numbers, stripes)


def pick_kernel(places_ref, own_ref, other_ref, *refs):
    *out_refs, whole = refs
    here = own_ref.shape[0]
    whole[:here] = own_ref[...]
    whole[here:] = other_ref[...]
    for d, out_ref in zip(distances(len(out_refs)), out_refs):
        device = (lax.axis_index("rows") ^ d) * lax.axis_size("cols") + lax.axis_index("cols")
        last = whole.shape[0] - 1
        copy_group(out_ref, [whole.at[jnp.minimum(places_ref[device, s], last)] for s in range(out_ref.shape[0])])


def pick(places, own, other, slots, members):
    shape = own.shape[1:]
    return pl.pallas_call(
        pick_kernel,
        out_shape=(jax.ShapeDtypeStruct((slots, *shape), own.dtype),) * members,
        in_specs=[SMEM, VMEM, VMEM],
        out_specs=(VMEM,) * members,
        scratch_shapes=[pltpu.VMEM((own.shape[0] + other.shape[0], *shape), own.dtype)],
        compiler_params=pltpu.CompilerParams(vmem_limit_bytes=24 * MIB),
        name="pick_stripes",
    )(places, own, other)


def product_kernel(start, rows_ref, counts_ref, blocks_ref, *refs):
    *chosen_refs, out_ref, whole = refs
    slots, width, _ = blocks_ref.shape
    columns = out_ref.shape[1]
    members = len(chosen_refs)
    me = lax.axis_index("rows") % members
    for ref, d in zip(chosen_refs, distances(members) if members > 1 else [0]):
        whole[me ^ d] = ref[:, :, start : start + columns]
    out_ref[...] = jnp.zeros_like(out_ref)
    for s in range(slots):

        @pl.when(s < counts_ref[0])
        def _():
            piece = whole[:, s].reshape(width, columns)
            product = jnp.dot(blocks_ref[s], piece, preferred_element_type=jnp.float32)
            at = pl.ds(pl.multiple_of(rows_ref[s] * width, width), width)
            out_ref[at, :] += product


def block_products(block_rows, counts, blocks, chosen, start, stop):
    _, width, _ = blocks.shape
    columns = stop - start
    return pl.pallas_call(
        functools.partial(product_kernel, start),
        out_shape=jax.ShapeDtypeStruct((RB * width, columns), jnp.float32),
        in_specs=[SMEM, SMEM, VMEM] + [VMEM] * len(chosen),
        out_specs=VMEM,
        scratch_shapes=[pltpu.VMEM((len(chosen), *chosen[0].shape[:2], columns), chosen[0].dtype)],
        compiler_params=pltpu.CompilerParams(vmem_limit_bytes=24 * MIB),
        name="block_products",
    )(block_rows, counts, blocks, *chosen)


def gram_kernel(*refs):
    mine_refs, other_refs, (own_ref, gram_ref, slab) = refs[:2], refs[2:4], refs[4:]
    c = lax.axis_index("cols")
    share, width = own_ref.shape[0], gram_ref.shape[1]
    for i, (mine_ref, other_ref) in enumerate(zip(mine_refs, other_refs)):
        slab[:, i * width : (i + 1) * width] = mine_ref[...] + other_ref[...]
    own_ref[...] = slab[pl.ds(pl.multiple_of(c * share, share), share), :]
    right = slab[:, pl.ds(pl.multiple_of(c * width, width), width)]
    gram_ref[...] = lax.dot_general(
        slab[...], right, (((0,), (0,)), ((), ())), precision=HIGHEST, preferred_element_type=jnp.float32
    )


def sum_and_gram(mine, other):
    rows, width = mine[0].shape
    columns = 2 * width
    return pl.pallas_call(
        gram_kernel,
        out_shape=(
            jax.ShapeDtypeStruct((rows // 2, columns), jnp.float32),
            jax.ShapeDtypeStruct((columns, width), jnp.float32),
        ),
        in_specs=[VMEM] * 4,
        out_specs=(VMEM, VMEM),
        scratch_shapes=[pltpu.VMEM((rows, columns), jnp.float32)],
        compiler_params=pltpu.CompilerParams(vmem_limit_bytes=24 * MIB),
        name="sum_and_gram",
    )(*mine, *other)


def matmul(a, b, precision):
    return jnp.dot(a, b, precision=precision, preferred_element_type=jnp.float32)


def matmul_nt(a, b, precision):
    return lax.dot_general(
        a, b, (((1,), (1,)), ((), ())), precision=precision, preferred_element_type=jnp.float32
    )


def split_matmul(times, passes, a, b):
    a_high, b_high = a.astype(jnp.bfloat16), b.astype(jnp.bfloat16)
    result = times(a_high, b_high, None)
    if passes == 3:
        a_low = (a - a_high.astype(jnp.float32)).astype(jnp.bfloat16)
        b_low = (b - b_high.astype(jnp.float32)).astype(jnp.bfloat16)
        result += times(a_high, b_low, None) + times(a_low, b_high, None)
    return result


def factor_kernel(total_rows, gram_ref, own_ref, basis_ref, factor_ref, whole, scaled, inverse, product):
    n = factor_ref.shape[0]
    width = gram_ref.shape[-1]
    for c in range(n // width):
        whole[:, c * width : (c + 1) * width] = gram_ref[:, c].reshape(n, width)
    row_ids = lax.broadcasted_iota(jnp.int32, (n, n), 0)
    col_ids = lax.broadcasted_iota(jnp.int32, (n, n), 1)
    diagonal = row_ids == col_ids
    identity = diagonal.astype(jnp.float32)
    half = jnp.where(row_ids > col_ids, 1.0, jnp.where(diagonal, 0.5, 0.0))
    gram = whole[...]
    on_diagonal = jnp.where(diagonal, gram, 0.0)
    down = jnp.sqrt(jnp.sum(on_diagonal, axis=1, keepdims=True))
    across = jnp.sqrt(jnp.sum(on_diagonal, axis=0, keepdims=True))
    up_down = 1.0 / down
    up_across = 1.0 / across
    scaled[...] = gram * up_down * up_across

    def refine(times, times_nt):
        w = inverse[...]
        upper = times(w, scaled[...])
        residual = times_nt(upper, w) - identity
        step = residual * half
        inverse[...] = w - matmul(step, w, lax.Precision.DEFAULT)
        product[...] = upper - matmul(step, upper, lax.Precision.DEFAULT)
        return jnp.sum(residual * residual)

    def exactly(times):
        return functools.partial(times, precision=HIGHEST)

    inverse[...] = identity - (scaled[...] - identity) * half
    for passes in (1, 3):
        refine(functools.partial(split_matmul, matmul, passes), functools.partial(split_matmul, matmul_nt, passes))

    def going(state):
        step, size = state
        return (step < 8) & (size > 1e-6)

    def advance(state):
        return state[0] + 1, refine(exactly(matmul), exactly(matmul_nt))

    _, size = lax.while_loop(going, advance, (jnp.int32(0), jnp.float32(1.0)))

    @pl.when(jnp.logical_not(size <= 1e-6))
    def _():
        inverse[...] = identity
        ids = lax.broadcasted_iota(jnp.int32, (n, 1), 0)

        def eliminate(j, carry):
            pivot_row = scaled[pl.ds(j, 1), :]
            inverse_row = inverse[pl.ds(j, 1), :]
            column = jnp.sum(jnp.where(col_ids == j, scaled[...], 0.0), axis=1, keepdims=True)
            pivot = jnp.sum(jnp.where(ids == j, column, 0.0), axis=0, keepdims=True)
            root = 1.0 / jnp.sqrt(pivot)
            ratio = jnp.where(ids > j, column / pivot, jnp.where(ids == j, 1.0 - root, 0.0))
            scaled[...] = scaled[...] - ratio * pivot_row
            inverse[...] = inverse[...] - ratio * inverse_row
            return carry

        lax.fori_loop(0, n, eliminate, 0)
        product[...] = matmul(inverse[...], whole[...] * up_down * up_across, HIGHEST)

    w = inverse[...]
    root_rows = jnp.sqrt(jnp.float32(total_rows))
    upper = product[...] * across / root_rows
    factor_ref[...] = jnp.where(row_ids <= col_ids, upper, 0.0)
    basis_ref[...] = matmul_nt(own_ref[...] * up_across, w, HIGHEST) * root_rows


def factor_and_basis(total_rows, gram, own):
    columns = own.shape[1]
    return pl.pallas_call(
        functools.partial(factor_kernel, total_rows),
        out_shape=(
            jax.ShapeDtypeStruct(own.shape, jnp.float32),
            jax.ShapeDtypeStruct((columns, columns), jnp.float32),
        ),
        in_specs=[VMEM, VMEM],
        out_specs=(VMEM, VMEM),
        scratch_shapes=[pltpu.VMEM((columns, columns), jnp.float32)] * 4,
        compiler_params=pltpu.CompilerParams(vmem_limit_bytes=24 * MIB),
        name="factor_and_basis",
    )(gram, own)


def spread(piece, axes, devices):
    copies = jnp.broadcast_to(piece[None], (devices, *piece.shape))
    return lax.all_to_all(copies, axes, split_axis=0, concat_axis=0, tiled=True)


def exchange(pieces, rows):
    order = distances(len(pieces))
    return [
        lax.ppermute(piece, "rows", [(r, r ^ d) for r in range(rows)]) if d else piece
        for piece, d in zip(pieces, order)
    ]


def fetch(sketch, block_cols, counts, slots, width):
    rows, cols = lax.axis_size("rows"), lax.axis_size("cols")
    members = rows // 2
    height = width // members
    columns = sketch.shape[1]
    sketch = sketch.reshape(-1, members, height, columns)
    per = sketch.shape[0]
    largest = min(per * members, slots * members, 128)
    within = min(per, WITHIN)
    across = tuple(level for level in ACROSS if level < largest)
    stripes = turn(sketch)
    table = table_copies(block_cols, counts, rows * cols)
    table = lax.all_to_all(table, ("rows", "cols"), split_axis=0, concat_axis=0, tiled=True)
    places, lists, more, far = plan(table, slots, per, within, across)
    first = exchange(cut(lists, stripes, 0, within), rows)

    def as_sent():
        return order(first, members, per)

    def with_rest():
        return order(first + exchange(cut(lists, stripes, within, per), rows), members, per)

    own = lax.cond(more[0] > 0, with_rest, as_sent) if within < per else as_sent()

    def across_halves(count):
        def run():
            swap = [(r, (r + members) % rows) for r in range(rows)]
            other = lax.ppermute(listed(lists, own, count), "rows", swap)
            return pick(places, own, other, slots, members)

        return run

    picked = lax.switch(far[0], [across_halves(count) for count in (*across, largest)])
    return exchange(picked, rows)


def local(sketch, blocks, block_rows, block_cols, counts):
    slots, width, _ = blocks.shape
    columns = sketch.shape[1]
    rows, cols = lax.axis_size("rows"), lax.axis_size("cols")
    chosen = fetch(sketch, block_cols, counts, slots, width)
    if chosen[0].shape[1] % 16:
        order = jnp.argsort(lax.axis_index("rows") % len(chosen) ^ jnp.array(distances(len(chosen))))
        chosen = [jnp.stack(chosen)[order].swapaxes(0, 1).reshape(1, slots, width, columns)[0]]
    if cols == 2:
        halves = ((0, columns // 2), (columns // 2, columns))
        mine = [block_products(block_rows, counts, blocks, chosen, *half) for half in halves]
        own, gram = sum_and_gram(mine, [lax.ppermute(half, "cols", [(0, 1), (1, 0)]) for half in mine])
        pieces = gram.reshape(rows, -1, columns // 2)
        pieces = lax.all_to_all(pieces, "rows", split_axis=0, concat_axis=0, tiled=True)
        gram = spread(jnp.sum(pieces, axis=0), ("rows", "cols"), rows * cols)
        gram = gram.reshape(rows, cols, -1, columns // 2)
    else:
        partial_rows = block_products(block_rows, counts, blocks, chosen, 0, columns)
        own = lax.psum_scatter(partial_rows, "cols", scatter_dimension=0, tiled=True)
        gram = lax.psum(matmul(own.T, own, HIGHEST), ("rows", "cols"))
        gram = gram.reshape(1, 1, columns, columns)
    return factor_and_basis(RB * width * rows, gram, own)


def solution(mesh):
    in_specs = (
        P(("rows", "cols"), None),
        P(("rows", "cols"), None, None),
        P(("rows", "cols")),
        P(("rows", "cols")),
        P(("rows", "cols")),
    )
    out_specs = (P(("rows", "cols"), None), P())
    return jax.shard_map(local, mesh=mesh, in_specs=in_specs, out_specs=out_specs, check_vma=False)
```

```python
import functools

import jax
import jax.numpy as jnp
from jax import lax
from jax.experimental import pallas as pl
from jax.experimental.pallas import tpu as pltpu
from jax.sharding import PartitionSpec as P

RB = 4
HIGHEST = lax.Precision.HIGHEST
VMEM = pl.BlockSpec(memory_space=pltpu.VMEM)
SMEM = pl.BlockSpec(memory_space=pltpu.SMEM)
MIB = 1024 * 1024


ACROSS = (*range(11, 21), 22, 24, 28, 36)
WITHIN = 8


def table_kernel(cols_ref, counts_ref, out_ref):
    slots = cols_ref.shape[0]
    lane = lax.broadcasted_iota(jnp.int32, out_ref.shape, 2)
    table = jnp.where(lane == slots, counts_ref[0], 0)
    for s in range(slots):
        table = jnp.where(lane == s, cols_ref[s], table)
    out_ref[...] = table


def table_copies(block_cols, counts, devices):
    return pl.pallas_call(
        table_kernel,
        out_shape=jax.ShapeDtypeStruct((devices, 1, 128), jnp.int32),
        in_specs=[SMEM, SMEM],
        out_specs=VMEM,
        name="table_copies",
    )(block_cols, counts)


def over(values, size):
    return values >> (size.bit_length() - 1)


def plan_kernel(slots, per, within, across, table_ref, places_ref, lists_ref, *level_refs):
    devices = table_ref.shape[0]
    rows, cols = lax.axis_size("rows"), lax.axis_size("cols")
    panel = per * rows
    part = panel // 2
    groups = [range(at, min(at + 64, devices)) for at in range(0, devices, 64)]

    def read(group):
        table = table_ref[group.start : group.stop, 0, :]
        lane = lax.broadcasted_iota(jnp.int32, table.shape, 1)
        counts = table[:, slots : slots + 1]
        table = jnp.where(lane < counts, table, -1)
        block = lax.broadcasted_iota(jnp.int32, (len(group), panel), 1)
        return table, counts, [table[:, s : s + 1] == block for s in range(slots)]

    lines = -(-cols // 8) * 8
    line = lax.broadcasted_iota(jnp.int32, (3 * lines, panel), 0)
    ids = lax.broadcasted_iota(jnp.int32, (1, panel), 1)
    asks = jnp.zeros((3 * lines, panel), jnp.float32)
    for group in groups:
        _, _, asked = read(group)
        some = jnp.where(functools.reduce(jnp.logical_or, asked), 1.0, 0.0).astype(jnp.bfloat16)
        shape = (3 * lines, len(group))
        number = lax.broadcasted_iota(jnp.int32, shape, 0)
        device = lax.broadcasted_iota(jnp.int32, shape, 1) + group.start
        core, side = device & (cols - 1), over(device, devices // 2)
        reads = (number == core) | (number == lines * (1 + side) + core)
        asks += jnp.dot(jnp.where(reads, 1.0, 0.0).astype(jnp.bfloat16), some, preferred_element_type=jnp.float32)
    own_half = (line >= lines) & (over(line - lines, lines) == over(lax.broadcasted_iota(jnp.int32, line.shape, 1), part))
    asks = jnp.where((asks > 0.5) & jnp.logical_not(own_half), 1.0, 0.0)
    first = lax.broadcasted_iota(jnp.int32, (panel, panel), 0)
    second = lax.broadcasted_iota(jnp.int32, (panel, panel), 1)
    after = first > second
    near = jnp.where(after & ((first ^ second) < per), 1.0, 0.0).astype(jnp.bfloat16)
    after = jnp.where(after, 1.0, 0.0).astype(jnp.bfloat16)
    same = jnp.where(first == second, 1.0, 0.0).astype(jnp.bfloat16)
    nt = (((1,), (1,)), ((), ()))

    def ranks(a, b):
        return lax.dot_general(a, b, nt, preferred_element_type=jnp.float32)

    short = asks.astype(jnp.bfloat16)
    near_rank = ranks(short, near)
    far_rank = ranks(short, after)
    longest = jnp.max(jnp.where(line < lines, near_rank + asks, 0.0)).astype(jnp.int32)
    level_refs[0][0] = (longest > within).astype(jnp.int32)
    longest = jnp.max(jnp.where(line < lines, 0.0, far_rank + asks)).astype(jnp.int32)
    level_refs[1][0] = sum((longest > level).astype(jnp.int32) for level in across)
    me = lax.axis_index("rows")
    half, c = over(me, rows // 2), lax.axis_index("cols")

    def row(values, number):
        return jnp.sum(jnp.where(line == number, values, 0.0), axis=0, keepdims=True)

    here = (ids & -per) - half * part + row(near_rank, c).astype(jnp.int32)
    there = part + row(far_rank, lines * (1 + half) + c).astype(jnp.int32)
    place = jnp.where(over(ids, part) == half, here, there)
    for group in groups:
        table, _, asked = read(group)
        lane = lax.broadcasted_iota(jnp.int32, table.shape, 1)
        places = jnp.zeros(table.shape, jnp.int32)
        for s in range(slots):
            found = jnp.sum(jnp.where(asked[s], place, 0), axis=1, keepdims=True)
            places = jnp.where(lane == s, found, places)
        places_ref[group.start : group.stop] = places
    line = lax.broadcasted_iota(jnp.int32, (panel, 3 * lines), 1)

    def column(values, number):
        return jnp.sum(jnp.where(line == number, values, 0.0), axis=1, keepdims=True)

    turned, near_rank, far_rank = ranks(same, short), ranks(near, short), ranks(after, short)
    ids = lax.broadcasted_iota(jnp.int32, (panel, 1), 0)
    number = lax.broadcasted_iota(jnp.int32, (panel, lists_ref.shape[1]), 1)
    near_rank = column(near_rank, c).astype(jnp.int32)
    here = (ids & -per) - half * part + near_rank
    other = lines * (2 - half) + c
    sent = (column(turned, other) > 0.5) & (column(far_rank, other).astype(jnp.int32) == number)
    sent = jnp.sum(jnp.where(sent, here, 0), axis=0, keepdims=True)
    kept = (column(turned, c) > 0.5) & (over(ids, per) == me) & (near_rank == number)
    kept = jnp.sum(jnp.where(kept, ids & (per - 1), 0), axis=0, keepdims=True)
    lists_ref[...] = jnp.where(lax.broadcasted_iota(jnp.int32, lists_ref.shape, 0) == 0, sent, kept)


def plan(table, slots, per, within, across):
    devices = table.shape[0]
    return pl.pallas_call(
        functools.partial(plan_kernel, slots, per, within, across),
        out_shape=(
            jax.ShapeDtypeStruct((devices, 128), jnp.int32),
            jax.ShapeDtypeStruct((8, 128), jnp.int32),
            jax.ShapeDtypeStruct((1,), jnp.int32),
            jax.ShapeDtypeStruct((1,), jnp.int32),
        ),
        in_specs=[VMEM],
        out_specs=(VMEM, VMEM, SMEM, SMEM),
        compiler_params=pltpu.CompilerParams(vmem_limit_bytes=48 * MIB),
        name="plan",
    )(table)


def distances(members):
    return [0, *sorted(range(1, members), key=lambda d: (-d.bit_count(), -d))]


def turn_kernel(sketch_ref, out_ref):
    members = out_ref.shape[0]
    me = lax.axis_index("rows") % members
    for i, d in enumerate(distances(members)):
        out_ref[i] = sketch_ref[:, me ^ d]


def turn(sketch):
    blocks, members, height, columns = sketch.shape
    return pl.pallas_call(
        turn_kernel,
        out_shape=jax.ShapeDtypeStruct((members, blocks, height, columns), sketch.dtype),
        in_specs=[VMEM],
        out_specs=VMEM,
        compiler_params=pltpu.CompilerParams(vmem_limit_bytes=24 * MIB),
        cost_estimate=pl.CostEstimate(flops=0, bytes_accessed=4 * sketch.size, transcendentals=0),
        name="turn_stripes",
    )(sketch)


def cut_kernel(start, lists_ref, stripes_ref, *out_refs):
    for k in range(out_refs[0].shape[0]):
        for i, out_ref in enumerate(out_refs):
            out_ref[k] = stripes_ref[i, lists_ref[1, start + k]]


def cut(lists, stripes, start, stop):
    members, _, height, columns = stripes.shape
    return pl.pallas_call(
        functools.partial(cut_kernel, start),
        out_shape=(jax.ShapeDtypeStruct((stop - start, height, columns), stripes.dtype),) * members,
        in_specs=[SMEM, VMEM],
        out_specs=(VMEM,) * members,
        compiler_params=pltpu.CompilerParams(vmem_limit_bytes=24 * MIB),
        name="cut_stripes",
    )(lists, stripes)


def order_kernel(members, *refs):
    *stripe_refs, all_ref = refs
    me = lax.axis_index("rows") % members
    per = all_ref.shape[0] // members
    for i, d in enumerate(distances(members)):
        at = (me ^ d) * per
        for ref in stripe_refs[i::members]:
            all_ref[pl.ds(at, ref.shape[0])] = ref[...]
            at = at + ref.shape[0]


def order(stripes, members, per):
    _, height, columns = stripes[0].shape
    return pl.pallas_call(
        functools.partial(order_kernel, members),
        out_shape=jax.ShapeDtypeStruct((members * per, height, columns), stripes[0].dtype),
        in_specs=[VMEM] * len(stripes),
        out_specs=VMEM,
        compiler_params=pltpu.CompilerParams(vmem_limit_bytes=24 * MIB),
        name="order_stripes",
    )(*stripes)


def list_kernel(list_ref, all_ref, out_ref):
    for k in range(out_ref.shape[0]):
        out_ref[k] = all_ref[list_ref[0, k]]


def listed(numbers, stripes, count):
    return pl.pallas_call(
        list_kernel,
        out_shape=jax.ShapeDtypeStruct((count, *stripes.shape[1:]), stripes.dtype),
        in_specs=[SMEM, VMEM],
        out_specs=VMEM,
        compiler_params=pltpu.CompilerParams(vmem_limit_bytes=24 * MIB),
        name="listed_stripes",
    )(numbers, stripes)


def pick_kernel(places_ref, own_ref, other_ref, *refs):
    *out_refs, whole = refs
    here = own_ref.shape[0]
    whole[:here] = own_ref[...]
    whole[here:] = other_ref[...]
    for d, out_ref in zip(distances(len(out_refs)), out_refs):
        device = (lax.axis_index("rows") ^ d) * lax.axis_size("cols") + lax.axis_index("cols")
        for s in range(out_ref.shape[0]):
            out_ref[s] = whole[jnp.minimum(places_ref[device, s], whole.shape[0] - 1)]


def pick(places, own, other, slots, members):
    shape = own.shape[1:]
    return pl.pallas_call(
        pick_kernel,
        out_shape=(jax.ShapeDtypeStruct((slots, *shape), own.dtype),) * members,
        in_specs=[SMEM, VMEM, VMEM],
        out_specs=(VMEM,) * members,
        scratch_shapes=[pltpu.VMEM((own.shape[0] + other.shape[0], *shape), own.dtype)],
        compiler_params=pltpu.CompilerParams(vmem_limit_bytes=24 * MIB),
        name="pick_stripes",
    )(places, own, other)


def product_kernel(rows_ref, counts_ref, blocks_ref, *refs):
    *chosen_refs, out_ref, whole = refs
    slots, width, _ = blocks_ref.shape
    columns = out_ref.shape[1]
    members = len(chosen_refs)
    me = lax.axis_index("rows") % members
    for ref, d in zip(chosen_refs, distances(members) if members > 1 else [0]):
        whole[me ^ d] = ref[...]
    out_ref[...] = jnp.zeros_like(out_ref)
    for s in range(slots):

        @pl.when(s < counts_ref[0])
        def _():
            piece = whole[:, s].reshape(width, columns)
            product = jnp.dot(blocks_ref[s], piece, preferred_element_type=jnp.float32)
            at = pl.ds(pl.multiple_of(rows_ref[s] * width, width), width)
            out_ref[at, :] += product


def block_products(block_rows, counts, blocks, chosen):
    _, width, _ = blocks.shape
    columns = chosen[0].shape[-1]
    return pl.pallas_call(
        product_kernel,
        out_shape=jax.ShapeDtypeStruct((RB * width, columns), jnp.float32),
        in_specs=[SMEM, SMEM, VMEM] + [VMEM] * len(chosen),
        out_specs=VMEM,
        scratch_shapes=[pltpu.VMEM((len(chosen), *chosen[0].shape), chosen[0].dtype)],
        compiler_params=pltpu.CompilerParams(vmem_limit_bytes=24 * MIB),
        name="block_products",
    )(block_rows, counts, blocks, *chosen)


def gram_kernel(mine_ref, other_ref, own_ref, gram_ref, slab):
    c = lax.axis_index("cols")
    share, width = own_ref.shape[0], gram_ref.shape[1]
    slab[...] = mine_ref[...] + other_ref[...]
    own_ref[...] = slab[pl.ds(pl.multiple_of(c * share, share), share), :]
    right = slab[:, pl.ds(pl.multiple_of(c * width, width), width)]
    gram_ref[...] = lax.dot_general(
        slab[...], right, (((0,), (0,)), ((), ())), precision=HIGHEST, preferred_element_type=jnp.float32
    )


def sum_and_gram(mine, other):
    rows, columns = mine.shape
    return pl.pallas_call(
        gram_kernel,
        out_shape=(
            jax.ShapeDtypeStruct((rows // 2, columns), jnp.float32),
            jax.ShapeDtypeStruct((columns, columns // 2), jnp.float32),
        ),
        in_specs=[VMEM, VMEM],
        out_specs=(VMEM, VMEM),
        scratch_shapes=[pltpu.VMEM((rows, columns), jnp.float32)],
        compiler_params=pltpu.CompilerParams(vmem_limit_bytes=24 * MIB),
        name="sum_and_gram",
    )(mine, other)


def matmul(a, b, precision):
    return jnp.dot(a, b, precision=precision, preferred_element_type=jnp.float32)


def matmul_nt(a, b, precision):
    return lax.dot_general(
        a, b, (((1,), (1,)), ((), ())), precision=precision, preferred_element_type=jnp.float32
    )


def split_matmul(times, passes, a, b):
    a_high, b_high = a.astype(jnp.bfloat16), b.astype(jnp.bfloat16)
    result = times(a_high, b_high, None)
    if passes == 3:
        a_low = (a - a_high.astype(jnp.float32)).astype(jnp.bfloat16)
        b_low = (b - b_high.astype(jnp.float32)).astype(jnp.bfloat16)
        result += times(a_high, b_low, None) + times(a_low, b_high, None)
    return result


def factor_kernel(total_rows, gram_ref, own_ref, basis_ref, factor_ref, whole, scaled, inverse, product):
    n = factor_ref.shape[0]
    width = gram_ref.shape[-1]
    for c in range(n // width):
        whole[:, c * width : (c + 1) * width] = gram_ref[:, c].reshape(n, width)
    row_ids = lax.broadcasted_iota(jnp.int32, (n, n), 0)
    col_ids = lax.broadcasted_iota(jnp.int32, (n, n), 1)
    diagonal = row_ids == col_ids
    identity = diagonal.astype(jnp.float32)
    half = jnp.where(row_ids > col_ids, 1.0, jnp.where(diagonal, 0.5, 0.0))
    gram = whole[...]
    on_diagonal = jnp.where(diagonal, gram, 0.0)
    down = jnp.sqrt(jnp.sum(on_diagonal, axis=1, keepdims=True))
    across = jnp.sqrt(jnp.sum(on_diagonal, axis=0, keepdims=True))
    up_down = 1.0 / down
    up_across = 1.0 / across
    scaled[...] = gram * up_down * up_across

    def refine(times, times_nt):
        w = inverse[...]
        upper = times(w, scaled[...])
        residual = times_nt(upper, w) - identity
        step = residual * half
        inverse[...] = w - matmul(step, w, lax.Precision.DEFAULT)
        product[...] = upper - matmul(step, upper, lax.Precision.DEFAULT)
        return jnp.sum(residual * residual)

    def exactly(times):
        return functools.partial(times, precision=HIGHEST)

    inverse[...] = identity - (scaled[...] - identity) * half
    for passes in (1, 3):
        refine(functools.partial(split_matmul, matmul, passes), functools.partial(split_matmul, matmul_nt, passes))

    def going(state):
        step, size = state
        return (step < 8) & (size > 1e-6)

    def advance(state):
        return state[0] + 1, refine(exactly(matmul), exactly(matmul_nt))

    _, size = lax.while_loop(going, advance, (jnp.int32(0), jnp.float32(1.0)))

    @pl.when(jnp.logical_not(size <= 1e-6))
    def _():
        inverse[...] = identity
        ids = lax.broadcasted_iota(jnp.int32, (n, 1), 0)

        def eliminate(j, carry):
            pivot_row = scaled[pl.ds(j, 1), :]
            inverse_row = inverse[pl.ds(j, 1), :]
            column = jnp.sum(jnp.where(col_ids == j, scaled[...], 0.0), axis=1, keepdims=True)
            pivot = jnp.sum(jnp.where(ids == j, column, 0.0), axis=0, keepdims=True)
            root = 1.0 / jnp.sqrt(pivot)
            ratio = jnp.where(ids > j, column / pivot, jnp.where(ids == j, 1.0 - root, 0.0))
            scaled[...] = scaled[...] - ratio * pivot_row
            inverse[...] = inverse[...] - ratio * inverse_row
            return carry

        lax.fori_loop(0, n, eliminate, 0)
        product[...] = matmul(inverse[...], whole[...] * up_down * up_across, HIGHEST)

    w = inverse[...]
    root_rows = jnp.sqrt(jnp.float32(total_rows))
    upper = product[...] * across / root_rows
    factor_ref[...] = jnp.where(row_ids <= col_ids, upper, 0.0)
    basis_ref[...] = matmul_nt(own_ref[...] * up_across, w, HIGHEST) * root_rows


def factor_and_basis(total_rows, gram, own):
    columns = own.shape[1]
    return pl.pallas_call(
        functools.partial(factor_kernel, total_rows),
        out_shape=(
            jax.ShapeDtypeStruct(own.shape, jnp.float32),
            jax.ShapeDtypeStruct((columns, columns), jnp.float32),
        ),
        in_specs=[VMEM, VMEM],
        out_specs=(VMEM, VMEM),
        scratch_shapes=[pltpu.VMEM((columns, columns), jnp.float32)] * 4,
        compiler_params=pltpu.CompilerParams(vmem_limit_bytes=24 * MIB),
        name="factor_and_basis",
    )(gram, own)


def spread(piece, axes, devices):
    copies = jnp.broadcast_to(piece[None], (devices, *piece.shape))
    return lax.all_to_all(copies, axes, split_axis=0, concat_axis=0, tiled=True)


def exchange(pieces, rows):
    order = distances(len(pieces))
    return [
        lax.ppermute(piece, "rows", [(r, r ^ d) for r in range(rows)]) if d else piece
        for piece, d in zip(pieces, order)
    ]


def fetch(sketch, block_cols, counts, slots, width):
    rows, cols = lax.axis_size("rows"), lax.axis_size("cols")
    members = rows // 2
    height = width // members
    columns = sketch.shape[1]
    sketch = sketch.reshape(-1, members, height, columns)
    per = sketch.shape[0]
    largest = min(per * members, slots * members, 128)
    within = min(per, WITHIN)
    across = tuple(level for level in ACROSS if level < largest and members <= 8)
    stripes = turn(sketch)
    table = table_copies(block_cols, counts, rows * cols)
    table = lax.all_to_all(table, ("rows", "cols"), split_axis=0, concat_axis=0, tiled=True)
    places, lists, more, far = plan(table, slots, per, within, across)
    first = exchange(cut(lists, stripes, 0, within), rows)

    def as_sent():
        return order(first, members, per)

    def with_rest():
        return order(first + exchange(cut(lists, stripes, within, per), rows), members, per)

    own = lax.cond(more[0] > 0, with_rest, as_sent) if within < per else as_sent()

    def across_halves(count):
        def run():
            swap = [(r, (r + members) % rows) for r in range(rows)]
            other = lax.ppermute(listed(lists, own, count), "rows", swap)
            return pick(places, own, other, slots, members)

        return run

    picked = lax.switch(far[0], [across_halves(count) for count in (*across, largest)])
    return exchange(picked, rows)


def local(sketch, blocks, block_rows, block_cols, counts):
    slots, width, _ = blocks.shape
    columns = sketch.shape[1]
    rows, cols = lax.axis_size("rows"), lax.axis_size("cols")
    chosen = fetch(sketch, block_cols, counts, slots, width)
    if chosen[0].shape[1] % 16:
        order = jnp.argsort(lax.axis_index("rows") % len(chosen) ^ jnp.array(distances(len(chosen))))
        chosen = [jnp.stack(chosen)[order].swapaxes(0, 1).reshape(1, slots, width, columns)[0]]
    partial_rows = block_products(block_rows, counts, blocks, chosen)
    if cols == 2:
        other = lax.ppermute(partial_rows, "cols", [(0, 1), (1, 0)])
        own, gram = sum_and_gram(partial_rows, other)
        pieces = gram.reshape(rows, -1, columns // 2)
        pieces = lax.all_to_all(pieces, "rows", split_axis=0, concat_axis=0, tiled=True)
        gram = spread(jnp.sum(pieces, axis=0), ("rows", "cols"), rows * cols)
        gram = gram.reshape(rows, cols, -1, columns // 2)
    else:
        own = lax.psum_scatter(partial_rows, "cols", scatter_dimension=0, tiled=True)
        gram = lax.psum(matmul(own.T, own, HIGHEST), ("rows", "cols"))
        gram = gram.reshape(1, 1, columns, columns)
    return factor_and_basis(RB * width * rows, gram, own)


def solution(mesh):
    in_specs = (
        P(("rows", "cols"), None),
        P(("rows", "cols"), None, None),
        P(("rows", "cols")),
        P(("rows", "cols")),
        P(("rows", "cols")),
    )
    out_specs = (P(("rows", "cols"), None), P())
    return jax.shard_map(local, mesh=mesh, in_specs=in_specs, out_specs=out_specs, check_vma=False)
```

```python
import functools

import jax
import jax.numpy as jnp
from jax import lax
from jax.experimental import pallas as pl
from jax.experimental.pallas import tpu as pltpu
from jax.sharding import PartitionSpec as P

RB = 4
HIGHEST = lax.Precision.HIGHEST
VMEM = pl.BlockSpec(memory_space=pltpu.VMEM)
SMEM = pl.BlockSpec(memory_space=pltpu.SMEM)
MIB = 1024 * 1024


ACROSS = (*range(11, 21), 22, 24, 28, 36)
WITHIN = (5, 6, 7, 8, 9, 10, 12)


def table_kernel(cols_ref, counts_ref, out_ref):
    slots = cols_ref.shape[0]
    lane = lax.broadcasted_iota(jnp.int32, out_ref.shape, 2)
    table = jnp.where(lane == slots, counts_ref[0], 0)
    for s in range(slots):
        table = jnp.where(lane == s, cols_ref[s], table)
    out_ref[...] = table


def table_copies(block_cols, counts, devices):
    return pl.pallas_call(
        table_kernel,
        out_shape=jax.ShapeDtypeStruct((devices, 1, 128), jnp.int32),
        in_specs=[SMEM, SMEM],
        out_specs=VMEM,
        name="table_copies",
    )(block_cols, counts)


def over(values, size):
    return values >> (size.bit_length() - 1)


def plan_kernel(slots, per, within, across, table_ref, places_ref, lists_ref, *level_refs):
    devices = table_ref.shape[0]
    rows, cols = lax.axis_size("rows"), lax.axis_size("cols")
    panel = per * rows
    part = panel // 2
    groups = [range(at, min(at + 64, devices)) for at in range(0, devices, 64)]

    def read(group):
        table = table_ref[group.start : group.stop, 0, :]
        lane = lax.broadcasted_iota(jnp.int32, table.shape, 1)
        counts = table[:, slots : slots + 1]
        table = jnp.where(lane < counts, table, -1)
        block = lax.broadcasted_iota(jnp.int32, (len(group), panel), 1)
        return table, counts, [table[:, s : s + 1] == block for s in range(slots)]

    lines = -(-cols // 8) * 8
    line = lax.broadcasted_iota(jnp.int32, (3 * lines, panel), 0)
    ids = lax.broadcasted_iota(jnp.int32, (1, panel), 1)
    asks = jnp.zeros((3 * lines, panel), jnp.float32)
    for group in groups:
        _, _, asked = read(group)
        some = jnp.where(functools.reduce(jnp.logical_or, asked), 1.0, 0.0).astype(jnp.bfloat16)
        shape = (3 * lines, len(group))
        number = lax.broadcasted_iota(jnp.int32, shape, 0)
        device = lax.broadcasted_iota(jnp.int32, shape, 1) + group.start
        core, side = device & (cols - 1), over(device, devices // 2)
        reads = (number == core) | (number == lines * (1 + side) + core)
        asks += jnp.dot(jnp.where(reads, 1.0, 0.0).astype(jnp.bfloat16), some, preferred_element_type=jnp.float32)
    own_half = (line >= lines) & (over(line - lines, lines) == over(lax.broadcasted_iota(jnp.int32, line.shape, 1), part))
    asks = jnp.where((asks > 0.5) & jnp.logical_not(own_half), 1.0, 0.0)
    first = lax.broadcasted_iota(jnp.int32, (panel, panel), 0)
    second = lax.broadcasted_iota(jnp.int32, (panel, panel), 1)
    after = first > second
    near = jnp.where(after & ((first ^ second) < per), 1.0, 0.0).astype(jnp.bfloat16)
    after = jnp.where(after, 1.0, 0.0).astype(jnp.bfloat16)
    same = jnp.where(first == second, 1.0, 0.0).astype(jnp.bfloat16)
    nt = (((1,), (1,)), ((), ()))

    def ranks(a, b):
        return lax.dot_general(a, b, nt, preferred_element_type=jnp.float32)

    short = asks.astype(jnp.bfloat16)
    near_rank = ranks(short, near)
    far_rank = ranks(short, after)
    longest = jnp.max(jnp.where(line < lines, near_rank + asks, 0.0)).astype(jnp.int32)
    level_refs[0][0] = sum((longest > level).astype(jnp.int32) for level in within)
    longest = jnp.max(jnp.where(line < lines, 0.0, far_rank + asks)).astype(jnp.int32)
    level_refs[1][0] = sum((longest > level).astype(jnp.int32) for level in across)
    me = lax.axis_index("rows")
    half, c = over(me, rows // 2), lax.axis_index("cols")

    def row(values, number):
        return jnp.sum(jnp.where(line == number, values, 0.0), axis=0, keepdims=True)

    here = (ids & -per) - half * part + row(near_rank, c).astype(jnp.int32)
    there = part + row(far_rank, lines * (1 + half) + c).astype(jnp.int32)
    place = jnp.where(over(ids, part) == half, here, there)
    for group in groups:
        table, _, asked = read(group)
        lane = lax.broadcasted_iota(jnp.int32, table.shape, 1)
        places = jnp.zeros(table.shape, jnp.int32)
        for s in range(slots):
            found = jnp.sum(jnp.where(asked[s], place, 0), axis=1, keepdims=True)
            places = jnp.where(lane == s, found, places)
        places_ref[group.start : group.stop] = places
    line = lax.broadcasted_iota(jnp.int32, (panel, 3 * lines), 1)

    def column(values, number):
        return jnp.sum(jnp.where(line == number, values, 0.0), axis=1, keepdims=True)

    turned, near_rank, far_rank = ranks(same, short), ranks(near, short), ranks(after, short)
    ids = lax.broadcasted_iota(jnp.int32, (panel, 1), 0)
    number = lax.broadcasted_iota(jnp.int32, (panel, lists_ref.shape[1]), 1)
    near_rank = column(near_rank, c).astype(jnp.int32)
    here = (ids & -per) - half * part + near_rank
    other = lines * (2 - half) + c
    sent = (column(turned, other) > 0.5) & (column(far_rank, other).astype(jnp.int32) == number)
    sent = jnp.sum(jnp.where(sent, here, 0), axis=0, keepdims=True)
    kept = (column(turned, c) > 0.5) & (over(ids, per) == me) & (near_rank == number)
    kept = jnp.sum(jnp.where(kept, ids & (per - 1), 0), axis=0, keepdims=True)
    lists_ref[...] = jnp.where(lax.broadcasted_iota(jnp.int32, lists_ref.shape, 0) == 0, sent, kept)


def plan(table, slots, per, within, across):
    devices = table.shape[0]
    return pl.pallas_call(
        functools.partial(plan_kernel, slots, per, within, across),
        out_shape=(
            jax.ShapeDtypeStruct((devices, 128), jnp.int32),
            jax.ShapeDtypeStruct((8, 128), jnp.int32),
            jax.ShapeDtypeStruct((1,), jnp.int32),
            jax.ShapeDtypeStruct((1,), jnp.int32),
        ),
        in_specs=[VMEM],
        out_specs=(VMEM, VMEM, SMEM, SMEM),
        compiler_params=pltpu.CompilerParams(vmem_limit_bytes=48 * MIB),
        name="plan",
    )(table)


def distances(members):
    return [0, *sorted(range(1, members), key=lambda d: (-d.bit_count(), -d))]


def turn_kernel(sketch_ref, out_ref):
    members = out_ref.shape[0]
    me = lax.axis_index("rows") % members
    for i, d in enumerate(distances(members)):
        out_ref[i] = sketch_ref[:, me ^ d]


def turn(sketch):
    blocks, members, height, columns = sketch.shape
    return pl.pallas_call(
        turn_kernel,
        out_shape=jax.ShapeDtypeStruct((members, blocks, height, columns), sketch.dtype),
        in_specs=[VMEM],
        out_specs=VMEM,
        compiler_params=pltpu.CompilerParams(vmem_limit_bytes=24 * MIB),
        cost_estimate=pl.CostEstimate(flops=0, bytes_accessed=4 * sketch.size, transcendentals=0),
        name="turn_stripes",
    )(sketch)


def cut_kernel(lists_ref, stripes_ref, *out_refs):
    for k in range(out_refs[0].shape[0]):
        for i, out_ref in enumerate(out_refs):
            out_ref[k] = stripes_ref[i, lists_ref[1, k]]


def cut(lists, stripes, count):
    members, _, height, columns = stripes.shape
    return pl.pallas_call(
        cut_kernel,
        out_shape=(jax.ShapeDtypeStruct((count, height, columns), stripes.dtype),) * members,
        in_specs=[SMEM, VMEM],
        out_specs=(VMEM,) * members,
        compiler_params=pltpu.CompilerParams(vmem_limit_bytes=24 * MIB),
        name="cut_stripes",
    )(lists, stripes)


def order_kernel(*refs):
    *stripe_refs, all_ref = refs
    members = len(stripe_refs)
    me = lax.axis_index("rows") % members
    per = all_ref.shape[0] // members
    for ref, d in zip(stripe_refs, distances(members)):
        all_ref[pl.ds((me ^ d) * per, ref.shape[0])] = ref[...]


def order(stripes, per):
    _, height, columns = stripes[0].shape
    return pl.pallas_call(
        order_kernel,
        out_shape=jax.ShapeDtypeStruct((len(stripes) * per, height, columns), stripes[0].dtype),
        in_specs=[VMEM] * len(stripes),
        out_specs=VMEM,
        compiler_params=pltpu.CompilerParams(vmem_limit_bytes=24 * MIB),
        name="order_stripes",
    )(*stripes)


def list_kernel(list_ref, all_ref, out_ref):
    for k in range(out_ref.shape[0]):
        out_ref[k] = all_ref[list_ref[0, k]]


def listed(numbers, stripes, count):
    return pl.pallas_call(
        list_kernel,
        out_shape=jax.ShapeDtypeStruct((count, *stripes.shape[1:]), stripes.dtype),
        in_specs=[SMEM, VMEM],
        out_specs=VMEM,
        compiler_params=pltpu.CompilerParams(vmem_limit_bytes=24 * MIB),
        name="listed_stripes",
    )(numbers, stripes)


def pick_kernel(places_ref, own_ref, other_ref, *refs):
    *out_refs, whole = refs
    here = own_ref.shape[0]
    whole[:here] = own_ref[...]
    whole[here:] = other_ref[...]
    for d, out_ref in zip(distances(len(out_refs)), out_refs):
        device = (lax.axis_index("rows") ^ d) * lax.axis_size("cols") + lax.axis_index("cols")
        for s in range(out_ref.shape[0]):
            out_ref[s] = whole[jnp.minimum(places_ref[device, s], whole.shape[0] - 1)]


def pick(places, own, other, slots, members):
    shape = own.shape[1:]
    return pl.pallas_call(
        pick_kernel,
        out_shape=(jax.ShapeDtypeStruct((slots, *shape), own.dtype),) * members,
        in_specs=[SMEM, VMEM, VMEM],
        out_specs=(VMEM,) * members,
        scratch_shapes=[pltpu.VMEM((own.shape[0] + other.shape[0], *shape), own.dtype)],
        compiler_params=pltpu.CompilerParams(vmem_limit_bytes=24 * MIB),
        name="pick_stripes",
    )(places, own, other)


def product_kernel(rows_ref, counts_ref, blocks_ref, *refs):
    *chosen_refs, out_ref, whole = refs
    slots, width, _ = blocks_ref.shape
    columns = out_ref.shape[1]
    members = len(chosen_refs)
    me = lax.axis_index("rows") % members
    for ref, d in zip(chosen_refs, distances(members) if members > 1 else [0]):
        whole[me ^ d] = ref[...]
    out_ref[...] = jnp.zeros_like(out_ref)
    for s in range(slots):

        @pl.when(s < counts_ref[0])
        def _():
            piece = whole[:, s].reshape(width, columns)
            product = jnp.dot(blocks_ref[s], piece, preferred_element_type=jnp.float32)
            at = pl.ds(pl.multiple_of(rows_ref[s] * width, width), width)
            out_ref[at, :] += product


def block_products(block_rows, counts, blocks, chosen):
    _, width, _ = blocks.shape
    columns = chosen[0].shape[-1]
    return pl.pallas_call(
        product_kernel,
        out_shape=jax.ShapeDtypeStruct((RB * width, columns), jnp.float32),
        in_specs=[SMEM, SMEM, VMEM] + [VMEM] * len(chosen),
        out_specs=VMEM,
        scratch_shapes=[pltpu.VMEM((len(chosen), *chosen[0].shape), chosen[0].dtype)],
        compiler_params=pltpu.CompilerParams(vmem_limit_bytes=24 * MIB),
        name="block_products",
    )(block_rows, counts, blocks, *chosen)


def gram_kernel(mine_ref, other_ref, own_ref, gram_ref, slab):
    c = lax.axis_index("cols")
    share, width = own_ref.shape[0], gram_ref.shape[1]
    slab[...] = mine_ref[...] + other_ref[...]
    own_ref[...] = slab[pl.ds(pl.multiple_of(c * share, share), share), :]
    right = slab[:, pl.ds(pl.multiple_of(c * width, width), width)]
    gram_ref[...] = lax.dot_general(
        slab[...], right, (((0,), (0,)), ((), ())), precision=HIGHEST, preferred_element_type=jnp.float32
    )


def sum_and_gram(mine, other):
    rows, columns = mine.shape
    return pl.pallas_call(
        gram_kernel,
        out_shape=(
            jax.ShapeDtypeStruct((rows // 2, columns), jnp.float32),
            jax.ShapeDtypeStruct((columns, columns // 2), jnp.float32),
        ),
        in_specs=[VMEM, VMEM],
        out_specs=(VMEM, VMEM),
        scratch_shapes=[pltpu.VMEM((rows, columns), jnp.float32)],
        compiler_params=pltpu.CompilerParams(vmem_limit_bytes=24 * MIB),
        name="sum_and_gram",
    )(mine, other)


def matmul(a, b, precision):
    return jnp.dot(a, b, precision=precision, preferred_element_type=jnp.float32)


def matmul_nt(a, b, precision):
    return lax.dot_general(
        a, b, (((1,), (1,)), ((), ())), precision=precision, preferred_element_type=jnp.float32
    )


def split_matmul(times, passes, a, b):
    a_high, b_high = a.astype(jnp.bfloat16), b.astype(jnp.bfloat16)
    result = times(a_high, b_high, None)
    if passes == 3:
        a_low = (a - a_high.astype(jnp.float32)).astype(jnp.bfloat16)
        b_low = (b - b_high.astype(jnp.float32)).astype(jnp.bfloat16)
        result += times(a_high, b_low, None) + times(a_low, b_high, None)
    return result


def factor_kernel(total_rows, gram_ref, own_ref, basis_ref, factor_ref, whole, scaled, inverse, product):
    n = factor_ref.shape[0]
    width = gram_ref.shape[-1]
    for c in range(n // width):
        whole[:, c * width : (c + 1) * width] = gram_ref[:, c].reshape(n, width)
    row_ids = lax.broadcasted_iota(jnp.int32, (n, n), 0)
    col_ids = lax.broadcasted_iota(jnp.int32, (n, n), 1)
    diagonal = row_ids == col_ids
    identity = diagonal.astype(jnp.float32)
    half = jnp.where(row_ids > col_ids, 1.0, jnp.where(diagonal, 0.5, 0.0))
    gram = whole[...]
    on_diagonal = jnp.where(diagonal, gram, 0.0)
    down = jnp.sqrt(jnp.sum(on_diagonal, axis=1, keepdims=True))
    across = jnp.sqrt(jnp.sum(on_diagonal, axis=0, keepdims=True))
    up_down = 1.0 / down
    up_across = 1.0 / across
    scaled[...] = gram * up_down * up_across

    def refine(times, times_nt):
        w = inverse[...]
        upper = times(w, scaled[...])
        residual = times_nt(upper, w) - identity
        step = residual * half
        inverse[...] = w - matmul(step, w, lax.Precision.DEFAULT)
        product[...] = upper - matmul(step, upper, lax.Precision.DEFAULT)
        return jnp.sum(residual * residual)

    def exactly(times):
        return functools.partial(times, precision=HIGHEST)

    inverse[...] = identity - (scaled[...] - identity) * half
    for passes in (1, 3):
        refine(functools.partial(split_matmul, matmul, passes), functools.partial(split_matmul, matmul_nt, passes))

    def going(state):
        step, size = state
        return (step < 8) & (size > 1e-6)

    def advance(state):
        return state[0] + 1, refine(exactly(matmul), exactly(matmul_nt))

    _, size = lax.while_loop(going, advance, (jnp.int32(0), jnp.float32(1.0)))

    @pl.when(jnp.logical_not(size <= 1e-6))
    def _():
        inverse[...] = identity
        ids = lax.broadcasted_iota(jnp.int32, (n, 1), 0)

        def eliminate(j, carry):
            pivot_row = scaled[pl.ds(j, 1), :]
            inverse_row = inverse[pl.ds(j, 1), :]
            column = jnp.sum(jnp.where(col_ids == j, scaled[...], 0.0), axis=1, keepdims=True)
            pivot = jnp.sum(jnp.where(ids == j, column, 0.0), axis=0, keepdims=True)
            root = 1.0 / jnp.sqrt(pivot)
            ratio = jnp.where(ids > j, column / pivot, jnp.where(ids == j, 1.0 - root, 0.0))
            scaled[...] = scaled[...] - ratio * pivot_row
            inverse[...] = inverse[...] - ratio * inverse_row
            return carry

        lax.fori_loop(0, n, eliminate, 0)
        product[...] = matmul(inverse[...], whole[...] * up_down * up_across, HIGHEST)

    w = inverse[...]
    root_rows = jnp.sqrt(jnp.float32(total_rows))
    upper = product[...] * across / root_rows
    factor_ref[...] = jnp.where(row_ids <= col_ids, upper, 0.0)
    basis_ref[...] = matmul_nt(own_ref[...] * up_across, w, HIGHEST) * root_rows


def factor_and_basis(total_rows, gram, own):
    columns = own.shape[1]
    return pl.pallas_call(
        functools.partial(factor_kernel, total_rows),
        out_shape=(
            jax.ShapeDtypeStruct(own.shape, jnp.float32),
            jax.ShapeDtypeStruct((columns, columns), jnp.float32),
        ),
        in_specs=[VMEM, VMEM],
        out_specs=(VMEM, VMEM),
        scratch_shapes=[pltpu.VMEM((columns, columns), jnp.float32)] * 4,
        compiler_params=pltpu.CompilerParams(vmem_limit_bytes=24 * MIB),
        name="factor_and_basis",
    )(gram, own)


def spread(piece, axes, devices):
    copies = jnp.broadcast_to(piece[None], (devices, *piece.shape))
    return lax.all_to_all(copies, axes, split_axis=0, concat_axis=0, tiled=True)


def exchange(pieces, rows):
    order = distances(len(pieces))
    return [
        lax.ppermute(piece, "rows", [(r, r ^ d) for r in range(rows)]) if d else piece
        for piece, d in zip(pieces, order)
    ]


def fetch(sketch, block_cols, counts, slots, width):
    rows, cols = lax.axis_size("rows"), lax.axis_size("cols")
    members = rows // 2
    height = width // members
    columns = sketch.shape[1]
    sketch = sketch.reshape(-1, members, height, columns)
    per = sketch.shape[0]
    largest = min(per * members, slots * members, 128)
    within = tuple(level for level in WITHIN if level < per)
    across = tuple(level for level in ACROSS if level < largest and members <= 8)
    stripes = turn(sketch)
    table = table_copies(block_cols, counts, rows * cols)
    table = lax.all_to_all(table, ("rows", "cols"), split_axis=0, concat_axis=0, tiled=True)
    places, lists, near, far = plan(table, slots, per, within, across)

    def within_half(count):
        def run():
            return order(exchange(cut(lists, stripes, count), rows), per)

        return run

    own = lax.switch(near[0], [within_half(count) for count in (*within, per)])

    def across_halves(count):
        def run():
            swap = [(r, (r + members) % rows) for r in range(rows)]
            other = lax.ppermute(listed(lists, own, count), "rows", swap)
            return pick(places, own, other, slots, members)

        return run

    picked = lax.switch(far[0], [across_halves(count) for count in (*across, largest)])
    return exchange(picked, rows)


def local(sketch, blocks, block_rows, block_cols, counts):
    slots, width, _ = blocks.shape
    columns = sketch.shape[1]
    rows, cols = lax.axis_size("rows"), lax.axis_size("cols")
    chosen = fetch(sketch, block_cols, counts, slots, width)
    if chosen[0].shape[1] % 16:
        order = jnp.argsort(lax.axis_index("rows") % len(chosen) ^ jnp.array(distances(len(chosen))))
        chosen = [jnp.stack(chosen)[order].swapaxes(0, 1).reshape(1, slots, width, columns)[0]]
    partial_rows = block_products(block_rows, counts, blocks, chosen)
    if cols == 2:
        other = lax.ppermute(partial_rows, "cols", [(0, 1), (1, 0)])
        own, gram = sum_and_gram(partial_rows, other)
        pieces = gram.reshape(rows, -1, columns // 2)
        pieces = lax.all_to_all(pieces, "rows", split_axis=0, concat_axis=0, tiled=True)
        gram = spread(jnp.sum(pieces, axis=0), ("rows", "cols"), rows * cols)
        gram = gram.reshape(rows, cols, -1, columns // 2)
    else:
        own = lax.psum_scatter(partial_rows, "cols", scatter_dimension=0, tiled=True)
        gram = lax.psum(matmul(own.T, own, HIGHEST), ("rows", "cols"))
        gram = gram.reshape(1, 1, columns, columns)
    return factor_and_basis(RB * width * rows, gram, own)


def solution(mesh):
    in_specs = (
        P(("rows", "cols"), None),
        P(("rows", "cols"), None, None),
        P(("rows", "cols")),
        P(("rows", "cols")),
        P(("rows", "cols")),
    )
    out_specs = (P(("rows", "cols"), None), P())
    return jax.shard_map(local, mesh=mesh, in_specs=in_specs, out_specs=out_specs, check_vma=False)
```

```python
import functools

import jax
import jax.numpy as jnp
from jax import lax
from jax.experimental import pallas as pl
from jax.experimental.pallas import tpu as pltpu
from jax.sharding import PartitionSpec as P

RB = 4
HIGHEST = lax.Precision.HIGHEST
VMEM = pl.BlockSpec(memory_space=pltpu.VMEM)
SMEM = pl.BlockSpec(memory_space=pltpu.SMEM)
MIB = 1024 * 1024


ACROSS = (*range(11, 21), 22, 24, 28, 36)
WITHIN = (5, 6, 7, 8, 9, 10, 12)


def table_kernel(cols_ref, counts_ref, out_ref):
    slots = cols_ref.shape[0]
    lane = lax.broadcasted_iota(jnp.int32, out_ref.shape, 2)
    table = jnp.where(lane == slots, counts_ref[0], 0)
    for s in range(slots):
        table = jnp.where(lane == s, cols_ref[s], table)
    out_ref[...] = table


def table_copies(block_cols, counts, devices):
    return pl.pallas_call(
        table_kernel,
        out_shape=jax.ShapeDtypeStruct((devices, 1, 128), jnp.int32),
        in_specs=[SMEM, SMEM],
        out_specs=VMEM,
        name="table_copies",
    )(block_cols, counts)


def over(values, size):
    return values >> (size.bit_length() - 1)


def plan_kernel(slots, per, within, across, table_ref, places_ref, lists_ref, *level_refs):
    devices = table_ref.shape[0]
    rows, cols = lax.axis_size("rows"), lax.axis_size("cols")
    panel = per * rows
    part = panel // 2
    groups = [range(at, min(at + 64, devices)) for at in range(0, devices, 64)]

    def read(group):
        table = table_ref[group.start : group.stop, 0, :]
        lane = lax.broadcasted_iota(jnp.int32, table.shape, 1)
        counts = table[:, slots : slots + 1]
        table = jnp.where(lane < counts, table, -1)
        block = lax.broadcasted_iota(jnp.int32, (len(group), panel), 1)
        return table, counts, [table[:, s : s + 1] == block for s in range(slots)]

    lines = -(-cols // 8) * 8
    line = lax.broadcasted_iota(jnp.int32, (3 * lines, panel), 0)
    ids = lax.broadcasted_iota(jnp.int32, (1, panel), 1)
    asks = jnp.zeros((3 * lines, panel), jnp.float32)
    for group in groups:
        _, _, asked = read(group)
        some = jnp.where(functools.reduce(jnp.logical_or, asked), 1.0, 0.0).astype(jnp.bfloat16)
        shape = (3 * lines, len(group))
        number = lax.broadcasted_iota(jnp.int32, shape, 0)
        device = lax.broadcasted_iota(jnp.int32, shape, 1) + group.start
        core, side = device & (cols - 1), over(device, devices // 2)
        reads = (number == core) | (number == lines * (1 + side) + core)
        asks += jnp.dot(jnp.where(reads, 1.0, 0.0).astype(jnp.bfloat16), some, preferred_element_type=jnp.float32)
    own_half = (line >= lines) & (over(line - lines, lines) == over(lax.broadcasted_iota(jnp.int32, line.shape, 1), part))
    asks = jnp.where((asks > 0.5) & jnp.logical_not(own_half), 1.0, 0.0)
    first = lax.broadcasted_iota(jnp.int32, (panel, panel), 0)
    second = lax.broadcasted_iota(jnp.int32, (panel, panel), 1)
    after = first > second
    near = jnp.where(after & ((first ^ second) < per), 1.0, 0.0).astype(jnp.bfloat16)
    after = jnp.where(after, 1.0, 0.0).astype(jnp.bfloat16)
    same = jnp.where(first == second, 1.0, 0.0).astype(jnp.bfloat16)
    nt = (((1,), (1,)), ((), ()))

    def ranks(a, b):
        return lax.dot_general(a, b, nt, preferred_element_type=jnp.float32)

    short = asks.astype(jnp.bfloat16)
    near_rank = ranks(short, near)
    far_rank = ranks(short, after)
    longest = jnp.max(jnp.where(line < lines, near_rank + asks, 0.0)).astype(jnp.int32)
    level_refs[0][0] = sum((longest > level).astype(jnp.int32) for level in within)
    longest = jnp.max(jnp.where(line < lines, 0.0, far_rank + asks)).astype(jnp.int32)
    level_refs[1][0] = sum((longest > level).astype(jnp.int32) for level in across)
    me = lax.axis_index("rows")
    half, c = over(me, rows // 2), lax.axis_index("cols")

    def row(values, number):
        return jnp.sum(jnp.where(line == number, values, 0.0), axis=0, keepdims=True)

    here = (ids & -per) - half * part + row(near_rank, c).astype(jnp.int32)
    there = part + row(far_rank, lines * (1 + half) + c).astype(jnp.int32)
    place = jnp.where(over(ids, part) == half, here, there)
    chosen = jnp.zeros(places_ref.shape, jnp.float32)
    for group in groups:
        table, _, asked = read(group)
        lane = lax.broadcasted_iota(jnp.int32, table.shape, 1)
        places = jnp.zeros(table.shape, jnp.int32)
        for s in range(slots):
            found = jnp.sum(jnp.where(asked[s], place, 0), axis=1, keepdims=True)
            places = jnp.where(lane == s, found, places)
        shape = (places_ref.shape[0], len(group))
        number = lax.broadcasted_iota(jnp.int32, shape, 0)
        device = lax.broadcasted_iota(jnp.int32, shape, 1) + group.start
        reads = functools.reduce(
            jnp.logical_or,
            [(number == i) & (device == (me ^ d) * cols + c) for i, d in enumerate(distances(shape[0]))],
        )
        chosen += jnp.dot(
            jnp.where(reads, 1.0, 0.0).astype(jnp.bfloat16),
            places.astype(jnp.float32).astype(jnp.bfloat16),
            preferred_element_type=jnp.float32,
        )
    places_ref[...] = chosen.astype(jnp.int32)
    line = lax.broadcasted_iota(jnp.int32, (panel, 3 * lines), 1)

    def column(values, number):
        return jnp.sum(jnp.where(line == number, values, 0.0), axis=1, keepdims=True)

    turned, near_rank, far_rank = ranks(same, short), ranks(near, short), ranks(after, short)
    ids = lax.broadcasted_iota(jnp.int32, (panel, 1), 0)
    number = lax.broadcasted_iota(jnp.int32, (panel, lists_ref.shape[1]), 1)
    near_rank = column(near_rank, c).astype(jnp.int32)
    here = (ids & -per) - half * part + near_rank
    other = lines * (2 - half) + c
    sent = (column(turned, other) > 0.5) & (column(far_rank, other).astype(jnp.int32) == number)
    sent = jnp.sum(jnp.where(sent, here, 0), axis=0, keepdims=True)
    kept = (column(turned, c) > 0.5) & (over(ids, per) == me) & (near_rank == number)
    kept = jnp.sum(jnp.where(kept, ids & (per - 1), 0), axis=0, keepdims=True)
    lists_ref[...] = jnp.where(lax.broadcasted_iota(jnp.int32, lists_ref.shape, 0) == 0, sent, kept)


def plan(table, slots, per, within, across):
    devices = table.shape[0]
    return pl.pallas_call(
        functools.partial(plan_kernel, slots, per, within, across),
        out_shape=(
            jax.ShapeDtypeStruct((lax.axis_size("rows") // 2, 128), jnp.int32),
            jax.ShapeDtypeStruct((8, 128), jnp.int32),
            jax.ShapeDtypeStruct((1,), jnp.int32),
            jax.ShapeDtypeStruct((1,), jnp.int32),
        ),
        in_specs=[VMEM],
        out_specs=(VMEM, VMEM, SMEM, SMEM),
        compiler_params=pltpu.CompilerParams(vmem_limit_bytes=48 * MIB),
        name="plan",
    )(table)


def distances(members):
    return [0, *sorted(range(1, members), key=lambda d: (-d.bit_count(), -d))]


def turn_kernel(sketch_ref, out_ref):
    members = out_ref.shape[0]
    me = lax.axis_index("rows") % members
    for i, d in enumerate(distances(members)):
        out_ref[i] = sketch_ref[:, me ^ d]


def turn(sketch):
    blocks, members, height, columns = sketch.shape
    return pl.pallas_call(
        turn_kernel,
        out_shape=jax.ShapeDtypeStruct((members, blocks, height, columns), sketch.dtype),
        in_specs=[VMEM],
        out_specs=VMEM,
        compiler_params=pltpu.CompilerParams(vmem_limit_bytes=24 * MIB),
        cost_estimate=pl.CostEstimate(flops=0, bytes_accessed=4 * sketch.size, transcendentals=0),
        name="turn_stripes",
    )(sketch)


def cut_kernel(lists_ref, stripes_ref, *out_refs):
    for k in range(out_refs[0].shape[0]):
        for i, out_ref in enumerate(out_refs):
            out_ref[k] = stripes_ref[i, lists_ref[1, k]]


def cut(lists, stripes, count):
    members, _, height, columns = stripes.shape
    return pl.pallas_call(
        cut_kernel,
        out_shape=(jax.ShapeDtypeStruct((count, height, columns), stripes.dtype),) * members,
        in_specs=[SMEM, VMEM],
        out_specs=(VMEM,) * members,
        compiler_params=pltpu.CompilerParams(vmem_limit_bytes=24 * MIB),
        name="cut_stripes",
    )(lists, stripes)


def order_kernel(*refs):
    *stripe_refs, all_ref = refs
    members = len(stripe_refs)
    me = lax.axis_index("rows") % members
    per = all_ref.shape[0] // members
    for ref, d in zip(stripe_refs, distances(members)):
        all_ref[pl.ds((me ^ d) * per, ref.shape[0])] = ref[...]


def order(stripes, per):
    _, height, columns = stripes[0].shape
    return pl.pallas_call(
        order_kernel,
        out_shape=jax.ShapeDtypeStruct((len(stripes) * per, height, columns), stripes[0].dtype),
        in_specs=[VMEM] * len(stripes),
        out_specs=VMEM,
        compiler_params=pltpu.CompilerParams(vmem_limit_bytes=24 * MIB),
        name="order_stripes",
    )(*stripes)


def list_kernel(list_ref, all_ref, out_ref):
    for k in range(out_ref.shape[0]):
        out_ref[k] = all_ref[list_ref[0, k]]


def listed(numbers, stripes, count):
    return pl.pallas_call(
        list_kernel,
        out_shape=jax.ShapeDtypeStruct((count, *stripes.shape[1:]), stripes.dtype),
        in_specs=[SMEM, VMEM],
        out_specs=VMEM,
        compiler_params=pltpu.CompilerParams(vmem_limit_bytes=24 * MIB),
        name="listed_stripes",
    )(numbers, stripes)


def pick_kernel(places_ref, own_ref, other_ref, *refs):
    *out_refs, whole = refs
    here = own_ref.shape[0]
    whole[:here] = own_ref[...]
    whole[here:] = other_ref[...]
    for i, out_ref in enumerate(out_refs):
        for s in range(out_ref.shape[0]):
            out_ref[s] = whole[jnp.minimum(places_ref[i, s], whole.shape[0] - 1)]


def pick(places, own, other, slots, members):
    shape = own.shape[1:]
    return pl.pallas_call(
        pick_kernel,
        out_shape=(jax.ShapeDtypeStruct((slots, *shape), own.dtype),) * members,
        in_specs=[SMEM, VMEM, VMEM],
        out_specs=(VMEM,) * members,
        scratch_shapes=[pltpu.VMEM((own.shape[0] + other.shape[0], *shape), own.dtype)],
        compiler_params=pltpu.CompilerParams(vmem_limit_bytes=24 * MIB),
        name="pick_stripes",
    )(places, own, other)


def product_kernel(rows_ref, counts_ref, blocks_ref, *refs):
    *chosen_refs, out_ref, whole = refs
    slots, width, _ = blocks_ref.shape
    columns = out_ref.shape[1]
    members = len(chosen_refs)
    me = lax.axis_index("rows") % members
    for ref, d in zip(chosen_refs, distances(members) if members > 1 else [0]):
        whole[me ^ d] = ref[...]
    out_ref[...] = jnp.zeros_like(out_ref)
    for s in range(slots):

        @pl.when(s < counts_ref[0])
        def _():
            piece = whole[:, s].reshape(width, columns)
            product = jnp.dot(blocks_ref[s], piece, preferred_element_type=jnp.float32)
            at = pl.ds(pl.multiple_of(rows_ref[s] * width, width), width)
            out_ref[at, :] += product


def block_products(block_rows, counts, blocks, chosen):
    _, width, _ = blocks.shape
    columns = chosen[0].shape[-1]
    return pl.pallas_call(
        product_kernel,
        out_shape=jax.ShapeDtypeStruct((RB * width, columns), jnp.float32),
        in_specs=[SMEM, SMEM, VMEM] + [VMEM] * len(chosen),
        out_specs=VMEM,
        scratch_shapes=[pltpu.VMEM((len(chosen), *chosen[0].shape), chosen[0].dtype)],
        compiler_params=pltpu.CompilerParams(vmem_limit_bytes=24 * MIB),
        name="block_products",
    )(block_rows, counts, blocks, *chosen)


def gram_kernel(mine_ref, other_ref, own_ref, gram_ref, slab):
    c = lax.axis_index("cols")
    share, width = own_ref.shape[0], gram_ref.shape[1]
    slab[...] = mine_ref[...] + other_ref[...]
    own_ref[...] = slab[pl.ds(pl.multiple_of(c * share, share), share), :]
    right = slab[:, pl.ds(pl.multiple_of(c * width, width), width)]
    gram_ref[...] = lax.dot_general(
        slab[...], right, (((0,), (0,)), ((), ())), precision=HIGHEST, preferred_element_type=jnp.float32
    )


def sum_and_gram(mine, other):
    rows, columns = mine.shape
    return pl.pallas_call(
        gram_kernel,
        out_shape=(
            jax.ShapeDtypeStruct((rows // 2, columns), jnp.float32),
            jax.ShapeDtypeStruct((columns, columns // 2), jnp.float32),
        ),
        in_specs=[VMEM, VMEM],
        out_specs=(VMEM, VMEM),
        scratch_shapes=[pltpu.VMEM((rows, columns), jnp.float32)],
        compiler_params=pltpu.CompilerParams(vmem_limit_bytes=24 * MIB),
        name="sum_and_gram",
    )(mine, other)


def matmul(a, b, precision):
    return jnp.dot(a, b, precision=precision, preferred_element_type=jnp.float32)


def matmul_nt(a, b, precision):
    return lax.dot_general(
        a, b, (((1,), (1,)), ((), ())), precision=precision, preferred_element_type=jnp.float32
    )


def split_matmul(times, passes, a, b):
    a_high, b_high = a.astype(jnp.bfloat16), b.astype(jnp.bfloat16)
    result = times(a_high, b_high, None)
    if passes == 3:
        a_low = (a - a_high.astype(jnp.float32)).astype(jnp.bfloat16)
        b_low = (b - b_high.astype(jnp.float32)).astype(jnp.bfloat16)
        result += times(a_high, b_low, None) + times(a_low, b_high, None)
    return result


def factor_kernel(total_rows, gram_ref, own_ref, basis_ref, factor_ref, whole, scaled, inverse, product):
    n = factor_ref.shape[0]
    width = gram_ref.shape[-1]
    for c in range(n // width):
        whole[:, c * width : (c + 1) * width] = gram_ref[:, c].reshape(n, width)
    row_ids = lax.broadcasted_iota(jnp.int32, (n, n), 0)
    col_ids = lax.broadcasted_iota(jnp.int32, (n, n), 1)
    diagonal = row_ids == col_ids
    identity = diagonal.astype(jnp.float32)
    half = jnp.where(row_ids > col_ids, 1.0, jnp.where(diagonal, 0.5, 0.0))
    gram = whole[...]
    on_diagonal = jnp.where(diagonal, gram, 0.0)
    down = jnp.sqrt(jnp.sum(on_diagonal, axis=1, keepdims=True))
    across = jnp.sqrt(jnp.sum(on_diagonal, axis=0, keepdims=True))
    up_down = 1.0 / down
    up_across = 1.0 / across
    scaled[...] = gram * up_down * up_across

    def refine(times, times_nt):
        w = inverse[...]
        upper = times(w, scaled[...])
        residual = times_nt(upper, w) - identity
        step = residual * half
        inverse[...] = w - matmul(step, w, lax.Precision.DEFAULT)
        product[...] = upper - matmul(step, upper, lax.Precision.DEFAULT)
        return jnp.sum(residual * residual)

    def exactly(times):
        return functools.partial(times, precision=HIGHEST)

    inverse[...] = identity - (scaled[...] - identity) * half
    for passes in (1, 3):
        refine(functools.partial(split_matmul, matmul, passes), functools.partial(split_matmul, matmul_nt, passes))

    def going(state):
        step, size = state
        return (step < 8) & (size > 1e-6)

    def advance(state):
        return state[0] + 1, refine(exactly(matmul), exactly(matmul_nt))

    _, size = lax.while_loop(going, advance, (jnp.int32(0), jnp.float32(1.0)))

    @pl.when(jnp.logical_not(size <= 1e-6))
    def _():
        inverse[...] = identity
        ids = lax.broadcasted_iota(jnp.int32, (n, 1), 0)

        def eliminate(j, carry):
            pivot_row = scaled[pl.ds(j, 1), :]
            inverse_row = inverse[pl.ds(j, 1), :]
            column = jnp.sum(jnp.where(col_ids == j, scaled[...], 0.0), axis=1, keepdims=True)
            pivot = jnp.sum(jnp.where(ids == j, column, 0.0), axis=0, keepdims=True)
            root = 1.0 / jnp.sqrt(pivot)
            ratio = jnp.where(ids > j, column / pivot, jnp.where(ids == j, 1.0 - root, 0.0))
            scaled[...] = scaled[...] - ratio * pivot_row
            inverse[...] = inverse[...] - ratio * inverse_row
            return carry

        lax.fori_loop(0, n, eliminate, 0)
        product[...] = matmul(inverse[...], whole[...] * up_down * up_across, HIGHEST)

    w = inverse[...]
    root_rows = jnp.sqrt(jnp.float32(total_rows))
    upper = product[...] * across / root_rows
    factor_ref[...] = jnp.where(row_ids <= col_ids, upper, 0.0)
    basis_ref[...] = matmul_nt(own_ref[...] * up_across, w, HIGHEST) * root_rows


def factor_and_basis(total_rows, gram, own):
    columns = own.shape[1]
    return pl.pallas_call(
        functools.partial(factor_kernel, total_rows),
        out_shape=(
            jax.ShapeDtypeStruct(own.shape, jnp.float32),
            jax.ShapeDtypeStruct((columns, columns), jnp.float32),
        ),
        in_specs=[VMEM, VMEM],
        out_specs=(VMEM, VMEM),
        scratch_shapes=[pltpu.VMEM((columns, columns), jnp.float32)] * 4,
        compiler_params=pltpu.CompilerParams(vmem_limit_bytes=24 * MIB),
        name="factor_and_basis",
    )(gram, own)


def spread(piece, axes, devices):
    copies = jnp.broadcast_to(piece[None], (devices, *piece.shape))
    return lax.all_to_all(copies, axes, split_axis=0, concat_axis=0, tiled=True)


def exchange(pieces, rows):
    order = distances(len(pieces))
    return [
        lax.ppermute(piece, "rows", [(r, r ^ d) for r in range(rows)]) if d else piece
        for piece, d in zip(pieces, order)
    ]


def fetch(sketch, block_cols, counts, slots, width):
    rows, cols = lax.axis_size("rows"), lax.axis_size("cols")
    members = rows // 2
    height = width // members
    columns = sketch.shape[1]
    sketch = sketch.reshape(-1, members, height, columns)
    per = sketch.shape[0]
    largest = min(per * members, slots * members, 128)
    within = tuple(level for level in WITHIN if level < per)
    across = tuple(level for level in ACROSS if level < largest and members <= 8)
    stripes = turn(sketch)
    table = table_copies(block_cols, counts, rows * cols)
    table = lax.all_to_all(table, ("rows", "cols"), split_axis=0, concat_axis=0, tiled=True)
    places, lists, near, far = plan(table, slots, per, within, across)

    def within_half(count):
        def run():
            return order(exchange(cut(lists, stripes, count), rows), per)

        return run

    own = lax.switch(near[0], [within_half(count) for count in (*within, per)])

    def across_halves(count):
        def run():
            swap = [(r, (r + members) % rows) for r in range(rows)]
            other = lax.ppermute(listed(lists, own, count), "rows", swap)
            return pick(places, own, other, slots, members)

        return run

    picked = lax.switch(far[0], [across_halves(count) for count in (*across, largest)])
    return exchange(picked, rows)


def local(sketch, blocks, block_rows, block_cols, counts):
    slots, width, _ = blocks.shape
    columns = sketch.shape[1]
    rows, cols = lax.axis_size("rows"), lax.axis_size("cols")
    chosen = fetch(sketch, block_cols, counts, slots, width)
    if chosen[0].shape[1] % 16:
        order = jnp.argsort(lax.axis_index("rows") % len(chosen) ^ jnp.array(distances(len(chosen))))
        chosen = [jnp.stack(chosen)[order].swapaxes(0, 1).reshape(1, slots, width, columns)[0]]
    partial_rows = block_products(block_rows, counts, blocks, chosen)
    if cols == 2:
        other = lax.ppermute(partial_rows, "cols", [(0, 1), (1, 0)])
        own, gram = sum_and_gram(partial_rows, other)
        pieces = gram.reshape(rows, -1, columns // 2)
        pieces = lax.all_to_all(pieces, "rows", split_axis=0, concat_axis=0, tiled=True)
        gram = spread(jnp.sum(pieces, axis=0), ("rows", "cols"), rows * cols)
        gram = gram.reshape(rows, cols, -1, columns // 2)
    else:
        own = lax.psum_scatter(partial_rows, "cols", scatter_dimension=0, tiled=True)
        gram = lax.psum(matmul(own.T, own, HIGHEST), ("rows", "cols"))
        gram = gram.reshape(1, 1, columns, columns)
    return factor_and_basis(RB * width * rows, gram, own)


def solution(mesh):
    in_specs = (
        P(("rows", "cols"), None),
        P(("rows", "cols"), None, None),
        P(("rows", "cols")),
        P(("rows", "cols")),
        P(("rows", "cols")),
    )
    out_specs = (P(("rows", "cols"), None), P())
    return jax.shard_map(local, mesh=mesh, in_specs=in_specs, out_specs=out_specs, check_vma=False)
```

```python
import functools

import jax
import jax.numpy as jnp
from jax import lax
from jax.experimental import pallas as pl
from jax.experimental.pallas import tpu as pltpu
from jax.sharding import PartitionSpec as P

RB = 4
HIGHEST = lax.Precision.HIGHEST
VMEM = pl.BlockSpec(memory_space=pltpu.VMEM)
SMEM = pl.BlockSpec(memory_space=pltpu.SMEM)
MIB = 1024 * 1024


ACROSS = (*range(11, 21), 22, 24, 28, 36)
WITHIN = (5, 6, 7, 8, 9, 10, 12)


def table_kernel(cols_ref, counts_ref, out_ref):
    slots = cols_ref.shape[0]
    lane = lax.broadcasted_iota(jnp.int32, out_ref.shape, 2)
    table = jnp.where(lane == slots, counts_ref[0], 0)
    for s in range(slots):
        table = jnp.where(lane == s, cols_ref[s], table)
    out_ref[...] = table


def table_copies(block_cols, counts, devices):
    return pl.pallas_call(
        table_kernel,
        out_shape=jax.ShapeDtypeStruct((devices, 1, 128), jnp.int32),
        in_specs=[SMEM, SMEM],
        out_specs=VMEM,
        name="table_copies",
    )(block_cols, counts)


def over(values, size):
    return values >> (size.bit_length() - 1)


def plan_kernel(slots, per, within, across, table_ref, places_ref, lists_ref, *level_refs):
    devices = table_ref.shape[0]
    rows, cols = lax.axis_size("rows"), lax.axis_size("cols")
    panel = per * rows
    part = panel // 2
    groups = [range(at, min(at + 64, devices)) for at in range(0, devices, 64)]

    def read(group):
        table = table_ref[group.start : group.stop, 0, :]
        lane = lax.broadcasted_iota(jnp.int32, table.shape, 1)
        counts = table[:, slots : slots + 1]
        table = jnp.where(lane < counts, table, -1)
        block = lax.broadcasted_iota(jnp.int32, (len(group), panel), 1)
        return table, counts, [table[:, s : s + 1] == block for s in range(slots)]

    lines = -(-cols // 8) * 8
    line = lax.broadcasted_iota(jnp.int32, (3 * lines, panel), 0)
    ids = lax.broadcasted_iota(jnp.int32, (1, panel), 1)
    asks = jnp.zeros((3 * lines, panel), jnp.float32)
    for group in groups:
        _, _, asked = read(group)
        some = jnp.where(functools.reduce(jnp.logical_or, asked), 1.0, 0.0).astype(jnp.bfloat16)
        shape = (3 * lines, len(group))
        number = lax.broadcasted_iota(jnp.int32, shape, 0)
        device = lax.broadcasted_iota(jnp.int32, shape, 1) + group.start
        core, side = device & (cols - 1), over(device, devices // 2)
        reads = (number == core) | (number == lines * (1 + side) + core)
        asks += jnp.dot(jnp.where(reads, 1.0, 0.0).astype(jnp.bfloat16), some, preferred_element_type=jnp.float32)
    own_half = (line >= lines) & (over(line - lines, lines) == over(lax.broadcasted_iota(jnp.int32, line.shape, 1), part))
    asks = jnp.where((asks > 0.5) & jnp.logical_not(own_half), 1.0, 0.0)
    first = lax.broadcasted_iota(jnp.int32, (panel, panel), 0)
    second = lax.broadcasted_iota(jnp.int32, (panel, panel), 1)
    after = first > second
    near = jnp.where(after & ((first ^ second) < per), 1.0, 0.0).astype(jnp.bfloat16)
    after = jnp.where(after, 1.0, 0.0).astype(jnp.bfloat16)
    same = jnp.where(first == second, 1.0, 0.0).astype(jnp.bfloat16)
    nt = (((1,), (1,)), ((), ()))

    def ranks(a, b):
        return lax.dot_general(a, b, nt, preferred_element_type=jnp.float32)

    short = asks.astype(jnp.bfloat16)
    near_rank = ranks(short, near)
    far_rank = ranks(short, after)
    longest = jnp.max(jnp.where(line < lines, near_rank + asks, 0.0)).astype(jnp.int32)
    level_refs[0][0] = sum((longest > level).astype(jnp.int32) for level in within)
    longest = jnp.max(jnp.where(line < lines, 0.0, far_rank + asks)).astype(jnp.int32)
    level_refs[1][0] = sum((longest > level).astype(jnp.int32) for level in across)
    me = lax.axis_index("rows")
    half, c = over(me, rows // 2), lax.axis_index("cols")

    def row(values, number):
        return jnp.sum(jnp.where(line == number, values, 0.0), axis=0, keepdims=True)

    here = (ids & -per) - half * part + row(near_rank, c).astype(jnp.int32)
    there = part + row(far_rank, lines * (1 + half) + c).astype(jnp.int32)
    place = jnp.where(over(ids, part) == half, here, there)
    chosen = jnp.zeros(places_ref.shape, jnp.float32)
    for group in groups:
        table, _, asked = read(group)
        lane = lax.broadcasted_iota(jnp.int32, table.shape, 1)
        places = jnp.zeros(table.shape, jnp.int32)
        for s in range(slots):
            found = jnp.sum(jnp.where(asked[s], place, 0), axis=1, keepdims=True)
            places = jnp.where(lane == s, found, places)
        shape = (places_ref.shape[0], len(group))
        number = lax.broadcasted_iota(jnp.int32, shape, 0)
        device = lax.broadcasted_iota(jnp.int32, shape, 1) + group.start
        reads = functools.reduce(
            jnp.logical_or,
            [(number == i) & (device == (me ^ d) * cols + c) for i, d in enumerate(distances(shape[0]))],
        )
        chosen += jnp.dot(
            jnp.where(reads, 1.0, 0.0).astype(jnp.bfloat16),
            places.astype(jnp.float32).astype(jnp.bfloat16),
            preferred_element_type=jnp.float32,
        )
    places_ref[...] = chosen.astype(jnp.int32)
    line = lax.broadcasted_iota(jnp.int32, (panel, 3 * lines), 1)

    def column(values, number):
        return jnp.sum(jnp.where(line == number, values, 0.0), axis=1, keepdims=True)

    turned, near_rank, far_rank = ranks(same, short), ranks(near, short), ranks(after, short)
    ids = lax.broadcasted_iota(jnp.int32, (panel, 1), 0)
    number = lax.broadcasted_iota(jnp.int32, (panel, lists_ref.shape[1]), 1)
    near_rank = column(near_rank, c).astype(jnp.int32)
    here = (ids & -per) - half * part + near_rank
    other = lines * (2 - half) + c
    sent = (column(turned, other) > 0.5) & (column(far_rank, other).astype(jnp.int32) == number)
    sent = jnp.sum(jnp.where(sent, here, 0), axis=0, keepdims=True)
    kept = (column(turned, c) > 0.5) & (over(ids, per) == me) & (near_rank == number)
    kept = jnp.sum(jnp.where(kept, ids & (per - 1), 0), axis=0, keepdims=True)
    lists_ref[...] = jnp.where(lax.broadcasted_iota(jnp.int32, lists_ref.shape, 0) == 0, sent, kept)


def plan(table, slots, per, within, across):
    devices = table.shape[0]
    return pl.pallas_call(
        functools.partial(plan_kernel, slots, per, within, across),
        out_shape=(
            jax.ShapeDtypeStruct((lax.axis_size("rows") // 2, 128), jnp.int32),
            jax.ShapeDtypeStruct((8, 128), jnp.int32),
            jax.ShapeDtypeStruct((1,), jnp.int32),
            jax.ShapeDtypeStruct((1,), jnp.int32),
        ),
        in_specs=[VMEM],
        out_specs=(VMEM, VMEM, SMEM, SMEM),
        compiler_params=pltpu.CompilerParams(vmem_limit_bytes=48 * MIB),
        name="plan",
    )(table)


def distances(members):
    return [0, *sorted(range(1, members), key=lambda d: (-d.bit_count(), -d))]


def turn_kernel(sketch_ref, out_ref):
    members = out_ref.shape[0]
    me = lax.axis_index("rows") % members
    for i, d in enumerate(distances(members)):
        out_ref[i] = sketch_ref[:, me ^ d]


def turn(sketch):
    blocks, members, height, columns = sketch.shape
    return pl.pallas_call(
        turn_kernel,
        out_shape=jax.ShapeDtypeStruct((members, blocks, height, columns), sketch.dtype),
        in_specs=[VMEM],
        out_specs=VMEM,
        compiler_params=pltpu.CompilerParams(vmem_limit_bytes=24 * MIB),
        cost_estimate=pl.CostEstimate(flops=0, bytes_accessed=4 * sketch.size, transcendentals=0),
        name="turn_stripes",
    )(sketch)


def cut_kernel(lists_ref, stripes_ref, *out_refs):
    for k in range(out_refs[0].shape[0]):
        for i, out_ref in enumerate(out_refs):
            out_ref[k] = stripes_ref[i, lists_ref[1, k]]


def cut(lists, stripes, count):
    members, _, height, columns = stripes.shape
    return pl.pallas_call(
        cut_kernel,
        out_shape=(jax.ShapeDtypeStruct((count, height, columns), stripes.dtype),) * members,
        in_specs=[SMEM, VMEM],
        out_specs=(VMEM,) * members,
        compiler_params=pltpu.CompilerParams(vmem_limit_bytes=24 * MIB),
        name="cut_stripes",
    )(lists, stripes)


def order_kernel(*refs):
    *stripe_refs, all_ref = refs
    members = len(stripe_refs)
    me = lax.axis_index("rows") % members
    per = all_ref.shape[0] // members
    for ref, d in zip(stripe_refs, distances(members)):
        all_ref[pl.ds((me ^ d) * per, ref.shape[0])] = ref[...]


def order(stripes, per):
    _, height, columns = stripes[0].shape
    return pl.pallas_call(
        order_kernel,
        out_shape=jax.ShapeDtypeStruct((len(stripes) * per, height, columns), stripes[0].dtype),
        in_specs=[VMEM] * len(stripes),
        out_specs=VMEM,
        compiler_params=pltpu.CompilerParams(vmem_limit_bytes=24 * MIB),
        name="order_stripes",
    )(*stripes)


def list_kernel(list_ref, all_ref, out_ref):
    for k in range(out_ref.shape[0]):
        out_ref[k] = all_ref[list_ref[0, k]]


def listed(numbers, stripes, count):
    return pl.pallas_call(
        list_kernel,
        out_shape=jax.ShapeDtypeStruct((count, *stripes.shape[1:]), stripes.dtype),
        in_specs=[SMEM, VMEM],
        out_specs=VMEM,
        compiler_params=pltpu.CompilerParams(vmem_limit_bytes=24 * MIB),
        name="listed_stripes",
    )(numbers, stripes)


def pick_kernel(places_ref, own_ref, other_ref, *refs):
    *out_refs, whole = refs
    here = own_ref.shape[0]
    whole[:here] = own_ref[...]
    whole[here:] = other_ref[...]
    for i, out_ref in enumerate(out_refs):
        for s in range(out_ref.shape[0]):
            out_ref[s] = whole[jnp.minimum(places_ref[i, s], whole.shape[0] - 1)]


def pick(places, own, other, slots, members):
    shape = own.shape[1:]
    return pl.pallas_call(
        pick_kernel,
        out_shape=(jax.ShapeDtypeStruct((slots, *shape), own.dtype),) * members,
        in_specs=[SMEM, VMEM, VMEM],
        out_specs=(VMEM,) * members,
        scratch_shapes=[pltpu.VMEM((own.shape[0] + other.shape[0], *shape), own.dtype)],
        compiler_params=pltpu.CompilerParams(vmem_limit_bytes=24 * MIB),
        name="pick_stripes",
    )(places, own, other)


def product_kernel(rows_ref, counts_ref, blocks_ref, *refs):
    *chosen_refs, out_ref, whole = refs
    slots, width, _ = blocks_ref.shape
    columns = out_ref.shape[1]
    members = len(chosen_refs)
    me = lax.axis_index("rows") % members
    for ref, d in zip(chosen_refs, distances(members) if members > 1 else [0]):
        whole[me ^ d] = ref[...]
    out_ref[...] = jnp.zeros_like(out_ref)
    for s in range(slots):
        piece = whole[:, s].reshape(width, columns)
        product = jnp.dot(blocks_ref[s], piece, preferred_element_type=jnp.float32)
        at = pl.ds(pl.multiple_of(rows_ref[s] * width, width), width)
        out_ref[at, :] += jnp.where(s < counts_ref[0], product, 0.0)


def block_products(block_rows, counts, blocks, chosen):
    _, width, _ = blocks.shape
    columns = chosen[0].shape[-1]
    return pl.pallas_call(
        product_kernel,
        out_shape=jax.ShapeDtypeStruct((RB * width, columns), jnp.float32),
        in_specs=[SMEM, SMEM, VMEM] + [VMEM] * len(chosen),
        out_specs=VMEM,
        scratch_shapes=[pltpu.VMEM((len(chosen), *chosen[0].shape), chosen[0].dtype)],
        compiler_params=pltpu.CompilerParams(vmem_limit_bytes=24 * MIB),
        name="block_products",
    )(block_rows, counts, blocks, *chosen)


def gram_kernel(mine_ref, other_ref, own_ref, gram_ref, slab):
    c = lax.axis_index("cols")
    share, width = own_ref.shape[0], gram_ref.shape[1]
    slab[...] = mine_ref[...] + other_ref[...]
    own_ref[...] = slab[pl.ds(pl.multiple_of(c * share, share), share), :]
    right = slab[:, pl.ds(pl.multiple_of(c * width, width), width)]
    gram_ref[...] = lax.dot_general(
        slab[...], right, (((0,), (0,)), ((), ())), precision=HIGHEST, preferred_element_type=jnp.float32
    )


def sum_and_gram(mine, other):
    rows, columns = mine.shape
    return pl.pallas_call(
        gram_kernel,
        out_shape=(
            jax.ShapeDtypeStruct((rows // 2, columns), jnp.float32),
            jax.ShapeDtypeStruct((columns, columns // 2), jnp.float32),
        ),
        in_specs=[VMEM, VMEM],
        out_specs=(VMEM, VMEM),
        scratch_shapes=[pltpu.VMEM((rows, columns), jnp.float32)],
        compiler_params=pltpu.CompilerParams(vmem_limit_bytes=24 * MIB),
        name="sum_and_gram",
    )(mine, other)


def matmul(a, b, precision):
    return jnp.dot(a, b, precision=precision, preferred_element_type=jnp.float32)


def matmul_nt(a, b, precision):
    return lax.dot_general(
        a, b, (((1,), (1,)), ((), ())), precision=precision, preferred_element_type=jnp.float32
    )


def split_matmul(times, passes, a, b):
    a_high, b_high = a.astype(jnp.bfloat16), b.astype(jnp.bfloat16)
    result = times(a_high, b_high, None)
    if passes == 3:
        a_low = (a - a_high.astype(jnp.float32)).astype(jnp.bfloat16)
        b_low = (b - b_high.astype(jnp.float32)).astype(jnp.bfloat16)
        result += times(a_high, b_low, None) + times(a_low, b_high, None)
    return result


def factor_kernel(total_rows, gram_ref, own_ref, basis_ref, factor_ref, whole, scaled, inverse, product):
    n = factor_ref.shape[0]
    width = gram_ref.shape[-1]
    for c in range(n // width):
        whole[:, c * width : (c + 1) * width] = gram_ref[:, c].reshape(n, width)
    row_ids = lax.broadcasted_iota(jnp.int32, (n, n), 0)
    col_ids = lax.broadcasted_iota(jnp.int32, (n, n), 1)
    diagonal = row_ids == col_ids
    identity = diagonal.astype(jnp.float32)
    half = jnp.where(row_ids > col_ids, 1.0, jnp.where(diagonal, 0.5, 0.0))
    gram = whole[...]
    on_diagonal = jnp.where(diagonal, gram, 0.0)
    down = jnp.sqrt(jnp.sum(on_diagonal, axis=1, keepdims=True))
    across = jnp.sqrt(jnp.sum(on_diagonal, axis=0, keepdims=True))
    up_down = 1.0 / down
    up_across = 1.0 / across
    scaled[...] = gram * up_down * up_across

    def refine(times, times_nt):
        w = inverse[...]
        upper = times(w, scaled[...])
        residual = times_nt(upper, w) - identity
        step = residual * half
        inverse[...] = w - matmul(step, w, lax.Precision.DEFAULT)
        product[...] = upper - matmul(step, upper, lax.Precision.DEFAULT)
        return jnp.sum(residual * residual)

    def exactly(times):
        return functools.partial(times, precision=HIGHEST)

    inverse[...] = identity - (scaled[...] - identity) * half
    for passes in (1, 3):
        refine(functools.partial(split_matmul, matmul, passes), functools.partial(split_matmul, matmul_nt, passes))

    def going(state):
        step, size = state
        return (step < 8) & (size > 1e-6)

    def advance(state):
        return state[0] + 1, refine(exactly(matmul), exactly(matmul_nt))

    _, size = lax.while_loop(going, advance, (jnp.int32(0), jnp.float32(1.0)))

    @pl.when(jnp.logical_not(size <= 1e-6))
    def _():
        inverse[...] = identity
        ids = lax.broadcasted_iota(jnp.int32, (n, 1), 0)

        def eliminate(j, carry):
            pivot_row = scaled[pl.ds(j, 1), :]
            inverse_row = inverse[pl.ds(j, 1), :]
            column = jnp.sum(jnp.where(col_ids == j, scaled[...], 0.0), axis=1, keepdims=True)
            pivot = jnp.sum(jnp.where(ids == j, column, 0.0), axis=0, keepdims=True)
            root = 1.0 / jnp.sqrt(pivot)
            ratio = jnp.where(ids > j, column / pivot, jnp.where(ids == j, 1.0 - root, 0.0))
            scaled[...] = scaled[...] - ratio * pivot_row
            inverse[...] = inverse[...] - ratio * inverse_row
            return carry

        lax.fori_loop(0, n, eliminate, 0)
        product[...] = matmul(inverse[...], whole[...] * up_down * up_across, HIGHEST)

    w = inverse[...]
    root_rows = jnp.sqrt(jnp.float32(total_rows))
    upper = product[...] * across / root_rows
    factor_ref[...] = jnp.where(row_ids <= col_ids, upper, 0.0)
    basis_ref[...] = matmul_nt(own_ref[...] * up_across, w, HIGHEST) * root_rows


def factor_and_basis(total_rows, gram, own):
    columns = own.shape[1]
    return pl.pallas_call(
        functools.partial(factor_kernel, total_rows),
        out_shape=(
            jax.ShapeDtypeStruct(own.shape, jnp.float32),
            jax.ShapeDtypeStruct((columns, columns), jnp.float32),
        ),
        in_specs=[VMEM, VMEM],
        out_specs=(VMEM, VMEM),
        scratch_shapes=[pltpu.VMEM((columns, columns), jnp.float32)] * 4,
        compiler_params=pltpu.CompilerParams(vmem_limit_bytes=24 * MIB),
        name="factor_and_basis",
    )(gram, own)


def spread(piece, axes, devices):
    copies = jnp.broadcast_to(piece[None], (devices, *piece.shape))
    return lax.all_to_all(copies, axes, split_axis=0, concat_axis=0, tiled=True)


def exchange(pieces, rows):
    order = distances(len(pieces))
    return [
        lax.ppermute(piece, "rows", [(r, r ^ d) for r in range(rows)]) if d else piece
        for piece, d in zip(pieces, order)
    ]


def fetch(sketch, block_cols, counts, slots, width):
    rows, cols = lax.axis_size("rows"), lax.axis_size("cols")
    members = rows // 2
    height = width // members
    columns = sketch.shape[1]
    sketch = sketch.reshape(-1, members, height, columns)
    per = sketch.shape[0]
    largest = min(per * members, slots * members, 128)
    within = tuple(level for level in WITHIN if level < per)
    across = tuple(level for level in ACROSS if level < largest and members <= 8)
    stripes = turn(sketch)
    table = table_copies(block_cols, counts, rows * cols)
    table = lax.all_to_all(table, ("rows", "cols"), split_axis=0, concat_axis=0, tiled=True)
    places, lists, near, far = plan(table, slots, per, within, across)

    def within_half(count):
        def run():
            return order(exchange(cut(lists, stripes, count), rows), per)

        return run

    own = lax.switch(near[0], [within_half(count) for count in (*within, per)])

    def across_halves(count):
        def run():
            swap = [(r, (r + members) % rows) for r in range(rows)]
            other = lax.ppermute(listed(lists, own, count), "rows", swap)
            return pick(places, own, other, slots, members)

        return run

    picked = lax.switch(far[0], [across_halves(count) for count in (*across, largest)])
    return exchange(picked, rows)


def local(sketch, blocks, block_rows, block_cols, counts):
    slots, width, _ = blocks.shape
    columns = sketch.shape[1]
    rows, cols = lax.axis_size("rows"), lax.axis_size("cols")
    chosen = fetch(sketch, block_cols, counts, slots, width)
    if chosen[0].shape[1] % 16:
        order = jnp.argsort(lax.axis_index("rows") % len(chosen) ^ jnp.array(distances(len(chosen))))
        chosen = [jnp.stack(chosen)[order].swapaxes(0, 1).reshape(1, slots, width, columns)[0]]
    partial_rows = block_products(block_rows, counts, blocks, chosen)
    if cols == 2:
        other = lax.ppermute(partial_rows, "cols", [(0, 1), (1, 0)])
        own, gram = sum_and_gram(partial_rows, other)
        pieces = gram.reshape(rows, -1, columns // 2)
        pieces = lax.all_to_all(pieces, "rows", split_axis=0, concat_axis=0, tiled=True)
        gram = spread(jnp.sum(pieces, axis=0), ("rows", "cols"), rows * cols)
        gram = gram.reshape(rows, cols, -1, columns // 2)
    else:
        own = lax.psum_scatter(partial_rows, "cols", scatter_dimension=0, tiled=True)
        gram = lax.psum(matmul(own.T, own, HIGHEST), ("rows", "cols"))
        gram = gram.reshape(1, 1, columns, columns)
    return factor_and_basis(RB * width * rows, gram, own)


def solution(mesh):
    in_specs = (
        P(("rows", "cols"), None),
        P(("rows", "cols"), None, None),
        P(("rows", "cols")),
        P(("rows", "cols")),
        P(("rows", "cols")),
    )
    out_specs = (P(("rows", "cols"), None), P())
    return jax.shard_map(local, mesh=mesh, in_specs=in_specs, out_specs=out_specs, check_vma=False)
```

```python
import functools

import jax
import jax.numpy as jnp
from jax import lax
from jax.experimental import pallas as pl
from jax.experimental.pallas import tpu as pltpu
from jax.sharding import PartitionSpec as P

RB = 4
HIGHEST = lax.Precision.HIGHEST
VMEM = pl.BlockSpec(memory_space=pltpu.VMEM)
SMEM = pl.BlockSpec(memory_space=pltpu.SMEM)
MIB = 1024 * 1024


ACROSS = (*range(11, 21), 22, 24, 28, 36)
WITHIN = (5, 6, 7, 8, 9, 10, 12)


def table_kernel(cols_ref, counts_ref, out_ref):
    slots = cols_ref.shape[0]
    lane = lax.broadcasted_iota(jnp.int32, out_ref.shape, 2)
    table = jnp.where(lane == slots, counts_ref[0], 0)
    for s in range(slots):
        table = jnp.where(lane == s, cols_ref[s], table)
    out_ref[...] = table


def table_copies(block_cols, counts, devices):
    return pl.pallas_call(
        table_kernel,
        out_shape=jax.ShapeDtypeStruct((devices, 1, 128), jnp.int32),
        in_specs=[SMEM, SMEM],
        out_specs=VMEM,
        compiler_params=pltpu.CompilerParams(vmem_limit_bytes=24 * MIB),
        name="table_copies",
    )(block_cols, counts)


def over(values, size):
    return values >> (size.bit_length() - 1)


def plan_kernel(slots, per, within, across, table_ref, places_ref, lists_ref, *level_refs):
    devices = table_ref.shape[0]
    rows, cols = lax.axis_size("rows"), lax.axis_size("cols")
    panel = per * rows
    part = panel // 2
    groups = [range(at, min(at + 64, devices)) for at in range(0, devices, 64)]

    def read(group):
        table = table_ref[group.start : group.stop, 0, :]
        lane = lax.broadcasted_iota(jnp.int32, table.shape, 1)
        counts = table[:, slots : slots + 1]
        table = jnp.where(lane < counts, table, -1)
        block = lax.broadcasted_iota(jnp.int32, (len(group), panel), 1)
        return table, counts, [table[:, s : s + 1] == block for s in range(slots)]

    lines = -(-cols // 8) * 8
    line = lax.broadcasted_iota(jnp.int32, (3 * lines, panel), 0)
    ids = lax.broadcasted_iota(jnp.int32, (1, panel), 1)
    asks = jnp.zeros((3 * lines, panel), jnp.float32)
    for group in groups:
        _, _, asked = read(group)
        some = jnp.where(functools.reduce(jnp.logical_or, asked), 1.0, 0.0).astype(jnp.bfloat16)
        shape = (3 * lines, len(group))
        number = lax.broadcasted_iota(jnp.int32, shape, 0)
        device = lax.broadcasted_iota(jnp.int32, shape, 1) + group.start
        core, side = device & (cols - 1), over(device, devices // 2)
        reads = (number == core) | (number == lines * (1 + side) + core)
        asks += jnp.dot(jnp.where(reads, 1.0, 0.0).astype(jnp.bfloat16), some, preferred_element_type=jnp.float32)
    own_half = (line >= lines) & (over(line - lines, lines) == over(lax.broadcasted_iota(jnp.int32, line.shape, 1), part))
    asks = jnp.where((asks > 0.5) & jnp.logical_not(own_half), 1.0, 0.0)
    first = lax.broadcasted_iota(jnp.int32, (panel, panel), 0)
    second = lax.broadcasted_iota(jnp.int32, (panel, panel), 1)
    after = first > second
    near = jnp.where(after & ((first ^ second) < per), 1.0, 0.0).astype(jnp.bfloat16)
    after = jnp.where(after, 1.0, 0.0).astype(jnp.bfloat16)
    same = jnp.where(first == second, 1.0, 0.0).astype(jnp.bfloat16)
    nt = (((1,), (1,)), ((), ()))

    def ranks(a, b):
        return lax.dot_general(a, b, nt, preferred_element_type=jnp.float32)

    short = asks.astype(jnp.bfloat16)
    near_rank = ranks(short, near)
    far_rank = ranks(short, after)
    longest = jnp.max(jnp.where(line < lines, near_rank + asks, 0.0)).astype(jnp.int32)
    level_refs[0][0] = sum((longest > level).astype(jnp.int32) for level in within)
    longest = jnp.max(jnp.where(line < lines, 0.0, far_rank + asks)).astype(jnp.int32)
    level_refs[1][0] = sum((longest > level).astype(jnp.int32) for level in across)
    me = lax.axis_index("rows")
    half, c = over(me, rows // 2), lax.axis_index("cols")

    def row(values, number):
        return jnp.sum(jnp.where(line == number, values, 0.0), axis=0, keepdims=True)

    here = (ids & -per) - half * part + row(near_rank, c).astype(jnp.int32)
    there = part + row(far_rank, lines * (1 + half) + c).astype(jnp.int32)
    place = jnp.where(over(ids, part) == half, here, there)
    chosen = jnp.zeros(places_ref.shape, jnp.float32)
    for group in groups:
        table, _, asked = read(group)
        lane = lax.broadcasted_iota(jnp.int32, table.shape, 1)
        places = jnp.zeros(table.shape, jnp.int32)
        for s in range(slots):
            found = jnp.sum(jnp.where(asked[s], place, 0), axis=1, keepdims=True)
            places = jnp.where(lane == s, found, places)
        shape = (places_ref.shape[0], len(group))
        number = lax.broadcasted_iota(jnp.int32, shape, 0)
        device = lax.broadcasted_iota(jnp.int32, shape, 1) + group.start
        reads = functools.reduce(
            jnp.logical_or,
            [(number == i) & (device == (me ^ d) * cols + c) for i, d in enumerate(distances(shape[0]))],
        )
        chosen += jnp.dot(
            jnp.where(reads, 1.0, 0.0).astype(jnp.bfloat16),
            places.astype(jnp.float32).astype(jnp.bfloat16),
            preferred_element_type=jnp.float32,
        )
    places_ref[...] = chosen.astype(jnp.int32)
    line = lax.broadcasted_iota(jnp.int32, (panel, 3 * lines), 1)

    def column(values, number):
        return jnp.sum(jnp.where(line == number, values, 0.0), axis=1, keepdims=True)

    turned, near_rank, far_rank = ranks(same, short), ranks(near, short), ranks(after, short)
    ids = lax.broadcasted_iota(jnp.int32, (panel, 1), 0)
    number = lax.broadcasted_iota(jnp.int32, (panel, lists_ref.shape[1]), 1)
    near_rank = column(near_rank, c).astype(jnp.int32)
    here = (ids & -per) - half * part + near_rank
    other = lines * (2 - half) + c
    sent = (column(turned, other) > 0.5) & (column(far_rank, other).astype(jnp.int32) == number)
    sent = jnp.sum(jnp.where(sent, here, 0), axis=0, keepdims=True)
    kept = (column(turned, c) > 0.5) & (over(ids, per) == me) & (near_rank == number)
    kept = jnp.sum(jnp.where(kept, ids & (per - 1), 0), axis=0, keepdims=True)
    lists_ref[...] = jnp.where(lax.broadcasted_iota(jnp.int32, lists_ref.shape, 0) == 0, sent, kept)


def plan(table, slots, per, within, across):
    devices = table.shape[0]
    return pl.pallas_call(
        functools.partial(plan_kernel, slots, per, within, across),
        out_shape=(
            jax.ShapeDtypeStruct((lax.axis_size("rows") // 2, 128), jnp.int32),
            jax.ShapeDtypeStruct((8, 128), jnp.int32),
            jax.ShapeDtypeStruct((1,), jnp.int32),
            jax.ShapeDtypeStruct((1,), jnp.int32),
        ),
        in_specs=[VMEM],
        out_specs=(VMEM, VMEM, SMEM, SMEM),
        compiler_params=pltpu.CompilerParams(vmem_limit_bytes=48 * MIB),
        name="plan",
    )(table)


def distances(members):
    return [0, *sorted(range(1, members), key=lambda d: (-d.bit_count(), -d))]


def turn_kernel(sketch_ref, out_ref):
    members = out_ref.shape[0]
    me = lax.axis_index("rows") % members
    for i, d in enumerate(distances(members)):
        out_ref[i] = sketch_ref[:, me ^ d]


def turn(sketch):
    blocks, members, height, columns = sketch.shape
    return pl.pallas_call(
        turn_kernel,
        out_shape=jax.ShapeDtypeStruct((members, blocks, height, columns), sketch.dtype),
        in_specs=[VMEM],
        out_specs=VMEM,
        compiler_params=pltpu.CompilerParams(vmem_limit_bytes=24 * MIB),
        cost_estimate=pl.CostEstimate(flops=0, bytes_accessed=4 * sketch.size, transcendentals=0),
        name="turn_stripes",
    )(sketch)


def cut_kernel(lists_ref, stripes_ref, *out_refs):
    for k in range(out_refs[0].shape[0]):
        for i, out_ref in enumerate(out_refs):
            out_ref[k] = stripes_ref[i, lists_ref[1, k]]


def cut(lists, stripes, count):
    members, _, height, columns = stripes.shape
    return pl.pallas_call(
        cut_kernel,
        out_shape=(jax.ShapeDtypeStruct((count, height, columns), stripes.dtype),) * members,
        in_specs=[SMEM, VMEM],
        out_specs=(VMEM,) * members,
        compiler_params=pltpu.CompilerParams(vmem_limit_bytes=24 * MIB),
        name="cut_stripes",
    )(lists, stripes)


def order_kernel(*refs):
    *stripe_refs, all_ref = refs
    members = len(stripe_refs)
    me = lax.axis_index("rows") % members
    per = all_ref.shape[0] // members
    for ref, d in zip(stripe_refs, distances(members)):
        all_ref[pl.ds((me ^ d) * per, ref.shape[0])] = ref[...]


def order(stripes, per):
    _, height, columns = stripes[0].shape
    return pl.pallas_call(
        order_kernel,
        out_shape=jax.ShapeDtypeStruct((len(stripes) * per, height, columns), stripes[0].dtype),
        in_specs=[VMEM] * len(stripes),
        out_specs=VMEM,
        compiler_params=pltpu.CompilerParams(vmem_limit_bytes=24 * MIB),
        name="order_stripes",
    )(*stripes)


def list_kernel(list_ref, all_ref, out_ref):
    for k in range(out_ref.shape[0]):
        out_ref[k] = all_ref[list_ref[0, k]]


def listed(numbers, stripes, count):
    return pl.pallas_call(
        list_kernel,
        out_shape=jax.ShapeDtypeStruct((count, *stripes.shape[1:]), stripes.dtype),
        in_specs=[SMEM, VMEM],
        out_specs=VMEM,
        compiler_params=pltpu.CompilerParams(vmem_limit_bytes=24 * MIB),
        name="listed_stripes",
    )(numbers, stripes)


def pick_kernel(places_ref, own_ref, other_ref, *refs):
    *out_refs, whole = refs
    here = own_ref.shape[0]
    whole[:here] = own_ref[...]
    whole[here:] = other_ref[...]
    for i, out_ref in enumerate(out_refs):
        for s in range(out_ref.shape[0]):
            out_ref[s] = whole[jnp.minimum(places_ref[i, s], whole.shape[0] - 1)]


def pick(places, own, other, slots, members):
    shape = own.shape[1:]
    return pl.pallas_call(
        pick_kernel,
        out_shape=(jax.ShapeDtypeStruct((slots, *shape), own.dtype),) * members,
        in_specs=[SMEM, VMEM, VMEM],
        out_specs=(VMEM,) * members,
        scratch_shapes=[pltpu.VMEM((own.shape[0] + other.shape[0], *shape), own.dtype)],
        compiler_params=pltpu.CompilerParams(vmem_limit_bytes=24 * MIB),
        name="pick_stripes",
    )(places, own, other)


def product_kernel(rows_ref, counts_ref, blocks_ref, *refs):
    *chosen_refs, out_ref, whole = refs
    slots, width, _ = blocks_ref.shape
    columns = out_ref.shape[1]
    members = len(chosen_refs)
    me = lax.axis_index("rows") % members
    for ref, d in zip(chosen_refs, distances(members) if members > 1 else [0]):
        whole[me ^ d] = ref[...]
    out_ref[...] = jnp.zeros_like(out_ref)
    for s in range(slots):
        piece = whole[:, s].reshape(width, columns)
        product = jnp.dot(blocks_ref[s], piece, preferred_element_type=jnp.float32)
        at = pl.ds(pl.multiple_of(rows_ref[s] * width, width), width)
        out_ref[at, :] += jnp.where(s < counts_ref[0], product, 0.0)


def block_products(block_rows, counts, blocks, chosen):
    _, width, _ = blocks.shape
    columns = chosen[0].shape[-1]
    return pl.pallas_call(
        product_kernel,
        out_shape=jax.ShapeDtypeStruct((RB * width, columns), jnp.float32),
        in_specs=[SMEM, SMEM, VMEM] + [VMEM] * len(chosen),
        out_specs=VMEM,
        scratch_shapes=[pltpu.VMEM((len(chosen), *chosen[0].shape), chosen[0].dtype)],
        compiler_params=pltpu.CompilerParams(vmem_limit_bytes=24 * MIB),
        name="block_products",
    )(block_rows, counts, blocks, *chosen)


def gram_kernel(mine_ref, other_ref, own_ref, *refs):
    *gram_refs, slab = refs
    c = lax.axis_index("cols")
    me = lax.axis_index("rows") % len(gram_refs)
    share, (height, width) = own_ref.shape[0], gram_refs[0].shape
    slab[...] = mine_ref[...] + other_ref[...]
    own_ref[...] = slab[pl.ds(pl.multiple_of(c * share, share), share), :]
    right = slab[:, pl.ds(pl.multiple_of(c * width, width), width)]
    gram = lax.dot_general(
        slab[...], right, (((0,), (0,)), ((), ())), precision=HIGHEST, preferred_element_type=jnp.float32
    )
    for q in range(len(gram_refs)):
        for d in range(len(gram_refs)):

            @pl.when(me ^ d == q)
            def _():
                gram_refs[d][...] = gram[q * height : (q + 1) * height]


def sum_and_gram(mine, other):
    rows, columns = mine.shape
    return pl.pallas_call(
        gram_kernel,
        out_shape=(
            jax.ShapeDtypeStruct((rows // 2, columns), jnp.float32),
            *[jax.ShapeDtypeStruct((columns // 4, columns // 2), jnp.float32)] * 4,
        ),
        in_specs=[VMEM, VMEM],
        out_specs=(VMEM,) * 5,
        scratch_shapes=[pltpu.VMEM((rows, columns), jnp.float32)],
        compiler_params=pltpu.CompilerParams(vmem_limit_bytes=24 * MIB),
        name="sum_and_gram",
    )(mine, other)


def stack_kernel(*refs):
    *quarter_refs, out_ref = refs
    me = lax.axis_index("rows") % len(quarter_refs)
    height = quarter_refs[0].shape[0]
    for d, ref in enumerate(quarter_refs):
        out_ref[pl.ds(pl.multiple_of((me ^ d) * height, height), height), :] = ref[...]


def stack(quarters):
    height, width = quarters[0].shape
    return pl.pallas_call(
        stack_kernel,
        out_shape=jax.ShapeDtypeStruct((len(quarters) * height, width), jnp.float32),
        in_specs=[VMEM] * len(quarters),
        out_specs=VMEM,
        compiler_params=pltpu.CompilerParams(vmem_limit_bytes=24 * MIB),
        name="stack_quarters",
    )(*quarters)


def matmul(a, b, precision):
    return jnp.dot(a, b, precision=precision, preferred_element_type=jnp.float32)


def matmul_nt(a, b, precision):
    return lax.dot_general(
        a, b, (((1,), (1,)), ((), ())), precision=precision, preferred_element_type=jnp.float32
    )


def split_matmul(times, passes, a, b):
    a_high, b_high = a.astype(jnp.bfloat16), b.astype(jnp.bfloat16)
    result = times(a_high, b_high, None)
    if passes == 3:
        a_low = (a - a_high.astype(jnp.float32)).astype(jnp.bfloat16)
        b_low = (b - b_high.astype(jnp.float32)).astype(jnp.bfloat16)
        result += times(a_high, b_low, None) + times(a_low, b_high, None)
    return result


def factor_kernel(total_rows, *refs):
    *gram_refs, own_ref, basis_ref, factor_ref, whole, scaled, inverse, product = refs
    n = factor_ref.shape[0]
    if len(gram_refs) == 1:
        whole[...] = gram_refs[0][...]
    else:
        c = lax.axis_index("cols")
        width = n // 2
        whole[:, pl.ds(pl.multiple_of(c * width, width), width)] = gram_refs[0][...]
        whole[:, pl.ds(pl.multiple_of((1 - c) * width, width), width)] = gram_refs[1][...]
    row_ids = lax.broadcasted_iota(jnp.int32, (n, n), 0)
    col_ids = lax.broadcasted_iota(jnp.int32, (n, n), 1)
    diagonal = row_ids == col_ids
    identity = diagonal.astype(jnp.float32)
    half = jnp.where(row_ids > col_ids, 1.0, jnp.where(diagonal, 0.5, 0.0))
    gram = whole[...]
    on_diagonal = jnp.where(diagonal, gram, 0.0)
    down = jnp.sqrt(jnp.sum(on_diagonal, axis=1, keepdims=True))
    across = jnp.sqrt(jnp.sum(on_diagonal, axis=0, keepdims=True))
    up_down = 1.0 / down
    up_across = 1.0 / across
    scaled[...] = gram * up_down * up_across

    def refine(times, times_nt):
        w = inverse[...]
        upper = times(w, scaled[...])
        residual = times_nt(upper, w) - identity
        step = residual * half
        inverse[...] = w - matmul(step, w, lax.Precision.DEFAULT)
        product[...] = upper - matmul(step, upper, lax.Precision.DEFAULT)
        return jnp.sum(residual * residual)

    def exactly(times):
        return functools.partial(times, precision=HIGHEST)

    inverse[...] = identity - (scaled[...] - identity) * half
    for passes in (1, 3):
        refine(functools.partial(split_matmul, matmul, passes), functools.partial(split_matmul, matmul_nt, passes))

    def going(state):
        step, size = state
        return (step < 8) & (size > 1e-6)

    def advance(state):
        return state[0] + 1, refine(exactly(matmul), exactly(matmul_nt))

    _, size = lax.while_loop(going, advance, (jnp.int32(0), jnp.float32(1.0)))

    @pl.when(jnp.logical_not(size <= 1e-6))
    def _():
        inverse[...] = identity
        ids = lax.broadcasted_iota(jnp.int32, (n, 1), 0)

        def eliminate(j, carry):
            pivot_row = scaled[pl.ds(j, 1), :]
            inverse_row = inverse[pl.ds(j, 1), :]
            column = jnp.sum(jnp.where(col_ids == j, scaled[...], 0.0), axis=1, keepdims=True)
            pivot = jnp.sum(jnp.where(ids == j, column, 0.0), axis=0, keepdims=True)
            root = 1.0 / jnp.sqrt(pivot)
            ratio = jnp.where(ids > j, column / pivot, jnp.where(ids == j, 1.0 - root, 0.0))
            scaled[...] = scaled[...] - ratio * pivot_row
            inverse[...] = inverse[...] - ratio * inverse_row
            return carry

        lax.fori_loop(0, n, eliminate, 0)
        product[...] = matmul(inverse[...], whole[...] * up_down * up_across, HIGHEST)

    w = inverse[...]
    root_rows = jnp.sqrt(jnp.float32(total_rows))
    upper = product[...] * across / root_rows
    factor_ref[...] = jnp.where(row_ids <= col_ids, upper, 0.0)
    basis_ref[...] = matmul_nt(own_ref[...] * up_across, w, HIGHEST) * root_rows


def factor_and_basis(total_rows, grams, own):
    columns = own.shape[1]
    return pl.pallas_call(
        functools.partial(factor_kernel, total_rows),
        out_shape=(
            jax.ShapeDtypeStruct(own.shape, jnp.float32),
            jax.ShapeDtypeStruct((columns, columns), jnp.float32),
        ),
        in_specs=[VMEM] * (len(grams) + 1),
        out_specs=(VMEM, VMEM),
        scratch_shapes=[pltpu.VMEM((columns, columns), jnp.float32)] * 4,
        compiler_params=pltpu.CompilerParams(vmem_limit_bytes=24 * MIB),
        name="factor_and_basis",
    )(*grams, own)


def exchange(pieces, rows):
    order = distances(len(pieces))
    return [
        lax.ppermute(piece, "rows", [(r, r ^ d) for r in range(rows)]) if d else piece
        for piece, d in zip(pieces, order)
    ]


def fetch(sketch, block_cols, counts, slots, width):
    rows, cols = lax.axis_size("rows"), lax.axis_size("cols")
    members = rows // 2
    height = width // members
    columns = sketch.shape[1]
    sketch = sketch.reshape(-1, members, height, columns)
    per = sketch.shape[0]
    largest = min(per * members, slots * members, 128)
    within = tuple(level for level in WITHIN if level < per)
    across = tuple(level for level in ACROSS if level < largest and members <= 8)
    stripes = turn(sketch)
    table = table_copies(block_cols, counts, rows * cols)
    table = lax.all_to_all(table, ("rows", "cols"), split_axis=0, concat_axis=0, tiled=True)
    places, lists, near, far = plan(table, slots, per, within, across)

    def within_half(count):
        def run():
            return order(exchange(cut(lists, stripes, count), rows), per)

        return run

    own = lax.switch(near[0], [within_half(count) for count in (*within, per)])

    def across_halves(count):
        def run():
            swap = [(r, (r + members) % rows) for r in range(rows)]
            other = lax.ppermute(listed(lists, own, count), "rows", swap)
            return pick(places, own, other, slots, members)

        return run

    picked = lax.switch(far[0], [across_halves(count) for count in (*across, largest)])
    return exchange(picked, rows)


def moved(piece, rows, d):
    return lax.ppermute(piece, "rows", [(r, r ^ d) for r in range(rows)])


def gram_halves(quarters, rows):
    first, *rest = quarters
    for d, quarter in enumerate(rest):
        first = first + moved(quarter, rows, d + 1)
    total = (first + moved(first, rows, 4)) + (moved(first, rows, 8) + moved(first, rows, 12))
    half = stack([total] + [moved(total, rows, d) for d in range(1, 4)])
    return half, lax.ppermute(half, "cols", [(0, 1), (1, 0)])


def local(sketch, blocks, block_rows, block_cols, counts):
    slots, width, _ = blocks.shape
    columns = sketch.shape[1]
    rows, cols = lax.axis_size("rows"), lax.axis_size("cols")
    chosen = fetch(sketch, block_cols, counts, slots, width)
    if chosen[0].shape[1] % 16:
        order = jnp.argsort(lax.axis_index("rows") % len(chosen) ^ jnp.array(distances(len(chosen))))
        chosen = [jnp.stack(chosen)[order].swapaxes(0, 1).reshape(1, slots, width, columns)[0]]
    partial_rows = block_products(block_rows, counts, blocks, chosen)
    if (rows, cols) == (16, 2):
        other = lax.ppermute(partial_rows, "cols", [(0, 1), (1, 0)])
        own, *quarters = sum_and_gram(partial_rows, other)
        grams = gram_halves(quarters, rows)
    else:
        own = lax.psum_scatter(partial_rows, "cols", scatter_dimension=0, tiled=True)
        grams = [lax.psum(matmul(own.T, own, HIGHEST), ("rows", "cols"))]
    return factor_and_basis(RB * width * rows, grams, own)


def solution(mesh):
    in_specs = (
        P(("rows", "cols"), None),
        P(("rows", "cols"), None, None),
        P(("rows", "cols")),
        P(("rows", "cols")),
        P(("rows", "cols")),
    )
    out_specs = (P(("rows", "cols"), None), P())
    return jax.shard_map(local, mesh=mesh, in_specs=in_specs, out_specs=out_specs, check_vma=False)
```

```python
import functools

import jax
import jax.numpy as jnp
from jax import lax
from jax.experimental import pallas as pl
from jax.experimental.pallas import tpu as pltpu
from jax.sharding import PartitionSpec as P

RB = 4
HIGHEST = lax.Precision.HIGHEST
VMEM = pl.BlockSpec(memory_space=pltpu.VMEM)
SMEM = pl.BlockSpec(memory_space=pltpu.SMEM)
MIB = 1024 * 1024


ACROSS = (*range(11, 21), 22, 24, 28, 36)
WITHIN = (5, 6, 7, 8, 9, 10, 12)


def table_kernel(cols_ref, counts_ref, out_ref):
    slots = cols_ref.shape[0]
    lane = lax.broadcasted_iota(jnp.int32, out_ref.shape, 2)
    table = jnp.where(lane == slots, counts_ref[0], 0)
    for s in range(slots):
        table = jnp.where(lane == s, cols_ref[s], table)
    out_ref[...] = table


def table_copies(block_cols, counts, devices):
    return pl.pallas_call(
        table_kernel,
        out_shape=jax.ShapeDtypeStruct((devices, 1, 128), jnp.int32),
        in_specs=[SMEM, SMEM],
        out_specs=VMEM,
        name="table_copies",
    )(block_cols, counts)


def over(values, size):
    return values >> (size.bit_length() - 1)


def plan_kernel(slots, per, within, across, table_ref, places_ref, lists_ref, *level_refs):
    devices = table_ref.shape[0]
    rows, cols = lax.axis_size("rows"), lax.axis_size("cols")
    panel = per * rows
    part = panel // 2
    groups = [range(at, min(at + 64, devices)) for at in range(0, devices, 64)]

    def read(group):
        table = table_ref[group.start : group.stop, 0, :]
        lane = lax.broadcasted_iota(jnp.int32, table.shape, 1)
        counts = table[:, slots : slots + 1]
        table = jnp.where(lane < counts, table, -1)
        block = lax.broadcasted_iota(jnp.int32, (len(group), panel), 1)
        return table, counts, [table[:, s : s + 1] == block for s in range(slots)]

    lines = -(-cols // 8) * 8
    line = lax.broadcasted_iota(jnp.int32, (3 * lines, panel), 0)
    ids = lax.broadcasted_iota(jnp.int32, (1, panel), 1)
    asks = jnp.zeros((3 * lines, panel), jnp.float32)
    for group in groups:
        _, _, asked = read(group)
        some = jnp.where(functools.reduce(jnp.logical_or, asked), 1.0, 0.0).astype(jnp.bfloat16)
        shape = (3 * lines, len(group))
        number = lax.broadcasted_iota(jnp.int32, shape, 0)
        device = lax.broadcasted_iota(jnp.int32, shape, 1) + group.start
        core, side = device & (cols - 1), over(device, devices // 2)
        reads = (number == core) | (number == lines * (1 + side) + core)
        asks += jnp.dot(jnp.where(reads, 1.0, 0.0).astype(jnp.bfloat16), some, preferred_element_type=jnp.float32)
    own_half = (line >= lines) & (over(line - lines, lines) == over(lax.broadcasted_iota(jnp.int32, line.shape, 1), part))
    asks = jnp.where((asks > 0.5) & jnp.logical_not(own_half), 1.0, 0.0)
    first = lax.broadcasted_iota(jnp.int32, (panel, panel), 0)
    second = lax.broadcasted_iota(jnp.int32, (panel, panel), 1)
    after = first > second
    near = jnp.where(after & ((first ^ second) < per), 1.0, 0.0).astype(jnp.bfloat16)
    after = jnp.where(after, 1.0, 0.0).astype(jnp.bfloat16)
    same = jnp.where(first == second, 1.0, 0.0).astype(jnp.bfloat16)
    nt = (((1,), (1,)), ((), ()))

    def ranks(a, b):
        return lax.dot_general(a, b, nt, preferred_element_type=jnp.float32)

    short = asks.astype(jnp.bfloat16)
    near_rank = ranks(short, near)
    far_rank = ranks(short, after)
    longest = jnp.max(jnp.where(line < lines, near_rank + asks, 0.0)).astype(jnp.int32)
    level_refs[0][0] = sum((longest > level).astype(jnp.int32) for level in within)
    longest = jnp.max(jnp.where(line < lines, 0.0, far_rank + asks)).astype(jnp.int32)
    level_refs[1][0] = sum((longest > level).astype(jnp.int32) for level in across)
    me = lax.axis_index("rows")
    half, c = over(me, rows // 2), lax.axis_index("cols")

    def row(values, number):
        return jnp.sum(jnp.where(line == number, values, 0.0), axis=0, keepdims=True)

    here = (ids & -per) - half * part + row(near_rank, c).astype(jnp.int32)
    there = part + row(far_rank, lines * (1 + half) + c).astype(jnp.int32)
    place = jnp.where(over(ids, part) == half, here, there)
    chosen = jnp.zeros(places_ref.shape, jnp.float32)
    for group in groups:
        table, _, asked = read(group)
        lane = lax.broadcasted_iota(jnp.int32, table.shape, 1)
        places = jnp.zeros(table.shape, jnp.int32)
        for s in range(slots):
            found = jnp.sum(jnp.where(asked[s], place, 0), axis=1, keepdims=True)
            places = jnp.where(lane == s, found, places)
        shape = (places_ref.shape[0], len(group))
        number = lax.broadcasted_iota(jnp.int32, shape, 0)
        device = lax.broadcasted_iota(jnp.int32, shape, 1) + group.start
        reads = functools.reduce(
            jnp.logical_or,
            [(number == i) & (device == (me ^ d) * cols + c) for i, d in enumerate(distances(shape[0]))],
        )
        chosen += jnp.dot(
            jnp.where(reads, 1.0, 0.0).astype(jnp.bfloat16),
            places.astype(jnp.float32).astype(jnp.bfloat16),
            preferred_element_type=jnp.float32,
        )
    places_ref[...] = chosen.astype(jnp.int32)
    line = lax.broadcasted_iota(jnp.int32, (panel, 3 * lines), 1)

    def column(values, number):
        return jnp.sum(jnp.where(line == number, values, 0.0), axis=1, keepdims=True)

    turned, near_rank, far_rank = ranks(same, short), ranks(near, short), ranks(after, short)
    ids = lax.broadcasted_iota(jnp.int32, (panel, 1), 0)
    number = lax.broadcasted_iota(jnp.int32, (panel, lists_ref.shape[1]), 1)
    near_rank = column(near_rank, c).astype(jnp.int32)
    here = (ids & -per) - half * part + near_rank
    other = lines * (2 - half) + c
    sent = (column(turned, other) > 0.5) & (column(far_rank, other).astype(jnp.int32) == number)
    sent = jnp.sum(jnp.where(sent, here, 0), axis=0, keepdims=True)
    kept = (column(turned, c) > 0.5) & (over(ids, per) == me) & (near_rank == number)
    kept = jnp.sum(jnp.where(kept, ids & (per - 1), 0), axis=0, keepdims=True)
    lists_ref[...] = jnp.where(lax.broadcasted_iota(jnp.int32, lists_ref.shape, 0) == 0, sent, kept)


def plan(table, slots, per, within, across):
    devices = table.shape[0]
    return pl.pallas_call(
        functools.partial(plan_kernel, slots, per, within, across),
        out_shape=(
            jax.ShapeDtypeStruct((lax.axis_size("rows") // 2, 128), jnp.int32),
            jax.ShapeDtypeStruct((8, 128), jnp.int32),
            jax.ShapeDtypeStruct((1,), jnp.int32),
            jax.ShapeDtypeStruct((1,), jnp.int32),
        ),
        in_specs=[VMEM],
        out_specs=(VMEM, VMEM, SMEM, SMEM),
        compiler_params=pltpu.CompilerParams(vmem_limit_bytes=48 * MIB),
        name="plan",
    )(table)


def distances(members):
    order = [0]
    for near in sorted(range(1, members), key=lambda d: (d.bit_count(), d)):
        far = (members - 1) ^ near
        if near not in order and far:
            order += [near, far]
    return [*order[:-2], members - 1, *order[-2:]] if members > 2 else list(range(members))


def turn_kernel(sketch_ref, out_ref):
    members = out_ref.shape[0]
    me = lax.axis_index("rows") % members
    for i, d in enumerate(distances(members)):
        out_ref[i] = sketch_ref[:, me ^ d]


def turn(sketch):
    blocks, members, height, columns = sketch.shape
    return pl.pallas_call(
        turn_kernel,
        out_shape=jax.ShapeDtypeStruct((members, blocks, height, columns), sketch.dtype),
        in_specs=[VMEM],
        out_specs=VMEM,
        compiler_params=pltpu.CompilerParams(vmem_limit_bytes=24 * MIB),
        cost_estimate=pl.CostEstimate(flops=0, bytes_accessed=4 * sketch.size, transcendentals=0),
        name="turn_stripes",
    )(sketch)


def cut_kernel(lists_ref, stripes_ref, *out_refs):
    for k in range(out_refs[0].shape[0]):
        for i, out_ref in enumerate(out_refs):
            out_ref[k] = stripes_ref[i, lists_ref[1, k]]


def cut(lists, stripes, count):
    members, _, height, columns = stripes.shape
    return pl.pallas_call(
        cut_kernel,
        out_shape=(jax.ShapeDtypeStruct((count, height, columns), stripes.dtype),) * members,
        in_specs=[SMEM, VMEM],
        out_specs=(VMEM,) * members,
        compiler_params=pltpu.CompilerParams(vmem_limit_bytes=24 * MIB),
        name="cut_stripes",
    )(lists, stripes)


def order_kernel(*refs):
    *stripe_refs, all_ref = refs
    members = len(stripe_refs)
    me = lax.axis_index("rows") % members
    per = all_ref.shape[0] // members
    for ref, d in zip(stripe_refs, distances(members)):
        all_ref[pl.ds((me ^ d) * per, ref.shape[0])] = ref[...]


def order(stripes, per):
    _, height, columns = stripes[0].shape
    return pl.pallas_call(
        order_kernel,
        out_shape=jax.ShapeDtypeStruct((len(stripes) * per, height, columns), stripes[0].dtype),
        in_specs=[VMEM] * len(stripes),
        out_specs=VMEM,
        compiler_params=pltpu.CompilerParams(vmem_limit_bytes=24 * MIB),
        name="order_stripes",
    )(*stripes)


def list_kernel(list_ref, all_ref, out_ref):
    for k in range(out_ref.shape[0]):
        out_ref[k] = all_ref[list_ref[0, k]]


def listed(numbers, stripes, count):
    return pl.pallas_call(
        list_kernel,
        out_shape=jax.ShapeDtypeStruct((count, *stripes.shape[1:]), stripes.dtype),
        in_specs=[SMEM, VMEM],
        out_specs=VMEM,
        compiler_params=pltpu.CompilerParams(vmem_limit_bytes=24 * MIB),
        name="listed_stripes",
    )(numbers, stripes)


def pick_kernel(places_ref, own_ref, other_ref, *refs):
    *out_refs, whole = refs
    here = own_ref.shape[0]
    whole[:here] = own_ref[...]
    whole[here:] = other_ref[...]
    for i, out_ref in enumerate(out_refs):
        for s in range(out_ref.shape[0]):
            out_ref[s] = whole[jnp.minimum(places_ref[i, s], whole.shape[0] - 1)]


def pick(places, own, other, slots, members):
    shape = own.shape[1:]
    return pl.pallas_call(
        pick_kernel,
        out_shape=(jax.ShapeDtypeStruct((slots, *shape), own.dtype),) * members,
        in_specs=[SMEM, VMEM, VMEM],
        out_specs=(VMEM,) * members,
        scratch_shapes=[pltpu.VMEM((own.shape[0] + other.shape[0], *shape), own.dtype)],
        compiler_params=pltpu.CompilerParams(vmem_limit_bytes=24 * MIB),
        name="pick_stripes",
    )(places, own, other)


def product_kernel(rows_ref, counts_ref, blocks_ref, *refs):
    *chosen_refs, out_ref, whole = refs
    slots, width, _ = blocks_ref.shape
    columns = out_ref.shape[1]
    members = len(chosen_refs)
    me = lax.axis_index("rows") % members
    for ref, d in zip(chosen_refs, distances(members) if members > 1 else [0]):
        whole[me ^ d] = ref[...]
    out_ref[...] = jnp.zeros_like(out_ref)
    for s in range(slots):
        piece = whole[:, s].reshape(width, columns)
        product = jnp.dot(blocks_ref[s], piece, preferred_element_type=jnp.float32)
        at = pl.ds(pl.multiple_of(rows_ref[s] * width, width), width)
        out_ref[at, :] += jnp.where(s < counts_ref[0], product, 0.0)


def block_products(block_rows, counts, blocks, chosen):
    _, width, _ = blocks.shape
    columns = chosen[0].shape[-1]
    return pl.pallas_call(
        product_kernel,
        out_shape=jax.ShapeDtypeStruct((RB * width, columns), jnp.float32),
        in_specs=[SMEM, SMEM, VMEM] + [VMEM] * len(chosen),
        out_specs=VMEM,
        scratch_shapes=[pltpu.VMEM((len(chosen), *chosen[0].shape), chosen[0].dtype)],
        compiler_params=pltpu.CompilerParams(vmem_limit_bytes=24 * MIB),
        name="block_products",
    )(block_rows, counts, blocks, *chosen)


def gram_kernel(mine_ref, other_ref, own_ref, *refs):
    *gram_refs, slab = refs
    c = lax.axis_index("cols")
    me = lax.axis_index("rows") % len(gram_refs)
    share, (height, width) = own_ref.shape[0], gram_refs[0].shape
    slab[...] = mine_ref[...] + other_ref[...]
    own_ref[...] = slab[pl.ds(pl.multiple_of(c * share, share), share), :]
    right = slab[:, pl.ds(pl.multiple_of(c * width, width), width)]
    gram = lax.dot_general(
        slab[...], right, (((0,), (0,)), ((), ())), precision=HIGHEST, preferred_element_type=jnp.float32
    )
    for q in range(len(gram_refs)):
        for d in range(len(gram_refs)):

            @pl.when(me ^ d == q)
            def _():
                gram_refs[d][...] = gram[q * height : (q + 1) * height]


def sum_and_gram(mine, other):
    rows, columns = mine.shape
    return pl.pallas_call(
        gram_kernel,
        out_shape=(
            jax.ShapeDtypeStruct((rows // 2, columns), jnp.float32),
            *[jax.ShapeDtypeStruct((columns // 4, columns // 2), jnp.float32)] * 4,
        ),
        in_specs=[VMEM, VMEM],
        out_specs=(VMEM,) * 5,
        scratch_shapes=[pltpu.VMEM((rows, columns), jnp.float32)],
        compiler_params=pltpu.CompilerParams(vmem_limit_bytes=24 * MIB),
        name="sum_and_gram",
    )(mine, other)


def stack_kernel(*refs):
    *quarter_refs, out_ref = refs
    me = lax.axis_index("rows") % len(quarter_refs)
    height = quarter_refs[0].shape[0]
    for d, ref in enumerate(quarter_refs):
        out_ref[pl.ds(pl.multiple_of((me ^ d) * height, height), height), :] = ref[...]


def stack(quarters):
    height, width = quarters[0].shape
    return pl.pallas_call(
        stack_kernel,
        out_shape=jax.ShapeDtypeStruct((len(quarters) * height, width), jnp.float32),
        in_specs=[VMEM] * len(quarters),
        out_specs=VMEM,
        compiler_params=pltpu.CompilerParams(vmem_limit_bytes=24 * MIB),
        name="stack_quarters",
    )(*quarters)


def matmul(a, b, precision):
    return jnp.dot(a, b, precision=precision, preferred_element_type=jnp.float32)


def matmul_nt(a, b, precision):
    return lax.dot_general(
        a, b, (((1,), (1,)), ((), ())), precision=precision, preferred_element_type=jnp.float32
    )


def split_matmul(times, passes, a, b):
    a_high, b_high = a.astype(jnp.bfloat16), b.astype(jnp.bfloat16)
    result = times(a_high, b_high, None)
    if passes == 3:
        a_low = (a - a_high.astype(jnp.float32)).astype(jnp.bfloat16)
        b_low = (b - b_high.astype(jnp.float32)).astype(jnp.bfloat16)
        result += times(a_high, b_low, None) + times(a_low, b_high, None)
    return result


def factor_kernel(total_rows, *refs):
    *gram_refs, own_ref, basis_ref, factor_ref, whole, scaled, inverse, product = refs
    n = factor_ref.shape[0]
    if len(gram_refs) == 1:
        whole[...] = gram_refs[0][...]
    else:
        c = lax.axis_index("cols")
        width = n // 2
        whole[:, pl.ds(pl.multiple_of(c * width, width), width)] = gram_refs[0][...]
        whole[:, pl.ds(pl.multiple_of((1 - c) * width, width), width)] = gram_refs[1][...]
    row_ids = lax.broadcasted_iota(jnp.int32, (n, n), 0)
    col_ids = lax.broadcasted_iota(jnp.int32, (n, n), 1)
    diagonal = row_ids == col_ids
    identity = diagonal.astype(jnp.float32)
    half = jnp.where(row_ids > col_ids, 1.0, jnp.where(diagonal, 0.5, 0.0))
    gram = whole[...]
    on_diagonal = jnp.where(diagonal, gram, 0.0)
    down = jnp.sqrt(jnp.sum(on_diagonal, axis=1, keepdims=True))
    across = jnp.sqrt(jnp.sum(on_diagonal, axis=0, keepdims=True))
    up_down = 1.0 / down
    up_across = 1.0 / across
    scaled[...] = gram * up_down * up_across

    def refine(times, times_nt, last=False):
        w = inverse[...]
        upper = times(w, scaled[...])
        residual = times_nt(upper, w) - identity
        step = residual * half
        inverse[...] = w - matmul(step, w, lax.Precision.DEFAULT)
        if last:
            product[...] = upper - matmul(step, upper, lax.Precision.DEFAULT)
        return jnp.sum(residual * residual)

    def exactly(times):
        return functools.partial(times, precision=HIGHEST)

    inverse[...] = identity - (scaled[...] - identity) * half
    for passes in (1, 3):
        refine(functools.partial(split_matmul, matmul, passes), functools.partial(split_matmul, matmul_nt, passes))

    def going(state):
        step, size = state
        return (step < 8) & (size > 1e-6)

    def advance(state):
        return state[0] + 1, refine(exactly(matmul), exactly(matmul_nt), last=True)

    _, size = lax.while_loop(going, advance, (jnp.int32(0), jnp.float32(1.0)))

    @pl.when(jnp.logical_not(size <= 1e-6))
    def _():
        inverse[...] = identity
        ids = lax.broadcasted_iota(jnp.int32, (n, 1), 0)

        def eliminate(j, carry):
            pivot_row = scaled[pl.ds(j, 1), :]
            inverse_row = inverse[pl.ds(j, 1), :]
            column = jnp.sum(jnp.where(col_ids == j, scaled[...], 0.0), axis=1, keepdims=True)
            pivot = jnp.sum(jnp.where(ids == j, column, 0.0), axis=0, keepdims=True)
            root = 1.0 / jnp.sqrt(pivot)
            ratio = jnp.where(ids > j, column / pivot, jnp.where(ids == j, 1.0 - root, 0.0))
            scaled[...] = scaled[...] - ratio * pivot_row
            inverse[...] = inverse[...] - ratio * inverse_row
            return carry

        lax.fori_loop(0, n, eliminate, 0)
        product[...] = matmul(inverse[...], whole[...] * up_down * up_across, HIGHEST)

    w = inverse[...]
    root_rows = jnp.sqrt(jnp.float32(total_rows))
    upper = product[...] * across / root_rows
    factor_ref[...] = jnp.where(row_ids <= col_ids, upper, 0.0)
    basis_ref[...] = matmul_nt(own_ref[...] * up_across, w, HIGHEST) * root_rows


def factor_and_basis(total_rows, grams, own):
    columns = own.shape[1]
    return pl.pallas_call(
        functools.partial(factor_kernel, total_rows),
        out_shape=(
            jax.ShapeDtypeStruct(own.shape, jnp.float32),
            jax.ShapeDtypeStruct((columns, columns), jnp.float32),
        ),
        in_specs=[VMEM] * (len(grams) + 1),
        out_specs=(VMEM, VMEM),
        scratch_shapes=[pltpu.VMEM((columns, columns), jnp.float32)] * 4,
        compiler_params=pltpu.CompilerParams(vmem_limit_bytes=24 * MIB),
        name="factor_and_basis",
    )(*grams, own)


def exchange(pieces, rows):
    order = distances(len(pieces))
    return [
        lax.ppermute(piece, "rows", [(r, r ^ d) for r in range(rows)]) if d else piece
        for piece, d in zip(pieces, order)
    ]


def fetch(sketch, block_cols, counts, slots, width):
    rows, cols = lax.axis_size("rows"), lax.axis_size("cols")
    members = rows // 2
    height = width // members
    columns = sketch.shape[1]
    sketch = sketch.reshape(-1, members, height, columns)
    per = sketch.shape[0]
    largest = min(per * members, slots * members, 128)
    within = tuple(level for level in WITHIN if level < per)
    across = tuple(level for level in ACROSS if level < largest and members <= 8)
    stripes = turn(sketch)
    table = table_copies(block_cols, counts, rows * cols)
    table = lax.all_to_all(table, ("rows", "cols"), split_axis=0, concat_axis=0, tiled=True)
    places, lists, near, far = plan(table, slots, per, within, across)

    def within_half(count):
        def run():
            return order(exchange(cut(lists, stripes, count), rows), per)

        return run

    own = lax.switch(near[0], [within_half(count) for count in (*within, per)])

    def across_halves(count):
        def run():
            swap = [(r, (r + members) % rows) for r in range(rows)]
            other = lax.ppermute(listed(lists, own, count), "rows", swap)
            return pick(places, own, other, slots, members)

        return run

    picked = lax.switch(far[0], [across_halves(count) for count in (*across, largest)])
    return exchange(picked, rows)


def moved(piece, rows, d):
    return lax.ppermute(piece, "rows", [(r, r ^ d) for r in range(rows)])


def gram_halves(quarters, rows):
    first, *rest = quarters
    for d, quarter in enumerate(rest):
        first = first + moved(quarter, rows, d + 1)
    total = (first + moved(first, rows, 4)) + (moved(first, rows, 8) + moved(first, rows, 12))
    half = stack([total] + [moved(total, rows, d) for d in range(1, 4)])
    return half, lax.ppermute(half, "cols", [(0, 1), (1, 0)])


def local(sketch, blocks, block_rows, block_cols, counts):
    slots, width, _ = blocks.shape
    columns = sketch.shape[1]
    rows, cols = lax.axis_size("rows"), lax.axis_size("cols")
    chosen = fetch(sketch, block_cols, counts, slots, width)
    if chosen[0].shape[1] % 16:
        order = jnp.argsort(lax.axis_index("rows") % len(chosen) ^ jnp.array(distances(len(chosen))))
        chosen = [jnp.stack(chosen)[order].swapaxes(0, 1).reshape(1, slots, width, columns)[0]]
    partial_rows = block_products(block_rows, counts, blocks, chosen)
    if (rows, cols) == (16, 2):
        other = lax.ppermute(partial_rows, "cols", [(0, 1), (1, 0)])
        own, *quarters = sum_and_gram(partial_rows, other)
        grams = gram_halves(quarters, rows)
    else:
        own = lax.psum_scatter(partial_rows, "cols", scatter_dimension=0, tiled=True)
        grams = [lax.psum(matmul(own.T, own, HIGHEST), ("rows", "cols"))]
    return factor_and_basis(RB * width * rows, grams, own)


def solution(mesh):
    in_specs = (
        P(("rows", "cols"), None),
        P(("rows", "cols"), None, None),
        P(("rows", "cols")),
        P(("rows", "cols")),
        P(("rows", "cols")),
    )
    out_specs = (P(("rows", "cols"), None), P())
    return jax.shard_map(local, mesh=mesh, in_specs=in_specs, out_specs=out_specs, check_vma=False)
```

```python
import functools

import jax
import jax.numpy as jnp
from jax import lax
from jax.experimental import pallas as pl
from jax.experimental.pallas import tpu as pltpu
from jax.sharding import PartitionSpec as P

RB = 4
HIGHEST = lax.Precision.HIGHEST
VMEM = pl.BlockSpec(memory_space=pltpu.VMEM)
SMEM = pl.BlockSpec(memory_space=pltpu.SMEM)
MIB = 1024 * 1024


ACROSS = (*range(11, 21), 22, 24, 28, 36)
WITHIN = (5, 6, 7, 8, 9, 10, 12)


def table_kernel(cols_ref, counts_ref, out_ref):
    slots = cols_ref.shape[0]
    lane = lax.broadcasted_iota(jnp.int32, out_ref.shape, 2)
    table = jnp.where(lane == slots, counts_ref[0], 0)
    for s in range(slots):
        table = jnp.where(lane == s, cols_ref[s], table)
    out_ref[...] = table


def table_copies(block_cols, counts, devices):
    return pl.pallas_call(
        table_kernel,
        out_shape=jax.ShapeDtypeStruct((devices, 1, 128), jnp.int32),
        in_specs=[SMEM, SMEM],
        out_specs=VMEM,
        name="table_copies",
    )(block_cols, counts)


def over(values, size):
    return values >> (size.bit_length() - 1)


def plan_kernel(slots, per, within, across, table_ref, places_ref, lists_ref, *level_refs):
    devices = table_ref.shape[0]
    rows, cols = lax.axis_size("rows"), lax.axis_size("cols")
    panel = per * rows
    part = panel // 2
    groups = [range(at, min(at + 64, devices)) for at in range(0, devices, 64)]

    def read(group):
        table = table_ref[group.start : group.stop, 0, :]
        lane = lax.broadcasted_iota(jnp.int32, table.shape, 1)
        counts = table[:, slots : slots + 1]
        table = jnp.where(lane < counts, table, -1)
        block = lax.broadcasted_iota(jnp.int32, (len(group), panel), 1)
        return table, counts, [table[:, s : s + 1] == block for s in range(slots)]

    lines = -(-cols // 8) * 8
    line = lax.broadcasted_iota(jnp.int32, (3 * lines, panel), 0)
    ids = lax.broadcasted_iota(jnp.int32, (1, panel), 1)
    asks = jnp.zeros((3 * lines, panel), jnp.float32)
    for group in groups:
        _, _, asked = read(group)
        some = jnp.where(functools.reduce(jnp.logical_or, asked), 1.0, 0.0).astype(jnp.bfloat16)
        shape = (3 * lines, len(group))
        number = lax.broadcasted_iota(jnp.int32, shape, 0)
        device = lax.broadcasted_iota(jnp.int32, shape, 1) + group.start
        core, side = device & (cols - 1), over(device, devices // 2)
        reads = (number == core) | (number == lines * (1 + side) + core)
        asks += jnp.dot(jnp.where(reads, 1.0, 0.0).astype(jnp.bfloat16), some, preferred_element_type=jnp.float32)
    own_half = (line >= lines) & (over(line - lines, lines) == over(lax.broadcasted_iota(jnp.int32, line.shape, 1), part))
    asks = jnp.where((asks > 0.5) & jnp.logical_not(own_half), 1.0, 0.0)
    first = lax.broadcasted_iota(jnp.int32, (panel, panel), 0)
    second = lax.broadcasted_iota(jnp.int32, (panel, panel), 1)
    after = first > second
    near = jnp.where(after & ((first ^ second) < per), 1.0, 0.0).astype(jnp.bfloat16)
    after = jnp.where(after, 1.0, 0.0).astype(jnp.bfloat16)
    same = jnp.where(first == second, 1.0, 0.0).astype(jnp.bfloat16)
    nt = (((1,), (1,)), ((), ()))

    def ranks(a, b):
        return lax.dot_general(a, b, nt, preferred_element_type=jnp.float32)

    short = asks.astype(jnp.bfloat16)
    near_rank = ranks(short, near)
    far_rank = ranks(short, after)
    longest = jnp.max(jnp.where(line < lines, near_rank + asks, 0.0)).astype(jnp.int32)
    level_refs[0][0] = sum((longest > level).astype(jnp.int32) for level in within)
    longest = jnp.max(jnp.where(line < lines, 0.0, far_rank + asks)).astype(jnp.int32)
    level_refs[1][0] = sum((longest > level).astype(jnp.int32) for level in across)
    me = lax.axis_index("rows")
    half, c = over(me, rows // 2), lax.axis_index("cols")

    def row(values, number):
        return jnp.sum(jnp.where(line == number, values, 0.0), axis=0, keepdims=True)

    here = (ids & -per) - half * part + row(near_rank, c).astype(jnp.int32)
    there = part + row(far_rank, lines * (1 + half) + c).astype(jnp.int32)
    place = jnp.where(over(ids, part) == half, here, there)
    chosen = jnp.zeros(places_ref.shape, jnp.float32)
    for group in groups:
        table, _, asked = read(group)
        lane = lax.broadcasted_iota(jnp.int32, table.shape, 1)
        places = jnp.zeros(table.shape, jnp.int32)
        for s in range(slots):
            found = jnp.sum(jnp.where(asked[s], place, 0), axis=1, keepdims=True)
            places = jnp.where(lane == s, found, places)
        shape = (places_ref.shape[0], len(group))
        number = lax.broadcasted_iota(jnp.int32, shape, 0)
        device = lax.broadcasted_iota(jnp.int32, shape, 1) + group.start
        reads = functools.reduce(
            jnp.logical_or,
            [(number == i) & (device == (me ^ d) * cols + c) for i, d in enumerate(distances(shape[0]))],
        )
        chosen += jnp.dot(
            jnp.where(reads, 1.0, 0.0).astype(jnp.bfloat16),
            places.astype(jnp.float32).astype(jnp.bfloat16),
            preferred_element_type=jnp.float32,
        )
    places_ref[...] = chosen.astype(jnp.int32)
    line = lax.broadcasted_iota(jnp.int32, (panel, 3 * lines), 1)

    def column(values, number):
        return jnp.sum(jnp.where(line == number, values, 0.0), axis=1, keepdims=True)

    turned, near_rank, far_rank = ranks(same, short), ranks(near, short), ranks(after, short)
    ids = lax.broadcasted_iota(jnp.int32, (panel, 1), 0)
    number = lax.broadcasted_iota(jnp.int32, (panel, lists_ref.shape[1]), 1)
    near_rank = column(near_rank, c).astype(jnp.int32)
    here = (ids & -per) - half * part + near_rank
    other = lines * (2 - half) + c
    sent = (column(turned, other) > 0.5) & (column(far_rank, other).astype(jnp.int32) == number)
    sent = jnp.sum(jnp.where(sent, here, 0), axis=0, keepdims=True)
    kept = (column(turned, c) > 0.5) & (over(ids, per) == me) & (near_rank == number)
    kept = jnp.sum(jnp.where(kept, ids & (per - 1), 0), axis=0, keepdims=True)
    lists_ref[...] = jnp.where(lax.broadcasted_iota(jnp.int32, lists_ref.shape, 0) == 0, sent, kept)


def plan(table, slots, per, within, across):
    devices = table.shape[0]
    return pl.pallas_call(
        functools.partial(plan_kernel, slots, per, within, across),
        out_shape=(
            jax.ShapeDtypeStruct((lax.axis_size("rows") // 2, 128), jnp.int32),
            jax.ShapeDtypeStruct((8, 128), jnp.int32),
            jax.ShapeDtypeStruct((1,), jnp.int32),
            jax.ShapeDtypeStruct((1,), jnp.int32),
        ),
        in_specs=[VMEM],
        out_specs=(VMEM, VMEM, SMEM, SMEM),
        compiler_params=pltpu.CompilerParams(vmem_limit_bytes=48 * MIB),
        name="plan",
    )(table)


def distances(members):
    order = [0]
    for near in sorted(range(1, members), key=lambda d: (d.bit_count(), d)):
        far = (members - 1) ^ near
        if near not in order and far:
            order += [near, far]
    return [*order[:-2], members - 1, *order[-2:]] if members > 2 else list(range(members))


def turn_kernel(sketch_ref, out_ref):
    members = out_ref.shape[0]
    me = lax.axis_index("rows") % members
    for i, d in enumerate(distances(members)):
        out_ref[i] = sketch_ref[:, me ^ d]


def turn(sketch):
    blocks, members, height, columns = sketch.shape
    return pl.pallas_call(
        turn_kernel,
        out_shape=jax.ShapeDtypeStruct((members, blocks, height, columns), sketch.dtype),
        in_specs=[VMEM],
        out_specs=VMEM,
        compiler_params=pltpu.CompilerParams(vmem_limit_bytes=24 * MIB),
        cost_estimate=pl.CostEstimate(flops=0, bytes_accessed=4 * sketch.size, transcendentals=0),
        name="turn_stripes",
    )(sketch)


def cut_kernel(lists_ref, stripes_ref, *out_refs):
    for k in range(out_refs[0].shape[0]):
        for i, out_ref in enumerate(out_refs):
            out_ref[k] = stripes_ref[i, lists_ref[1, k]]


def cut(lists, stripes, count):
    members, _, height, columns = stripes.shape
    return pl.pallas_call(
        cut_kernel,
        out_shape=(jax.ShapeDtypeStruct((count, height, columns), stripes.dtype),) * members,
        in_specs=[SMEM, VMEM],
        out_specs=(VMEM,) * members,
        compiler_params=pltpu.CompilerParams(vmem_limit_bytes=24 * MIB),
        name="cut_stripes",
    )(lists, stripes)


def order_kernel(*refs):
    *stripe_refs, all_ref = refs
    members = len(stripe_refs)
    me = lax.axis_index("rows") % members
    per = all_ref.shape[0] // members
    for ref, d in zip(stripe_refs, distances(members)):
        all_ref[pl.ds((me ^ d) * per, ref.shape[0])] = ref[...]


def order(stripes, per):
    _, height, columns = stripes[0].shape
    return pl.pallas_call(
        order_kernel,
        out_shape=jax.ShapeDtypeStruct((len(stripes) * per, height, columns), stripes[0].dtype),
        in_specs=[VMEM] * len(stripes),
        out_specs=VMEM,
        compiler_params=pltpu.CompilerParams(vmem_limit_bytes=24 * MIB),
        name="order_stripes",
    )(*stripes)


def list_kernel(list_ref, all_ref, out_ref):
    for k in range(out_ref.shape[0]):
        out_ref[k] = all_ref[list_ref[0, k]]


def listed(numbers, stripes, count):
    return pl.pallas_call(
        list_kernel,
        out_shape=jax.ShapeDtypeStruct((count, *stripes.shape[1:]), stripes.dtype),
        in_specs=[SMEM, VMEM],
        out_specs=VMEM,
        compiler_params=pltpu.CompilerParams(vmem_limit_bytes=24 * MIB),
        name="listed_stripes",
    )(numbers, stripes)


def pick_kernel(places_ref, own_ref, other_ref, *refs):
    *out_refs, whole = refs
    here = own_ref.shape[0]
    whole[:here] = own_ref[...]
    whole[here:] = other_ref[...]
    for i, out_ref in enumerate(out_refs):
        for s in range(out_ref.shape[0]):
            out_ref[s] = whole[jnp.minimum(places_ref[i, s], whole.shape[0] - 1)]


def pick(places, own, other, slots, members):
    shape = own.shape[1:]
    return pl.pallas_call(
        pick_kernel,
        out_shape=(jax.ShapeDtypeStruct((slots, *shape), own.dtype),) * members,
        in_specs=[SMEM, VMEM, VMEM],
        out_specs=(VMEM,) * members,
        scratch_shapes=[pltpu.VMEM((own.shape[0] + other.shape[0], *shape), own.dtype)],
        compiler_params=pltpu.CompilerParams(vmem_limit_bytes=24 * MIB),
        name="pick_stripes",
    )(places, own, other)


def product_kernel(rows_ref, counts_ref, blocks_ref, *refs):
    *chosen_refs, out_ref, whole = refs
    slots, width, _ = blocks_ref.shape
    columns = out_ref.shape[1]
    members = len(chosen_refs)
    me = lax.axis_index("rows") % members
    for ref, d in zip(chosen_refs, distances(members) if members > 1 else [0]):
        whole[me ^ d] = ref[...]
    out_ref[...] = jnp.zeros_like(out_ref)
    for s in range(slots):
        piece = whole[:, s].reshape(width, columns)
        product = jnp.dot(blocks_ref[s], piece, preferred_element_type=jnp.float32)
        at = pl.ds(pl.multiple_of(rows_ref[s] * width, width), width)
        out_ref[at, :] += jnp.where(s < counts_ref[0], product, 0.0)


def block_products(block_rows, counts, blocks, chosen):
    _, width, _ = blocks.shape
    columns = chosen[0].shape[-1]
    return pl.pallas_call(
        product_kernel,
        out_shape=jax.ShapeDtypeStruct((RB * width, columns), jnp.float32),
        in_specs=[SMEM, SMEM, VMEM] + [VMEM] * len(chosen),
        out_specs=VMEM,
        scratch_shapes=[pltpu.VMEM((len(chosen), *chosen[0].shape), chosen[0].dtype)],
        compiler_params=pltpu.CompilerParams(vmem_limit_bytes=24 * MIB),
        name="block_products",
    )(block_rows, counts, blocks, *chosen)


def gram_kernel(mine_ref, other_ref, own_ref, *refs):
    *gram_refs, slab = refs
    c = lax.axis_index("cols")
    me = lax.axis_index("rows") % len(gram_refs)
    share, (height, width) = own_ref.shape[0], gram_refs[0].shape
    slab[...] = mine_ref[...] + other_ref[...]
    own_ref[...] = slab[pl.ds(pl.multiple_of(c * share, share), share), :]
    right = slab[:, pl.ds(pl.multiple_of(c * width, width), width)]
    gram = lax.dot_general(
        slab[...], right, (((0,), (0,)), ((), ())), precision=HIGHEST, preferred_element_type=jnp.float32
    )
    for q in range(len(gram_refs)):
        for d in range(len(gram_refs)):

            @pl.when(me ^ d == q)
            def _():
                gram_refs[d][...] = gram[q * height : (q + 1) * height]


def sum_and_gram(mine, other):
    rows, columns = mine.shape
    return pl.pallas_call(
        gram_kernel,
        out_shape=(
            jax.ShapeDtypeStruct((rows // 2, columns), jnp.float32),
            *[jax.ShapeDtypeStruct((columns // 4, columns // 2), jnp.float32)] * 4,
        ),
        in_specs=[VMEM, VMEM],
        out_specs=(VMEM,) * 5,
        scratch_shapes=[pltpu.VMEM((rows, columns), jnp.float32)],
        compiler_params=pltpu.CompilerParams(vmem_limit_bytes=24 * MIB),
        name="sum_and_gram",
    )(mine, other)


def add_kernel(*refs):
    *piece_refs, out_ref = refs
    out_ref[...] = functools.reduce(jnp.add, [ref[...] for ref in piece_refs])


def add(pieces):
    return pl.pallas_call(
        add_kernel,
        out_shape=jax.ShapeDtypeStruct(pieces[0].shape, jnp.float32),
        in_specs=[VMEM] * len(pieces),
        out_specs=VMEM,
        compiler_params=pltpu.CompilerParams(vmem_limit_bytes=24 * MIB),
        name="add_pieces",
    )(*pieces)


def stack_kernel(*refs):
    *quarter_refs, out_ref = refs
    me = lax.axis_index("rows") % len(quarter_refs)
    height = quarter_refs[0].shape[0]
    for d, ref in enumerate(quarter_refs):
        out_ref[pl.ds(pl.multiple_of((me ^ d) * height, height), height), :] = ref[...]


def stack(quarters):
    height, width = quarters[0].shape
    return pl.pallas_call(
        stack_kernel,
        out_shape=jax.ShapeDtypeStruct((len(quarters) * height, width), jnp.float32),
        in_specs=[VMEM] * len(quarters),
        out_specs=VMEM,
        compiler_params=pltpu.CompilerParams(vmem_limit_bytes=24 * MIB),
        name="stack_quarters",
    )(*quarters)


def matmul(a, b, precision):
    return jnp.dot(a, b, precision=precision, preferred_element_type=jnp.float32)


def matmul_nt(a, b, precision):
    return lax.dot_general(
        a, b, (((1,), (1,)), ((), ())), precision=precision, preferred_element_type=jnp.float32
    )


def split_matmul(times, passes, a, b):
    a_high, b_high = a.astype(jnp.bfloat16), b.astype(jnp.bfloat16)
    result = times(a_high, b_high, None)
    if passes == 3:
        a_low = (a - a_high.astype(jnp.float32)).astype(jnp.bfloat16)
        b_low = (b - b_high.astype(jnp.float32)).astype(jnp.bfloat16)
        result += times(a_high, b_low, None) + times(a_low, b_high, None)
    return result


def factor_kernel(total_rows, *refs):
    *gram_refs, own_ref, basis_ref, factor_ref, whole, scaled, inverse, product = refs
    n = factor_ref.shape[0]
    if len(gram_refs) == 1:
        whole[...] = gram_refs[0][...]
    else:
        c = lax.axis_index("cols")
        width = n // 2
        whole[:, pl.ds(pl.multiple_of(c * width, width), width)] = gram_refs[0][...]
        whole[:, pl.ds(pl.multiple_of((1 - c) * width, width), width)] = gram_refs[1][...]
    row_ids = lax.broadcasted_iota(jnp.int32, (n, n), 0)
    col_ids = lax.broadcasted_iota(jnp.int32, (n, n), 1)
    diagonal = row_ids == col_ids
    identity = diagonal.astype(jnp.float32)
    half = jnp.where(row_ids > col_ids, 1.0, jnp.where(diagonal, 0.5, 0.0))
    gram = whole[...]
    on_diagonal = jnp.where(diagonal, gram, 0.0)
    down = jnp.sqrt(jnp.sum(on_diagonal, axis=1, keepdims=True))
    across = jnp.sqrt(jnp.sum(on_diagonal, axis=0, keepdims=True))
    up_down = 1.0 / down
    up_across = 1.0 / across
    scaled[...] = gram * up_down * up_across

    def refine(times, times_nt, last=False):
        w = inverse[...]
        upper = times(w, scaled[...])
        residual = times_nt(upper, w) - identity
        step = residual * half
        inverse[...] = w - matmul(step, w, lax.Precision.DEFAULT)
        if last:
            product[...] = upper - matmul(step, upper, lax.Precision.DEFAULT)
        return jnp.sum(residual * residual)

    def exactly(times):
        return functools.partial(times, precision=HIGHEST)

    inverse[...] = identity - (scaled[...] - identity) * half
    for passes in (1, 3):
        refine(functools.partial(split_matmul, matmul, passes), functools.partial(split_matmul, matmul_nt, passes))

    def going(state):
        step, size = state
        return (step < 8) & (size > 1e-6)

    def advance(state):
        return state[0] + 1, refine(exactly(matmul), exactly(matmul_nt), last=True)

    _, size = lax.while_loop(going, advance, (jnp.int32(0), jnp.float32(1.0)))

    @pl.when(jnp.logical_not(size <= 1e-6))
    def _():
        inverse[...] = identity
        ids = lax.broadcasted_iota(jnp.int32, (n, 1), 0)

        def eliminate(j, carry):
            pivot_row = scaled[pl.ds(j, 1), :]
            inverse_row = inverse[pl.ds(j, 1), :]
            column = jnp.sum(jnp.where(col_ids == j, scaled[...], 0.0), axis=1, keepdims=True)
            pivot = jnp.sum(jnp.where(ids == j, column, 0.0), axis=0, keepdims=True)
            root = 1.0 / jnp.sqrt(pivot)
            ratio = jnp.where(ids > j, column / pivot, jnp.where(ids == j, 1.0 - root, 0.0))
            scaled[...] = scaled[...] - ratio * pivot_row
            inverse[...] = inverse[...] - ratio * inverse_row
            return carry

        lax.fori_loop(0, n, eliminate, 0)
        product[...] = matmul(inverse[...], whole[...] * up_down * up_across, HIGHEST)

    w = inverse[...]
    root_rows = jnp.sqrt(jnp.float32(total_rows))
    upper = product[...] * across / root_rows
    factor_ref[...] = jnp.where(row_ids <= col_ids, upper, 0.0)
    basis_ref[...] = matmul_nt(own_ref[...] * up_across, w, HIGHEST) * root_rows


def factor_and_basis(total_rows, grams, own):
    columns = own.shape[1]
    return pl.pallas_call(
        functools.partial(factor_kernel, total_rows),
        out_shape=(
            jax.ShapeDtypeStruct(own.shape, jnp.float32),
            jax.ShapeDtypeStruct((columns, columns), jnp.float32),
        ),
        in_specs=[VMEM] * (len(grams) + 1),
        out_specs=(VMEM, VMEM),
        scratch_shapes=[pltpu.VMEM((columns, columns), jnp.float32)] * 4,
        compiler_params=pltpu.CompilerParams(vmem_limit_bytes=24 * MIB),
        name="factor_and_basis",
    )(*grams, own)


def exchange(pieces, rows):
    order = distances(len(pieces))
    return [
        lax.ppermute(piece, "rows", [(r, r ^ d) for r in range(rows)]) if d else piece
        for piece, d in zip(pieces, order)
    ]


def fetch(sketch, block_cols, counts, slots, width):
    rows, cols = lax.axis_size("rows"), lax.axis_size("cols")
    members = rows // 2
    height = width // members
    columns = sketch.shape[1]
    sketch = sketch.reshape(-1, members, height, columns)
    per = sketch.shape[0]
    largest = min(per * members, slots * members, 128)
    within = tuple(level for level in WITHIN if level < per)
    across = tuple(level for level in ACROSS if level < largest and members <= 8)
    stripes = turn(sketch)
    table = table_copies(block_cols, counts, rows * cols)
    table = lax.all_to_all(table, ("rows", "cols"), split_axis=0, concat_axis=0, tiled=True)
    places, lists, near, far = plan(table, slots, per, within, across)

    def within_half(count):
        def run():
            return order(exchange(cut(lists, stripes, count), rows), per)

        return run

    own = lax.switch(near[0], [within_half(count) for count in (*within, per)])

    def across_halves(count):
        def run():
            swap = [(r, (r + members) % rows) for r in range(rows)]
            other = lax.ppermute(listed(lists, own, count), "rows", swap)
            return pick(places, own, other, slots, members)

        return run

    picked = lax.switch(far[0], [across_halves(count) for count in (*across, largest)])
    return exchange(picked, rows)


def moved(piece, rows, d):
    return lax.ppermute(piece, "rows", [(r, r ^ d) for r in range(rows)])


def gram_halves(quarters, rows):
    first = add([quarters[0]] + [moved(quarters[d], rows, d) for d in (3, 1, 2)])
    total = (first + moved(first, rows, 4)) + (moved(first, rows, 8) + moved(first, rows, 12))
    half = stack([total] + [moved(total, rows, d) for d in range(1, 4)])
    return half, lax.ppermute(half, "cols", [(0, 1), (1, 0)])


def local(sketch, blocks, block_rows, block_cols, counts):
    slots, width, _ = blocks.shape
    columns = sketch.shape[1]
    rows, cols = lax.axis_size("rows"), lax.axis_size("cols")
    chosen = fetch(sketch, block_cols, counts, slots, width)
    if chosen[0].shape[1] % 16:
        order = jnp.argsort(lax.axis_index("rows") % len(chosen) ^ jnp.array(distances(len(chosen))))
        chosen = [jnp.stack(chosen)[order].swapaxes(0, 1).reshape(1, slots, width, columns)[0]]
    partial_rows = block_products(block_rows, counts, blocks, chosen)
    if (rows, cols) == (16, 2):
        other = lax.ppermute(partial_rows, "cols", [(0, 1), (1, 0)])
        own, *quarters = sum_and_gram(partial_rows, other)
        grams = gram_halves(quarters, rows)
    else:
        own = lax.psum_scatter(partial_rows, "cols", scatter_dimension=0, tiled=True)
        grams = [lax.psum(matmul(own.T, own, HIGHEST), ("rows", "cols"))]
    return factor_and_basis(RB * width * rows, grams, own)


def solution(mesh):
    in_specs = (
        P(("rows", "cols"), None),
        P(("rows", "cols"), None, None),
        P(("rows", "cols")),
        P(("rows", "cols")),
        P(("rows", "cols")),
    )
    out_specs = (P(("rows", "cols"), None), P())
    return jax.shard_map(local, mesh=mesh, in_specs=in_specs, out_specs=out_specs, check_vma=False)
```

```python
import functools

import jax
import jax.numpy as jnp
from jax import lax
from jax.experimental import pallas as pl
from jax.experimental.pallas import tpu as pltpu
from jax.sharding import PartitionSpec as P

RB = 4
HIGHEST = lax.Precision.HIGHEST
VMEM = pl.BlockSpec(memory_space=pltpu.VMEM)
SMEM = pl.BlockSpec(memory_space=pltpu.SMEM)
MIB = 1024 * 1024


ACROSS = (*range(11, 21), 22, 24, 28, 36)
WITHIN = (5, 6, 7, 8, 9, 10, 12)


def table_kernel(cols_ref, counts_ref, out_ref):
    slots = cols_ref.shape[0]
    lane = lax.broadcasted_iota(jnp.int32, out_ref.shape, 2)
    table = jnp.where(lane == slots, counts_ref[0], 0)
    for s in range(slots):
        table = jnp.where(lane == s, cols_ref[s], table)
    out_ref[...] = table


def table_copies(block_cols, counts, devices):
    return pl.pallas_call(
        table_kernel,
        out_shape=jax.ShapeDtypeStruct((devices, 1, 128), jnp.int32),
        in_specs=[SMEM, SMEM],
        out_specs=VMEM,
        name="table_copies",
    )(block_cols, counts)


def over(values, size):
    return values >> (size.bit_length() - 1)


def plan_kernel(slots, per, within, across, table_ref, places_ref, lists_ref, *level_refs):
    devices = table_ref.shape[0]
    rows, cols = lax.axis_size("rows"), lax.axis_size("cols")
    panel = per * rows
    part = panel // 2
    groups = [range(at, min(at + 64, devices)) for at in range(0, devices, 64)]

    def read(group):
        table = table_ref[group.start : group.stop, 0, :]
        lane = lax.broadcasted_iota(jnp.int32, table.shape, 1)
        counts = table[:, slots : slots + 1]
        table = jnp.where(lane < counts, table, -1)
        block = lax.broadcasted_iota(jnp.int32, (len(group), panel), 1)
        return table, counts, [table[:, s : s + 1] == block for s in range(slots)]

    lines = -(-cols // 8) * 8
    line = lax.broadcasted_iota(jnp.int32, (3 * lines, panel), 0)
    ids = lax.broadcasted_iota(jnp.int32, (1, panel), 1)
    asks = jnp.zeros((3 * lines, panel), jnp.float32)
    for group in groups:
        _, _, asked = read(group)
        some = jnp.where(functools.reduce(jnp.logical_or, asked), 1.0, 0.0).astype(jnp.bfloat16)
        shape = (3 * lines, len(group))
        number = lax.broadcasted_iota(jnp.int32, shape, 0)
        device = lax.broadcasted_iota(jnp.int32, shape, 1) + group.start
        core, side = device & (cols - 1), over(device, devices // 2)
        reads = (number == core) | (number == lines * (1 + side) + core)
        asks += jnp.dot(jnp.where(reads, 1.0, 0.0).astype(jnp.bfloat16), some, preferred_element_type=jnp.float32)
    own_half = (line >= lines) & (over(line - lines, lines) == over(lax.broadcasted_iota(jnp.int32, line.shape, 1), part))
    asks = jnp.where((asks > 0.5) & jnp.logical_not(own_half), 1.0, 0.0)
    first = lax.broadcasted_iota(jnp.int32, (panel, panel), 0)
    second = lax.broadcasted_iota(jnp.int32, (panel, panel), 1)
    after = first > second
    near = jnp.where(after & ((first ^ second) < per), 1.0, 0.0).astype(jnp.bfloat16)
    after = jnp.where(after, 1.0, 0.0).astype(jnp.bfloat16)
    same = jnp.where(first == second, 1.0, 0.0).astype(jnp.bfloat16)
    nt = (((1,), (1,)), ((), ()))

    def ranks(a, b):
        return lax.dot_general(a, b, nt, preferred_element_type=jnp.float32)

    short = asks.astype(jnp.bfloat16)
    near_rank = ranks(short, near)
    far_rank = ranks(short, after)
    longest = jnp.max(jnp.where(line < lines, near_rank + asks, 0.0)).astype(jnp.int32)
    level_refs[0][0] = sum((longest > level).astype(jnp.int32) for level in within)
    longest = jnp.max(jnp.where(line < lines, 0.0, far_rank + asks)).astype(jnp.int32)
    level_refs[1][0] = sum((longest > level).astype(jnp.int32) for level in across)
    me = lax.axis_index("rows")
    half, c = over(me, rows // 2), lax.axis_index("cols")

    def row(values, number):
        return jnp.sum(jnp.where(line == number, values, 0.0), axis=0, keepdims=True)

    here = (ids & -per) - half * part + row(near_rank, c).astype(jnp.int32)
    there = part + row(far_rank, lines * (1 + half) + c).astype(jnp.int32)
    place = jnp.where(over(ids, part) == half, here, there)
    chosen = jnp.zeros(places_ref.shape, jnp.float32)
    for group in groups:
        table, _, asked = read(group)
        lane = lax.broadcasted_iota(jnp.int32, table.shape, 1)
        places = jnp.zeros(table.shape, jnp.int32)
        for s in range(slots):
            found = jnp.sum(jnp.where(asked[s], place, 0), axis=1, keepdims=True)
            places = jnp.where(lane == s, found, places)
        shape = (places_ref.shape[0], len(group))
        number = lax.broadcasted_iota(jnp.int32, shape, 0)
        device = lax.broadcasted_iota(jnp.int32, shape, 1) + group.start
        reads = functools.reduce(
            jnp.logical_or,
            [(number == i) & (device == (me ^ d) * cols + c) for i, d in enumerate(distances(shape[0]))],
        )
        chosen += jnp.dot(
            jnp.where(reads, 1.0, 0.0).astype(jnp.bfloat16),
            places.astype(jnp.float32).astype(jnp.bfloat16),
            preferred_element_type=jnp.float32,
        )
    places_ref[...] = chosen.astype(jnp.int32)
    line = lax.broadcasted_iota(jnp.int32, (panel, 3 * lines), 1)

    def column(values, number):
        return jnp.sum(jnp.where(line == number, values, 0.0), axis=1, keepdims=True)

    turned, near_rank, far_rank = ranks(same, short), ranks(near, short), ranks(after, short)
    ids = lax.broadcasted_iota(jnp.int32, (panel, 1), 0)
    number = lax.broadcasted_iota(jnp.int32, (panel, lists_ref.shape[1]), 1)
    near_rank = column(near_rank, c).astype(jnp.int32)
    here = (ids & -per) - half * part + near_rank
    other = lines * (2 - half) + c
    sent = (column(turned, other) > 0.5) & (column(far_rank, other).astype(jnp.int32) == number)
    sent = jnp.sum(jnp.where(sent, here, 0), axis=0, keepdims=True)
    kept = (column(turned, c) > 0.5) & (over(ids, per) == me) & (near_rank == number)
    kept = jnp.sum(jnp.where(kept, ids & (per - 1), 0), axis=0, keepdims=True)
    lists_ref[...] = jnp.where(lax.broadcasted_iota(jnp.int32, lists_ref.shape, 0) == 0, sent, kept)


def plan(table, slots, per, within, across):
    devices = table.shape[0]
    return pl.pallas_call(
        functools.partial(plan_kernel, slots, per, within, across),
        out_shape=(
            jax.ShapeDtypeStruct((lax.axis_size("rows") // 2, 128), jnp.int32),
            jax.ShapeDtypeStruct((8, 128), jnp.int32),
            jax.ShapeDtypeStruct((1,), jnp.int32),
            jax.ShapeDtypeStruct((1,), jnp.int32),
        ),
        in_specs=[VMEM],
        out_specs=(VMEM, VMEM, SMEM, SMEM),
        compiler_params=pltpu.CompilerParams(vmem_limit_bytes=(16 if devices <= 64 else 48) * MIB),
        name="plan",
    )(table)


def distances(members):
    order = [0]
    for near in sorted(range(1, members), key=lambda d: (d.bit_count(), d)):
        far = (members - 1) ^ near
        if near not in order and far:
            order += [near, far]
    return [*order[:-2], members - 1, *order[-2:]] if members > 2 else list(range(members))


def turn_kernel(sketch_ref, out_ref):
    members = out_ref.shape[0]
    me = lax.axis_index("rows") % members
    for i, d in enumerate(distances(members)):
        out_ref[i] = sketch_ref[:, me ^ d]


def turn(sketch):
    blocks, members, height, columns = sketch.shape
    return pl.pallas_call(
        turn_kernel,
        out_shape=jax.ShapeDtypeStruct((members, blocks, height, columns), sketch.dtype),
        in_specs=[VMEM],
        out_specs=VMEM,
        compiler_params=pltpu.CompilerParams(vmem_limit_bytes=10 * MIB),
        cost_estimate=pl.CostEstimate(flops=0, bytes_accessed=4 * sketch.size, transcendentals=0),
        name="turn_stripes",
    )(sketch)


def cut_kernel(lists_ref, stripes_ref, *out_refs):
    for k in range(out_refs[0].shape[0]):
        for i, out_ref in enumerate(out_refs):
            out_ref[k] = stripes_ref[i, lists_ref[1, k]]


def cut(lists, stripes, count):
    members, _, height, columns = stripes.shape
    return pl.pallas_call(
        cut_kernel,
        out_shape=(jax.ShapeDtypeStruct((count, height, columns), stripes.dtype),) * members,
        in_specs=[SMEM, VMEM],
        out_specs=(VMEM,) * members,
        compiler_params=pltpu.CompilerParams(vmem_limit_bytes=10 * MIB),
        name="cut_stripes",
    )(lists, stripes)


def order_kernel(*refs):
    *stripe_refs, all_ref = refs
    members = len(stripe_refs)
    me = lax.axis_index("rows") % members
    per = all_ref.shape[0] // members
    for ref, d in zip(stripe_refs, distances(members)):
        all_ref[pl.ds((me ^ d) * per, ref.shape[0])] = ref[...]


def order(stripes, per):
    _, height, columns = stripes[0].shape
    return pl.pallas_call(
        order_kernel,
        out_shape=jax.ShapeDtypeStruct((len(stripes) * per, height, columns), stripes[0].dtype),
        in_specs=[VMEM] * len(stripes),
        out_specs=VMEM,
        compiler_params=pltpu.CompilerParams(vmem_limit_bytes=10 * MIB),
        name="order_stripes",
    )(*stripes)


def list_kernel(list_ref, all_ref, out_ref):
    for k in range(out_ref.shape[0]):
        out_ref[k] = all_ref[list_ref[0, k]]


def listed(numbers, stripes, count):
    return pl.pallas_call(
        list_kernel,
        out_shape=jax.ShapeDtypeStruct((count, *stripes.shape[1:]), stripes.dtype),
        in_specs=[SMEM, VMEM],
        out_specs=VMEM,
        compiler_params=pltpu.CompilerParams(vmem_limit_bytes=10 * MIB),
        name="listed_stripes",
    )(numbers, stripes)


def pick_kernel(places_ref, own_ref, other_ref, *refs):
    *out_refs, whole = refs
    here = own_ref.shape[0]
    whole[:here] = own_ref[...]
    whole[here:] = other_ref[...]
    for i, out_ref in enumerate(out_refs):
        for s in range(out_ref.shape[0]):
            out_ref[s] = whole[jnp.minimum(places_ref[i, s], whole.shape[0] - 1)]


def pick(places, own, other, slots, members):
    shape = own.shape[1:]
    return pl.pallas_call(
        pick_kernel,
        out_shape=(jax.ShapeDtypeStruct((slots, *shape), own.dtype),) * members,
        in_specs=[SMEM, VMEM, VMEM],
        out_specs=(VMEM,) * members,
        scratch_shapes=[pltpu.VMEM((own.shape[0] + other.shape[0], *shape), own.dtype)],
        compiler_params=pltpu.CompilerParams(vmem_limit_bytes=10 * MIB),
        name="pick_stripes",
    )(places, own, other)


def product_kernel(rows_ref, counts_ref, blocks_ref, *refs):
    *chosen_refs, out_ref, whole = refs
    slots, width, _ = blocks_ref.shape
    columns = out_ref.shape[1]
    members = len(chosen_refs)
    me = lax.axis_index("rows") % members
    for ref, d in zip(chosen_refs, distances(members) if members > 1 else [0]):
        whole[me ^ d] = ref[...]
    out_ref[...] = jnp.zeros_like(out_ref)
    for s in range(slots):
        piece = whole[:, s].reshape(width, columns)
        product = jnp.dot(blocks_ref[s], piece, preferred_element_type=jnp.float32)
        at = pl.ds(pl.multiple_of(rows_ref[s] * width, width), width)
        out_ref[at, :] += jnp.where(s < counts_ref[0], product, 0.0)


def block_products(block_rows, counts, blocks, chosen):
    _, width, _ = blocks.shape
    columns = chosen[0].shape[-1]
    return pl.pallas_call(
        product_kernel,
        out_shape=jax.ShapeDtypeStruct((RB * width, columns), jnp.float32),
        in_specs=[SMEM, SMEM, VMEM] + [VMEM] * len(chosen),
        out_specs=VMEM,
        scratch_shapes=[pltpu.VMEM((len(chosen), *chosen[0].shape), chosen[0].dtype)],
        compiler_params=pltpu.CompilerParams(vmem_limit_bytes=10 * MIB),
        name="block_products",
    )(block_rows, counts, blocks, *chosen)


def gram_kernel(mine_ref, other_ref, own_ref, *refs):
    *gram_refs, slab = refs
    c = lax.axis_index("cols")
    me = lax.axis_index("rows") % len(gram_refs)
    share, (height, width) = own_ref.shape[0], gram_refs[0].shape
    slab[...] = mine_ref[...] + other_ref[...]
    own_ref[...] = slab[pl.ds(pl.multiple_of(c * share, share), share), :]
    right = slab[:, pl.ds(pl.multiple_of(c * width, width), width)]
    gram = lax.dot_general(
        slab[...], right, (((0,), (0,)), ((), ())), precision=HIGHEST, preferred_element_type=jnp.float32
    )
    for q in range(len(gram_refs)):
        for d in range(len(gram_refs)):

            @pl.when(me ^ d == q)
            def _():
                gram_refs[d][...] = gram[q * height : (q + 1) * height]


def sum_and_gram(mine, other):
    rows, columns = mine.shape
    return pl.pallas_call(
        gram_kernel,
        out_shape=(
            jax.ShapeDtypeStruct((rows // 2, columns), jnp.float32),
            *[jax.ShapeDtypeStruct((columns // 4, columns // 2), jnp.float32)] * 4,
        ),
        in_specs=[VMEM, VMEM],
        out_specs=(VMEM,) * 5,
        scratch_shapes=[pltpu.VMEM((rows, columns), jnp.float32)],
        compiler_params=pltpu.CompilerParams(vmem_limit_bytes=10 * MIB),
        name="sum_and_gram",
    )(mine, other)


def add_kernel(*refs):
    *piece_refs, out_ref = refs
    out_ref[...] = functools.reduce(jnp.add, [ref[...] for ref in piece_refs])


def add(pieces):
    return pl.pallas_call(
        add_kernel,
        out_shape=jax.ShapeDtypeStruct(pieces[0].shape, jnp.float32),
        in_specs=[VMEM] * len(pieces),
        out_specs=VMEM,
        compiler_params=pltpu.CompilerParams(vmem_limit_bytes=10 * MIB),
        name="add_pieces",
    )(*pieces)


def stack_kernel(*refs):
    *quarter_refs, out_ref = refs
    me = lax.axis_index("rows") % len(quarter_refs)
    height = quarter_refs[0].shape[0]
    for d, ref in enumerate(quarter_refs):
        out_ref[pl.ds(pl.multiple_of((me ^ d) * height, height), height), :] = ref[...]


def stack(quarters):
    height, width = quarters[0].shape
    return pl.pallas_call(
        stack_kernel,
        out_shape=jax.ShapeDtypeStruct((len(quarters) * height, width), jnp.float32),
        in_specs=[VMEM] * len(quarters),
        out_specs=VMEM,
        compiler_params=pltpu.CompilerParams(vmem_limit_bytes=10 * MIB),
        name="stack_quarters",
    )(*quarters)


def matmul(a, b, precision):
    return jnp.dot(a, b, precision=precision, preferred_element_type=jnp.float32)


def matmul_nt(a, b, precision):
    return lax.dot_general(
        a, b, (((1,), (1,)), ((), ())), precision=precision, preferred_element_type=jnp.float32
    )


def split_matmul(times, passes, a, b):
    a_high, b_high = a.astype(jnp.bfloat16), b.astype(jnp.bfloat16)
    result = times(a_high, b_high, None)
    if passes == 3:
        a_low = (a - a_high.astype(jnp.float32)).astype(jnp.bfloat16)
        b_low = (b - b_high.astype(jnp.float32)).astype(jnp.bfloat16)
        result += times(a_high, b_low, None) + times(a_low, b_high, None)
    return result


def factor_kernel(total_rows, *refs):
    *gram_refs, own_ref, basis_ref, factor_ref, whole, scaled, inverse, product = refs
    n = factor_ref.shape[0]
    if len(gram_refs) == 1:
        whole[...] = gram_refs[0][...]
    else:
        c = lax.axis_index("cols")
        width = n // 2
        whole[:, pl.ds(pl.multiple_of(c * width, width), width)] = gram_refs[0][...]
        whole[:, pl.ds(pl.multiple_of((1 - c) * width, width), width)] = gram_refs[1][...]
    row_ids = lax.broadcasted_iota(jnp.int32, (n, n), 0)
    col_ids = lax.broadcasted_iota(jnp.int32, (n, n), 1)
    diagonal = row_ids == col_ids
    identity = diagonal.astype(jnp.float32)
    half = jnp.where(row_ids > col_ids, 1.0, jnp.where(diagonal, 0.5, 0.0))
    gram = whole[...]
    on_diagonal = jnp.where(diagonal, gram, 0.0)
    down = jnp.sqrt(jnp.sum(on_diagonal, axis=1, keepdims=True))
    across = jnp.sqrt(jnp.sum(on_diagonal, axis=0, keepdims=True))
    up_down = 1.0 / down
    up_across = 1.0 / across
    scaled[...] = gram * up_down * up_across

    def refine(times, times_nt, last=False):
        w = inverse[...]
        upper = times(w, scaled[...])
        residual = times_nt(upper, w) - identity
        step = residual * half
        inverse[...] = w - matmul(step, w, lax.Precision.DEFAULT)
        if last:
            product[...] = upper - matmul(step, upper, lax.Precision.DEFAULT)
        return jnp.sum(residual * residual)

    def exactly(times):
        return functools.partial(times, precision=HIGHEST)

    inverse[...] = identity - (scaled[...] - identity) * half
    for passes in (1, 3):
        refine(functools.partial(split_matmul, matmul, passes), functools.partial(split_matmul, matmul_nt, passes))

    def going(state):
        step, size = state
        return (step < 8) & (size > 1e-6)

    def advance(state):
        return state[0] + 1, refine(exactly(matmul), exactly(matmul_nt), last=True)

    _, size = lax.while_loop(going, advance, (jnp.int32(0), jnp.float32(1.0)))

    @pl.when(jnp.logical_not(size <= 1e-6))
    def _():
        inverse[...] = identity
        ids = lax.broadcasted_iota(jnp.int32, (n, 1), 0)

        def eliminate(j, carry):
            pivot_row = scaled[pl.ds(j, 1), :]
            inverse_row = inverse[pl.ds(j, 1), :]
            column = jnp.sum(jnp.where(col_ids == j, scaled[...], 0.0), axis=1, keepdims=True)
            pivot = jnp.sum(jnp.where(ids == j, column, 0.0), axis=0, keepdims=True)
            root = 1.0 / jnp.sqrt(pivot)
            ratio = jnp.where(ids > j, column / pivot, jnp.where(ids == j, 1.0 - root, 0.0))
            scaled[...] = scaled[...] - ratio * pivot_row
            inverse[...] = inverse[...] - ratio * inverse_row
            return carry

        lax.fori_loop(0, n, eliminate, 0)
        product[...] = matmul(inverse[...], whole[...] * up_down * up_across, HIGHEST)

    w = inverse[...]
    root_rows = jnp.sqrt(jnp.float32(total_rows))
    upper = product[...] * across / root_rows
    factor_ref[...] = jnp.where(row_ids <= col_ids, upper, 0.0)
    basis_ref[...] = matmul_nt(own_ref[...] * up_across, w, HIGHEST) * root_rows


def factor_and_basis(total_rows, grams, own):
    columns = own.shape[1]
    return pl.pallas_call(
        functools.partial(factor_kernel, total_rows),
        out_shape=(
            jax.ShapeDtypeStruct(own.shape, jnp.float32),
            jax.ShapeDtypeStruct((columns, columns), jnp.float32),
        ),
        in_specs=[VMEM] * (len(grams) + 1),
        out_specs=(VMEM, VMEM),
        scratch_shapes=[pltpu.VMEM((columns, columns), jnp.float32)] * 4,
        compiler_params=pltpu.CompilerParams(vmem_limit_bytes=10 * MIB),
        name="factor_and_basis",
    )(*grams, own)


def exchange(pieces, rows):
    order = distances(len(pieces))
    return [
        lax.ppermute(piece, "rows", [(r, r ^ d) for r in range(rows)]) if d else piece
        for piece, d in zip(pieces, order)
    ]


def fetch(sketch, block_cols, counts, slots, width):
    rows, cols = lax.axis_size("rows"), lax.axis_size("cols")
    members = rows // 2
    height = width // members
    columns = sketch.shape[1]
    sketch = sketch.reshape(-1, members, height, columns)
    per = sketch.shape[0]
    largest = min(per * members, slots * members, 128)
    within = tuple(level for level in WITHIN if level < per)
    across = tuple(level for level in ACROSS if level < largest and members <= 8)
    stripes = turn(sketch)
    table = table_copies(block_cols, counts, rows * cols)
    table = lax.all_to_all(table, ("rows", "cols"), split_axis=0, concat_axis=0, tiled=True)
    places, lists, near, far = plan(table, slots, per, within, across)

    def within_half(count):
        def run():
            return order(exchange(cut(lists, stripes, count), rows), per)

        return run

    own = lax.switch(near[0], [within_half(count) for count in (*within, per)])

    def across_halves(count):
        def run():
            swap = [(r, (r + members) % rows) for r in range(rows)]
            other = lax.ppermute(listed(lists, own, count), "rows", swap)
            return pick(places, own, other, slots, members)

        return run

    picked = lax.switch(far[0], [across_halves(count) for count in (*across, largest)])
    return exchange(picked, rows)


def moved(piece, rows, d):
    return lax.ppermute(piece, "rows", [(r, r ^ d) for r in range(rows)])


def gram_halves(quarters, rows):
    first = add([quarters[0]] + [moved(quarters[d], rows, d) for d in (3, 1, 2)])
    total = (first + moved(first, rows, 4)) + (moved(first, rows, 8) + moved(first, rows, 12))
    half = stack([total] + [moved(total, rows, d) for d in range(1, 4)])
    return half, lax.ppermute(half, "cols", [(0, 1), (1, 0)])


def local(sketch, blocks, block_rows, block_cols, counts):
    slots, width, _ = blocks.shape
    columns = sketch.shape[1]
    rows, cols = lax.axis_size("rows"), lax.axis_size("cols")
    chosen = fetch(sketch, block_cols, counts, slots, width)
    if chosen[0].shape[1] % 16:
        order = jnp.argsort(lax.axis_index("rows") % len(chosen) ^ jnp.array(distances(len(chosen))))
        chosen = [jnp.stack(chosen)[order].swapaxes(0, 1).reshape(1, slots, width, columns)[0]]
    partial_rows = block_products(block_rows, counts, blocks, chosen)
    if (rows, cols) == (16, 2):
        other = lax.ppermute(partial_rows, "cols", [(0, 1), (1, 0)])
        own, *quarters = sum_and_gram(partial_rows, other)
        grams = gram_halves(quarters, rows)
    else:
        own = lax.psum_scatter(partial_rows, "cols", scatter_dimension=0, tiled=True)
        grams = [lax.psum(matmul(own.T, own, HIGHEST), ("rows", "cols"))]
    return factor_and_basis(RB * width * rows, grams, own)


def solution(mesh):
    in_specs = (
        P(("rows", "cols"), None),
        P(("rows", "cols"), None, None),
        P(("rows", "cols")),
        P(("rows", "cols")),
        P(("rows", "cols")),
    )
    out_specs = (P(("rows", "cols"), None), P())
    return jax.shard_map(local, mesh=mesh, in_specs=in_specs, out_specs=out_specs, check_vma=False)
```

```python
import functools

import jax
import jax.numpy as jnp
from jax import lax
from jax.experimental import pallas as pl
from jax.experimental.pallas import tpu as pltpu
from jax.sharding import PartitionSpec as P

RB = 4
HIGHEST = lax.Precision.HIGHEST
VMEM = pl.BlockSpec(memory_space=pltpu.VMEM)
SMEM = pl.BlockSpec(memory_space=pltpu.SMEM)
MIB = 1024 * 1024


ACROSS = (*range(11, 21), 22, 24, 28, 36)
WITHIN = (5, 6, 7, 8, 9, 10, 12)


def table_kernel(cols_ref, counts_ref, out_ref):
    slots = cols_ref.shape[0]
    lane = lax.broadcasted_iota(jnp.int32, out_ref.shape, 2)
    table = jnp.where(lane == slots, counts_ref[0], 0)
    for s in range(slots):
        table = jnp.where(lane == s, cols_ref[s], table)
    out_ref[...] = table


def table_copies(block_cols, counts, devices):
    return pl.pallas_call(
        table_kernel,
        out_shape=jax.ShapeDtypeStruct((devices, 1, 128), jnp.int32),
        in_specs=[SMEM, SMEM],
        out_specs=VMEM,
        name="table_copies",
    )(block_cols, counts)


def over(values, size):
    return values >> (size.bit_length() - 1)


def plan_kernel(slots, per, within, across, table_ref, places_ref, lists_ref, *level_refs):
    devices = table_ref.shape[0]
    rows, cols = lax.axis_size("rows"), lax.axis_size("cols")
    panel = per * rows
    part = panel // 2
    groups = [range(at, min(at + 64, devices)) for at in range(0, devices, 64)]

    def read(group):
        table = table_ref[group.start : group.stop, 0, :]
        lane = lax.broadcasted_iota(jnp.int32, table.shape, 1)
        counts = table[:, slots : slots + 1]
        table = jnp.where(lane < counts, table, -1)
        block = lax.broadcasted_iota(jnp.int32, (len(group), panel), 1)
        return table, counts, [table[:, s : s + 1] == block for s in range(slots)]

    lines = -(-cols // 8) * 8
    line = lax.broadcasted_iota(jnp.int32, (3 * lines, panel), 0)
    ids = lax.broadcasted_iota(jnp.int32, (1, panel), 1)
    asks = jnp.zeros((3 * lines, panel), jnp.float32)
    for group in groups:
        _, _, asked = read(group)
        some = jnp.where(functools.reduce(jnp.logical_or, asked), 1.0, 0.0).astype(jnp.bfloat16)
        shape = (3 * lines, len(group))
        number = lax.broadcasted_iota(jnp.int32, shape, 0)
        device = lax.broadcasted_iota(jnp.int32, shape, 1) + group.start
        core, side = device & (cols - 1), over(device, devices // 2)
        reads = (number == core) | (number == lines * (1 + side) + core)
        asks += jnp.dot(jnp.where(reads, 1.0, 0.0).astype(jnp.bfloat16), some, preferred_element_type=jnp.float32)
    own_half = (line >= lines) & (over(line - lines, lines) == over(lax.broadcasted_iota(jnp.int32, line.shape, 1), part))
    asks = jnp.where((asks > 0.5) & jnp.logical_not(own_half), 1.0, 0.0)
    first = lax.broadcasted_iota(jnp.int32, (panel, panel), 0)
    second = lax.broadcasted_iota(jnp.int32, (panel, panel), 1)
    after = first > second
    near = jnp.where(after & ((first ^ second) < per), 1.0, 0.0).astype(jnp.bfloat16)
    after = jnp.where(after, 1.0, 0.0).astype(jnp.bfloat16)
    same = jnp.where(first == second, 1.0, 0.0).astype(jnp.bfloat16)
    nt = (((1,), (1,)), ((), ()))

    def ranks(a, b):
        return lax.dot_general(a, b, nt, preferred_element_type=jnp.float32)

    short = asks.astype(jnp.bfloat16)
    near_rank = ranks(short, near)
    far_rank = ranks(short, after)
    longest = jnp.max(jnp.where(line < lines, near_rank + asks, 0.0)).astype(jnp.int32)
    level_refs[0][0] = sum((longest > level).astype(jnp.int32) for level in within)
    longest = jnp.max(jnp.where(line < lines, 0.0, far_rank + asks)).astype(jnp.int32)
    level_refs[1][0] = sum((longest > level).astype(jnp.int32) for level in across)
    me = lax.axis_index("rows")
    half, c = over(me, rows // 2), lax.axis_index("cols")

    def row(values, number):
        return jnp.sum(jnp.where(line == number, values, 0.0), axis=0, keepdims=True)

    here = (ids & -per) - half * part + row(near_rank, c).astype(jnp.int32)
    there = part + row(far_rank, lines * (1 + half) + c).astype(jnp.int32)
    place = jnp.where(over(ids, part) == half, here, there)
    chosen = jnp.zeros(places_ref.shape, jnp.float32)
    for group in groups:
        table, _, asked = read(group)
        lane = lax.broadcasted_iota(jnp.int32, table.shape, 1)
        places = jnp.zeros(table.shape, jnp.int32)
        for s in range(slots):
            found = jnp.sum(jnp.where(asked[s], place, 0), axis=1, keepdims=True)
            places = jnp.where(lane == s, found, places)
        shape = (places_ref.shape[0], len(group))
        number = lax.broadcasted_iota(jnp.int32, shape, 0)
        device = lax.broadcasted_iota(jnp.int32, shape, 1) + group.start
        reads = functools.reduce(
            jnp.logical_or,
            [(number == i) & (device == (me ^ d) * cols + c) for i, d in enumerate(distances(shape[0]))],
        )
        chosen += jnp.dot(
            jnp.where(reads, 1.0, 0.0).astype(jnp.bfloat16),
            places.astype(jnp.float32).astype(jnp.bfloat16),
            preferred_element_type=jnp.float32,
        )
    places_ref[...] = chosen.astype(jnp.int32)
    line = lax.broadcasted_iota(jnp.int32, (panel, 3 * lines), 1)

    def column(values, number):
        return jnp.sum(jnp.where(line == number, values, 0.0), axis=1, keepdims=True)

    turned, near_rank, far_rank = ranks(same, short), ranks(near, short), ranks(after, short)
    ids = lax.broadcasted_iota(jnp.int32, (panel, 1), 0)
    number = lax.broadcasted_iota(jnp.int32, (panel, lists_ref.shape[1]), 1)
    near_rank = column(near_rank, c).astype(jnp.int32)
    here = (ids & -per) - half * part + near_rank
    other = lines * (2 - half) + c
    sent = (column(turned, other) > 0.5) & (column(far_rank, other).astype(jnp.int32) == number)
    sent = jnp.sum(jnp.where(sent, here, 0), axis=0, keepdims=True)
    kept = (column(turned, c) > 0.5) & (over(ids, per) == me) & (near_rank == number)
    kept = jnp.sum(jnp.where(kept, ids & (per - 1), 0), axis=0, keepdims=True)
    lists_ref[...] = jnp.where(lax.broadcasted_iota(jnp.int32, lists_ref.shape, 0) == 0, sent, kept)


def plan(table, slots, per, within, across):
    devices = table.shape[0]
    return pl.pallas_call(
        functools.partial(plan_kernel, slots, per, within, across),
        out_shape=(
            jax.ShapeDtypeStruct((lax.axis_size("rows") // 2, 128), jnp.int32),
            jax.ShapeDtypeStruct((8, 128), jnp.int32),
            jax.ShapeDtypeStruct((1,), jnp.int32),
            jax.ShapeDtypeStruct((1,), jnp.int32),
        ),
        in_specs=[VMEM],
        out_specs=(VMEM, VMEM, SMEM, SMEM),
        compiler_params=pltpu.CompilerParams(vmem_limit_bytes=48 * MIB),
        name="plan",
    )(table)


def distances(members):
    order = [0]
    for near in sorted(range(1, members), key=lambda d: (d.bit_count(), d)):
        far = (members - 1) ^ near
        if near not in order and far:
            order += [near, far]
    return [*order[:-2], members - 1, *order[-2:]] if members > 2 else list(range(members))


def turn_kernel(sketch_ref, out_ref):
    members = out_ref.shape[0]
    me = lax.axis_index("rows") % members
    for i, d in enumerate(distances(members)):
        out_ref[i] = sketch_ref[:, me ^ d]


def turn(sketch):
    blocks, members, height, columns = sketch.shape
    return pl.pallas_call(
        turn_kernel,
        out_shape=jax.ShapeDtypeStruct((members, blocks, height, columns), sketch.dtype),
        in_specs=[VMEM],
        out_specs=VMEM,
        compiler_params=pltpu.CompilerParams(vmem_limit_bytes=24 * MIB),
        cost_estimate=pl.CostEstimate(flops=0, bytes_accessed=4 * sketch.size, transcendentals=0),
        name="turn_stripes",
    )(sketch)


def cut_kernel(lists_ref, stripes_ref, *out_refs):
    for k in range(out_refs[0].shape[0]):
        for i, out_ref in enumerate(out_refs):
            out_ref[k] = stripes_ref[i, lists_ref[1, k]]


def cut(lists, stripes, count):
    members, _, height, columns = stripes.shape
    return pl.pallas_call(
        cut_kernel,
        out_shape=(jax.ShapeDtypeStruct((count, height, columns), stripes.dtype),) * members,
        in_specs=[SMEM, VMEM],
        out_specs=(VMEM,) * members,
        compiler_params=pltpu.CompilerParams(vmem_limit_bytes=24 * MIB),
        name="cut_stripes",
    )(lists, stripes)


def order_kernel(*refs):
    *stripe_refs, all_ref = refs
    members = len(stripe_refs)
    me = lax.axis_index("rows") % members
    per = all_ref.shape[0] // members
    for ref, d in zip(stripe_refs, distances(members)):
        all_ref[pl.ds((me ^ d) * per, ref.shape[0])] = ref[...]


def order(stripes, per):
    _, height, columns = stripes[0].shape
    return pl.pallas_call(
        order_kernel,
        out_shape=jax.ShapeDtypeStruct((len(stripes) * per, height, columns), stripes[0].dtype),
        in_specs=[VMEM] * len(stripes),
        out_specs=VMEM,
        compiler_params=pltpu.CompilerParams(vmem_limit_bytes=24 * MIB),
        name="order_stripes",
    )(*stripes)


def list_kernel(list_ref, all_ref, out_ref):
    for k in range(out_ref.shape[0]):
        out_ref[k] = all_ref[list_ref[0, k]]


def listed(numbers, stripes, count):
    return pl.pallas_call(
        list_kernel,
        out_shape=jax.ShapeDtypeStruct((count, *stripes.shape[1:]), stripes.dtype),
        in_specs=[SMEM, VMEM],
        out_specs=VMEM,
        compiler_params=pltpu.CompilerParams(vmem_limit_bytes=24 * MIB),
        name="listed_stripes",
    )(numbers, stripes)


def pick_kernel(places_ref, own_ref, other_ref, *refs):
    *out_refs, whole = refs
    here = own_ref.shape[0]
    whole[:here] = own_ref[...]
    whole[here:] = other_ref[...]
    for i, out_ref in enumerate(out_refs):
        for s in range(out_ref.shape[0]):
            out_ref[s] = whole[jnp.minimum(places_ref[i, s], whole.shape[0] - 1)]


def pick(places, own, other, slots, members):
    shape = own.shape[1:]
    return pl.pallas_call(
        pick_kernel,
        out_shape=(jax.ShapeDtypeStruct((slots, *shape), own.dtype),) * members,
        in_specs=[SMEM, VMEM, VMEM],
        out_specs=(VMEM,) * members,
        scratch_shapes=[pltpu.VMEM((own.shape[0] + other.shape[0], *shape), own.dtype)],
        compiler_params=pltpu.CompilerParams(vmem_limit_bytes=24 * MIB),
        name="pick_stripes",
    )(places, own, other)


def product_kernel(rows_ref, counts_ref, blocks_ref, chosen_ref, out_ref):
    slots, width, _ = blocks_ref.shape
    columns = out_ref.shape[1]
    out_ref[...] = jnp.zeros_like(out_ref)
    for s in range(slots):
        piece = chosen_ref[:, s].reshape(width, columns)
        product = jnp.dot(blocks_ref[s], piece, preferred_element_type=jnp.float32)
        at = pl.ds(pl.multiple_of(rows_ref[s] * width, width), width)
        out_ref[at, :] += jnp.where(s < counts_ref[0], product, 0.0)


def block_products(block_rows, counts, blocks, chosen):
    _, width, _ = blocks.shape
    columns = chosen.shape[-1]
    return pl.pallas_call(
        product_kernel,
        out_shape=jax.ShapeDtypeStruct((RB * width, columns), jnp.float32),
        in_specs=[SMEM, SMEM, VMEM, VMEM],
        out_specs=VMEM,
        compiler_params=pltpu.CompilerParams(vmem_limit_bytes=24 * MIB),
        name="block_products",
    )(block_rows, counts, blocks, chosen)


def gram_kernel(mine_ref, other_ref, own_ref, *refs):
    *gram_refs, slab = refs
    c = lax.axis_index("cols")
    me = lax.axis_index("rows") % len(gram_refs)
    share, (height, width) = own_ref.shape[0], gram_refs[0].shape
    slab[...] = mine_ref[...] + other_ref[...]
    own_ref[...] = slab[pl.ds(pl.multiple_of(c * share, share), share), :]
    right = slab[:, pl.ds(pl.multiple_of(c * width, width), width)]
    gram = lax.dot_general(
        slab[...], right, (((0,), (0,)), ((), ())), precision=HIGHEST, preferred_element_type=jnp.float32
    )
    for q in range(len(gram_refs)):
        for d in range(len(gram_refs)):

            @pl.when(me ^ d == q)
            def _():
                gram_refs[d][...] = gram[q * height : (q + 1) * height]


def sum_and_gram(mine, other):
    rows, columns = mine.shape
    return pl.pallas_call(
        gram_kernel,
        out_shape=(
            jax.ShapeDtypeStruct((rows // 2, columns), jnp.float32),
            *[jax.ShapeDtypeStruct((columns // 4, columns // 2), jnp.float32)] * 4,
        ),
        in_specs=[VMEM, VMEM],
        out_specs=(VMEM,) * 5,
        scratch_shapes=[pltpu.VMEM((rows, columns), jnp.float32)],
        compiler_params=pltpu.CompilerParams(vmem_limit_bytes=24 * MIB),
        name="sum_and_gram",
    )(mine, other)


def add_kernel(*refs):
    *piece_refs, out_ref = refs
    out_ref[...] = functools.reduce(jnp.add, [ref[...] for ref in piece_refs])


def add(pieces):
    return pl.pallas_call(
        add_kernel,
        out_shape=jax.ShapeDtypeStruct(pieces[0].shape, jnp.float32),
        in_specs=[VMEM] * len(pieces),
        out_specs=VMEM,
        compiler_params=pltpu.CompilerParams(vmem_limit_bytes=24 * MIB),
        name="add_pieces",
    )(*pieces)


def stack_kernel(*refs):
    *quarter_refs, out_ref = refs
    me = lax.axis_index("rows") % len(quarter_refs)
    height = quarter_refs[0].shape[0]
    for d, ref in enumerate(quarter_refs):
        out_ref[pl.ds(pl.multiple_of((me ^ d) * height, height), height), :] = ref[...]


def stack(quarters):
    height, width = quarters[0].shape
    return pl.pallas_call(
        stack_kernel,
        out_shape=jax.ShapeDtypeStruct((len(quarters) * height, width), jnp.float32),
        in_specs=[VMEM] * len(quarters),
        out_specs=VMEM,
        compiler_params=pltpu.CompilerParams(vmem_limit_bytes=24 * MIB),
        name="stack_quarters",
    )(*quarters)


def matmul(a, b, precision):
    return jnp.dot(a, b, precision=precision, preferred_element_type=jnp.float32)


def matmul_nt(a, b, precision):
    return lax.dot_general(
        a, b, (((1,), (1,)), ((), ())), precision=precision, preferred_element_type=jnp.float32
    )


def split_matmul(times, passes, a, b):
    a_high, b_high = a.astype(jnp.bfloat16), b.astype(jnp.bfloat16)
    result = times(a_high, b_high, None)
    if passes == 3:
        a_low = (a - a_high.astype(jnp.float32)).astype(jnp.bfloat16)
        b_low = (b - b_high.astype(jnp.float32)).astype(jnp.bfloat16)
        result += times(a_high, b_low, None) + times(a_low, b_high, None)
    return result


def factor_kernel(total_rows, *refs):
    *gram_refs, own_ref, basis_ref, factor_ref, whole, scaled, inverse, product = refs
    n = factor_ref.shape[0]
    if len(gram_refs) == 1:
        whole[...] = gram_refs[0][...]
    else:
        c = lax.axis_index("cols")
        width = n // 2
        whole[:, pl.ds(pl.multiple_of(c * width, width), width)] = gram_refs[0][...]
        whole[:, pl.ds(pl.multiple_of((1 - c) * width, width), width)] = gram_refs[1][...]
    row_ids = lax.broadcasted_iota(jnp.int32, (n, n), 0)
    col_ids = lax.broadcasted_iota(jnp.int32, (n, n), 1)
    diagonal = row_ids == col_ids
    identity = diagonal.astype(jnp.float32)
    half = jnp.where(row_ids > col_ids, 1.0, jnp.where(diagonal, 0.5, 0.0))
    gram = whole[...]
    on_diagonal = jnp.where(diagonal, gram, 0.0)
    down = jnp.sqrt(jnp.sum(on_diagonal, axis=1, keepdims=True))
    across = jnp.sqrt(jnp.sum(on_diagonal, axis=0, keepdims=True))
    up_down = 1.0 / down
    up_across = 1.0 / across
    scaled[...] = gram * up_down * up_across

    def refine(times, times_nt, last=False):
        w = inverse[...]
        upper = times(w, scaled[...])
        residual = times_nt(upper, w) - identity
        step = residual * half
        inverse[...] = w - matmul(step, w, lax.Precision.DEFAULT)
        if last:
            product[...] = upper - matmul(step, upper, lax.Precision.DEFAULT)
        return jnp.sum(residual * residual)

    def exactly(times):
        return functools.partial(times, precision=HIGHEST)

    inverse[...] = identity - (scaled[...] - identity) * half
    for passes in (1, 3):
        refine(functools.partial(split_matmul, matmul, passes), functools.partial(split_matmul, matmul_nt, passes))

    def going(state):
        step, size = state
        return (step < 8) & (size > 1e-6)

    def advance(state):
        return state[0] + 1, refine(exactly(matmul), exactly(matmul_nt), last=True)

    _, size = lax.while_loop(going, advance, (jnp.int32(0), jnp.float32(1.0)))

    @pl.when(jnp.logical_not(size <= 1e-6))
    def _():
        inverse[...] = identity
        ids = lax.broadcasted_iota(jnp.int32, (n, 1), 0)

        def eliminate(j, carry):
            pivot_row = scaled[pl.ds(j, 1), :]
            inverse_row = inverse[pl.ds(j, 1), :]
            column = jnp.sum(jnp.where(col_ids == j, scaled[...], 0.0), axis=1, keepdims=True)
            pivot = jnp.sum(jnp.where(ids == j, column, 0.0), axis=0, keepdims=True)
            root = 1.0 / jnp.sqrt(pivot)
            ratio = jnp.where(ids > j, column / pivot, jnp.where(ids == j, 1.0 - root, 0.0))
            scaled[...] = scaled[...] - ratio * pivot_row
            inverse[...] = inverse[...] - ratio * inverse_row
            return carry

        lax.fori_loop(0, n, eliminate, 0)
        product[...] = matmul(inverse[...], whole[...] * up_down * up_across, HIGHEST)

    w = inverse[...]
    root_rows = jnp.sqrt(jnp.float32(total_rows))
    upper = product[...] * across / root_rows
    factor_ref[...] = jnp.where(row_ids <= col_ids, upper, 0.0)
    basis_ref[...] = matmul_nt(own_ref[...] * up_across, w, HIGHEST) * root_rows


def factor_and_basis(total_rows, grams, own):
    columns = own.shape[1]
    return pl.pallas_call(
        functools.partial(factor_kernel, total_rows),
        out_shape=(
            jax.ShapeDtypeStruct(own.shape, jnp.float32),
            jax.ShapeDtypeStruct((columns, columns), jnp.float32),
        ),
        in_specs=[VMEM] * (len(grams) + 1),
        out_specs=(VMEM, VMEM),
        scratch_shapes=[pltpu.VMEM((columns, columns), jnp.float32)] * 4,
        compiler_params=pltpu.CompilerParams(vmem_limit_bytes=24 * MIB),
        name="factor_and_basis",
    )(*grams, own)


def exchange(pieces, rows):
    order = distances(len(pieces))
    return [
        lax.ppermute(piece, "rows", [(r, r ^ d) for r in range(rows)]) if d else piece
        for piece, d in zip(pieces, order)
    ]


def fetch(sketch, block_cols, counts, slots, width):
    rows, cols = lax.axis_size("rows"), lax.axis_size("cols")
    members = rows // 2
    height = width // members
    columns = sketch.shape[1]
    sketch = sketch.reshape(-1, members, height, columns)
    per = sketch.shape[0]
    largest = min(per * members, slots * members, 128)
    within = tuple(level for level in WITHIN if level < per)
    across = tuple(level for level in ACROSS if level < largest and members <= 8)
    stripes = turn(sketch)
    table = table_copies(block_cols, counts, rows * cols)
    table = lax.all_to_all(table, ("rows", "cols"), split_axis=0, concat_axis=0, tiled=True)
    places, lists, near, far = plan(table, slots, per, within, across)

    def within_half(count):
        def run():
            return order(exchange(cut(lists, stripes, count), rows), per)

        return run

    own = lax.switch(near[0], [within_half(count) for count in (*within, per)])

    def across_halves(count):
        def run():
            swap = [(r, (r + members) % rows) for r in range(rows)]
            other = lax.ppermute(listed(lists, own, count), "rows", swap)
            return order(exchange(pick(places, own, other, slots, members), rows), slots)

        return run

    chosen = lax.switch(far[0], [across_halves(count) for count in (*across, largest)])
    return chosen.reshape(members, slots, height, columns)


def moved(piece, rows, d):
    return lax.ppermute(piece, "rows", [(r, r ^ d) for r in range(rows)])


def gram_halves(quarters, rows):
    first = add([quarters[0]] + [moved(quarters[d], rows, d) for d in (3, 1, 2)])
    total = (first + moved(first, rows, 4)) + (moved(first, rows, 8) + moved(first, rows, 12))
    half = stack([total] + [moved(total, rows, d) for d in range(1, 4)])
    return half, lax.ppermute(half, "cols", [(0, 1), (1, 0)])


def local(sketch, blocks, block_rows, block_cols, counts):
    slots, width, _ = blocks.shape
    columns = sketch.shape[1]
    rows, cols = lax.axis_size("rows"), lax.axis_size("cols")
    chosen = fetch(sketch, block_cols, counts, slots, width)
    if chosen.shape[2] % 16:
        chosen = chosen.swapaxes(0, 1).reshape(1, slots, width, columns)
    partial_rows = block_products(block_rows, counts, blocks, chosen)
    if (rows, cols) == (16, 2):
        other = lax.ppermute(partial_rows, "cols", [(0, 1), (1, 0)])
        own, *quarters = sum_and_gram(partial_rows, other)
        grams = gram_halves(quarters, rows)
    else:
        own = lax.psum_scatter(partial_rows, "cols", scatter_dimension=0, tiled=True)
        grams = [lax.psum(matmul(own.T, own, HIGHEST), ("rows", "cols"))]
    return factor_and_basis(RB * width * rows, grams, own)


def solution(mesh):
    in_specs = (
        P(("rows", "cols"), None),
        P(("rows", "cols"), None, None),
        P(("rows", "cols")),
        P(("rows", "cols")),
        P(("rows", "cols")),
    )
    out_specs = (P(("rows", "cols"), None), P())
    return jax.shard_map(local, mesh=mesh, in_specs=in_specs, out_specs=out_specs, check_vma=False)
```

```python
import functools

import jax
import jax.numpy as jnp
from jax import lax
from jax.experimental import pallas as pl
from jax.experimental.pallas import tpu as pltpu
from jax.sharding import PartitionSpec as P

RB = 4
HIGHEST = lax.Precision.HIGHEST
VMEM = pl.BlockSpec(memory_space=pltpu.VMEM)
SMEM = pl.BlockSpec(memory_space=pltpu.SMEM)
MIB = 1024 * 1024


ACROSS = (*range(11, 21), 22, 24, 28, 36)
WITHIN = (5, 6, 7, 8, 9, 10, 12)


def table_kernel(cols_ref, counts_ref, out_ref):
    slots = cols_ref.shape[0]
    lane = lax.broadcasted_iota(jnp.int32, out_ref.shape, 2)
    table = jnp.where(lane == slots, counts_ref[0], 0)
    for s in range(slots):
        table = jnp.where(lane == s, cols_ref[s], table)
    out_ref[...] = table


def table_copies(block_cols, counts, devices):
    return pl.pallas_call(
        table_kernel,
        out_shape=jax.ShapeDtypeStruct((devices, 1, 128), jnp.int32),
        in_specs=[SMEM, SMEM],
        out_specs=VMEM,
        name="table_copies",
    )(block_cols, counts)


def over(values, size):
    return values >> (size.bit_length() - 1)


def plan_kernel(slots, per, within, across, table_ref, places_ref, lists_ref, *level_refs):
    devices = table_ref.shape[0]
    rows, cols = lax.axis_size("rows"), lax.axis_size("cols")
    panel = per * rows
    part = panel // 2
    groups = [range(at, min(at + 64, devices)) for at in range(0, devices, 64)]

    def read(group):
        table = table_ref[group.start : group.stop, 0, :]
        lane = lax.broadcasted_iota(jnp.int32, table.shape, 1)
        counts = table[:, slots : slots + 1]
        table = jnp.where(lane < counts, table, -1)
        block = lax.broadcasted_iota(jnp.int32, (len(group), panel), 1)
        return table, counts, [table[:, s : s + 1] == block for s in range(slots)]

    lines = -(-cols // 8) * 8
    line = lax.broadcasted_iota(jnp.int32, (3 * lines, panel), 0)
    ids = lax.broadcasted_iota(jnp.int32, (1, panel), 1)
    asks = jnp.zeros((3 * lines, panel), jnp.float32)
    for group in groups:
        _, _, asked = read(group)
        some = jnp.where(functools.reduce(jnp.logical_or, asked), 1.0, 0.0).astype(jnp.bfloat16)
        shape = (3 * lines, len(group))
        number = lax.broadcasted_iota(jnp.int32, shape, 0)
        device = lax.broadcasted_iota(jnp.int32, shape, 1) + group.start
        core, side = device & (cols - 1), over(device, devices // 2)
        reads = (number == core) | (number == lines * (1 + side) + core)
        asks += jnp.dot(jnp.where(reads, 1.0, 0.0).astype(jnp.bfloat16), some, preferred_element_type=jnp.float32)
    own_half = (line >= lines) & (over(line - lines, lines) == over(lax.broadcasted_iota(jnp.int32, line.shape, 1), part))
    asks = jnp.where((asks > 0.5) & jnp.logical_not(own_half), 1.0, 0.0)
    first = lax.broadcasted_iota(jnp.int32, (panel, panel), 0)
    second = lax.broadcasted_iota(jnp.int32, (panel, panel), 1)
    after = first > second
    near = jnp.where(after & ((first ^ second) < per), 1.0, 0.0).astype(jnp.bfloat16)
    after = jnp.where(after, 1.0, 0.0).astype(jnp.bfloat16)
    same = jnp.where(first == second, 1.0, 0.0).astype(jnp.bfloat16)
    nt = (((1,), (1,)), ((), ()))

    def ranks(a, b):
        return lax.dot_general(a, b, nt, preferred_element_type=jnp.float32)

    short = asks.astype(jnp.bfloat16)
    near_rank = ranks(short, near)
    far_rank = ranks(short, after)
    longest = jnp.max(jnp.where(line < lines, near_rank + asks, 0.0)).astype(jnp.int32)
    level_refs[0][0] = sum((longest > level).astype(jnp.int32) for level in within)
    longest = jnp.max(jnp.where(line < lines, 0.0, far_rank + asks)).astype(jnp.int32)
    level_refs[1][0] = sum((longest > level).astype(jnp.int32) for level in across)
    me = lax.axis_index("rows")
    half, c = over(me, rows // 2), lax.axis_index("cols")

    def row(values, number):
        return jnp.sum(jnp.where(line == number, values, 0.0), axis=0, keepdims=True)

    here = (ids & -per) - half * part + row(near_rank, c).astype(jnp.int32)
    there = part + row(far_rank, lines * (1 + half) + c).astype(jnp.int32)
    place = jnp.where(over(ids, part) == half, here, there)
    chosen = jnp.zeros(places_ref.shape, jnp.float32)
    for group in groups:
        table, _, asked = read(group)
        lane = lax.broadcasted_iota(jnp.int32, table.shape, 1)
        places = jnp.zeros(table.shape, jnp.int32)
        for s in range(slots):
            found = jnp.sum(jnp.where(asked[s], place, 0), axis=1, keepdims=True)
            places = jnp.where(lane == s, found, places)
        shape = (places_ref.shape[0], len(group))
        number = lax.broadcasted_iota(jnp.int32, shape, 0)
        device = lax.broadcasted_iota(jnp.int32, shape, 1) + group.start
        reads = functools.reduce(
            jnp.logical_or,
            [(number == i) & (device == (me ^ d) * cols + c) for i, d in enumerate(distances(shape[0]))],
        )
        chosen += jnp.dot(
            jnp.where(reads, 1.0, 0.0).astype(jnp.bfloat16),
            places.astype(jnp.float32).astype(jnp.bfloat16),
            preferred_element_type=jnp.float32,
        )
    places_ref[...] = chosen.astype(jnp.int32)
    line = lax.broadcasted_iota(jnp.int32, (panel, 3 * lines), 1)

    def column(values, number):
        return jnp.sum(jnp.where(line == number, values, 0.0), axis=1, keepdims=True)

    turned, near_rank, far_rank = ranks(same, short), ranks(near, short), ranks(after, short)
    ids = lax.broadcasted_iota(jnp.int32, (panel, 1), 0)
    number = lax.broadcasted_iota(jnp.int32, (panel, lists_ref.shape[1]), 1)
    near_rank = column(near_rank, c).astype(jnp.int32)
    here = (ids & -per) - half * part + near_rank
    other = lines * (2 - half) + c
    sent = (column(turned, other) > 0.5) & (column(far_rank, other).astype(jnp.int32) == number)
    sent = jnp.sum(jnp.where(sent, here, 0), axis=0, keepdims=True)
    kept = (column(turned, c) > 0.5) & (over(ids, per) == me) & (near_rank == number)
    kept = jnp.sum(jnp.where(kept, ids & (per - 1), 0), axis=0, keepdims=True)
    lists_ref[...] = jnp.where(lax.broadcasted_iota(jnp.int32, lists_ref.shape, 0) == 0, sent, kept)


def plan(table, slots, per, within, across):
    devices = table.shape[0]
    return pl.pallas_call(
        functools.partial(plan_kernel, slots, per, within, across),
        out_shape=(
            jax.ShapeDtypeStruct((lax.axis_size("rows") // 2, 128), jnp.int32),
            jax.ShapeDtypeStruct((8, 128), jnp.int32),
            jax.ShapeDtypeStruct((1,), jnp.int32),
            jax.ShapeDtypeStruct((1,), jnp.int32),
        ),
        in_specs=[VMEM],
        out_specs=(VMEM, VMEM, SMEM, SMEM),
        compiler_params=pltpu.CompilerParams(vmem_limit_bytes=48 * MIB),
        name="plan",
    )(table)


def distances(members):
    order = [0]
    for near in sorted(range(1, members), key=lambda d: (d.bit_count(), d)):
        far = (members - 1) ^ near
        if near not in order and far:
            order += [near, far]
    return [*order[:3], members - 1, *order[3:]] if members > 2 else list(range(members))


def turn_kernel(sketch_ref, out_ref):
    members = out_ref.shape[0]
    me = lax.axis_index("rows") % members
    for i, d in enumerate(distances(members)):
        out_ref[i] = sketch_ref[:, me ^ d]


def turn(sketch):
    blocks, members, height, columns = sketch.shape
    return pl.pallas_call(
        turn_kernel,
        out_shape=jax.ShapeDtypeStruct((members, blocks, height, columns), sketch.dtype),
        in_specs=[VMEM],
        out_specs=VMEM,
        compiler_params=pltpu.CompilerParams(vmem_limit_bytes=24 * MIB),
        cost_estimate=pl.CostEstimate(flops=0, bytes_accessed=4 * sketch.size, transcendentals=0),
        name="turn_stripes",
    )(sketch)


def cut_kernel(lists_ref, stripes_ref, *out_refs):
    for k in range(out_refs[0].shape[0]):
        for i, out_ref in enumerate(out_refs):
            out_ref[k] = stripes_ref[i, lists_ref[1, k]]


def cut(lists, stripes, count):
    members, _, height, columns = stripes.shape
    return pl.pallas_call(
        cut_kernel,
        out_shape=(jax.ShapeDtypeStruct((count, height, columns), stripes.dtype),) * members,
        in_specs=[SMEM, VMEM],
        out_specs=(VMEM,) * members,
        compiler_params=pltpu.CompilerParams(vmem_limit_bytes=24 * MIB),
        name="cut_stripes",
    )(lists, stripes)


def order_kernel(*refs):
    *stripe_refs, all_ref = refs
    members = len(stripe_refs)
    me = lax.axis_index("rows") % members
    per = all_ref.shape[0] // members
    for ref, d in zip(stripe_refs, distances(members)):
        all_ref[pl.ds((me ^ d) * per, ref.shape[0])] = ref[...]


def order(stripes, per):
    _, height, columns = stripes[0].shape
    return pl.pallas_call(
        order_kernel,
        out_shape=jax.ShapeDtypeStruct((len(stripes) * per, height, columns), stripes[0].dtype),
        in_specs=[VMEM] * len(stripes),
        out_specs=VMEM,
        compiler_params=pltpu.CompilerParams(vmem_limit_bytes=24 * MIB),
        name="order_stripes",
    )(*stripes)


def list_kernel(list_ref, all_ref, out_ref):
    for k in range(out_ref.shape[0]):
        out_ref[k] = all_ref[list_ref[0, k]]


def listed(numbers, stripes, count):
    return pl.pallas_call(
        list_kernel,
        out_shape=jax.ShapeDtypeStruct((count, *stripes.shape[1:]), stripes.dtype),
        in_specs=[SMEM, VMEM],
        out_specs=VMEM,
        compiler_params=pltpu.CompilerParams(vmem_limit_bytes=24 * MIB),
        name="listed_stripes",
    )(numbers, stripes)


def pick_kernel(places_ref, own_ref, other_ref, *refs):
    *out_refs, whole = refs
    here = own_ref.shape[0]
    whole[:here] = own_ref[...]
    whole[here:] = other_ref[...]
    for i, out_ref in enumerate(out_refs):
        for s in range(out_ref.shape[0]):
            out_ref[s] = whole[jnp.minimum(places_ref[i, s], whole.shape[0] - 1)]


def pick(places, own, other, slots, members):
    shape = own.shape[1:]
    return pl.pallas_call(
        pick_kernel,
        out_shape=(jax.ShapeDtypeStruct((slots, *shape), own.dtype),) * members,
        in_specs=[SMEM, VMEM, VMEM],
        out_specs=(VMEM,) * members,
        scratch_shapes=[pltpu.VMEM((own.shape[0] + other.shape[0], *shape), own.dtype)],
        compiler_params=pltpu.CompilerParams(vmem_limit_bytes=24 * MIB),
        name="pick_stripes",
    )(places, own, other)


def product_kernel(rows_ref, counts_ref, blocks_ref, chosen_ref, out_ref):
    slots, width, _ = blocks_ref.shape
    columns = out_ref.shape[1]
    out_ref[...] = jnp.zeros_like(out_ref)
    for s in range(slots):
        piece = chosen_ref[:, s].reshape(width, columns)
        product = jnp.dot(blocks_ref[s], piece, preferred_element_type=jnp.float32)
        at = pl.ds(pl.multiple_of(rows_ref[s] * width, width), width)
        out_ref[at, :] += jnp.where(s < counts_ref[0], product, 0.0)


def block_products(block_rows, counts, blocks, chosen):
    _, width, _ = blocks.shape
    columns = chosen.shape[-1]
    return pl.pallas_call(
        product_kernel,
        out_shape=jax.ShapeDtypeStruct((RB * width, columns), jnp.float32),
        in_specs=[SMEM, SMEM, VMEM, VMEM],
        out_specs=VMEM,
        compiler_params=pltpu.CompilerParams(vmem_limit_bytes=24 * MIB),
        name="block_products",
    )(block_rows, counts, blocks, chosen)


def gram_kernel(mine_ref, other_ref, own_ref, *refs):
    *gram_refs, slab = refs
    c = lax.axis_index("cols")
    me = lax.axis_index("rows") % len(gram_refs)
    share, (height, width) = own_ref.shape[0], gram_refs[0].shape
    slab[...] = mine_ref[...] + other_ref[...]
    own_ref[...] = slab[pl.ds(pl.multiple_of(c * share, share), share), :]
    right = slab[:, pl.ds(pl.multiple_of(c * width, width), width)]
    gram = lax.dot_general(
        slab[...], right, (((0,), (0,)), ((), ())), precision=HIGHEST, preferred_element_type=jnp.float32
    )
    for q in range(len(gram_refs)):
        for d in range(len(gram_refs)):

            @pl.when(me ^ d == q)
            def _():
                gram_refs[d][...] = gram[q * height : (q + 1) * height]


def sum_and_gram(mine, other):
    rows, columns = mine.shape
    return pl.pallas_call(
        gram_kernel,
        out_shape=(
            jax.ShapeDtypeStruct((rows // 2, columns), jnp.float32),
            *[jax.ShapeDtypeStruct((columns // 4, columns // 2), jnp.float32)] * 4,
        ),
        in_specs=[VMEM, VMEM],
        out_specs=(VMEM,) * 5,
        scratch_shapes=[pltpu.VMEM((rows, columns), jnp.float32)],
        compiler_params=pltpu.CompilerParams(vmem_limit_bytes=24 * MIB),
        name="sum_and_gram",
    )(mine, other)


def add_kernel(*refs):
    *piece_refs, out_ref = refs
    out_ref[...] = functools.reduce(jnp.add, [ref[...] for ref in piece_refs])


def add(pieces):
    return pl.pallas_call(
        add_kernel,
        out_shape=jax.ShapeDtypeStruct(pieces[0].shape, jnp.float32),
        in_specs=[VMEM] * len(pieces),
        out_specs=VMEM,
        compiler_params=pltpu.CompilerParams(vmem_limit_bytes=24 * MIB),
        name="add_pieces",
    )(*pieces)


def stack_kernel(*refs):
    *quarter_refs, out_ref = refs
    me = lax.axis_index("rows") % len(quarter_refs)
    height = quarter_refs[0].shape[0]
    for d, ref in enumerate(quarter_refs):
        out_ref[pl.ds(pl.multiple_of((me ^ d) * height, height), height), :] = ref[...]


def stack(quarters):
    height, width = quarters[0].shape
    return pl.pallas_call(
        stack_kernel,
        out_shape=jax.ShapeDtypeStruct((len(quarters) * height, width), jnp.float32),
        in_specs=[VMEM] * len(quarters),
        out_specs=VMEM,
        compiler_params=pltpu.CompilerParams(vmem_limit_bytes=24 * MIB),
        name="stack_quarters",
    )(*quarters)


def matmul(a, b, precision):
    return jnp.dot(a, b, precision=precision, preferred_element_type=jnp.float32)


def matmul_nt(a, b, precision):
    return lax.dot_general(
        a, b, (((1,), (1,)), ((), ())), precision=precision, preferred_element_type=jnp.float32
    )


def split_matmul(times, passes, a, b):
    a_high, b_high = a.astype(jnp.bfloat16), b.astype(jnp.bfloat16)
    result = times(a_high, b_high, None)
    if passes == 3:
        a_low = (a - a_high.astype(jnp.float32)).astype(jnp.bfloat16)
        b_low = (b - b_high.astype(jnp.float32)).astype(jnp.bfloat16)
        result += times(a_high, b_low, None) + times(a_low, b_high, None)
    return result


def factor_kernel(total_rows, *refs):
    *gram_refs, own_ref, basis_ref, factor_ref, whole, scaled, inverse, product = refs
    n = factor_ref.shape[0]
    if len(gram_refs) == 1:
        whole[...] = gram_refs[0][...]
    else:
        c = lax.axis_index("cols")
        width = n // 2
        whole[:, pl.ds(pl.multiple_of(c * width, width), width)] = gram_refs[0][...]
        whole[:, pl.ds(pl.multiple_of((1 - c) * width, width), width)] = gram_refs[1][...]
    row_ids = lax.broadcasted_iota(jnp.int32, (n, n), 0)
    col_ids = lax.broadcasted_iota(jnp.int32, (n, n), 1)
    diagonal = row_ids == col_ids
    identity = diagonal.astype(jnp.float32)
    half = jnp.where(row_ids > col_ids, 1.0, jnp.where(diagonal, 0.5, 0.0))
    gram = whole[...]
    on_diagonal = jnp.where(diagonal, gram, 0.0)
    down = jnp.sqrt(jnp.sum(on_diagonal, axis=1, keepdims=True))
    across = jnp.sqrt(jnp.sum(on_diagonal, axis=0, keepdims=True))
    up_down = 1.0 / down
    up_across = 1.0 / across
    scaled[...] = gram * up_down * up_across

    def refine(times, times_nt, last=False):
        w = inverse[...]
        upper = times(w, scaled[...])
        residual = times_nt(upper, w) - identity
        step = residual * half
        inverse[...] = w - matmul(step, w, lax.Precision.DEFAULT)
        if last:
            product[...] = upper - matmul(step, upper, lax.Precision.DEFAULT)
        return jnp.sum(residual * residual)

    def exactly(times):
        return functools.partial(times, precision=HIGHEST)

    inverse[...] = identity - (scaled[...] - identity) * half
    for passes in (1, 3):
        refine(functools.partial(split_matmul, matmul, passes), functools.partial(split_matmul, matmul_nt, passes))

    def going(state):
        step, size = state
        return (step < 8) & (size > 1e-6)

    def advance(state):
        return state[0] + 1, refine(exactly(matmul), exactly(matmul_nt), last=True)

    _, size = lax.while_loop(going, advance, (jnp.int32(0), jnp.float32(1.0)))

    @pl.when(jnp.logical_not(size <= 1e-6))
    def _():
        inverse[...] = identity
        ids = lax.broadcasted_iota(jnp.int32, (n, 1), 0)

        def eliminate(j, carry):
            pivot_row = scaled[pl.ds(j, 1), :]
            inverse_row = inverse[pl.ds(j, 1), :]
            column = jnp.sum(jnp.where(col_ids == j, scaled[...], 0.0), axis=1, keepdims=True)
            pivot = jnp.sum(jnp.where(ids == j, column, 0.0), axis=0, keepdims=True)
            root = 1.0 / jnp.sqrt(pivot)
            ratio = jnp.where(ids > j, column / pivot, jnp.where(ids == j, 1.0 - root, 0.0))
            scaled[...] = scaled[...] - ratio * pivot_row
            inverse[...] = inverse[...] - ratio * inverse_row
            return carry

        lax.fori_loop(0, n, eliminate, 0)
        product[...] = matmul(inverse[...], whole[...] * up_down * up_across, HIGHEST)

    w = inverse[...]
    root_rows = jnp.sqrt(jnp.float32(total_rows))
    upper = product[...] * across / root_rows
    factor_ref[...] = jnp.where(row_ids <= col_ids, upper, 0.0)
    basis_ref[...] = matmul_nt(own_ref[...] * up_across, w, HIGHEST) * root_rows


def factor_and_basis(total_rows, grams, own):
    columns = own.shape[1]
    return pl.pallas_call(
        functools.partial(factor_kernel, total_rows),
        out_shape=(
            jax.ShapeDtypeStruct(own.shape, jnp.float32),
            jax.ShapeDtypeStruct((columns, columns), jnp.float32),
        ),
        in_specs=[VMEM] * (len(grams) + 1),
        out_specs=(VMEM, VMEM),
        scratch_shapes=[pltpu.VMEM((columns, columns), jnp.float32)] * 4,
        compiler_params=pltpu.CompilerParams(vmem_limit_bytes=24 * MIB),
        name="factor_and_basis",
    )(*grams, own)


def exchange(pieces, rows):
    order = distances(len(pieces))
    return [
        lax.ppermute(piece, "rows", [(r, r ^ d) for r in range(rows)]) if d else piece
        for piece, d in zip(pieces, order)
    ]


def fetch(sketch, block_cols, counts, slots, width):
    rows, cols = lax.axis_size("rows"), lax.axis_size("cols")
    members = rows // 2
    height = width // members
    columns = sketch.shape[1]
    sketch = sketch.reshape(-1, members, height, columns)
    per = sketch.shape[0]
    largest = min(per * members, slots * members, 128)
    within = tuple(level for level in WITHIN if level < per)
    across = tuple(level for level in ACROSS if level < largest and members <= 8)
    stripes = turn(sketch)
    table = table_copies(block_cols, counts, rows * cols)
    table = lax.all_to_all(table, ("rows", "cols"), split_axis=0, concat_axis=0, tiled=True)
    places, lists, near, far = plan(table, slots, per, within, across)

    def within_half(count):
        def run():
            return order(exchange(cut(lists, stripes, count), rows), per)

        return run

    own = lax.switch(near[0], [within_half(count) for count in (*within, per)])

    def across_halves(count):
        def run():
            swap = [(r, (r + members) % rows) for r in range(rows)]
            other = lax.ppermute(listed(lists, own, count), "rows", swap)
            return order(exchange(pick(places, own, other, slots, members), rows), slots)

        return run

    chosen = lax.switch(far[0], [across_halves(count) for count in (*across, largest)])
    return chosen.reshape(members, slots, height, columns)


def moved(piece, rows, d):
    return lax.ppermute(piece, "rows", [(r, r ^ d) for r in range(rows)])


def gram_halves(quarters, rows):
    first = add([quarters[0]] + [moved(quarters[d], rows, d) for d in (3, 1, 2)])
    total = (first + moved(first, rows, 4)) + (moved(first, rows, 8) + moved(first, rows, 12))
    half = stack([total] + [moved(total, rows, d) for d in range(1, 4)])
    return half, lax.ppermute(half, "cols", [(0, 1), (1, 0)])


def local(sketch, blocks, block_rows, block_cols, counts):
    slots, width, _ = blocks.shape
    columns = sketch.shape[1]
    rows, cols = lax.axis_size("rows"), lax.axis_size("cols")
    chosen = fetch(sketch, block_cols, counts, slots, width)
    if chosen.shape[2] % 16:
        chosen = chosen.swapaxes(0, 1).reshape(1, slots, width, columns)
    partial_rows = block_products(block_rows, counts, blocks, chosen)
    if (rows, cols) == (16, 2):
        other = lax.ppermute(partial_rows, "cols", [(0, 1), (1, 0)])
        own, *quarters = sum_and_gram(partial_rows, other)
        grams = gram_halves(quarters, rows)
    else:
        own = lax.psum_scatter(partial_rows, "cols", scatter_dimension=0, tiled=True)
        grams = [lax.psum(matmul(own.T, own, HIGHEST), ("rows", "cols"))]
    return factor_and_basis(RB * width * rows, grams, own)


def solution(mesh):
    in_specs = (
        P(("rows", "cols"), None),
        P(("rows", "cols"), None, None),
        P(("rows", "cols")),
        P(("rows", "cols")),
        P(("rows", "cols")),
    )
    out_specs = (P(("rows", "cols"), None), P())
    return jax.shard_map(local, mesh=mesh, in_specs=in_specs, out_specs=out_specs, check_vma=False)
```
